32 devices in a mesh: seq: 8 (over z, core), tp: 4 (over y, x).
Axes of the slice: x: 2, y: 2, z: 4, core: 2. Of those that a mesh axis runs over, the one named last changes fastest.
Arguments:
- tokens: bfloat16 [96, 6, 32, 1024], P('seq'), may hold values from -6 to 6
- context: bfloat16 [4096, 6, 768], replicated, may hold values from -6 to 6
- group_ids: int32 [6], replicated, may hold values from 0 to 15
- source_table: float32 [16, 9216], replicated, may hold values from -3 to 3
- w_query: bfloat16 [1024, 1024], P(None, 'tp'), may hold values from -0.1875 to 0.1875
- w_key: bfloat16 [768, 1024], P(None, 'tp'), may hold values from -0.21875 to 0.21875
- w_value: bfloat16 [768, 1024], P(None, 'tp'), may hold values from -0.21875 to 0.21875
- w_out: bfloat16 [1024, 1024], P('tp'), may hold values from -4 to 4
- w_self_query: bfloat16 [1024, 1024], P(None, 'tp'), may hold values from -0.1875 to 0.1875
- w_self_key: bfloat16 [1024, 1024], P(None, 'tp'), may hold values from -0.1875 to 0.1875
- w_self_value: bfloat16 [1024, 1024], P(None, 'tp'), may hold values from -0.1875 to 0.1875
- w_self_out: bfloat16 [1024, 1024], P('tp'), may hold values from -4 to 4
- w_up: bfloat16 [1024, 4096], P(None, 'tp'), may hold values from -0.1875 to 0.1875
- w_down: bfloat16 [4096, 1024], P('tp'), may hold values from -0.4375 to 0.4375
- w_deconv: bfloat16 [1024, 1280], replicated, may hold values from -0.1875 to 0.1875
- deconv_bias: float32 [80], replicated, may hold values from -4 to 4
- out_cotangent: bfloat16 [96, 6, 32, 1024], P('seq', None, 'tp'), may hold values from -6 to 6
- plane_cotangent: bfloat16 [192, 6, 5120], P('seq', None, 'tp'), may hold values from -6 to 6
Outputs:
- out_tokens: bfloat16 [96, 6, 32, 1024], P('seq', None, 'tp')
- planes: float32 [192, 6, 5120], P('seq', None, 'tp')
- grad_tokens: float32 [96, 6, 32, 1024], P('seq')
- grad_query: float32 [1024, 1024], P('seq', 'tp')
- grad_key: float32 [768, 1024], P('seq', 'tp')
- grad_value: float32 [768, 1024], P('seq', 'tp')
- grad_out: float32 [1024, 1024], P('tp', 'seq')
- grad_self_query: float32 [1024, 1024], P('seq', 'tp')
- grad_self_key: float32 [1024, 1024], P('seq', 'tp')
- grad_self_value: float32 [1024, 1024], P('seq', 'tp')
- grad_self_out: float32 [1024, 1024], P('tp', 'seq')
- grad_up: float32 [1024, 4096], P('seq', 'tp')
- grad_down: float32 [4096, 1024], P('tp', 'seq')
- grad_deconv: float32 [1024, 1280], replicated
- grad_bias: float32 [80], replicated
- grad_table: float32 [16, 9216], replicated
The draws below stay inside these ranges and needn't reach their ends.
Inputs may be any that keep to these rules, and one draw needn't show every extreme that they name: `group_ids`: each item's row of source_table.
All inputs are finite; a program needn't handle non-finite values.
Results may differ from the reference program's by a relative error of at most 0.025.
The reference program's roundings to bfloat16 on the way count: a program that leaves them out, or rounds other values in their place, can miss the bound.
Values may be sent and summed in bfloat16 or wider, within the bound.
No kernel may reach another device: no remote copies, remote signals or barrier semaphores. Data moves between devices by JAX's collectives and lax.ppermute only.
A program may use at most 896 MiB of HBM per device.

```python
import math
import jax
import jax.numpy as jnp
from jax import lax

D = 1024
HEADS = 16
HEAD = 64
FF = 4096
COUT = 80
CTX = 768
PLANE = 32
IMG = 4096
GROUPS = 16
ITEMS = 6
HD = 1024
ROWS = 96
TAPS = 1280


def touch_ends(values, rng, smallest, high):
    dims = values.shape
    index_at = [jax.random.randint(jax.random.fold_in(rng, axis), (), 0, dims[axis]) for axis in range(len(dims))]
    values = values.at[tuple(index_at)].set(smallest)
    longest = dims.index(max(dims))
    index_at[longest] = (index_at[longest] + 1) % dims[longest]
    return values.at[tuple(index_at)].set(high)


def shard_levels(own_key, extent, pieces, least, high):
    def one(position, shards_of):
        steps = jax.random.uniform(jax.random.fold_in(jax.random.fold_in(own_key, 6), position), (shards_of,), jnp.float32, least / len(pieces), high / len(pieces))
        return jnp.repeat(jnp.exp(steps), extent[position] // shards_of).reshape((-1,) + (1,) * (len(extent) - position - 1))

    loudness = one(*pieces[0])
    for cut in pieces[1:]:
        loudness = loudness * one(*cut)
    return loudness


def noise(rng, extent, width, reach, cuts=(), kind=jnp.bfloat16):
    entries = jax.random.normal(rng, extent, jnp.float32) * width
    if len(cuts) > 0:
        entries = shard_levels(rng, extent, cuts, -0.22, 0.18) * entries
    return jnp.clip(entries, min=-reach, max=reach).astype(kind)


def setup_inputs(seed: int = 0) -> dict:
    splits = jax.random.split(jax.random.key(seed), 19)
    return {
        "tokens": noise(splits[0], (ROWS, ITEMS, PLANE, D), 1.0, 6.0, ((0, 8),)),
        "context": noise(splits[1], (IMG, ITEMS, CTX), 1.0, 6.0),
        "group_ids": touch_ends(jax.random.randint(splits[2], (ITEMS,), 0, GROUPS), jax.random.fold_in(splits[2], 1), 0, GROUPS - 1).astype(jnp.int32),
        "source_table": noise(splits[3], (GROUPS, 9 * D), 0.5, 3.0, (), jnp.float32),
        "w_query": noise(splits[4], (D, HD), D ** -0.5, 0.1875, ((1, 4),)),
        "w_key": noise(splits[5], (CTX, HD), CTX ** -0.5, 0.21875, ((1, 4),)),
        "w_value": noise(splits[6], (CTX, HD), CTX ** -0.5, 0.21875, ((1, 4),)),
        "w_out": noise(splits[7], (HD, D), (max(D // 512, 1)) ** -0.5, 4.0, ((0, 4),)),
        "w_self_query": noise(splits[8], (D, HD), D ** -0.5, 0.1875, ((1, 4),)),
        "w_self_key": noise(splits[9], (D, HD), D ** -0.5, 0.1875, ((1, 4),)),
        "w_self_value": noise(splits[10], (D, HD), D ** -0.5, 0.1875, ((1, 4),)),
        "w_self_out": noise(splits[11], (HD, D), (max(D // 512, 1)) ** -0.5, 4.0, ((0, 4),)),
        "w_up": noise(splits[12], (D, FF), D ** -0.5, 0.1875, ((1, 4),)),
        "w_down": noise(splits[13], (FF, D), (max(FF // 24, 1)) ** -0.5, 0.4375, ((0, 4),)),
        "w_deconv": noise(splits[14], (D, TAPS), D ** -0.5, 0.1875),
        "deconv_bias": noise(splits[15], (COUT,), 1.0, 4.0, (), jnp.float32),
        "out_cotangent": noise(splits[16], (ROWS, ITEMS, PLANE, D), 1.0, 6.0, ((0, 8), (2, 4))),
        "plane_cotangent": noise(splits[17], (2 * ROWS, ITEMS, 2 * PLANE * COUT), 1.0, 6.0, ((0, 8), (2, 4))),
    }


@jax.custom_vjp
def low(v):
    return lax.optimization_barrier(v.astype(jnp.bfloat16)).astype(jnp.float32)

@jax.custom_vjp
def low_back(v):
    return v

def low_keep(v):
    return (low(v), None)

def low_pass(kept, grad):
    return (grad,)

def back_keep(v):
    return (v, None)

def back_low(kept, grad):
    return (low(grad),)
low.defvjp(low_keep, low_pass)
low_back.defvjp(back_keep, back_low)
highest = lax.Precision.HIGHEST
epsilon = 1e-06

def both_low(value):
    return low_back(low(value))

def layer_norm(value):
    centred = value - lax.optimization_barrier(jnp.mean(value, axis=-1, keepdims=True))
    spread = lax.optimization_barrier(jnp.mean(centred * centred, axis=-1, keepdims=True))
    return centred * lax.rsqrt(spread + epsilon)

def spread_taps(padded, upper, lower):
    even_rows = padded[1:-1, :, :, 1] + upper * padded[:-2, :, :, 3]
    odd_rows = lower * padded[2:, :, :, 0] + padded[1:-1, :, :, 2]
    rows_both = jnp.stack([even_rows, odd_rows], axis=1)
    even_cols = rows_both[:, :, :, 1:-1, 1] + rows_both[:, :, :, :-2, 3]
    odd_cols = rows_both[:, :, :, 2:, 0] + rows_both[:, :, :, 1:-1, 2]
    joined = jnp.stack([even_cols, odd_cols], axis=4)
    shape = joined.shape
    return joined.reshape(shape[0] * 2, shape[2], shape[3] * 2 * shape[5])

def head_attention(block):
    query, key_mat, value_mat = block
    scores = low_back(jnp.dot(query, key_mat.T, precision=highest) * (1.0 / math.sqrt(HEAD)))
    probs = jax.nn.softmax(scores, axis=-1)
    return jnp.dot(low(probs), value_mat, precision=highest)

def heads_first(array):
    return array.transpose(0, 2, 1, 3).reshape(ITEMS * HEADS, array.shape[1], HEAD)

def attention_rows(queries, key_rows, value_rows):
    attended = lax.map(jax.checkpoint(head_attention), (heads_first(queries), heads_first(key_rows), heads_first(value_rows)))
    attended = attended.reshape(ITEMS, HEADS, ROWS, PLANE, HEAD).transpose(0, 2, 3, 1, 4).reshape(ITEMS, ROWS, PLANE, HD)
    return both_low(attended)

def reference(tokens, context, group_ids, source_table, w_query, w_key, w_value, w_out, w_self_query, w_self_key, w_self_value, w_self_out, w_up, w_down, w_deconv, deconv_bias, out_cotangent, plane_cotangent):
    image = context.astype(jnp.float32)
    picker = (group_ids[:, None] == jnp.arange(GROUPS, dtype=jnp.int32)[None, :]).astype(jnp.float32)

    def forward(tokens_f, table, wq, wk, wv, wo, wsq, wsk, wsv, wso, wu, wdn, wdc, bias):
        modulate = jnp.dot(picker, table, precision=highest).reshape(ITEMS, 9, D)

        def piece(index):
            return modulate[None, :, index][:, :, None, :]
        normed = low(layer_norm(tokens_f) * (1.0 + piece(1)) + piece(0))
        queries = both_low(jnp.einsum('ricd,de->irce', normed, wq, precision=highest)).reshape(ITEMS, ROWS * PLANE, HEADS, HEAD)
        key_rows = both_low(jnp.einsum('pid,de->ipe', image, wk, precision=highest)).reshape(ITEMS, IMG, HEADS, HEAD)
        value_rows = both_low(jnp.einsum('pid,de->ipe', image, wv, precision=highest)).reshape(ITEMS, IMG, HEADS, HEAD)
        attended = attention_rows(queries, key_rows, value_rows)
        branch_a = low_back(jnp.einsum('irce,ef->ricf', attended, wo, precision=highest))
        middle = tokens_f + piece(2) * branch_a
        normed_s = low(layer_norm(middle) * (1.0 + piece(4)) + piece(3))
        self_q = both_low(jnp.einsum('ricd,de->irce', normed_s, wsq, precision=highest)).reshape(ITEMS, ROWS * PLANE, HEADS, HEAD)
        self_k = both_low(jnp.einsum('ricd,de->irce', normed_s, wsk, precision=highest)).reshape(ITEMS, ROWS * PLANE, HEADS, HEAD)
        self_v = both_low(jnp.einsum('ricd,de->irce', normed_s, wsv, precision=highest)).reshape(ITEMS, ROWS * PLANE, HEADS, HEAD)
        self_att = attention_rows(self_q, self_k, self_v)
        branch_s = low_back(jnp.einsum('irce,ef->ricf', self_att, wso, precision=highest))
        middle_two = middle + piece(5) * branch_s
        normed_b = low(layer_norm(middle_two) * (1.0 + piece(7)) + piece(6))
        hidden = low_back(jnp.einsum('ricd,df->ricf', normed_b, wu, precision=highest))
        active = low(jax.nn.gelu(hidden, approximate=False))
        branch_b = low_back(jnp.einsum('ricf,fd->ricd', active, wdn, precision=highest))
        result = middle_two + piece(8) * branch_b
        rounded = low(result)
        taps = jnp.einsum('ricd,dt->rict', rounded, wdc, precision=highest)
        taps = taps.reshape(3, PLANE, ITEMS, PLANE, 4, 4, COUT).transpose(1, 0, 2, 3, 4, 5, 6)
        taps = taps.reshape(PLANE, 3 * ITEMS, PLANE, 4, 4, COUT)
        padded = jnp.pad(taps, ((1, 1), (0, 0), (1, 1), (0, 0), (0, 0), (0, 0)))
        spread = spread_taps(padded, 1.0, 1.0)
        spread = spread.reshape(2 * PLANE, 3, ITEMS, 2 * PLANE * COUT).transpose(1, 0, 2, 3)
        planes = spread.reshape(6 * PLANE, ITEMS, 2 * PLANE * COUT) + jnp.tile(bias, 2 * PLANE)
        return (rounded, planes)
    primals = (tokens.astype(jnp.float32), source_table, w_query.astype(jnp.float32), w_key.astype(jnp.float32), w_value.astype(jnp.float32), w_out.astype(jnp.float32), w_self_query.astype(jnp.float32), w_self_key.astype(jnp.float32), w_self_value.astype(jnp.float32), w_self_out.astype(jnp.float32), w_up.astype(jnp.float32), w_down.astype(jnp.float32), w_deconv.astype(jnp.float32), deconv_bias)
    outputs, pullback = jax.vjp(forward, *primals)
    grads = pullback((out_cotangent.astype(jnp.float32), plane_cotangent.astype(jnp.float32)))
    return (outputs[0].astype(jnp.bfloat16), outputs[1], grads[0], grads[2], grads[3], grads[4], grads[5], grads[6], grads[7], grads[8], grads[9], grads[10], grads[11], grads[12], grads[13], grads[1])
```

```python
import jax
import jax.numpy as jnp
from jax import lax
from jax.experimental import pallas as pl
from jax.experimental.pallas import tpu as pltpu
from jax.sharding import PartitionSpec as P

HEAD = 64
COUT = 80
PLANE = 32
IMG = 4096
LOG2E = 1.4426950408889634
bf16 = jnp.bfloat16
f32 = jnp.float32
GROUPS = 16


highest = lax.Precision.HIGHEST
epsilon = 1e-06


def with_halo(x, sides, width):
    for axis, dim in sides:
        peers, length = (lax.axis_size(axis), x.shape[dim])
        up = [(i, (i + 1) % peers) for i in range(peers - 1)]
        down = [(j, i) for i, j in up]
        last = lax.slice_in_dim(x, length - width, length, axis=dim)
        initial = lax.slice_in_dim(x, 0, width, axis=dim)
        before = lax.ppermute(last, axis, up)
        after = lax.ppermute(initial, axis, down)
        x = jnp.concatenate([before, x, after], axis=dim)
    return x


def spread_taps(padded, upper, lower):
    even_rows = padded[1:-1, :, :, 1] + upper * padded[:-2, :, :, 3]
    odd_rows = lower * padded[2:, :, :, 0] + padded[1:-1, :, :, 2]
    rows_both = jnp.stack([even_rows, odd_rows], axis=1)
    even_cols = rows_both[:, :, :, 1:-1, 1] + rows_both[:, :, :, :-2, 3]
    odd_cols = rows_both[:, :, :, 2:, 0] + rows_both[:, :, :, 1:-1, 2]
    joined = jnp.stack([even_cols, odd_cols], axis=4)
    shape = joined.shape
    return joined.reshape(shape[0] * 2, shape[2], shape[3] * 2 * shape[5])


def norm_parts(value):
    centred = value - jnp.mean(value, axis=-1, keepdims=True)
    inverse = lax.rsqrt(jnp.mean(centred * centred, axis=-1, keepdims=True) + epsilon)
    return (centred * inverse, inverse)


def norm_back(normed, inverse, incoming):
    return inverse * (
        incoming
        - jnp.mean(incoming, axis=-1, keepdims=True)
        - normed * jnp.mean(incoming * normed, axis=-1, keepdims=True)
    )


NT = (((1,), (1,)), ((), ()))


def dot_nt(a, b):
    return lax.dot_general(a, b, NT, preferred_element_type=f32)


def dot_nn(a, b):
    return jnp.dot(a, b, preferred_element_type=f32)


def flip(x):
    return x.astype(f32).T.astype(bf16)


def chunk_of(keys):
    return 512 if keys % 512 == 0 else keys


def softmax_sweep(scores, values, chunks, columns):
    top = jnp.full((1, columns), -1e30, f32)
    total = jnp.zeros((1, columns), f32)
    mixed = None
    ahead = scores(0)
    for c in range(chunks):
        now = ahead
        ahead = scores(c + 1) if c + 1 < chunks else None
        new_top = jnp.maximum(top, jnp.max(now, axis=0, keepdims=True))
        fade = jnp.exp2((top - new_top) * LOG2E)
        expon = jnp.exp2(now * LOG2E - new_top * LOG2E)
        total = total * fade + jnp.sum(expon, axis=0, keepdims=True)
        parts = values(c, expon.astype(bf16))
        width = columns // len(parts)
        if mixed is None:
            mixed = parts
        else:
            mixed = [
                m * fade[:, j * width : (j + 1) * width] + part
                for j, (m, part) in enumerate(zip(mixed, parts))
            ]
        top = new_top
    width = columns // len(mixed)
    inverse = 1.0 / total
    mixed = [m * inverse[:, j * width : (j + 1) * width] for j, m in enumerate(mixed)]
    return mixed, top + jnp.log(total)


def cross_forward(q, k, vt):
    items, queries, width = q.shape
    keys = k.shape[1]
    heads = width // HEAD
    step = chunk_of(keys)

    def kernel(q_ref, k_ref, vt_ref, o_ref, log_ref):
        pair = pl.program_id(1)
        owner = lax.broadcasted_iota(jnp.int32, (queries, width), 1) // HEAD
        both = jnp.concatenate(
            [jnp.where(owner == pair * 2 + j, q_ref[0], 0.0).astype(bf16) for j in range(2)], axis=0
        )

        def scores(c):
            return dot_nt(k_ref[0, pl.ds(c * step, step), :], both)

        def values(c, p):
            out = []
            for j in range(2):
                rows = pl.ds(pl.multiple_of((pair * 2 + j) * HEAD, HEAD), HEAD)
                v = vt_ref[0, rows, pl.ds(c * step, step)]
                out.append(dot_nn(v, p[:, j * queries : (j + 1) * queries]))
            return out

        mixed, log_total = softmax_sweep(scores, values, keys // step, 2 * queries)
        o_ref[0] = jnp.concatenate(mixed, axis=0).T.astype(bf16)
        for j in range(2):
            log_ref[0, j] = jnp.broadcast_to(
                log_total[:, j * queries : (j + 1) * queries], (8, queries)
            )

    return pl.pallas_call(
        kernel,
        grid=(items, heads // 2),
        in_specs=[
            pl.BlockSpec((1, queries, width), lambda i, h: (i, 0, 0)),
            pl.BlockSpec((1, keys, width), lambda i, h: (i, 0, 0)),
            pl.BlockSpec((1, width, keys), lambda i, h: (i, 0, 0)),
        ],
        out_specs=[
            pl.BlockSpec((1, queries, 2 * HEAD), lambda i, h: (i, 0, h)),
            pl.BlockSpec((1, 2, 8, queries), lambda i, h: (i, h, 0, 0)),
        ],
        out_shape=[
            jax.ShapeDtypeStruct((items, queries, width), bf16),
            jax.ShapeDtypeStruct((items, heads, 8, queries), f32),
        ],
        compiler_params=pltpu.CompilerParams(vmem_limit_bytes=48 << 20),
        cost_estimate=pl.CostEstimate(
            flops=16 * items * queries * keys * width,
            bytes_accessed=4 * items * (queries + keys) * width,
            transcendentals=items * queries * keys * heads,
        ),
        name="cross_forward",
    )(q, k, vt)


def cross_backward(q, do, o, logs, k, vt):
    items, queries, width = q.shape
    keys = k.shape[1]
    heads = width // HEAD
    step = chunk_of(keys)

    def kernel(q_ref, do_ref, o_ref, log_ref, k_ref, vt_ref, dq_ref, dk_ref, dv_ref, qt, dot):
        head = pl.program_id(1)

        @pl.when(head == 0)
        def _():
            qt[...] = flip(q_ref[0])
            dot[...] = flip(do_ref[0])

        mine = lax.broadcasted_iota(jnp.int32, (queries, width), 1) // HEAD == head
        q_mine = jnp.where(mine, q_ref[0], 0.0).astype(bf16)
        do_mine = jnp.where(mine, do_ref[0], 0.0).astype(bf16)
        delta = jnp.sum(do_mine.astype(f32) * o_ref[0].astype(f32), axis=1, keepdims=True)
        log_total = log_ref[0, 0].T[:, :1] * LOG2E
        rows = pl.ds(pl.multiple_of(head * HEAD, HEAD), HEAD)
        qt_mine = qt[rows, :]
        dot_mine = dot[rows, :]

        def scores(c):
            s = dot_nt(q_mine, k_ref[0, pl.ds(c * step, step), :])
            return s, dot_nn(do_mine, vt_ref[0, :, pl.ds(c * step, step)])

        dq = jnp.zeros((queries, width), f32)
        ahead = scores(0)
        for c in range(keys // step):
            s, dp = ahead
            ahead = scores(c + 1) if c + 1 < keys // step else None
            p = jnp.exp2(s * LOG2E - log_total)
            ds = (p * (dp - delta)).astype(bf16)
            cols = pl.ds(c * step, step)
            dv_ref[0, :, cols] = dot_nn(dot_mine, p.astype(bf16)).astype(bf16)
            dk_ref[0, :, cols] = dot_nn(qt_mine, ds).astype(bf16)
            dq = dq + dot_nn(ds, k_ref[0, cols, :])
        dq = (dq * 0.125).astype(bf16)
        rest = jnp.where(head == 0, jnp.zeros_like(dq), dq_ref[0])
        dq_ref[0] = jnp.where(mine, dq, rest)

    rows_spec = pl.BlockSpec((1, queries, width), lambda i, h: (i, 0, 0))
    grads_spec = pl.BlockSpec((1, HEAD, keys), lambda i, h: (i, h, 0))
    return pl.pallas_call(
        kernel,
        grid=(items, heads),
        in_specs=[
            rows_spec,
            rows_spec,
            rows_spec,
            pl.BlockSpec((1, 1, 8, queries), lambda i, h: (i, h, 0, 0)),
            pl.BlockSpec((1, keys, width), lambda i, h: (i, 0, 0)),
            pl.BlockSpec((1, width, keys), lambda i, h: (i, 0, 0)),
        ],
        out_specs=[rows_spec, grads_spec, grads_spec],
        out_shape=[
            jax.ShapeDtypeStruct((items, queries, width), bf16),
            jax.ShapeDtypeStruct((items, width, keys), bf16),
            jax.ShapeDtypeStruct((items, width, keys), bf16),
        ],
        scratch_shapes=[pltpu.VMEM((width, queries), bf16), pltpu.VMEM((width, queries), bf16)],
        compiler_params=pltpu.CompilerParams(vmem_limit_bytes=48 << 20),
        cost_estimate=pl.CostEstimate(
            flops=40 * items * queries * keys * width,
            bytes_accessed=8 * items * (queries + keys) * width,
            transcendentals=items * queries * keys * heads,
        ),
        name="cross_backward",
    )(q, do, o, logs, k, vt)


def split_pair(x):
    low = lax.broadcasted_iota(jnp.int32, x.shape, 1) < HEAD
    wide = x.astype(f32)
    first = jnp.where(low, wide, 0.0)
    second = jnp.where(low, pltpu.roll(wide, HEAD, 1), 0.0)
    return jnp.concatenate([first, second], axis=0).astype(bf16)


def self_forward(q, kv):
    rows = q.shape[0]
    keys = kv.shape[0]
    block = 384 if rows % 384 == 0 else rows
    step = chunk_of(keys)

    def kernel(q_ref, kv_ref, o_ref, log_ref, vt):
        @pl.when(pl.program_id(0) == 0)
        def _():
            vt[...] = flip(kv_ref[...])

        both = split_pair(q_ref[...])

        def scores(c):
            return dot_nt(kv_ref[pl.ds(c * step, step), :], both)

        def values(c, p):
            return [dot_nn(vt[HEAD:, pl.ds(c * step, step)], p)]

        mixed, log_total = softmax_sweep(scores, values, keys // step, 2 * block)
        mixed = mixed[0]
        o_ref[...] = (
            jnp.concatenate([mixed[:, :block], mixed[:, block:]], axis=0).T.astype(bf16)
        )
        log_ref[0] = jnp.broadcast_to(log_total, (8, 2 * block))

    return pl.pallas_call(
        kernel,
        grid=(rows // block,),
        in_specs=[
            pl.BlockSpec((block, 2 * HEAD), lambda i: (i, 0)),
            pl.BlockSpec((keys, 2 * HEAD), lambda i: (0, 0)),
        ],
        out_specs=[
            pl.BlockSpec((block, 2 * HEAD), lambda i: (i, 0)),
            pl.BlockSpec((1, 8, 2 * block), lambda i: (i, 0, 0)),
        ],
        out_shape=[
            jax.ShapeDtypeStruct((rows, 2 * HEAD), bf16),
            jax.ShapeDtypeStruct((rows // block, 8, 2 * block), f32),
        ],
        scratch_shapes=[pltpu.VMEM((2 * HEAD, keys), bf16)],
        compiler_params=pltpu.CompilerParams(vmem_limit_bytes=48 << 20),
        cost_estimate=pl.CostEstimate(
            flops=16 * 2 * rows * keys * HEAD,
            bytes_accessed=4 * (rows + keys) * 2 * HEAD,
            transcendentals=2 * rows * keys,
        ),
        name="self_forward",
    )(q, kv)


def self_backward(q, do, o, logs, kv):
    rows = q.shape[0]
    keys = kv.shape[0]
    blocks = logs.shape[0]
    block = rows // blocks
    step = chunk_of(keys)

    def kernel(q_ref, do_ref, o_ref, log_ref, kv_ref, dq_ref, dkv_ref, vt, grads):
        i = pl.program_id(0)

        @pl.when(i == 0)
        def _():
            vt[...] = flip(kv_ref[...])
            grads[...] = jnp.zeros_like(grads)

        q_both = split_pair(q_ref[...])
        do_both = split_pair(do_ref[...])
        product = do_both.astype(f32) * split_pair(o_ref[...]).astype(f32)
        delta = jnp.sum(product, axis=1, keepdims=True)
        log_total = log_ref[0].T[:, :1] * LOG2E
        qt = flip(q_both)[:HEAD]
        dot = flip(do_both)[:HEAD]
        do_low = do_both[:, :HEAD]

        def scores(c):
            s = dot_nt(q_both, kv_ref[pl.ds(c * step, step), :])
            return s, dot_nn(do_low, vt[HEAD:, pl.ds(c * step, step)])

        dq = jnp.zeros((2 * block, 2 * HEAD), f32)
        ahead = scores(0)
        for c in range(keys // step):
            s, dp = ahead
            ahead = scores(c + 1) if c + 1 < keys // step else None
            p = jnp.exp2(s * LOG2E - log_total)
            ds = (p * (dp - delta)).astype(bf16)
            cols = pl.ds(c * step, step)
            grads[:HEAD, cols] += dot_nn(qt, ds)
            grads[HEAD:, cols] += dot_nn(dot, p.astype(bf16))
            dq = dq + dot_nn(ds, kv_ref[cols, :])
        dq = dq * 0.125
        low = lax.broadcasted_iota(jnp.int32, (block, 2 * HEAD), 1) < HEAD
        dq_ref[...] = jnp.where(low, dq[:block], pltpu.roll(dq[block:], HEAD, 1)).astype(bf16)

        @pl.when(i == blocks - 1)
        def _():
            dkv_ref[...] = grads[...].T.astype(bf16)

    rows_spec = pl.BlockSpec((block, 2 * HEAD), lambda i: (i, 0))
    keys_spec = pl.BlockSpec((keys, 2 * HEAD), lambda i: (0, 0))
    return pl.pallas_call(
        kernel,
        grid=(blocks,),
        in_specs=[
            rows_spec,
            rows_spec,
            rows_spec,
            pl.BlockSpec((1, 8, 2 * block), lambda i: (i, 0, 0)),
            keys_spec,
        ],
        out_specs=[rows_spec, keys_spec],
        out_shape=[
            jax.ShapeDtypeStruct((rows, 2 * HEAD), bf16),
            jax.ShapeDtypeStruct((keys, 2 * HEAD), bf16),
        ],
        scratch_shapes=[
            pltpu.VMEM((2 * HEAD, keys), bf16),
            pltpu.VMEM((2 * HEAD, keys), f32),
        ],
        compiler_params=pltpu.CompilerParams(vmem_limit_bytes=48 << 20),
        cost_estimate=pl.CostEstimate(
            flops=40 * 2 * rows * keys * HEAD,
            bytes_accessed=8 * (rows + keys) * 2 * HEAD,
            transcendentals=2 * rows * keys,
        ),
        name="self_backward",
    )(q, do, o, logs, kv)


def exchange(x, axis):
    return lax.all_to_all(x, axis, 0, 0, tiled=True)


def gather(x, axis):
    return exchange(jnp.broadcast_to(x[None], (lax.axis_size(axis),) + x.shape), axis)


def reduce_blocks(x, axis):
    return jnp.sum(exchange(x.astype(bf16), axis).astype(f32), axis=0)


def body(
    tokens,
    context,
    group_ids,
    source_table,
    w_query,
    w_key,
    w_value,
    w_out,
    w_self_query,
    w_self_key,
    w_self_value,
    w_self_out,
    w_up,
    w_down,
    w_deconv,
    deconv_bias,
    out_cotangent,
    plane_cotangent,
):
    rows_here, items, plane_cols, width = tokens.shape
    cols_here = out_cotangent.shape[2]
    tp = lax.axis_size("tp")
    seq = lax.axis_size("seq")
    devices = tp * seq
    local = w_query.shape[1]
    heads_here = local // HEAD
    heads = heads_here * tp
    tile = rows_here * cols_here
    half = tile // 2
    groups = devices // heads
    turns = -(-items // groups)
    spare = groups * turns - items
    me_tp = lax.axis_index("tp")

    picker = (group_ids[:, None] == jnp.arange(GROUPS, dtype=jnp.int32)[None, :]).astype(f32)
    mods = jnp.dot(picker, source_table, precision=highest).reshape(items, 9, 1, width)

    def piece(index):
        return mods[:, index]

    def dot(spec, a, b):
        return jnp.einsum(spec, a, b, preferred_element_type=f32)

    def to_tile(x):
        return x.transpose(1, 0, 2, 3).reshape(items, tile, width)

    def from_tile(x):
        return x.reshape(items, rows_here, cols_here, width).transpose(1, 0, 2, 3)

    out_whole = gather(w_out, "tp")
    self_local = jnp.concatenate(
        [
            jnp.concatenate(
                [
                    w_self_key.reshape(width, heads_here, HEAD),
                    w_self_value.reshape(width, heads_here, HEAD),
                ],
                axis=2,
            ).reshape(width, 2 * local),
            w_self_query,
        ],
        axis=1,
    )
    self_whole = gather(self_local, "tp")
    self_out_whole = gather(w_self_out, "tp")
    up_whole = gather(w_up, "tp")
    down_whole = gather(w_down, "tp")
    query_whole = gather(w_query, "tp")

    ordered = (
        tokens.reshape(rows_here, items, tp, cols_here, width)
        .transpose(1, 2, 0, 3, 4)
        .reshape(items, tp * tile, width)
    )
    first_hat, first_inv = norm_parts(ordered.astype(f32))
    first_in = (first_hat * (1.0 + piece(1)) + piece(0)).astype(bf16)
    queries = dot("iqd,de->iqe", first_in, w_query).astype(bf16) * bf16(0.125)
    keys = dot("pid,de->ipe", context, w_key).astype(bf16)
    values_t = dot("pid,de->iep", context, w_value).astype(bf16)
    mixed, cross_logs = cross_forward(queries, keys, values_t)
    mixed_send = mixed.reshape(items, tp, tile, local).transpose(1, 0, 2, 3)
    mixed_tile = exchange(mixed_send, "tp")
    branch_a = dot("time,tef->imf", mixed_tile, out_whole)
    residual = to_tile(
        lax.dynamic_slice_in_dim(tokens, me_tp * cols_here, cols_here, 2)
    ).astype(f32)
    middle = residual + piece(2) * branch_a

    self_hat, self_inv = norm_parts(middle)
    self_in = (self_hat * (1.0 + piece(4)) + piece(3)).astype(bf16)
    projected = dot("imd,tde->time", self_in, self_whole).astype(bf16)

    def pad_items(x):
        return jnp.pad(x, ((0, 0), (0, spare)) + ((0, 0),) * (x.ndim - 2)) if spare else x

    kv_send = (
        pad_items(projected[..., : 2 * local].reshape(tp, items, tile, heads_here, 2 * HEAD))
        .reshape(tp, groups, turns, tile, heads_here, 2 * HEAD)
        .transpose(2, 1, 0, 4, 3, 5)
        .reshape(turns, devices, tile, 2 * HEAD)
    )

    def pack_rows(x):
        return (
            pad_items(x)
            .reshape(tp, groups, turns, 2, half, heads_here, HEAD)
            .transpose(2, 1, 0, 5, 4, 3, 6)
            .reshape(turns, devices, half, 2 * HEAD)
        )

    def unpack_rows(x):
        return (
            x.reshape(turns, groups, tp, heads_here, half, 2, HEAD)
            .transpose(2, 1, 0, 5, 4, 3, 6)
            .reshape(tp, groups * turns, tile, local)[:, :items]
        )

    q_send = pack_rows(projected[..., 2 * local :] * bf16(0.125))
    both_axes = ("seq", "tp")
    q_mine, kv_mine, so_mine, self_logs, so_back = [], [], [], [], []
    for turn in range(turns):
        kv_mine.append(exchange(kv_send[turn], both_axes).reshape(devices * tile, 2 * HEAD))
        q_mine.append(exchange(q_send[turn], both_axes).reshape(devices * half, 2 * HEAD))
    for turn in range(turns):
        so, logs = self_forward(q_mine[turn], kv_mine[turn])
        so_mine.append(so)
        self_logs.append(logs)
        so_back.append(exchange(so.reshape(devices, half, 2 * HEAD), both_axes))
    self_tile = unpack_rows(jnp.stack(so_back))
    branch_s = dot("time,tef->imf", self_tile, self_out_whole)
    middle_two = middle + piece(5) * branch_s

    incoming = plane_cotangent.reshape(2 * rows_here, items, 2 * cols_here, COUT)
    plane_row = (lax.axis_index("seq") * rows_here + jnp.arange(rows_here, dtype=jnp.int32)) % PLANE
    upper_keep = (plane_row != 0).astype(f32)
    lower_keep = (plane_row != PLANE - 1).astype(f32)
    grad_edges = with_halo(incoming, (("seq", 0), ("tp", 2)), 1)
    upper_mask = upper_keep.astype(bf16)[:, None, None, None]
    lower_mask = lower_keep.astype(bf16)[:, None, None, None]
    first_pair = grad_edges[:-2].reshape(rows_here, 2, items, 2 * cols_here + 2, COUT)
    last_pair = grad_edges[2:].reshape(rows_here, 2, items, 2 * cols_here + 2, COUT)
    row_taps = jnp.stack(
        [
            first_pair[:, 0] * upper_mask,
            first_pair[:, 1],
            last_pair[:, 0],
            last_pair[:, 1] * lower_mask,
        ],
        axis=3,
    )
    left_pair = row_taps[:, :, :-2].reshape(rows_here, items, cols_here, 2, 4, COUT)
    right_pair = row_taps[:, :, 2:].reshape(rows_here, items, cols_here, 2, 4, COUT)
    tap_grads = jnp.stack(
        [
            left_pair[:, :, :, 0],
            left_pair[:, :, :, 1],
            right_pair[:, :, :, 0],
            right_pair[:, :, :, 1],
        ],
        axis=4,
    )
    tap_grads = tap_grads.reshape(rows_here, items, cols_here, 16 * COUT)
    grad_result = to_tile(
        out_cotangent.astype(f32) + dot("rict,dt->ricd", tap_grads, w_deconv)
    )
    grad_bias = jnp.sum(incoming.astype(f32), axis=(0, 1, 2))
    grad_mlp = (piece(8) * grad_result).astype(bf16)

    second_hat, second_inv = norm_parts(middle_two)
    second_in = (second_hat * (1.0 + piece(7)) + piece(6)).astype(bf16)
    hidden = dot("imd,tdf->timf", second_in, up_whole)
    active_f, gelu_back = jax.vjp(lambda value: jax.nn.gelu(value, approximate=False), hidden)
    active = active_f.astype(bf16)
    branch_b = dot("timf,tfd->imd", active, down_whole)
    result = middle_two + piece(8) * branch_b
    out_tile = from_tile(result.astype(bf16))

    grad_active = dot("imd,tfd->timf", grad_mlp, down_whole)
    grad_hidden = gelu_back(grad_active)[0].astype(bf16)
    grad_second = dot("timf,tdf->imd", grad_hidden, up_whole)
    grad_gate_b = jnp.sum(grad_result * branch_b, axis=1)
    grad_shift_b = jnp.sum(grad_second, axis=1)
    grad_scale_b = jnp.sum(grad_second * second_hat, axis=1)
    grad_mid_two = grad_result + norm_back(second_hat, second_inv, grad_second * (1.0 + piece(7)))

    grad_self = (piece(5) * grad_mid_two).astype(bf16)
    grad_gate_s = jnp.sum(grad_mid_two * branch_s, axis=1)
    dso_send = pack_rows(dot("imf,tef->time", grad_self, self_out_whole).astype(bf16))
    dq_back, dkv_back = [], []
    dso_mine = [exchange(dso_send[turn], both_axes) for turn in range(turns)]
    for turn in range(turns):
        dq, dkv = self_backward(
            q_mine[turn],
            dso_mine[turn].reshape(devices * half, 2 * HEAD),
            so_mine[turn],
            self_logs[turn],
            kv_mine[turn],
        )
        dq_back.append(exchange(dq.reshape(devices, half, 2 * HEAD), both_axes))
        dkv_back.append(exchange(dkv.reshape(devices, tile, 2 * HEAD), both_axes))
    dq_tile = unpack_rows(jnp.stack(dq_back))
    dkv_tile = (
        jnp.stack(dkv_back)
        .reshape(turns, groups, tp, heads_here, tile, 2 * HEAD)
        .transpose(2, 1, 0, 4, 3, 5)
        .reshape(tp, groups * turns, tile, 2 * local)[:, :items]
    )
    grad_projected = jnp.concatenate([dkv_tile, dq_tile], axis=3)
    grad_third = dot("time,tde->imd", grad_projected, self_whole)
    grad_shift_s = jnp.sum(grad_third, axis=1)
    grad_scale_s = jnp.sum(grad_third * self_hat, axis=1)
    grad_middle = grad_mid_two + norm_back(self_hat, self_inv, grad_third * (1.0 + piece(4)))

    grad_attn = (piece(2) * grad_middle).astype(bf16)
    grad_gate_a = jnp.sum(grad_middle * branch_a, axis=1)
    do_send = dot("imf,tef->time", grad_attn, out_whole).astype(bf16)
    do_mine = exchange(do_send, "tp").transpose(1, 0, 2, 3).reshape(items, tp * tile, local)
    middle_all = gather(grad_middle.astype(bf16), "tp")
    dq_cross, dk_t, dv_t = cross_backward(queries, do_mine, mixed, cross_logs, keys, values_t)
    dq_all = gather(dq_cross, "tp")
    grad_first = dot("tiqe,tde->iqd", dq_all, query_whole)
    grad_shift_a = jnp.sum(grad_first, axis=1)
    grad_scale_a = jnp.sum(grad_first * first_hat, axis=1)
    grad_tokens = middle_all.astype(f32).transpose(1, 0, 2, 3).reshape(
        items, tp * tile, width
    ) + norm_back(first_hat, first_inv, grad_first * (1.0 + piece(1)))
    grad_tokens = (
        grad_tokens.reshape(items, tp, rows_here, cols_here, width)
        .transpose(2, 0, 1, 3, 4)
        .reshape(rows_here, items, plane_cols, width)
    )

    widened = with_halo(out_tile, (("seq", 0), ("tp", 2)), 1)
    taps = dot("ricd,dt->rict", widened, w_deconv)
    taps = taps.reshape(rows_here + 2, items, cols_here + 2, 4, 4, COUT)
    planes = spread_taps(
        taps, upper_keep[:, None, None, None, None], lower_keep[:, None, None, None, None]
    )
    planes = planes + jnp.tile(deconv_bias, 2 * cols_here)

    def over_seq_rows(x):
        return reduce_blocks(x.reshape((seq, x.shape[0] // seq) + x.shape[1:]), "seq")

    def over_seq_columns(x):
        return reduce_blocks(
            x.reshape(x.shape[0], seq, x.shape[1] // seq).transpose(1, 0, 2), "seq"
        )

    grad_down = over_seq_columns(reduce_blocks(dot("timf,imd->tfd", active, grad_mlp), "tp"))
    grad_up = over_seq_rows(reduce_blocks(dot("imd,timf->tdf", second_in, grad_hidden), "tp"))
    grad_self_out = over_seq_columns(
        reduce_blocks(dot("time,imf->tef", self_tile, grad_self), "tp")
    )
    grad_three = over_seq_rows(
        reduce_blocks(dot("imd,time->tde", self_in, grad_projected), "tp")
    )
    grad_out = over_seq_columns(reduce_blocks(dot("time,imf->tef", mixed_tile, grad_attn), "tp"))
    share = grad_three.shape[0]
    grad_pair = grad_three[:, : 2 * local].reshape(share, heads_here, 2, HEAD)
    grad_self_key = grad_pair[:, :, 0].reshape(share, local)
    grad_self_value = grad_pair[:, :, 1].reshape(share, local)
    grad_self_query = grad_three[:, 2 * local :]
    grad_query = over_seq_rows(dot("iqd,iqe->de", first_in, dq_cross))
    grad_key = over_seq_rows(dot("pid,iep->de", context, dk_t))
    grad_value = over_seq_rows(dot("pid,iep->de", context, dv_t))

    grad_deconv = dot("ricd,rict->dt", out_tile, tap_grads)
    early = jnp.stack(
        [
            grad_gate_a,
            grad_shift_s,
            grad_scale_s,
            grad_gate_s,
            grad_shift_b,
            grad_scale_b,
            grad_gate_b,
        ],
        axis=1,
    )
    grad_deconv, grad_bias = lax.psum((grad_deconv, grad_bias), both_axes)
    early = lax.psum(early, both_axes)
    late = lax.psum(jnp.stack([grad_shift_a, grad_scale_a], axis=1), "seq")
    grad_mods = jnp.concatenate([late, early], axis=1)
    grad_table = jnp.dot(picker.T, grad_mods.reshape(items, 9 * width), precision=highest)
    return (
        out_tile,
        planes,
        grad_tokens,
        grad_query,
        grad_key,
        grad_value,
        grad_out,
        grad_self_query,
        grad_self_key,
        grad_self_value,
        grad_self_out,
        grad_up,
        grad_down,
        grad_deconv,
        grad_bias,
        grad_table,
    )


def solution(mesh):
    in_specs = (
        P("seq", None, None, None),
        P(),
        P(),
        P(),
        P(None, "tp"),
        P(None, "tp"),
        P(None, "tp"),
        P("tp", None),
        P(None, "tp"),
        P(None, "tp"),
        P(None, "tp"),
        P("tp", None),
        P(None, "tp"),
        P("tp", None),
        P(),
        P(),
        P("seq", None, "tp", None),
        P("seq", None, "tp"),
    )
    out_specs = (
        P("seq", None, "tp", None),
        P("seq", None, "tp"),
        P("seq", None, None, None),
        P("seq", "tp"),
        P("seq", "tp"),
        P("seq", "tp"),
        P("tp", "seq"),
        P("seq", "tp"),
        P("seq", "tp"),
        P("seq", "tp"),
        P("tp", "seq"),
        P("seq", "tp"),
        P("tp", "seq"),
        P(),
        P(),
        P(),
    )
    return jax.shard_map(body, mesh=mesh, in_specs=in_specs, out_specs=out_specs, check_vma=False)
```

```python
import jax
import jax.numpy as jnp
from jax import lax
from jax.experimental import pallas as pl
from jax.experimental.pallas import tpu as pltpu
from jax.sharding import PartitionSpec as P

HEAD = 64
COUT = 80
PLANE = 32
IMG = 4096
LOG2E = 1.4426950408889634
bf16 = jnp.bfloat16
f32 = jnp.float32
GROUPS = 16


highest = lax.Precision.HIGHEST
epsilon = 1e-06


def with_halo(x, sides, width):
    for axis, dim in sides:
        peers, length = (lax.axis_size(axis), x.shape[dim])
        up = [(i, (i + 1) % peers) for i in range(peers - 1)]
        down = [(j, i) for i, j in up]
        last = lax.slice_in_dim(x, length - width, length, axis=dim)
        initial = lax.slice_in_dim(x, 0, width, axis=dim)
        before = lax.ppermute(last, axis, up)
        after = lax.ppermute(initial, axis, down)
        x = jnp.concatenate([before, x, after], axis=dim)
    return x


def spread_taps(padded, upper, lower):
    even_rows = padded[1:-1, :, :, 1] + upper * padded[:-2, :, :, 3]
    odd_rows = lower * padded[2:, :, :, 0] + padded[1:-1, :, :, 2]
    rows_both = jnp.stack([even_rows, odd_rows], axis=1)
    even_cols = rows_both[:, :, :, 1:-1, 1] + rows_both[:, :, :, :-2, 3]
    odd_cols = rows_both[:, :, :, 2:, 0] + rows_both[:, :, :, 1:-1, 2]
    joined = jnp.stack([even_cols, odd_cols], axis=4)
    shape = joined.shape
    return joined.reshape(shape[0] * 2, shape[2], shape[3] * 2 * shape[5])


def norm_parts(value):
    centred = value - jnp.mean(value, axis=-1, keepdims=True)
    inverse = lax.rsqrt(jnp.mean(centred * centred, axis=-1, keepdims=True) + epsilon)
    return (centred * inverse, inverse)


def norm_back(normed, inverse, incoming):
    return inverse * (
        incoming
        - jnp.mean(incoming, axis=-1, keepdims=True)
        - normed * jnp.mean(incoming * normed, axis=-1, keepdims=True)
    )


NT = (((1,), (1,)), ((), ()))
BLOCKS = 4
FORCE_PLAIN = False


def dot_nt(a, b):
    return lax.dot_general(a, b, NT, preferred_element_type=f32)


def dot_nn(a, b):
    return jnp.dot(a, b, preferred_element_type=f32)


def flip(x):
    return x.astype(f32).T.astype(bf16)


def chunk_of(keys):
    return 512 if keys % 512 == 0 else keys


def softmax_sweep(scores, values, chunks, columns):
    top = jnp.full((1, columns), -1e30, f32)
    total = jnp.zeros((1, columns), f32)
    mixed = None
    ahead = scores(0)
    for c in range(chunks):
        now = ahead
        ahead = scores(c + 1) if c + 1 < chunks else None
        new_top = jnp.maximum(top, jnp.max(now, axis=0, keepdims=True))
        fade = jnp.exp2((top - new_top) * LOG2E)
        expon = jnp.exp2(now * LOG2E - new_top * LOG2E)
        total = total * fade + jnp.sum(expon, axis=0, keepdims=True)
        parts = values(c, expon.astype(bf16))
        width = columns // len(parts)
        if mixed is None:
            mixed = parts
        else:
            mixed = [
                m * fade[:, j * width : (j + 1) * width] + part
                for j, (m, part) in enumerate(zip(mixed, parts))
            ]
        top = new_top
    width = columns // len(mixed)
    inverse = 1.0 / total
    mixed = [m * inverse[:, j * width : (j + 1) * width] for j, m in enumerate(mixed)]
    return mixed, top + jnp.log(total)


def cross_forward(q, k, vt, tp):
    items, queries, width = q.shape
    tile = queries // tp
    keys = k.shape[1]
    heads = width // HEAD
    step = chunk_of(keys)

    def kernel(q_ref, k_ref, vt_ref, o_ref, wide_ref, log_ref):
        pair = pl.program_id(1)
        owner = lax.broadcasted_iota(jnp.int32, (queries, width), 1) // HEAD
        both = jnp.concatenate(
            [jnp.where(owner == pair * 2 + j, q_ref[0], 0.0).astype(bf16) for j in range(2)], axis=0
        )

        def scores(c):
            return dot_nt(k_ref[0, pl.ds(c * step, step), :], both)

        def values(c, p):
            out = []
            for j in range(2):
                rows = pl.ds(pl.multiple_of((pair * 2 + j) * HEAD, HEAD), HEAD)
                v = vt_ref[0, rows, pl.ds(c * step, step)]
                out.append(dot_nn(v, p[:, j * queries : (j + 1) * queries]))
            return out

        mixed, log_total = softmax_sweep(scores, values, keys // step, 2 * queries)
        rows = jnp.concatenate(mixed, axis=0).T.reshape(tp, 1, tile, 2 * HEAD)
        o_ref[...] = rows.astype(bf16)
        wide_ref[...] = rows
        for j in range(2):
            log_ref[0, j] = jnp.broadcast_to(
                log_total[:, j * queries : (j + 1) * queries], (8, queries)
            )

    return pl.pallas_call(
        kernel,
        grid=(items, heads // 2),
        in_specs=[
            pl.BlockSpec((1, queries, width), lambda i, h: (i, 0, 0)),
            pl.BlockSpec((1, keys, width), lambda i, h: (i, 0, 0)),
            pl.BlockSpec((1, width, keys), lambda i, h: (i, 0, 0)),
        ],
        out_specs=[
            pl.BlockSpec((tp, 1, tile, 2 * HEAD), lambda i, h: (0, i, 0, h)),
            pl.BlockSpec((tp, 1, tile, 2 * HEAD), lambda i, h: (0, i, 0, h)),
            pl.BlockSpec((1, 2, 8, queries), lambda i, h: (i, h, 0, 0)),
        ],
        out_shape=[
            jax.ShapeDtypeStruct((tp, items, tile, width), bf16),
            jax.ShapeDtypeStruct((tp, items, tile, width), f32),
            jax.ShapeDtypeStruct((items, heads, 8, queries), f32),
        ],
        compiler_params=pltpu.CompilerParams(vmem_limit_bytes=48 << 20),
        cost_estimate=pl.CostEstimate(
            flops=16 * items * queries * keys * width,
            bytes_accessed=4 * items * (queries + keys) * width,
            transcendentals=items * queries * keys * heads,
        ),
        name="cross_forward",
    )(q, k, vt)


def cross_backward(q, do, o, logs, k, vt):
    items, queries, width = q.shape
    tp, _, tile, _ = do.shape
    keys = k.shape[1]
    heads = width // HEAD
    step = chunk_of(keys)

    def kernel(q_ref, do_ref, o_ref, log_ref, k_ref, vt_ref, dq_ref, dk_ref, dv_ref, qt, dot):
        head = pl.program_id(1)

        @pl.when(head == 0)
        def _():
            qt[...] = flip(q_ref[0])
            dot[...] = do_ref[...].astype(f32).reshape(queries, width).T.astype(bf16)

        mine = lax.broadcasted_iota(jnp.int32, (queries, width), 1) // HEAD == head
        q_mine = jnp.where(mine, q_ref[0], 0.0).astype(bf16)
        do_wide = jnp.where(mine, do_ref[...].astype(f32).reshape(queries, width), 0.0)
        do_mine = do_wide.astype(bf16)
        o_wide = o_ref[...].reshape(queries, width)
        delta = jnp.sum(do_wide * o_wide, axis=1, keepdims=True)
        log_total = log_ref[0, 0].T[:, :1] * LOG2E
        rows = pl.ds(pl.multiple_of(head * HEAD, HEAD), HEAD)
        qt_mine = qt[rows, :]
        dot_mine = dot[rows, :]

        def scores(c):
            s = dot_nt(q_mine, k_ref[0, pl.ds(c * step, step), :])
            return s, dot_nn(do_mine, vt_ref[0, :, pl.ds(c * step, step)])

        dq = jnp.zeros((queries, width), f32)
        ahead = scores(0)
        for c in range(keys // step):
            s, dp = ahead
            ahead = scores(c + 1) if c + 1 < keys // step else None
            p = jnp.exp2(s * LOG2E - log_total)
            ds = (p * (dp - delta)).astype(bf16)
            cols = pl.ds(c * step, step)
            dv_ref[0, :, cols] = dot_nn(dot_mine, p.astype(bf16)).astype(bf16)
            dk_ref[0, :, cols] = dot_nn(qt_mine, ds).astype(bf16)
            dq = dq + dot_nn(ds, k_ref[0, cols, :])
        dq = (dq * 0.125).astype(bf16)
        rest = jnp.where(head == 0, jnp.zeros_like(dq), dq_ref[0])
        dq_ref[0] = jnp.where(mine, dq, rest)

    rows_spec = pl.BlockSpec((1, queries, width), lambda i, h: (i, 0, 0))
    tiles_spec = pl.BlockSpec((tp, 1, tile, width), lambda i, h: (0, i, 0, 0))
    grads_spec = pl.BlockSpec((1, HEAD, keys), lambda i, h: (i, h, 0))
    return pl.pallas_call(
        kernel,
        grid=(items, heads),
        in_specs=[
            rows_spec,
            tiles_spec,
            tiles_spec,
            pl.BlockSpec((1, 1, 8, queries), lambda i, h: (i, h, 0, 0)),
            pl.BlockSpec((1, keys, width), lambda i, h: (i, 0, 0)),
            pl.BlockSpec((1, width, keys), lambda i, h: (i, 0, 0)),
        ],
        out_specs=[rows_spec, grads_spec, grads_spec],
        out_shape=[
            jax.ShapeDtypeStruct((items, queries, width), bf16),
            jax.ShapeDtypeStruct((items, width, keys), bf16),
            jax.ShapeDtypeStruct((items, width, keys), bf16),
        ],
        scratch_shapes=[pltpu.VMEM((width, queries), bf16), pltpu.VMEM((width, queries), bf16)],
        compiler_params=pltpu.CompilerParams(vmem_limit_bytes=48 << 20),
        cost_estimate=pl.CostEstimate(
            flops=40 * items * queries * keys * width,
            bytes_accessed=8 * items * (queries + keys) * width,
            transcendentals=items * queries * keys * heads,
        ),
        name="cross_backward",
    )(q, do, o, logs, k, vt)


def split_wide(x):
    low = lax.broadcasted_iota(jnp.int32, x.shape, 1) < HEAD
    wide = x.astype(f32)
    first = jnp.where(low, wide, 0.0)
    second = jnp.where(low, pltpu.roll(wide, HEAD, 1), 0.0)
    return jnp.concatenate([first, second], axis=0)


def split_pair(x):
    return split_wide(x).astype(bf16)


def part_specs(parts, half):
    if len(parts) == 1:
        return [pl.BlockSpec(parts[0].shape, lambda i: (0, 0, 0))]
    rows = parts[1].shape[0] // BLOCKS
    return [
        pl.BlockSpec(parts[0].shape, lambda i: (0, 0)),
        pl.BlockSpec((rows, 2 * HEAD), lambda i: (i, 0)),
    ]


def read_keys(refs, half):
    if len(refs) == 2:
        return refs[0][...]
    devices = refs[0].shape[0]
    return refs[0][:, : 2 * half, :].reshape(devices * 2 * half, 2 * HEAD)


def read_queries(refs, half, i, share):
    if len(refs) == 2:
        return refs[1][...]
    return refs[0][pl.ds(i * share, share), 2 * half :, :].reshape(share * half, 2 * HEAD)


def self_forward(parts, devices, half):
    tile = 2 * half
    keys = devices * tile
    blocks = BLOCKS
    share = devices // blocks
    block = share * half
    step = chunk_of(keys)

    def kernel(*refs):
        ins, (o_ref, wide_ref, log_ref, kv, vt) = refs[: len(parts)], refs[len(parts) :]
        i = pl.program_id(0)

        @pl.when(i == 0)
        def _():
            kv[...] = read_keys(ins, half)
            vt[...] = flip(kv[...])

        both = split_pair(read_queries(ins, half, i, share))

        def scores(c):
            return dot_nt(kv[pl.ds(c * step, step), :], both)

        def values(c, p):
            return [dot_nn(vt[HEAD:, pl.ds(c * step, step)], p)]

        mixed, log_total = softmax_sweep(scores, values, keys // step, 2 * block)
        mixed = mixed[0]
        rows = jnp.concatenate([mixed[:, :block], mixed[:, block:]], axis=0).T
        o_ref[...] = rows.astype(bf16)
        wide_ref[...] = rows
        log_ref[0] = jnp.broadcast_to(log_total, (8, 2 * block))

    return pl.pallas_call(
        kernel,
        grid=(blocks,),
        in_specs=part_specs(parts, half),
        out_specs=[
            pl.BlockSpec((block, 2 * HEAD), lambda i: (i, 0)),
            pl.BlockSpec((block, 2 * HEAD), lambda i: (i, 0)),
            pl.BlockSpec((1, 8, 2 * block), lambda i: (i, 0, 0)),
        ],
        out_shape=[
            jax.ShapeDtypeStruct((devices * half, 2 * HEAD), bf16),
            jax.ShapeDtypeStruct((devices * half, 2 * HEAD), f32),
            jax.ShapeDtypeStruct((blocks, 8, 2 * block), f32),
        ],
        scratch_shapes=[pltpu.VMEM((keys, 2 * HEAD), bf16), pltpu.VMEM((2 * HEAD, keys), bf16)],
        compiler_params=pltpu.CompilerParams(vmem_limit_bytes=48 << 20),
        cost_estimate=pl.CostEstimate(
            flops=16 * keys * keys * HEAD,
            bytes_accessed=8 * keys * 2 * HEAD,
            transcendentals=keys * keys,
        ),
        name="self_forward",
    )(*parts)


def self_backward(parts, do, o, logs, devices, half):
    tile = 2 * half
    keys = devices * tile
    blocks = logs.shape[0]
    share = devices // blocks
    block = share * half
    step = chunk_of(keys)

    def kernel(*refs):
        n = len(parts)
        ins, (do_ref, o_ref, log_ref), outs = refs[:n], refs[n : n + 3], refs[n + 3 : 2 * n + 3]
        kv, vt, grads = refs[2 * n + 3 :]
        i = pl.program_id(0)
        mine = pl.ds(i * share, share)

        @pl.when(i == 0)
        def _():
            kv[...] = read_keys(ins, half)
            vt[...] = flip(kv[...])
            grads[...] = jnp.zeros_like(grads)

        q_both = split_pair(read_queries(ins, half, i, share))
        do_both = split_pair(do_ref[...])
        delta = jnp.sum(do_both.astype(f32) * split_wide(o_ref[...]), axis=1, keepdims=True)
        log_total = log_ref[0].T[:, :1] * LOG2E
        qt = flip(q_both)[:HEAD]
        dot = flip(do_both)[:HEAD]
        do_low = do_both[:, :HEAD]

        def scores(c):
            s = dot_nt(q_both, kv[pl.ds(c * step, step), :])
            return s, dot_nn(do_low, vt[HEAD:, pl.ds(c * step, step)])

        dq = jnp.zeros((2 * block, 2 * HEAD), f32)
        ahead = scores(0)
        for c in range(keys // step):
            s, dp = ahead
            ahead = scores(c + 1) if c + 1 < keys // step else None
            p = jnp.exp2(s * LOG2E - log_total)
            ds = (p * (dp - delta)).astype(bf16)
            cols = pl.ds(c * step, step)
            grads[:HEAD, cols] += dot_nn(qt, ds)
            grads[HEAD:, cols] += dot_nn(dot, p.astype(bf16))
            dq = dq + dot_nn(ds, kv[cols, :])
        dq = dq * 0.125
        low = lax.broadcasted_iota(jnp.int32, (block, 2 * HEAD), 1) < HEAD
        packed = jnp.where(low, dq[:block], pltpu.roll(dq[block:], HEAD, 1)).astype(bf16)
        if n == 1:
            outs[0][mine, tile:, :] = packed.reshape(share, half, 2 * HEAD)
        else:
            outs[1][...] = packed

        @pl.when(i == blocks - 1)
        def _():
            dkv = grads[...].T.astype(bf16)
            if n == 1:
                outs[0][:, :tile, :] = dkv.reshape(devices, tile, 2 * HEAD)
            else:
                outs[0][...] = dkv

    rows_spec = pl.BlockSpec((block, 2 * HEAD), lambda i: (i, 0))
    return pl.pallas_call(
        kernel,
        grid=(blocks,),
        in_specs=part_specs(parts, half)
        + [rows_spec, rows_spec, pl.BlockSpec((1, 8, 2 * block), lambda i: (i, 0, 0))],
        out_specs=part_specs(parts, half),
        out_shape=[jax.ShapeDtypeStruct(p.shape, bf16) for p in parts],
        scratch_shapes=[
            pltpu.VMEM((keys, 2 * HEAD), bf16),
            pltpu.VMEM((2 * HEAD, keys), bf16),
            pltpu.VMEM((2 * HEAD, keys), f32),
        ],
        compiler_params=pltpu.CompilerParams(vmem_limit_bytes=48 << 20),
        cost_estimate=pl.CostEstimate(
            flops=40 * keys * keys * HEAD,
            bytes_accessed=16 * keys * 2 * HEAD,
            transcendentals=keys * keys,
        ),
        name="self_backward",
    )(*parts, do, o, logs)


def swap_pairs(first, second):
    low = lax.broadcasted_iota(jnp.int32, first.shape, 1) < HEAD
    return (
        jnp.where(low, first, pltpu.roll(second, HEAD, 1)),
        jnp.where(low, pltpu.roll(first, HEAD, 1), second),
    )


def tile_places(items, turns, groups, tile):
    return [(i * tile, i % turns, i // turns) for i in range(items)]


def project_pack(x, kv_w, q_w, items, turns, groups):
    rows, width = x.shape
    slots = kv_w.shape[0]
    tile = rows // items
    half = tile // 2

    def kernel(x_ref, kv_ref, q_ref, out_ref):
        kv = dot_nt(x_ref[...], kv_ref[0]).astype(bf16)
        q = dot_nt(x_ref[...], q_ref[0]).astype(bf16).astype(f32) * 0.125
        for start, turn, group in tile_places(items, turns, groups, tile):
            upper, lower = swap_pairs(q[start : start + half], q[start + half : start + tile])
            for h, part in enumerate((upper, lower)):
                out_ref[turn, group, 0, h, :tile, :] = kv[
                    start : start + tile, h * 2 * HEAD : (h + 1) * 2 * HEAD
                ]
                out_ref[turn, group, 0, h, tile:, :] = part.astype(bf16)

    shape = (turns, groups, slots, 2, 3 * half, 2 * HEAD)
    return pl.pallas_call(
        kernel,
        grid=(slots,),
        in_specs=[
            pl.BlockSpec((rows, width), lambda i: (0, 0)),
            pl.BlockSpec((1,) + kv_w.shape[1:], lambda i: (i, 0, 0)),
            pl.BlockSpec((1,) + q_w.shape[1:], lambda i: (i, 0, 0)),
        ],
        out_specs=pl.BlockSpec(
            (turns, groups, 1, 2, 3 * half, 2 * HEAD), lambda i: (0, 0, i, 0, 0, 0)
        ),
        out_shape=jax.ShapeDtypeStruct(shape, bf16),
        compiler_params=pltpu.CompilerParams(vmem_limit_bytes=40 << 20),
        cost_estimate=pl.CostEstimate(
            flops=2 * rows * width * slots * 6 * HEAD,
            bytes_accessed=2 * (rows + slots * 6 * HEAD) * width,
            transcendentals=0,
        ),
        name="project_pack",
    )(x, kv_w, q_w)


def unpack_project(blocks, weights, items, groups):
    turns = len(blocks)
    slots = weights.shape[0]
    half = blocks[0].shape[3]
    tile = 2 * half
    width = weights.shape[2]

    def kernel(*refs):
        ins, w_ref, flat_ref, out_ref = refs[:turns], refs[turns], refs[turns + 1], refs[turns + 2]
        slot = pl.program_id(0)
        for start, turn, group in tile_places(items, turns, groups, tile):
            pair = [ins[turn][group, 0, h].astype(f32) for h in range(2)]
            upper, lower = swap_pairs(*pair)
            flat_ref[start : start + half, :] = upper.astype(bf16)
            flat_ref[start + half : start + tile, :] = lower.astype(bf16)
        part = dot_nn(flat_ref[...], w_ref[0])

        @pl.when(slot == 0)
        def _():
            out_ref[...] = part

        @pl.when(slot > 0)
        def _():
            out_ref[...] += part

    return pl.pallas_call(
        kernel,
        grid=(slots,),
        in_specs=[
            pl.BlockSpec((groups, 1, 2, half, 2 * HEAD), lambda i: (0, i, 0, 0, 0))
            for _ in range(turns)
        ]
        + [pl.BlockSpec((1,) + weights.shape[1:], lambda i: (i, 0, 0))],
        out_specs=[
            pl.BlockSpec((items * tile, 2 * HEAD), lambda i: (0, i)),
            pl.BlockSpec((items * tile, width), lambda i: (0, 0)),
        ],
        out_shape=[
            jax.ShapeDtypeStruct((items * tile, slots * 2 * HEAD), bf16),
            jax.ShapeDtypeStruct((items * tile, width), f32),
        ],
        compiler_params=pltpu.CompilerParams(vmem_limit_bytes=40 << 20),
        cost_estimate=pl.CostEstimate(
            flops=2 * items * tile * width * slots * 2 * HEAD,
            bytes_accessed=4 * items * tile * width,
            transcendentals=0,
        ),
        name="unpack_project",
    )(*blocks, weights)


def back_pack(x, weights, items, turns, groups):
    rows, width = x.shape
    slots = weights.shape[0]
    tile = rows // items
    half = tile // 2

    def kernel(x_ref, w_ref, out_ref):
        grads = dot_nt(x_ref[...], w_ref[0])
        for start, turn, group in tile_places(items, turns, groups, tile):
            pair = swap_pairs(grads[start : start + half], grads[start + half : start + tile])
            for h, part in enumerate(pair):
                out_ref[turn, group, 0, h] = part.astype(bf16)

    return pl.pallas_call(
        kernel,
        grid=(slots,),
        in_specs=[
            pl.BlockSpec((rows, width), lambda i: (0, 0)),
            pl.BlockSpec((1,) + weights.shape[1:], lambda i: (i, 0, 0)),
        ],
        out_specs=pl.BlockSpec(
            (turns, groups, 1, 2, half, 2 * HEAD), lambda i: (0, 0, i, 0, 0, 0)
        ),
        out_shape=jax.ShapeDtypeStruct((turns, groups, slots, 2, half, 2 * HEAD), bf16),
        compiler_params=pltpu.CompilerParams(vmem_limit_bytes=40 << 20),
        cost_estimate=pl.CostEstimate(
            flops=2 * rows * width * slots * 2 * HEAD,
            bytes_accessed=2 * (rows + slots * 2 * HEAD) * width,
            transcendentals=0,
        ),
        name="back_pack",
    )(x, weights)


def unpack_back(blocks, kv_w, q_w, items, groups):
    turns = len(blocks)
    slots, _, width = kv_w.shape
    half = blocks[0].shape[3] // 3
    tile = 2 * half
    rows = items * tile

    def kernel(*refs):
        ins = refs[:turns]
        kv_ref, q_ref, flat_ref, out_ref = refs[turns:]
        slot = pl.program_id(0)
        for start, turn, group in tile_places(items, turns, groups, tile):
            pair = []
            for h in range(2):
                flat_ref[0, start : start + tile, h * 2 * HEAD : (h + 1) * 2 * HEAD] = ins[turn][
                    group, 0, h, :tile, :
                ]
                pair.append(ins[turn][group, 0, h, tile:, :].astype(f32))
            upper, lower = swap_pairs(*pair)
            flat_ref[0, start : start + half, 4 * HEAD :] = upper.astype(bf16)
            flat_ref[0, start + half : start + tile, 4 * HEAD :] = lower.astype(bf16)
        part = dot_nn(flat_ref[0, :, : 4 * HEAD], kv_ref[0])
        part = part + dot_nn(flat_ref[0, :, 4 * HEAD :], q_ref[0])

        @pl.when(slot == 0)
        def _():
            out_ref[...] = part

        @pl.when(slot > 0)
        def _():
            out_ref[...] += part

    return pl.pallas_call(
        kernel,
        grid=(slots,),
        in_specs=[
            pl.BlockSpec((groups, 1, 2, 3 * half, 2 * HEAD), lambda i: (0, i, 0, 0, 0))
            for _ in range(turns)
        ]
        + [
            pl.BlockSpec((1,) + kv_w.shape[1:], lambda i: (i, 0, 0)),
            pl.BlockSpec((1,) + q_w.shape[1:], lambda i: (i, 0, 0)),
        ],
        out_specs=[
            pl.BlockSpec((1, rows, 6 * HEAD), lambda i: (i, 0, 0)),
            pl.BlockSpec((rows, width), lambda i: (0, 0)),
        ],
        out_shape=[
            jax.ShapeDtypeStruct((slots, rows, 6 * HEAD), bf16),
            jax.ShapeDtypeStruct((rows, width), f32),
        ],
        compiler_params=pltpu.CompilerParams(vmem_limit_bytes=40 << 20),
        cost_estimate=pl.CostEstimate(
            flops=2 * rows * width * slots * 6 * HEAD,
            bytes_accessed=4 * rows * width,
            transcendentals=0,
        ),
        name="unpack_back",
    )(*blocks, kv_w, q_w)


def exchange(x, axis):
    return lax.all_to_all(x, axis, 0, 0, tiled=True)


def gather(x, axis):
    return exchange(jnp.broadcast_to(x[None], (lax.axis_size(axis),) + x.shape), axis)


def reduce_blocks(x, axis):
    return jnp.sum(exchange(x.astype(bf16), axis).astype(f32), axis=0)


def body(
    tokens,
    context,
    group_ids,
    source_table,
    w_query,
    w_key,
    w_value,
    w_out,
    w_self_query,
    w_self_key,
    w_self_value,
    w_self_out,
    w_up,
    w_down,
    w_deconv,
    deconv_bias,
    out_cotangent,
    plane_cotangent,
):
    rows_here, items, plane_cols, width = tokens.shape
    cols_here = out_cotangent.shape[2]
    tp = lax.axis_size("tp")
    seq = lax.axis_size("seq")
    both_axes = ("seq", "tp")
    devices = tp * seq
    local = w_query.shape[1]
    hidden_here = w_up.shape[1]
    slots = 2 * tp
    slot_heads = local // HEAD // 2
    slot_width = local // 2
    heads = slots * slot_heads
    tile = rows_here * cols_here
    half = tile // 2
    groups = devices // heads
    turns = -(-items // groups)
    share = width // seq
    fast = slot_heads == 2 and half % 16 == 0 and items == groups * turns and not FORCE_PLAIN
    me_tp = lax.axis_index("tp")
    core = lax.axis_index("seq") % 2

    picker = (group_ids[:, None] == jnp.arange(GROUPS, dtype=jnp.int32)[None, :]).astype(f32)
    mods = jnp.dot(picker, source_table, precision=highest).reshape(items, 9, 1, width)

    def piece(index):
        return mods[:, index]

    def dot(spec, a, b):
        return jnp.einsum(spec, a, b, preferred_element_type=f32)

    def to_tile(x):
        return x.transpose(1, 0, 2, 3).reshape(items, tile, width)

    def from_tile(x):
        return x.reshape(items, rows_here, cols_here, width).transpose(1, 0, 2, 3)

    teams = [
        [(2 * pair + c) * tp + t for c in range(2) for t in range(tp)] for pair in range(seq // 2)
    ]

    def whole(x):
        return lax.all_gather(x, both_axes, axis=0, tiled=False, axis_index_groups=teams)

    def my_rows(x):
        return lax.dynamic_slice_in_dim(x, core * slot_width, slot_width, 0)

    def my_columns(x):
        size = x.shape[1] // 2
        return lax.dynamic_slice_in_dim(x, core * size, size, 1)

    key_value = jnp.stack(
        [
            my_columns(w_self_key).T.reshape(slot_heads, HEAD, width),
            my_columns(w_self_value).T.reshape(slot_heads, HEAD, width),
        ],
        axis=1,
    ).reshape(2 * slot_width, width)
    small = whole(
        jnp.concatenate(
            [
                my_rows(w_out),
                key_value,
                my_columns(w_self_query).T,
                my_rows(w_self_out),
                my_columns(w_query).T,
            ],
            axis=0,
        )
    )
    cuts = [slot_width * k for k in (0, 1, 3, 4, 5, 6)]
    out_slots, kv_slots, q_slots, so_slots, query_slots = [
        small[:, a:b] for a, b in zip(cuts[:-1], cuts[1:])
    ]
    up_slots = whole(my_columns(w_up))
    down_slots = whole(
        lax.dynamic_slice_in_dim(w_down, core * (hidden_here // 2), hidden_here // 2, 0)
    )

    def by_tp(x):
        return x.reshape(2, tp, slot_width, width).transpose(1, 0, 2, 3).reshape(tp, local, width)

    incoming = plane_cotangent.reshape(2 * rows_here, items, 2 * cols_here, COUT)
    plane_row = (lax.axis_index("seq") * rows_here + jnp.arange(rows_here, dtype=jnp.int32)) % PLANE
    upper_keep = (plane_row != 0).astype(f32)
    lower_keep = (plane_row != PLANE - 1).astype(f32)
    grad_edges = with_halo(incoming, (("seq", 0), ("tp", 2)), 1)
    upper_mask = upper_keep.astype(bf16)[:, None, None, None]
    lower_mask = lower_keep.astype(bf16)[:, None, None, None]
    first_pair = grad_edges[:-2].reshape(rows_here, 2, items, 2 * cols_here + 2, COUT)
    last_pair = grad_edges[2:].reshape(rows_here, 2, items, 2 * cols_here + 2, COUT)
    row_taps = jnp.stack(
        [
            first_pair[:, 0] * upper_mask,
            first_pair[:, 1],
            last_pair[:, 0],
            last_pair[:, 1] * lower_mask,
        ],
        axis=3,
    )
    left_pair = row_taps[:, :, :-2].reshape(rows_here, items, cols_here, 2, 4, COUT)
    right_pair = row_taps[:, :, 2:].reshape(rows_here, items, cols_here, 2, 4, COUT)
    tap_grads = jnp.stack(
        [
            left_pair[:, :, :, 0],
            left_pair[:, :, :, 1],
            right_pair[:, :, :, 0],
            right_pair[:, :, :, 1],
        ],
        axis=4,
    )
    tap_grads = tap_grads.reshape(rows_here, items, cols_here, 16 * COUT)
    grad_result = to_tile(out_cotangent.astype(f32) + dot("rict,dt->ricd", tap_grads, w_deconv))
    grad_bias = jnp.sum(incoming.astype(f32), axis=(0, 1, 2))
    grad_mlp = (piece(8) * grad_result).astype(bf16)

    ordered = (
        tokens.reshape(rows_here, items, tp, cols_here, width)
        .transpose(1, 2, 0, 3, 4)
        .reshape(items, tp * tile, width)
    )
    first_hat, first_inv = norm_parts(ordered.astype(f32))
    first_in = (first_hat * (1.0 + piece(1)) + piece(0)).astype(bf16)
    queries = dot("iqd,de->iqe", first_in, w_query).astype(bf16) * bf16(0.125)
    keys = dot("pid,de->ipe", context, w_key).astype(bf16)
    values_t = dot("pid,de->iep", context, w_value).astype(bf16)
    mixed, mixed_wide, cross_logs = cross_forward(queries, keys, values_t, tp)
    mixed_tile = exchange(mixed, "tp")
    out_whole = by_tp(out_slots)
    branch_a = dot("time,tef->imf", mixed_tile, out_whole)
    residual = to_tile(lax.dynamic_slice_in_dim(tokens, me_tp * cols_here, cols_here, 2)).astype(f32)
    middle = residual + piece(2) * branch_a

    self_hat, self_inv = norm_parts(middle)
    self_in = (self_hat * (1.0 + piece(4)) + piece(3)).astype(bf16)
    flat = (items * tile, width)
    spare = groups * turns - items

    def spread_items(x):
        if spare:
            x = jnp.pad(x, ((0, 0), (0, spare)) + ((0, 0),) * (x.ndim - 2))
        return x.reshape((slots, groups, turns) + x.shape[2:])

    def pack_keys(x):
        x = spread_items(x.reshape(slots, items, tile, slot_heads, 2 * HEAD))
        return x.transpose(2, 1, 0, 4, 3, 5).reshape(turns, devices, tile, 2 * HEAD)

    def unpack_keys(x):
        x = x.reshape(turns, groups, slots, slot_heads, tile, 2 * HEAD).transpose(2, 1, 0, 4, 3, 5)
        x = x.reshape(slots, groups * turns, tile, 2 * slot_width)[:, :items]
        return x.reshape(slots, items * tile, 2 * slot_width)

    def pack_rows(x):
        x = spread_items(x.reshape(slots, items, 2, half, slot_heads, HEAD))
        return x.transpose(2, 1, 0, 5, 4, 3, 6).reshape(turns, devices, half, 2 * HEAD)

    def unpack_rows(x):
        x = x.reshape(turns, groups, slots, slot_heads, half, 2, HEAD).transpose(2, 1, 0, 5, 4, 3, 6)
        x = x.reshape(slots, groups * turns, tile, slot_width)[:, :items]
        return x.reshape(slots, items * tile, slot_width)

    if fast:
        sends = project_pack(self_in.reshape(flat), kv_slots, q_slots, items, turns, groups)
        sends = sends.reshape(turns, devices, 3 * half, 2 * HEAD)
        parts = [[exchange(sends[turn], both_axes)] for turn in range(turns)]
    else:
        kv_sends = pack_keys(dot("nd,xed->xne", self_in.reshape(flat), kv_slots).astype(bf16))
        q_sends = dot("nd,xed->xne", self_in.reshape(flat), q_slots).astype(bf16)
        q_sends = pack_rows(q_sends * bf16(0.125))
        parts = [
            [
                exchange(kv_sends[turn], both_axes).reshape(devices * tile, 2 * HEAD),
                exchange(q_sends[turn], both_axes).reshape(devices * half, 2 * HEAD),
            ]
            for turn in range(turns)
        ]
    forward = [self_forward(parts[turn], devices, half) for turn in range(turns)]
    so_back = [exchange(so.reshape(devices, half, 2 * HEAD), both_axes) for so, _, _ in forward]
    if fast:
        blocks = [x.reshape(groups, slots, 2, half, 2 * HEAD) for x in so_back]
        so_tile, branch_s = unpack_project(blocks, so_slots, items, groups)
    else:
        so_tile = unpack_rows(jnp.stack(so_back)).transpose(1, 0, 2)
        branch_s = dot("nxe,xed->nd", so_tile, so_slots)
        so_tile = so_tile.reshape(items * tile, heads * HEAD)
    branch_s = branch_s.reshape(items, tile, width)
    middle_two = middle + piece(5) * branch_s

    second_hat, second_inv = norm_parts(middle_two)
    second_in = (second_hat * (1.0 + piece(7)) + piece(6)).astype(bf16)
    hidden = dot("imd,xdf->ximf", second_in, up_slots)
    active_f, gelu_back = jax.vjp(lambda value: jax.nn.gelu(value, approximate=False), hidden)
    active = active_f.astype(bf16)
    branch_b = dot("ximf,xfd->imd", active, down_slots)
    result = middle_two + piece(8) * branch_b
    out_tile = from_tile(result.astype(bf16))

    grad_active = dot("imd,xfd->ximf", grad_mlp, down_slots)
    grad_hidden = gelu_back(grad_active)[0].astype(bf16)
    grad_second = dot("ximf,xdf->imd", grad_hidden, up_slots)
    grad_gate_b = jnp.sum(grad_result * branch_b, axis=1)
    grad_shift_b = jnp.sum(grad_second, axis=1)
    grad_scale_b = jnp.sum(grad_second * second_hat, axis=1)
    grad_mid_two = grad_result + norm_back(second_hat, second_inv, grad_second * (1.0 + piece(7)))

    widened = with_halo(out_tile, (("seq", 0), ("tp", 2)), 1)
    taps = dot("ricd,dt->rict", widened, w_deconv)
    taps = taps.reshape(rows_here + 2, items, cols_here + 2, 4, 4, COUT)
    planes = spread_taps(
        taps, upper_keep[:, None, None, None, None], lower_keep[:, None, None, None, None]
    )
    planes = planes + jnp.tile(deconv_bias, 2 * cols_here)

    def by_device(x):
        lead = x.shape[0] // tp
        x = x.reshape(lead, tp, x.shape[1], seq, share).transpose(1, 3, 0, 2, 4)
        return x.reshape(devices, -1, share).astype(bf16)

    def total(parts):
        sizes = [p.shape[1] for p in parts]
        summed = lax.psum_scatter(
            jnp.concatenate(parts, axis=1), ("tp", "seq"), scatter_dimension=0, tiled=True
        )[0].astype(f32)
        out, at = [], 0
        for size in sizes:
            out.append(summed[at : at + size])
            at += size
        return out

    terms_b = [
        by_device(dot("ximf,imd->xfd", grad_hidden, second_in)),
        by_device(dot("ximf,imd->xfd", active, grad_mlp)),
        by_device(dot("rict,ricd->td", tap_grads, out_tile).reshape(tp, 16 * COUT // tp, width)),
    ]
    grad_self = (piece(5) * grad_mid_two).astype(bf16)
    grad_gate_s = jnp.sum(grad_mid_two * branch_s, axis=1)
    if fast:
        dso_send = back_pack(grad_self.reshape(flat), so_slots, items, turns, groups)
        dso_send = dso_send.reshape(turns, devices, half, 2 * HEAD)
    else:
        dso_send = pack_rows(dot("nd,xed->xne", grad_self.reshape(flat), so_slots).astype(bf16))
    dso_mine = [
        exchange(dso_send[turn], both_axes).reshape(devices * half, 2 * HEAD)
        for turn in range(turns)
    ]
    dso_mine[0], terms_b = lax.optimization_barrier((dso_mine[0], terms_b))
    grad_up, grad_down, grad_deconv = total(terms_b)
    backward = [
        self_backward(parts[turn], dso_mine[turn], *forward[turn][1:], devices, half)
        for turn in range(turns)
    ]
    if fast:
        blocks = [
            exchange(x[0], both_axes).reshape(groups, slots, 2, 3 * half, 2 * HEAD)
            for x in backward
        ]
        blocks[-1], planes = lax.optimization_barrier((blocks[-1], planes))
        grad_projected, grad_third = unpack_back(blocks, kv_slots, q_slots, items, groups)
    else:
        dkv = [exchange(x[0].reshape(devices, tile, 2 * HEAD), both_axes) for x in backward]
        dq = [exchange(x[1].reshape(devices, half, 2 * HEAD), both_axes) for x in backward]
        grad_projected = jnp.concatenate(
            [unpack_keys(jnp.stack(dkv)), unpack_rows(jnp.stack(dq))], axis=2
        )
        grad_third = dot(
            "xne,xed->nd", grad_projected, jnp.concatenate([kv_slots, q_slots], axis=1)
        )
    grad_third = grad_third.reshape(items, tile, width)
    grad_shift_s = jnp.sum(grad_third, axis=1)
    grad_scale_s = jnp.sum(grad_third * self_hat, axis=1)
    grad_middle = grad_mid_two + norm_back(self_hat, self_inv, grad_third * (1.0 + piece(4)))

    grad_attn = (piece(2) * grad_middle).astype(bf16)
    grad_gate_a = jnp.sum(grad_middle * branch_a, axis=1)
    do_mine = exchange(dot("imf,tef->time", grad_attn, out_whole).astype(bf16), "tp")
    middle_all = gather(grad_middle.astype(bf16), "tp")
    early = jnp.stack(
        [
            grad_gate_a,
            grad_shift_s,
            grad_scale_s,
            grad_gate_s,
            grad_shift_b,
            grad_scale_b,
            grad_gate_b,
        ],
        axis=0,
    ).reshape(7 * items, width)
    early = jnp.concatenate(
        [early, jnp.pad(grad_bias, (0, width - COUT))[None]], axis=0
    )
    spots = -(-early.shape[0] // (16 * tp)) * 16
    early = jnp.pad(early, ((0, spots * tp - early.shape[0]), (0, 0))).reshape(tp, spots, width)
    terms_a = [
            by_device(dot("xne,nd->xed", grad_projected, self_in.reshape(flat))),
            by_device(
                dot("ne,nd->ed", so_tile, grad_self.reshape(flat)).reshape(
                    slots, slot_width, width
                )
            ),
            by_device(dot("time,imf->tef", mixed_tile, grad_attn)),
            by_device(early),
    ]
    do_mine, terms_a = lax.optimization_barrier((do_mine, terms_a))
    terms_a, grad_up = lax.optimization_barrier((terms_a, grad_up))
    grad_three, grad_self_out, grad_out, grad_early = total(terms_a)
    dq_cross, dk_t, dv_t = cross_backward(queries, do_mine, mixed_wide, cross_logs, keys, values_t)
    dq_cross, middle_all = lax.optimization_barrier((dq_cross, middle_all))
    dq_all = gather(dq_cross, "tp")
    grad_three = grad_three.reshape(2, 3 * slot_width, share)
    grad_pair = grad_three[:, : 2 * slot_width].reshape(2, slot_heads, 2, HEAD, share)
    grad_self_key = grad_pair[:, :, 0].reshape(local, share).T
    grad_self_value = grad_pair[:, :, 1].reshape(local, share).T
    grad_self_query = grad_three[:, 2 * slot_width :].reshape(local, share).T

    shared = lax.all_gather(
        jnp.concatenate([grad_deconv, grad_early], axis=0), ("tp", "seq"), axis=0, tiled=False
    )
    shared = shared.reshape(tp, seq, -1, share).transpose(0, 2, 1, 3).reshape(tp, -1, width)
    grad_deconv = shared[:, : 16 * COUT // tp].reshape(16 * COUT, width).T
    early = shared[:, 16 * COUT // tp :].reshape(-1, width)
    grad_bias = early[7 * items, :COUT]
    early = early[: 7 * items].reshape(7, items, width)

    def by_seq(x):
        return x.reshape((seq, x.shape[0] // seq) + x.shape[1:]).astype(bf16)

    last = jnp.concatenate(
        [
            by_seq(dot("iqd,iqe->de", first_in, dq_cross)),
            by_seq(dot("pid,iep->de", context, dk_t)),
            by_seq(dot("pid,iep->de", context, dv_t)),
        ],
        axis=1,
    )
    last, dq_all = lax.optimization_barrier((last, dq_all))
    last = jnp.sum(exchange(last, "seq").astype(f32), axis=0)
    grad_first = dot("tiqe,ted->iqd", dq_all, by_tp(query_slots))
    grad_shift_a = jnp.sum(grad_first, axis=1)
    grad_scale_a = jnp.sum(grad_first * first_hat, axis=1)
    grad_tokens = middle_all.astype(f32).transpose(1, 0, 2, 3).reshape(
        items, tp * tile, width
    ) + norm_back(first_hat, first_inv, grad_first * (1.0 + piece(1)))
    grad_tokens = (
        grad_tokens.reshape(items, tp, rows_here, cols_here, width)
        .transpose(2, 0, 1, 3, 4)
        .reshape(rows_here, items, plane_cols, width)
    )

    depth = (last.shape[0] - share) // 2
    grad_query, grad_key, grad_value = (
        last[:share],
        last[share : share + depth],
        last[share + depth :],
    )
    late = jnp.sum(gather(jnp.stack([grad_shift_a, grad_scale_a], axis=0), "seq"), axis=0)
    grad_mods = jnp.concatenate([late, early], axis=0).transpose(1, 0, 2)
    grad_table = jnp.dot(picker.T, grad_mods.reshape(items, 9 * width), precision=highest)
    return (
        out_tile,
        planes,
        grad_tokens,
        grad_query,
        grad_key,
        grad_value,
        grad_out,
        grad_self_query,
        grad_self_key,
        grad_self_value,
        grad_self_out.reshape(local, share),
        grad_up.T,
        grad_down,
        grad_deconv,
        grad_bias,
        grad_table,
    )


def solution(mesh):
    in_specs = (
        P("seq", None, None, None),
        P(),
        P(),
        P(),
        P(None, "tp"),
        P(None, "tp"),
        P(None, "tp"),
        P("tp", None),
        P(None, "tp"),
        P(None, "tp"),
        P(None, "tp"),
        P("tp", None),
        P(None, "tp"),
        P("tp", None),
        P(),
        P(),
        P("seq", None, "tp", None),
        P("seq", None, "tp"),
    )
    out_specs = (
        P("seq", None, "tp", None),
        P("seq", None, "tp"),
        P("seq", None, None, None),
        P("seq", "tp"),
        P("seq", "tp"),
        P("seq", "tp"),
        P("tp", "seq"),
        P("seq", "tp"),
        P("seq", "tp"),
        P("seq", "tp"),
        P("tp", "seq"),
        P("seq", "tp"),
        P("tp", "seq"),
        P(),
        P(),
        P(),
    )
    return jax.shard_map(body, mesh=mesh, in_specs=in_specs, out_specs=out_specs, check_vma=False)
```

```python
import jax
import jax.numpy as jnp
from jax import lax
from jax.experimental import pallas as pl
from jax.experimental.pallas import tpu as pltpu
from jax.sharding import PartitionSpec as P

HEAD = 64
COUT = 80
PLANE = 32
IMG = 4096
LOG2E = 1.4426950408889634
bf16 = jnp.bfloat16
f32 = jnp.float32
GROUPS = 16


highest = lax.Precision.HIGHEST
epsilon = 1e-06


def with_halo(x, sides, width):
    for axis, dim in sides:
        peers, length = (lax.axis_size(axis), x.shape[dim])
        up = [(i, (i + 1) % peers) for i in range(peers - 1)]
        down = [(j, i) for i, j in up]
        last = lax.slice_in_dim(x, length - width, length, axis=dim)
        initial = lax.slice_in_dim(x, 0, width, axis=dim)
        before = lax.ppermute(last, axis, up)
        after = lax.ppermute(initial, axis, down)
        x = jnp.concatenate([before, x, after], axis=dim)
    return x


def spread_taps(padded, upper, lower):
    even_rows = padded[1:-1, :, :, 1] + upper * padded[:-2, :, :, 3]
    odd_rows = lower * padded[2:, :, :, 0] + padded[1:-1, :, :, 2]
    rows_both = jnp.stack([even_rows, odd_rows], axis=1)
    even_cols = rows_both[:, :, :, 1:-1, 1] + rows_both[:, :, :, :-2, 3]
    odd_cols = rows_both[:, :, :, 2:, 0] + rows_both[:, :, :, 1:-1, 2]
    joined = jnp.stack([even_cols, odd_cols], axis=4)
    shape = joined.shape
    return joined.reshape(shape[0] * 2, shape[2], shape[3] * 2 * shape[5])


def norm_parts(value):
    centred = value - jnp.mean(value, axis=-1, keepdims=True)
    inverse = lax.rsqrt(jnp.mean(centred * centred, axis=-1, keepdims=True) + epsilon)
    return (centred * inverse, inverse)


def norm_back(normed, inverse, incoming):
    return inverse * (
        incoming
        - jnp.mean(incoming, axis=-1, keepdims=True)
        - normed * jnp.mean(incoming * normed, axis=-1, keepdims=True)
    )


NT = (((1,), (1,)), ((), ()))
BLOCKS = 4


def dot_nt(a, b):
    return lax.dot_general(a, b, NT, preferred_element_type=f32)


def dot_nn(a, b):
    return jnp.dot(a, b, preferred_element_type=f32)


def flip(x):
    return x.astype(f32).T.astype(bf16)


def chunk_of(keys):
    return 512 if keys % 512 == 0 else keys


def softmax_sweep(scores, values, chunks, columns):
    top = jnp.full((1, columns), -1e30, f32)
    total = jnp.zeros((1, columns), f32)
    mixed = None
    ahead = scores(0)
    for c in range(chunks):
        now = ahead
        ahead = scores(c + 1) if c + 1 < chunks else None
        new_top = jnp.maximum(top, jnp.max(now, axis=0, keepdims=True))
        fade = jnp.exp2((top - new_top) * LOG2E)
        expon = jnp.exp2(now * LOG2E - new_top * LOG2E)
        total = total * fade + jnp.sum(expon, axis=0, keepdims=True)
        parts = values(c, expon.astype(bf16))
        width = columns // len(parts)
        if mixed is None:
            mixed = parts
        else:
            mixed = [
                m * fade[:, j * width : (j + 1) * width] + part
                for j, (m, part) in enumerate(zip(mixed, parts))
            ]
        top = new_top
    width = columns // len(mixed)
    inverse = 1.0 / total
    mixed = [m * inverse[:, j * width : (j + 1) * width] for j, m in enumerate(mixed)]
    return mixed, top + jnp.log(total)


def cross_forward(q, k, vt, tp):
    items, queries, width = q.shape
    tile = queries // tp
    keys = k.shape[1]
    heads = width // HEAD
    step = chunk_of(keys)

    def kernel(q_ref, k_ref, vt_ref, o_ref, wide_ref, log_ref):
        pair = pl.program_id(1)
        owner = lax.broadcasted_iota(jnp.int32, (queries, width), 1) // HEAD
        both = jnp.concatenate(
            [jnp.where(owner == pair * 2 + j, q_ref[0], 0.0).astype(bf16) for j in range(2)], axis=0
        )

        def scores(c):
            return dot_nt(k_ref[0, pl.ds(c * step, step), :], both)

        def values(c, p):
            out = []
            for j in range(2):
                rows = pl.ds(pl.multiple_of((pair * 2 + j) * HEAD, HEAD), HEAD)
                v = vt_ref[0, rows, pl.ds(c * step, step)]
                out.append(dot_nn(v, p[:, j * queries : (j + 1) * queries]))
            return out

        mixed, log_total = softmax_sweep(scores, values, keys // step, 2 * queries)
        rows = jnp.concatenate(mixed, axis=0).T.reshape(tp, 1, tile, 2 * HEAD)
        o_ref[...] = rows.astype(bf16)
        wide_ref[...] = rows
        for j in range(2):
            log_ref[0, j] = jnp.broadcast_to(
                log_total[:, j * queries : (j + 1) * queries], (8, queries)
            )

    return pl.pallas_call(
        kernel,
        grid=(items, heads // 2),
        in_specs=[
            pl.BlockSpec((1, queries, width), lambda i, h: (i, 0, 0)),
            pl.BlockSpec((1, keys, width), lambda i, h: (i, 0, 0)),
            pl.BlockSpec((1, width, keys), lambda i, h: (i, 0, 0)),
        ],
        out_specs=[
            pl.BlockSpec((tp, 1, tile, 2 * HEAD), lambda i, h: (0, i, 0, h)),
            pl.BlockSpec((tp, 1, tile, 2 * HEAD), lambda i, h: (0, i, 0, h)),
            pl.BlockSpec((1, 2, 8, queries), lambda i, h: (i, h, 0, 0)),
        ],
        out_shape=[
            jax.ShapeDtypeStruct((tp, items, tile, width), bf16),
            jax.ShapeDtypeStruct((tp, items, tile, width), f32),
            jax.ShapeDtypeStruct((items, heads, 8, queries), f32),
        ],
        compiler_params=pltpu.CompilerParams(vmem_limit_bytes=48 << 20),
        cost_estimate=pl.CostEstimate(
            flops=16 * items * queries * keys * width,
            bytes_accessed=4 * items * (queries + keys) * width,
            transcendentals=items * queries * keys * heads,
        ),
        name="cross_forward",
    )(q, k, vt)


def cross_backward(q, do, o, logs, k, vt):
    items, queries, width = q.shape
    tp, _, tile, _ = do.shape
    keys = k.shape[1]
    heads = width // HEAD
    step = chunk_of(keys)

    def kernel(q_ref, do_ref, o_ref, log_ref, k_ref, vt_ref, dq_ref, dk_ref, dv_ref, qt, dot):
        head = pl.program_id(1)

        @pl.when(head == 0)
        def _():
            qt[...] = flip(q_ref[0])
            dot[...] = do_ref[...].astype(f32).reshape(queries, width).T.astype(bf16)

        mine = lax.broadcasted_iota(jnp.int32, (queries, width), 1) // HEAD == head
        q_mine = jnp.where(mine, q_ref[0], 0.0).astype(bf16)
        do_wide = jnp.where(mine, do_ref[...].astype(f32).reshape(queries, width), 0.0)
        do_mine = do_wide.astype(bf16)
        o_wide = o_ref[...].reshape(queries, width)
        delta = jnp.sum(do_wide * o_wide, axis=1, keepdims=True)
        log_total = log_ref[0, 0].T[:, :1] * LOG2E
        rows = pl.ds(pl.multiple_of(head * HEAD, HEAD), HEAD)
        qt_mine = qt[rows, :]
        dot_mine = dot[rows, :]

        def scores(c):
            s = dot_nt(q_mine, k_ref[0, pl.ds(c * step, step), :])
            return s, dot_nn(do_mine, vt_ref[0, :, pl.ds(c * step, step)])

        dq = jnp.zeros((queries, width), f32)
        ahead = scores(0)
        for c in range(keys // step):
            s, dp = ahead
            ahead = scores(c + 1) if c + 1 < keys // step else None
            p = jnp.exp2(s * LOG2E - log_total)
            ds = (p * (dp - delta)).astype(bf16)
            cols = pl.ds(c * step, step)
            dv_ref[0, :, cols] = dot_nn(dot_mine, p.astype(bf16)).astype(bf16)
            dk_ref[0, :, cols] = dot_nn(qt_mine, ds).astype(bf16)
            dq = dq + dot_nn(ds, k_ref[0, cols, :])
        dq = (dq * 0.125).astype(bf16)
        rest = jnp.where(head == 0, jnp.zeros_like(dq), dq_ref[0])
        dq_ref[0] = jnp.where(mine, dq, rest)

    rows_spec = pl.BlockSpec((1, queries, width), lambda i, h: (i, 0, 0))
    tiles_spec = pl.BlockSpec((tp, 1, tile, width), lambda i, h: (0, i, 0, 0))
    grads_spec = pl.BlockSpec((1, HEAD, keys), lambda i, h: (i, h, 0))
    return pl.pallas_call(
        kernel,
        grid=(items, heads),
        in_specs=[
            rows_spec,
            tiles_spec,
            tiles_spec,
            pl.BlockSpec((1, 1, 8, queries), lambda i, h: (i, h, 0, 0)),
            pl.BlockSpec((1, keys, width), lambda i, h: (i, 0, 0)),
            pl.BlockSpec((1, width, keys), lambda i, h: (i, 0, 0)),
        ],
        out_specs=[rows_spec, grads_spec, grads_spec],
        out_shape=[
            jax.ShapeDtypeStruct((items, queries, width), bf16),
            jax.ShapeDtypeStruct((items, width, keys), bf16),
            jax.ShapeDtypeStruct((items, width, keys), bf16),
        ],
        scratch_shapes=[pltpu.VMEM((width, queries), bf16), pltpu.VMEM((width, queries), bf16)],
        compiler_params=pltpu.CompilerParams(vmem_limit_bytes=48 << 20),
        cost_estimate=pl.CostEstimate(
            flops=40 * items * queries * keys * width,
            bytes_accessed=8 * items * (queries + keys) * width,
            transcendentals=items * queries * keys * heads,
        ),
        name="cross_backward",
    )(q, do, o, logs, k, vt)


def split_wide(x):
    low = lax.broadcasted_iota(jnp.int32, x.shape, 1) < HEAD
    wide = x.astype(f32)
    first = jnp.where(low, wide, 0.0)
    second = jnp.where(low, pltpu.roll(wide, HEAD, 1), 0.0)
    return jnp.concatenate([first, second], axis=0)


def split_pair(x):
    return split_wide(x).astype(bf16)


def part_specs(parts, half):
    if len(parts) == 1:
        return [pl.BlockSpec(parts[0].shape, lambda i: (0, 0, 0))]
    rows = parts[1].shape[0] // BLOCKS
    return [
        pl.BlockSpec(parts[0].shape, lambda i: (0, 0)),
        pl.BlockSpec((rows, 2 * HEAD), lambda i: (i, 0)),
    ]


def read_keys(refs, half):
    if len(refs) == 2:
        return refs[0][...]
    devices = refs[0].shape[0]
    return refs[0][:, : 2 * half, :].reshape(devices * 2 * half, 2 * HEAD)


def read_queries(refs, half, i, share):
    if len(refs) == 2:
        return refs[1][...]
    return refs[0][pl.ds(i * share, share), 2 * half :, :].reshape(share * half, 2 * HEAD)


def self_forward(parts, devices, half):
    tile = 2 * half
    keys = devices * tile
    blocks = BLOCKS
    share = devices // blocks
    block = share * half
    step = chunk_of(keys)

    def kernel(*refs):
        ins, (o_ref, wide_ref, log_ref, kv, vt) = refs[: len(parts)], refs[len(parts) :]
        i = pl.program_id(0)

        @pl.when(i == 0)
        def _():
            kv[...] = read_keys(ins, half)
            vt[...] = flip(kv[...])

        both = split_pair(read_queries(ins, half, i, share))

        def scores(c):
            return dot_nt(kv[pl.ds(c * step, step), :], both)

        def values(c, p):
            return [dot_nn(vt[HEAD:, pl.ds(c * step, step)], p)]

        mixed, log_total = softmax_sweep(scores, values, keys // step, 2 * block)
        mixed = mixed[0]
        rows = jnp.concatenate([mixed[:, :block], mixed[:, block:]], axis=0).T
        o_ref[...] = rows.astype(bf16)
        wide_ref[...] = rows
        log_ref[0] = jnp.broadcast_to(log_total, (8, 2 * block))

    return pl.pallas_call(
        kernel,
        grid=(blocks,),
        in_specs=part_specs(parts, half),
        out_specs=[
            pl.BlockSpec((block, 2 * HEAD), lambda i: (i, 0)),
            pl.BlockSpec((block, 2 * HEAD), lambda i: (i, 0)),
            pl.BlockSpec((1, 8, 2 * block), lambda i: (i, 0, 0)),
        ],
        out_shape=[
            jax.ShapeDtypeStruct((devices * half, 2 * HEAD), bf16),
            jax.ShapeDtypeStruct((devices * half, 2 * HEAD), f32),
            jax.ShapeDtypeStruct((blocks, 8, 2 * block), f32),
        ],
        scratch_shapes=[pltpu.VMEM((keys, 2 * HEAD), bf16), pltpu.VMEM((2 * HEAD, keys), bf16)],
        compiler_params=pltpu.CompilerParams(vmem_limit_bytes=48 << 20),
        cost_estimate=pl.CostEstimate(
            flops=16 * keys * keys * HEAD,
            bytes_accessed=8 * keys * 2 * HEAD,
            transcendentals=keys * keys,
        ),
        name="self_forward",
    )(*parts)


def self_backward(parts, do, o, logs, devices, half):
    tile = 2 * half
    keys = devices * tile
    blocks = logs.shape[0]
    share = devices // blocks
    block = share * half
    step = chunk_of(keys)

    def kernel(*refs):
        n = len(parts)
        ins, (do_ref, o_ref, log_ref), outs = refs[:n], refs[n : n + 3], refs[n + 3 : 2 * n + 3]
        kv, vt, grads = refs[2 * n + 3 :]
        i = pl.program_id(0)
        mine = pl.ds(i * share, share)

        @pl.when(i == 0)
        def _():
            kv[...] = read_keys(ins, half)
            vt[...] = flip(kv[...])
            grads[...] = jnp.zeros_like(grads)

        q_both = split_pair(read_queries(ins, half, i, share))
        do_both = split_pair(do_ref[...])
        delta = jnp.sum(do_both.astype(f32) * split_wide(o_ref[...]), axis=1, keepdims=True)
        log_total = log_ref[0].T[:, :1] * LOG2E
        qt = flip(q_both)[:HEAD]
        dot = flip(do_both)[:HEAD]
        do_low = do_both[:, :HEAD]

        def scores(c):
            s = dot_nt(q_both, kv[pl.ds(c * step, step), :])
            return s, dot_nn(do_low, vt[HEAD:, pl.ds(c * step, step)])

        dq = jnp.zeros((2 * block, 2 * HEAD), f32)
        ahead = scores(0)
        for c in range(keys // step):
            s, dp = ahead
            ahead = scores(c + 1) if c + 1 < keys // step else None
            p = jnp.exp2(s * LOG2E - log_total)
            ds = (p * (dp - delta)).astype(bf16)
            cols = pl.ds(c * step, step)
            grads[:HEAD, cols] += dot_nn(qt, ds)
            grads[HEAD:, cols] += dot_nn(dot, p.astype(bf16))
            dq = dq + dot_nn(ds, kv[cols, :])
        dq = dq * 0.125
        low = lax.broadcasted_iota(jnp.int32, (block, 2 * HEAD), 1) < HEAD
        packed = jnp.where(low, dq[:block], pltpu.roll(dq[block:], HEAD, 1)).astype(bf16)
        if n == 1:
            outs[0][mine, tile:, :] = packed.reshape(share, half, 2 * HEAD)
        else:
            outs[1][...] = packed

        @pl.when(i == blocks - 1)
        def _():
            dkv = grads[...].T.astype(bf16)
            if n == 1:
                outs[0][:, :tile, :] = dkv.reshape(devices, tile, 2 * HEAD)
            else:
                outs[0][...] = dkv

    rows_spec = pl.BlockSpec((block, 2 * HEAD), lambda i: (i, 0))
    return pl.pallas_call(
        kernel,
        grid=(blocks,),
        in_specs=part_specs(parts, half)
        + [rows_spec, rows_spec, pl.BlockSpec((1, 8, 2 * block), lambda i: (i, 0, 0))],
        out_specs=part_specs(parts, half),
        out_shape=[jax.ShapeDtypeStruct(p.shape, bf16) for p in parts],
        scratch_shapes=[
            pltpu.VMEM((keys, 2 * HEAD), bf16),
            pltpu.VMEM((2 * HEAD, keys), bf16),
            pltpu.VMEM((2 * HEAD, keys), f32),
        ],
        compiler_params=pltpu.CompilerParams(vmem_limit_bytes=48 << 20),
        cost_estimate=pl.CostEstimate(
            flops=40 * keys * keys * HEAD,
            bytes_accessed=16 * keys * 2 * HEAD,
            transcendentals=keys * keys,
        ),
        name="self_backward",
    )(*parts, do, o, logs)


def swap_pairs(first, second):
    low = lax.broadcasted_iota(jnp.int32, first.shape, 1) < HEAD
    return (
        jnp.where(low, first, pltpu.roll(second, HEAD, 1)),
        jnp.where(low, pltpu.roll(first, HEAD, 1), second),
    )


def tile_places(items, turns, groups, tile):
    return [(i * tile, i % turns, i // turns) for i in range(items)]


def project_pack(x, kv_w, q_w, items, turns, groups):
    rows, width = x.shape
    slots = kv_w.shape[0]
    tile = rows // items
    half = tile // 2

    def kernel(x_ref, kv_ref, q_ref, out_ref):
        kv = dot_nt(x_ref[...], kv_ref[0]).astype(bf16)
        q = dot_nt(x_ref[...], q_ref[0]).astype(bf16).astype(f32) * 0.125
        for start, turn, group in tile_places(items, turns, groups, tile):
            upper, lower = swap_pairs(q[start : start + half], q[start + half : start + tile])
            for h, part in enumerate((upper, lower)):
                out_ref[turn, group, 0, h, :tile, :] = kv[
                    start : start + tile, h * 2 * HEAD : (h + 1) * 2 * HEAD
                ]
                out_ref[turn, group, 0, h, tile:, :] = part.astype(bf16)

    shape = (turns, groups, slots, 2, 3 * half, 2 * HEAD)
    return pl.pallas_call(
        kernel,
        grid=(slots,),
        in_specs=[
            pl.BlockSpec((rows, width), lambda i: (0, 0)),
            pl.BlockSpec((1,) + kv_w.shape[1:], lambda i: (i, 0, 0)),
            pl.BlockSpec((1,) + q_w.shape[1:], lambda i: (i, 0, 0)),
        ],
        out_specs=pl.BlockSpec(
            (turns, groups, 1, 2, 3 * half, 2 * HEAD), lambda i: (0, 0, i, 0, 0, 0)
        ),
        out_shape=jax.ShapeDtypeStruct(shape, bf16),
        compiler_params=pltpu.CompilerParams(vmem_limit_bytes=40 << 20),
        cost_estimate=pl.CostEstimate(
            flops=2 * rows * width * slots * 6 * HEAD,
            bytes_accessed=2 * (rows + slots * 6 * HEAD) * width,
            transcendentals=0,
        ),
        name="project_pack",
    )(x, kv_w, q_w)


def unpack_project(blocks, weights, items, groups):
    turns = len(blocks)
    slots = weights.shape[0]
    half = blocks[0].shape[3]
    tile = 2 * half
    width = weights.shape[2]

    def kernel(*refs):
        ins, w_ref, flat_ref, out_ref = refs[:turns], refs[turns], refs[turns + 1], refs[turns + 2]
        slot = pl.program_id(0)
        for start, turn, group in tile_places(items, turns, groups, tile):
            pair = [ins[turn][group, 0, h].astype(f32) for h in range(2)]
            upper, lower = swap_pairs(*pair)
            flat_ref[start : start + half, :] = upper.astype(bf16)
            flat_ref[start + half : start + tile, :] = lower.astype(bf16)
        part = dot_nn(flat_ref[...], w_ref[0])

        @pl.when(slot == 0)
        def _():
            out_ref[...] = part

        @pl.when(slot > 0)
        def _():
            out_ref[...] += part

    return pl.pallas_call(
        kernel,
        grid=(slots,),
        in_specs=[
            pl.BlockSpec((groups, 1, 2, half, 2 * HEAD), lambda i: (0, i, 0, 0, 0))
            for _ in range(turns)
        ]
        + [pl.BlockSpec((1,) + weights.shape[1:], lambda i: (i, 0, 0))],
        out_specs=[
            pl.BlockSpec((items * tile, 2 * HEAD), lambda i: (0, i)),
            pl.BlockSpec((items * tile, width), lambda i: (0, 0)),
        ],
        out_shape=[
            jax.ShapeDtypeStruct((items * tile, slots * 2 * HEAD), bf16),
            jax.ShapeDtypeStruct((items * tile, width), f32),
        ],
        compiler_params=pltpu.CompilerParams(vmem_limit_bytes=40 << 20),
        cost_estimate=pl.CostEstimate(
            flops=2 * items * tile * width * slots * 2 * HEAD,
            bytes_accessed=4 * items * tile * width,
            transcendentals=0,
        ),
        name="unpack_project",
    )(*blocks, weights)


def back_pack(x, weights, items, turns, groups):
    rows, width = x.shape
    slots = weights.shape[0]
    tile = rows // items
    half = tile // 2

    def kernel(x_ref, w_ref, out_ref):
        grads = dot_nt(x_ref[...], w_ref[0])
        for start, turn, group in tile_places(items, turns, groups, tile):
            pair = swap_pairs(grads[start : start + half], grads[start + half : start + tile])
            for h, part in enumerate(pair):
                out_ref[turn, group, 0, h] = part.astype(bf16)

    return pl.pallas_call(
        kernel,
        grid=(slots,),
        in_specs=[
            pl.BlockSpec((rows, width), lambda i: (0, 0)),
            pl.BlockSpec((1,) + weights.shape[1:], lambda i: (i, 0, 0)),
        ],
        out_specs=pl.BlockSpec(
            (turns, groups, 1, 2, half, 2 * HEAD), lambda i: (0, 0, i, 0, 0, 0)
        ),
        out_shape=jax.ShapeDtypeStruct((turns, groups, slots, 2, half, 2 * HEAD), bf16),
        compiler_params=pltpu.CompilerParams(vmem_limit_bytes=40 << 20),
        cost_estimate=pl.CostEstimate(
            flops=2 * rows * width * slots * 2 * HEAD,
            bytes_accessed=2 * (rows + slots * 2 * HEAD) * width,
            transcendentals=0,
        ),
        name="back_pack",
    )(x, weights)


def unpack_back(blocks, kv_w, q_w, items, groups):
    turns = len(blocks)
    slots, _, width = kv_w.shape
    half = blocks[0].shape[3] // 3
    tile = 2 * half
    rows = items * tile

    def kernel(*refs):
        ins = refs[:turns]
        kv_ref, q_ref, flat_ref, out_ref = refs[turns:]
        slot = pl.program_id(0)
        for start, turn, group in tile_places(items, turns, groups, tile):
            pair = []
            for h in range(2):
                flat_ref[0, start : start + tile, h * 2 * HEAD : (h + 1) * 2 * HEAD] = ins[turn][
                    group, 0, h, :tile, :
                ]
                pair.append(ins[turn][group, 0, h, tile:, :].astype(f32))
            upper, lower = swap_pairs(*pair)
            flat_ref[0, start : start + half, 4 * HEAD :] = upper.astype(bf16)
            flat_ref[0, start + half : start + tile, 4 * HEAD :] = lower.astype(bf16)
        part = dot_nn(flat_ref[0, :, : 4 * HEAD], kv_ref[0])
        part = part + dot_nn(flat_ref[0, :, 4 * HEAD :], q_ref[0])

        @pl.when(slot == 0)
        def _():
            out_ref[...] = part

        @pl.when(slot > 0)
        def _():
            out_ref[...] += part

    return pl.pallas_call(
        kernel,
        grid=(slots,),
        in_specs=[
            pl.BlockSpec((groups, 1, 2, 3 * half, 2 * HEAD), lambda i: (0, i, 0, 0, 0))
            for _ in range(turns)
        ]
        + [
            pl.BlockSpec((1,) + kv_w.shape[1:], lambda i: (i, 0, 0)),
            pl.BlockSpec((1,) + q_w.shape[1:], lambda i: (i, 0, 0)),
        ],
        out_specs=[
            pl.BlockSpec((1, rows, 6 * HEAD), lambda i: (i, 0, 0)),
            pl.BlockSpec((rows, width), lambda i: (0, 0)),
        ],
        out_shape=[
            jax.ShapeDtypeStruct((slots, rows, 6 * HEAD), bf16),
            jax.ShapeDtypeStruct((rows, width), f32),
        ],
        compiler_params=pltpu.CompilerParams(vmem_limit_bytes=40 << 20),
        cost_estimate=pl.CostEstimate(
            flops=2 * rows * width * slots * 6 * HEAD,
            bytes_accessed=4 * rows * width,
            transcendentals=0,
        ),
        name="unpack_back",
    )(*blocks, kv_w, q_w)


def first_kernel(tokens, shift, scale, w, tp):
    rows, items, cols, width = tokens.shape
    cols_here = cols // tp
    tile = rows * cols_here
    local = w.shape[1]

    def kernel(x_ref, shift_ref, scale_ref, w_ref, in_ref, q_ref):
        hat, _ = norm_parts(x_ref[...].astype(f32).reshape(rows, cols, width))
        value = hat * (1.0 + scale_ref[0]) + shift_ref[0]
        for t in range(tp):
            part = value[:, t * cols_here : (t + 1) * cols_here, :].reshape(tile, width)
            in_ref[0, t * tile : (t + 1) * tile, :] = part.astype(bf16)
        q = dot_nn(in_ref[0], w_ref[...]).astype(bf16).astype(f32) * 0.125
        q_ref[0] = q.astype(bf16)

    piece_spec = pl.BlockSpec((1, 1, width), lambda i: (i, 0, 0))
    return pl.pallas_call(
        kernel,
        grid=(items,),
        in_specs=[
            pl.BlockSpec((rows, 1, cols, width), lambda i: (0, i, 0, 0)),
            piece_spec,
            piece_spec,
            pl.BlockSpec(w.shape, lambda i: (0, 0)),
        ],
        out_specs=[
            pl.BlockSpec((1, tp * tile, width), lambda i: (i, 0, 0)),
            pl.BlockSpec((1, tp * tile, local), lambda i: (i, 0, 0)),
        ],
        out_shape=[
            jax.ShapeDtypeStruct((items, tp * tile, width), bf16),
            jax.ShapeDtypeStruct((items, tp * tile, local), bf16),
        ],
        compiler_params=pltpu.CompilerParams(vmem_limit_bytes=48 << 20),
        cost_estimate=pl.CostEstimate(
            flops=2 * items * tp * tile * width * local,
            bytes_accessed=4 * items * tp * tile * width,
            transcendentals=0,
        ),
        name="first_kernel",
    )(tokens, shift, scale, w)


def key_value_kernel(context, w_key, w_value_t):
    items, keys, depth = context.shape
    local = w_key.shape[1]
    step = 1024 if keys % 1024 == 0 else keys

    def kernel(x_ref, wk_ref, wv_ref, k_ref, vt_ref):
        k_ref[0] = dot_nn(x_ref[0], wk_ref[...]).astype(bf16)
        vt_ref[0] = dot_nt(wv_ref[...], x_ref[0]).astype(bf16)

    return pl.pallas_call(
        kernel,
        grid=(items, keys // step),
        in_specs=[
            pl.BlockSpec((1, step, depth), lambda i, j: (i, j, 0)),
            pl.BlockSpec(w_key.shape, lambda i, j: (0, 0)),
            pl.BlockSpec(w_value_t.shape, lambda i, j: (0, 0)),
        ],
        out_specs=[
            pl.BlockSpec((1, step, local), lambda i, j: (i, j, 0)),
            pl.BlockSpec((1, local, step), lambda i, j: (i, 0, j)),
        ],
        out_shape=[
            jax.ShapeDtypeStruct((items, keys, local), bf16),
            jax.ShapeDtypeStruct((items, local, keys), bf16),
        ],
        compiler_params=pltpu.CompilerParams(vmem_limit_bytes=40 << 20),
        cost_estimate=pl.CostEstimate(
            flops=4 * items * keys * depth * local,
            bytes_accessed=2 * items * keys * (depth + 2 * local),
            transcendentals=0,
        ),
        name="key_value_kernel",
    )(context, w_key, w_value_t)


def key_value_grads(dk_t, dv_t, context):
    items, local, keys = dk_t.shape
    depth = context.shape[2]
    step = 1024 if keys % 1024 == 0 else keys

    def kernel(dk_ref, dv_ref, x_ref, out_ref):
        first = (pl.program_id(0) == 0) & (pl.program_id(1) == 0)
        both = jnp.concatenate([dk_ref[0], dv_ref[0]], axis=0)
        part = dot_nn(both, x_ref[0])

        @pl.when(first)
        def _():
            out_ref[...] = part

        @pl.when(jnp.logical_not(first))
        def _():
            out_ref[...] += part

    grads_spec = pl.BlockSpec((1, local, step), lambda i, j: (i, 0, j))
    return pl.pallas_call(
        kernel,
        grid=(items, keys // step),
        in_specs=[grads_spec, grads_spec, pl.BlockSpec((1, step, depth), lambda i, j: (i, j, 0))],
        out_specs=pl.BlockSpec((2 * local, depth), lambda i, j: (0, 0)),
        out_shape=jax.ShapeDtypeStruct((2 * local, depth), f32),
        compiler_params=pltpu.CompilerParams(vmem_limit_bytes=40 << 20),
        cost_estimate=pl.CostEstimate(
            flops=4 * items * keys * depth * local,
            bytes_accessed=2 * items * keys * (depth + 2 * local),
            transcendentals=0,
        ),
        name="key_value_grads",
    )(dk_t, dv_t, context)


def feed_forward(x, g, up, down):
    rows, width = x.shape
    slots, _, hidden = up.shape
    parts = 4 if rows % 64 == 0 else 1
    size = rows // parts

    def kernel(x_ref, g_ref, up_ref, down_ref, active_ref, dh_ref, branch_ref, back_ref):
        slot = pl.program_id(0)

        @pl.when(slot == 0)
        def _():
            branch_ref[...] = jnp.zeros_like(branch_ref)
            back_ref[...] = jnp.zeros_like(back_ref)

        def products(r):
            mine = pl.ds(r * size, size)
            return dot_nn(x_ref[mine, :], up_ref[0]), dot_nt(g_ref[mine, :], down_ref[0])

        ahead = products(0)
        for r in range(parts):
            h, da = ahead
            ahead = products(r + 1) if r + 1 < parts else None
            mine = pl.ds(r * size, size)
            below = 0.5 * (1.0 + lax.erf(h * 0.7071067811865476))
            slope = below + h * (jnp.exp(h * h * -0.5) * 0.3989422804014327)
            active = (h * below).astype(bf16)
            dh = (da * slope).astype(bf16)
            active_ref[0, mine, :] = active
            dh_ref[0, mine, :] = dh
            branch_ref[mine, :] += dot_nn(active, down_ref[0])
            back_ref[mine, :] += dot_nt(dh, up_ref[0])

    rows_spec = pl.BlockSpec((rows, width), lambda i: (0, 0))
    hidden_spec = pl.BlockSpec((1, rows, hidden), lambda i: (i, 0, 0))
    return pl.pallas_call(
        kernel,
        grid=(slots,),
        in_specs=[
            rows_spec,
            rows_spec,
            pl.BlockSpec((1, width, hidden), lambda i: (i, 0, 0)),
            pl.BlockSpec((1, hidden, width), lambda i: (i, 0, 0)),
        ],
        out_specs=[hidden_spec, hidden_spec, rows_spec, rows_spec],
        out_shape=[
            jax.ShapeDtypeStruct((slots, rows, hidden), bf16),
            jax.ShapeDtypeStruct((slots, rows, hidden), bf16),
            jax.ShapeDtypeStruct((rows, width), f32),
            jax.ShapeDtypeStruct((rows, width), f32),
        ],
        compiler_params=pltpu.CompilerParams(vmem_limit_bytes=52 << 20),
        cost_estimate=pl.CostEstimate(
            flops=8 * slots * rows * width * hidden,
            bytes_accessed=4 * slots * width * hidden,
            transcendentals=2 * slots * rows * hidden,
        ),
        name="feed_forward",
    )(x, g, up, down)


def weight_terms(buffer, shape, lhs, lhs_block, lhs_place, rhs, tp, size, first):
    count, width = rhs.shape
    devices, _, share = shape
    seq = devices // tp
    depth = lhs_block[-1]

    def kernel(*refs):
        a_ref, b_ref, out_ref = refs[0], refs[1], refs[-1]
        a = a_ref[...]
        if len(lhs_block) > 3:
            a = a.astype(f32)
        a = a.reshape(count, depth).astype(bf16)
        terms = lax.dot_general(a, b_ref[...], (((0,), (0,)), ((), ())), preferred_element_type=f32)
        for s in range(seq):
            out_ref[s] = terms[:, s * share : (s + 1) * share].astype(bf16)

    return pl.pallas_call(
        kernel,
        grid=(tp, 2),
        in_specs=[
            pl.BlockSpec(lhs_block, lhs_place),
            pl.BlockSpec(rhs.shape, lambda t, c: (0, 0)),
        ]
        + ([] if buffer is None else [pl.BlockSpec(memory_space=pl.ANY)]),
        out_specs=pl.BlockSpec((seq, size, share), lambda t, c: (t, first // size + c, 0)),
        out_shape=jax.ShapeDtypeStruct(shape, bf16),
        input_output_aliases={} if buffer is None else {2: 0},
        compiler_params=pltpu.CompilerParams(vmem_limit_bytes=40 << 20),
        cost_estimate=pl.CostEstimate(
            flops=4 * tp * count * depth * width,
            bytes_accessed=4 * tp * (count + width) * depth,
            transcendentals=0,
        ),
        name="weight_terms",
    )(lhs, rhs, *([] if buffer is None else [buffer]))


def last_kernel(tokens, scale, middle, dq, query_slots):
    rows, items, cols, width = tokens.shape
    tp, _, queries, local = dq.shape
    cols_here = cols // tp
    tile = rows * cols_here
    slot_width = local // 2

    def kernel(x_ref, scale_ref, middle_ref, dq_ref, w_ref, out_ref, sums_ref):
        hat, inverse = norm_parts(x_ref[...].astype(f32).reshape(rows, cols, width))
        weights = w_ref[...].reshape(tp * local, width)
        shift_sum = jnp.zeros((1, width), f32)
        scale_sum = jnp.zeros((1, width), f32)
        for t in range(tp):
            pieces = [
                dq_ref[u, 0, t * tile : (t + 1) * tile, c * slot_width : (c + 1) * slot_width]
                for c in range(2)
                for u in range(tp)
            ]
            g = dot_nn(jnp.concatenate(pieces, axis=1), weights)
            mine = slice(t * cols_here, (t + 1) * cols_here)
            hat_t = hat[:, mine, :].reshape(tile, width)
            inverse_t = inverse[:, mine, :].reshape(tile, 1)
            shift_sum = shift_sum + jnp.sum(g, axis=0, keepdims=True)
            scale_sum = scale_sum + jnp.sum(g * hat_t, axis=0, keepdims=True)
            value = middle_ref[t, 0].astype(f32) + norm_back(
                hat_t, inverse_t, g * (1.0 + scale_ref[0])
            )
            out_ref[:, 0, mine, :] = value.reshape(rows, cols_here, width)
        sums_ref[0, 0:1, :] = shift_sum
        sums_ref[0, 1:2, :] = scale_sum

    return pl.pallas_call(
        kernel,
        grid=(items,),
        in_specs=[
            pl.BlockSpec((rows, 1, cols, width), lambda i: (0, i, 0, 0)),
            pl.BlockSpec((1, 1, width), lambda i: (i, 0, 0)),
            pl.BlockSpec((tp, 1, tile, width), lambda i: (0, i, 0, 0)),
            pl.BlockSpec((tp, 1, queries, local), lambda i: (0, i, 0, 0)),
            pl.BlockSpec(query_slots.shape, lambda i: (0, 0, 0)),
        ],
        out_specs=[
            pl.BlockSpec((rows, 1, cols, width), lambda i: (0, i, 0, 0)),
            pl.BlockSpec((1, 2, width), lambda i: (i, 0, 0)),
        ],
        out_shape=[
            jax.ShapeDtypeStruct(tokens.shape, f32),
            jax.ShapeDtypeStruct((items, 2, width), f32),
        ],
        compiler_params=pltpu.CompilerParams(vmem_limit_bytes=52 << 20),
        cost_estimate=pl.CostEstimate(
            flops=2 * items * queries * width * tp * local,
            bytes_accessed=10 * items * queries * width,
            transcendentals=0,
        ),
        name="last_kernel",
    )(tokens, scale, middle, dq, query_slots)


def exchange(x, axis):
    return lax.all_to_all(x, axis, 0, 0, tiled=True)


def gather(x, axis):
    return exchange(jnp.broadcast_to(x[None], (lax.axis_size(axis),) + x.shape), axis)


def reduce_blocks(x, axis):
    return jnp.sum(exchange(x.astype(bf16), axis).astype(f32), axis=0)


def body(
    tokens,
    context,
    group_ids,
    source_table,
    w_query,
    w_key,
    w_value,
    w_out,
    w_self_query,
    w_self_key,
    w_self_value,
    w_self_out,
    w_up,
    w_down,
    w_deconv,
    deconv_bias,
    out_cotangent,
    plane_cotangent,
):
    rows_here, items, plane_cols, width = tokens.shape
    cols_here = out_cotangent.shape[2]
    tp = lax.axis_size("tp")
    seq = lax.axis_size("seq")
    both_axes = ("seq", "tp")
    devices = tp * seq
    local = w_query.shape[1]
    hidden_here = w_up.shape[1]
    slots = 2 * tp
    slot_heads = local // HEAD // 2
    slot_width = local // 2
    heads = slots * slot_heads
    tile = rows_here * cols_here
    half = tile // 2
    groups = devices // heads
    turns = -(-items // groups)
    share = width // seq
    fast = slot_heads == 2 and half % 16 == 0 and items == groups * turns and share % 128 == 0
    me_tp = lax.axis_index("tp")
    core = lax.axis_index("seq") % 2

    picker = (group_ids[:, None] == jnp.arange(GROUPS, dtype=jnp.int32)[None, :]).astype(f32)
    mods = jnp.dot(picker, source_table, precision=highest).reshape(items, 9, 1, width)

    def piece(index):
        return mods[:, index]

    def dot(spec, a, b):
        return jnp.einsum(spec, a, b, preferred_element_type=f32)

    def to_tile(x):
        return x.transpose(1, 0, 2, 3).reshape(items, tile, width)

    def from_tile(x):
        return x.reshape(items, rows_here, cols_here, width).transpose(1, 0, 2, 3)

    teams = [
        [(2 * pair + c) * tp + t for c in range(2) for t in range(tp)] for pair in range(seq // 2)
    ]

    def whole(x):
        return lax.all_gather(x, both_axes, axis=0, tiled=False, axis_index_groups=teams)

    def my_rows(x):
        return lax.dynamic_slice_in_dim(x, core * slot_width, slot_width, 0)

    def my_columns(x):
        size = x.shape[1] // 2
        return lax.dynamic_slice_in_dim(x, core * size, size, 1)

    key_value = jnp.stack(
        [
            my_columns(w_self_key).T.reshape(slot_heads, HEAD, width),
            my_columns(w_self_value).T.reshape(slot_heads, HEAD, width),
        ],
        axis=1,
    ).reshape(2 * slot_width, width)
    small = whole(
        jnp.concatenate(
            [
                key_value,
                my_columns(w_self_query).T,
                my_rows(w_self_out),
                my_rows(w_out),
                my_columns(w_query).T,
            ],
            axis=0,
        )
    )
    cuts = [slot_width * k for k in (0, 2, 3, 4, 5, 6)]
    kv_slots, q_slots, so_slots, out_slots, query_slots = [
        small[:, a:b] for a, b in zip(cuts[:-1], cuts[1:])
    ]
    up_slots = whole(my_columns(w_up))
    down_slots = whole(
        lax.dynamic_slice_in_dim(w_down, core * (hidden_here // 2), hidden_here // 2, 0)
    )

    def by_tp(x):
        return x.reshape(2, tp, slot_width, width).transpose(1, 0, 2, 3).reshape(tp, local, width)

    incoming = plane_cotangent.reshape(2 * rows_here, items, 2 * cols_here, COUT)
    plane_row = (lax.axis_index("seq") * rows_here + jnp.arange(rows_here, dtype=jnp.int32)) % PLANE
    upper_keep = (plane_row != 0).astype(f32)
    lower_keep = (plane_row != PLANE - 1).astype(f32)
    grad_edges = with_halo(incoming, (("seq", 0), ("tp", 2)), 1)
    upper_mask = upper_keep.astype(bf16)[:, None, None, None]
    lower_mask = lower_keep.astype(bf16)[:, None, None, None]
    first_pair = grad_edges[:-2].reshape(rows_here, 2, items, 2 * cols_here + 2, COUT)
    last_pair = grad_edges[2:].reshape(rows_here, 2, items, 2 * cols_here + 2, COUT)
    row_taps = jnp.stack(
        [
            first_pair[:, 0] * upper_mask,
            first_pair[:, 1],
            last_pair[:, 0],
            last_pair[:, 1] * lower_mask,
        ],
        axis=3,
    )
    left_pair = row_taps[:, :, :-2].reshape(rows_here, items, cols_here, 2, 4, COUT)
    right_pair = row_taps[:, :, 2:].reshape(rows_here, items, cols_here, 2, 4, COUT)
    tap_grads = jnp.stack(
        [
            left_pair[:, :, :, 0],
            left_pair[:, :, :, 1],
            right_pair[:, :, :, 0],
            right_pair[:, :, :, 1],
        ],
        axis=4,
    )
    tap_grads = tap_grads.reshape(rows_here, items, cols_here, 16 * COUT)
    grad_result = to_tile(out_cotangent.astype(f32) + dot("rict,dt->ricd", tap_grads, w_deconv))
    grad_bias = jnp.sum(incoming.astype(f32), axis=(0, 1, 2))
    grad_mlp = (piece(8) * grad_result).astype(bf16)

    if fast:
        first_in, queries = first_kernel(tokens, piece(0), piece(1), w_query, tp)
    else:
        ordered = (
            tokens.reshape(rows_here, items, tp, cols_here, width)
            .transpose(1, 2, 0, 3, 4)
            .reshape(items, tp * tile, width)
        )
        first_hat, first_inv = norm_parts(ordered.astype(f32))
        first_in = (first_hat * (1.0 + piece(1)) + piece(0)).astype(bf16)
        queries = dot("iqd,de->iqe", first_in, w_query).astype(bf16) * bf16(0.125)
    image = context.transpose(1, 0, 2)
    keys, values_t = key_value_kernel(image, w_key, w_value.T)
    mixed, mixed_wide, cross_logs = cross_forward(queries, keys, values_t, tp)
    mixed_tile = exchange(mixed, "tp")
    out_whole = by_tp(out_slots)
    branch_a = dot("time,tef->imf", mixed_tile, out_whole)
    residual = to_tile(lax.dynamic_slice_in_dim(tokens, me_tp * cols_here, cols_here, 2)).astype(f32)
    middle = residual + piece(2) * branch_a

    self_hat, self_inv = norm_parts(middle)
    self_in = (self_hat * (1.0 + piece(4)) + piece(3)).astype(bf16)
    flat = (items * tile, width)
    spare = groups * turns - items

    def spread_items(x):
        if spare:
            x = jnp.pad(x, ((0, 0), (0, spare)) + ((0, 0),) * (x.ndim - 2))
        return x.reshape((slots, groups, turns) + x.shape[2:])

    def pack_keys(x):
        x = spread_items(x.reshape(slots, items, tile, slot_heads, 2 * HEAD))
        return x.transpose(2, 1, 0, 4, 3, 5).reshape(turns, devices, tile, 2 * HEAD)

    def unpack_keys(x):
        x = x.reshape(turns, groups, slots, slot_heads, tile, 2 * HEAD).transpose(2, 1, 0, 4, 3, 5)
        x = x.reshape(slots, groups * turns, tile, 2 * slot_width)[:, :items]
        return x.reshape(slots, items * tile, 2 * slot_width)

    def pack_rows(x):
        x = spread_items(x.reshape(slots, items, 2, half, slot_heads, HEAD))
        return x.transpose(2, 1, 0, 5, 4, 3, 6).reshape(turns, devices, half, 2 * HEAD)

    def unpack_rows(x):
        x = x.reshape(turns, groups, slots, slot_heads, half, 2, HEAD).transpose(2, 1, 0, 5, 4, 3, 6)
        x = x.reshape(slots, groups * turns, tile, slot_width)[:, :items]
        return x.reshape(slots, items * tile, slot_width)

    if fast:
        sends = project_pack(self_in.reshape(flat), kv_slots, q_slots, items, turns, groups)
        sends = sends.reshape(turns, devices, 3 * half, 2 * HEAD)
        sends = [sends[turn] for turn in range(turns)]
    else:
        kv_sends = pack_keys(dot("nd,xed->xne", self_in.reshape(flat), kv_slots).astype(bf16))
        q_sends = dot("nd,xed->xne", self_in.reshape(flat), q_slots).astype(bf16)
        q_sends = pack_rows(q_sends * bf16(0.125))
        parts = [
            [
                exchange(kv_sends[turn], both_axes).reshape(devices * tile, 2 * HEAD),
                exchange(q_sends[turn], both_axes).reshape(devices * half, 2 * HEAD),
            ]
            for turn in range(turns)
        ]
    if fast:
        parts, forward = [], []
        for turn in range(turns):
            if turn >= 2:
                sends[turn], forward[turn - 2] = lax.optimization_barrier(
                    (sends[turn], forward[turn - 2])
                )
            arrived = exchange(sends[turn], both_axes)
            if turn == 0:
                arrived, grad_result, grad_mlp = lax.optimization_barrier(
                    (arrived, grad_result, grad_mlp)
                )
            parts.append([arrived])
            forward.append(self_forward(parts[turn], devices, half))
    else:
        forward = [self_forward(parts[turn], devices, half) for turn in range(turns)]
    so_back = [exchange(so.reshape(devices, half, 2 * HEAD), both_axes) for so, _, _ in forward]
    if fast:
        blocks = [x.reshape(groups, slots, 2, half, 2 * HEAD) for x in so_back]
        so_tile, branch_s = unpack_project(blocks, so_slots, items, groups)
    else:
        so_tile = unpack_rows(jnp.stack(so_back)).transpose(1, 0, 2)
        branch_s = dot("nxe,xed->nd", so_tile, so_slots)
        so_tile = so_tile.reshape(items * tile, heads * HEAD)
    branch_s = branch_s.reshape(items, tile, width)
    middle_two = middle + piece(5) * branch_s

    second_hat, second_inv = norm_parts(middle_two)
    second_in = (second_hat * (1.0 + piece(7)) + piece(6)).astype(bf16)
    active, grad_hidden, branch_b, grad_second = feed_forward(
        second_in.reshape(flat), grad_mlp.reshape(flat), up_slots, down_slots
    )
    branch_b = branch_b.reshape(items, tile, width)
    grad_second = grad_second.reshape(items, tile, width)
    result = middle_two + piece(8) * branch_b
    out_tile = from_tile(result.astype(bf16))

    grad_gate_b = jnp.sum(grad_result * branch_b, axis=1)
    grad_shift_b = jnp.sum(grad_second, axis=1)
    grad_scale_b = jnp.sum(grad_second * second_hat, axis=1)
    grad_mid_two = grad_result + norm_back(second_hat, second_inv, grad_second * (1.0 + piece(7)))

    widened = with_halo(out_tile, (("seq", 0), ("tp", 2)), 1)
    taps = dot("ricd,dt->rict", widened, w_deconv)
    taps = taps.reshape(rows_here + 2, items, cols_here + 2, 4, 4, COUT)
    planes = spread_taps(
        taps, upper_keep[:, None, None, None, None], lower_keep[:, None, None, None, None]
    )
    planes = planes + jnp.tile(deconv_bias, 2 * cols_here)

    def by_device(x):
        lead = x.shape[0] // tp
        x = x.reshape(lead, tp, x.shape[1], seq, share).transpose(1, 3, 0, 2, 4)
        return x.reshape(devices, -1, share).astype(bf16)

    def total(terms, *cuts):
        summed = lax.psum_scatter(terms, ("tp", "seq"), scatter_dimension=0, tiled=True)[0]
        return jnp.split(summed.astype(f32), cuts, axis=0)

    terms_deconv = dot("rict,ricd->td", tap_grads, out_tile)
    terms_deconv = by_device(terms_deconv.reshape(tp, 16 * COUT // tp, width))
    size_b = (hidden_here // 2, hidden_here, 2 * hidden_here)
    if fast:
        shape = (devices, size_b[2] + terms_deconv.shape[1], share)
        hidden_block = (1, items * tile, size_b[0])

        def slot_place(t, c):
            return (c * tp + t, 0, 0)

        terms_b = None
        for lhs, rhs, first in (
            (grad_hidden, second_in, 0),
            (active, grad_mlp, size_b[1]),
        ):
            terms_b = weight_terms(
                terms_b, shape, lhs, hidden_block, slot_place, rhs.reshape(flat), tp, size_b[0], first
            )
        terms_b = lax.dynamic_update_slice_in_dim(terms_b, terms_deconv, size_b[2], 1)
    else:
        terms_b = jnp.concatenate(
            [
                by_device(dot("xnf,nd->xfd", grad_hidden, second_in.reshape(flat))),
                by_device(dot("xnf,nd->xfd", active, grad_mlp.reshape(flat))),
                terms_deconv,
            ],
            axis=1,
        )

    grad_self = (piece(5) * grad_mid_two).astype(bf16)
    grad_gate_s = jnp.sum(grad_mid_two * branch_s, axis=1)
    if fast:
        dso_send = back_pack(grad_self.reshape(flat), so_slots, items, turns, groups)
        dso_send = dso_send.reshape(turns, devices, half, 2 * HEAD)
    else:
        dso_send = pack_rows(dot("nd,xed->xne", grad_self.reshape(flat), so_slots).astype(bf16))
    dso_send = [dso_send[turn] for turn in range(turns)]
    dso_mine, backward = [], []
    for turn in range(turns):
        if turn >= 2:
            dso_send[turn], backward[turn - 2] = lax.optimization_barrier(
                (dso_send[turn], backward[turn - 2])
            )
        arrived = exchange(dso_send[turn], both_axes).reshape(devices * half, 2 * HEAD)
        if turn == 0:
            arrived, terms_b = lax.optimization_barrier((arrived, terms_b))
        dso_mine.append(arrived)
        backward.append(
            self_backward(parts[turn], dso_mine[turn], *forward[turn][1:], devices, half)
        )
    grad_up, grad_down, grad_deconv = total(terms_b, *size_b[1:])
    if fast:
        blocks = [
            exchange(x[0], both_axes).reshape(groups, slots, 2, 3 * half, 2 * HEAD)
            for x in backward
        ]
        blocks[-1], planes = lax.optimization_barrier((blocks[-1], planes))
        grad_projected, grad_third = unpack_back(blocks, kv_slots, q_slots, items, groups)
    else:
        dkv = [exchange(x[0].reshape(devices, tile, 2 * HEAD), both_axes) for x in backward]
        dq = [exchange(x[1].reshape(devices, half, 2 * HEAD), both_axes) for x in backward]
        grad_projected = jnp.concatenate(
            [unpack_keys(jnp.stack(dkv)), unpack_rows(jnp.stack(dq))], axis=2
        )
        grad_third = dot(
            "xne,xed->nd", grad_projected, jnp.concatenate([kv_slots, q_slots], axis=1)
        )
    grad_third = grad_third.reshape(items, tile, width)
    grad_shift_s = jnp.sum(grad_third, axis=1)
    grad_scale_s = jnp.sum(grad_third * self_hat, axis=1)
    grad_middle = grad_mid_two + norm_back(self_hat, self_inv, grad_third * (1.0 + piece(4)))

    grad_attn = (piece(2) * grad_middle).astype(bf16)
    grad_gate_a = jnp.sum(grad_middle * branch_a, axis=1)
    do_mine = exchange(dot("imf,tef->time", grad_attn, out_whole).astype(bf16), "tp")
    middle_all = gather(grad_middle.astype(bf16), "tp")
    early = jnp.stack(
        [
            grad_gate_a,
            grad_shift_s,
            grad_scale_s,
            grad_gate_s,
            grad_shift_b,
            grad_scale_b,
            grad_gate_b,
        ],
        axis=0,
    ).reshape(7 * items, width)
    early = jnp.concatenate(
        [early, jnp.pad(grad_bias, (0, width - COUT))[None]], axis=0
    )
    spots = -(-early.shape[0] // (16 * tp)) * 16
    early = jnp.pad(early, ((0, spots * tp - early.shape[0]), (0, 0))).reshape(tp, spots, width)
    early = by_device(early)
    size_a = [slot_width * k for k in (6, 8, 10)]
    if fast:
        shape = (devices, size_a[2] + early.shape[1], share)
        terms_a = weight_terms(
            None,
            shape,
            grad_projected,
            (1, items * tile, 3 * slot_width),
            lambda t, c: (c * tp + t, 0, 0),
            self_in.reshape(flat),
            tp,
            3 * slot_width,
            0,
        )
        terms_a = weight_terms(
            terms_a,
            shape,
            so_tile,
            (items * tile, slot_width),
            lambda t, c: (0, c * tp + t),
            grad_self.reshape(flat),
            tp,
            slot_width,
            size_a[0],
        )
        terms_a = weight_terms(
            terms_a,
            shape,
            mixed_tile,
            (1, items, tile, slot_width),
            lambda t, c: (t, 0, 0, c),
            grad_attn.reshape(flat),
            tp,
            slot_width,
            size_a[1],
        )
        terms_a = lax.dynamic_update_slice_in_dim(terms_a, early, size_a[2], 1)
    else:
        so_terms = dot("ne,nd->ed", so_tile, grad_self.reshape(flat))
        terms_a = jnp.concatenate(
            [
                by_device(dot("xne,nd->xed", grad_projected, self_in.reshape(flat))),
                by_device(so_terms.reshape(slots, slot_width, width)),
                by_device(dot("time,imf->tef", mixed_tile, grad_attn)),
                early,
            ],
            axis=1,
        )
    do_mine, terms_a = lax.optimization_barrier((do_mine, terms_a))
    terms_a, grad_up = lax.optimization_barrier((terms_a, grad_up))
    grad_three, grad_self_out, grad_out, grad_early = total(terms_a, *size_a)
    dq_cross, dk_t, dv_t = cross_backward(queries, do_mine, mixed_wide, cross_logs, keys, values_t)
    dq_cross, middle_all = lax.optimization_barrier((dq_cross, middle_all))
    dq_all = gather(dq_cross, "tp")
    grad_three = grad_three.reshape(2, 3 * slot_width, share)
    grad_pair = grad_three[:, : 2 * slot_width].reshape(2, slot_heads, 2, HEAD, share)
    grad_self_key = grad_pair[:, :, 0].reshape(local, share).T
    grad_self_value = grad_pair[:, :, 1].reshape(local, share).T
    grad_self_query = grad_three[:, 2 * slot_width :].reshape(local, share).T

    shared = lax.all_gather(
        jnp.concatenate([grad_deconv, grad_early], axis=0), ("tp", "seq"), axis=0, tiled=False
    )
    shared = shared.reshape(tp, seq, -1, share).transpose(0, 2, 1, 3).reshape(tp, -1, width)
    grad_deconv = shared[:, : 16 * COUT // tp].reshape(16 * COUT, width).T
    early = shared[:, 16 * COUT // tp :].reshape(-1, width)
    grad_bias = early[7 * items, :COUT]
    early = early[: 7 * items].reshape(7, items, width)

    def by_seq(x):
        return x.reshape((seq, x.shape[0] // seq) + x.shape[1:]).astype(bf16)

    grad_image = key_value_grads(dk_t, dv_t, image).T
    last = jnp.concatenate(
        [
            by_seq(dot("iqd,iqe->de", first_in, dq_cross)),
            by_seq(grad_image[:, :local]),
            by_seq(grad_image[:, local:]),
        ],
        axis=1,
    )
    last, dq_all = lax.optimization_barrier((last, dq_all))
    last = jnp.sum(exchange(last, "seq").astype(f32), axis=0)
    if fast:
        grad_tokens, late = last_kernel(tokens, piece(1), middle_all, dq_all, query_slots)
        late = late.transpose(1, 0, 2)
    else:
        grad_first = dot("tiqe,ted->iqd", dq_all, by_tp(query_slots))
        grad_shift_a = jnp.sum(grad_first, axis=1)
        grad_scale_a = jnp.sum(grad_first * first_hat, axis=1)
        grad_tokens = middle_all.astype(f32).transpose(1, 0, 2, 3).reshape(
            items, tp * tile, width
        ) + norm_back(first_hat, first_inv, grad_first * (1.0 + piece(1)))
        grad_tokens = (
            grad_tokens.reshape(items, tp, rows_here, cols_here, width)
            .transpose(2, 0, 1, 3, 4)
            .reshape(rows_here, items, plane_cols, width)
        )
        late = jnp.stack([grad_shift_a, grad_scale_a], axis=0)

    depth = (last.shape[0] - share) // 2
    grad_query, grad_key, grad_value = (
        last[:share],
        last[share : share + depth],
        last[share + depth :],
    )
    late = jnp.sum(gather(late, "seq"), axis=0)
    grad_mods = jnp.concatenate([late, early], axis=0).transpose(1, 0, 2)
    grad_table = jnp.dot(picker.T, grad_mods.reshape(items, 9 * width), precision=highest)
    return (
        out_tile,
        planes,
        grad_tokens,
        grad_query,
        grad_key,
        grad_value,
        grad_out,
        grad_self_query,
        grad_self_key,
        grad_self_value,
        grad_self_out.reshape(local, share),
        grad_up.T,
        grad_down,
        grad_deconv,
        grad_bias,
        grad_table,
    )


def solution(mesh):
    in_specs = (
        P("seq", None, None, None),
        P(),
        P(),
        P(),
        P(None, "tp"),
        P(None, "tp"),
        P(None, "tp"),
        P("tp", None),
        P(None, "tp"),
        P(None, "tp"),
        P(None, "tp"),
        P("tp", None),
        P(None, "tp"),
        P("tp", None),
        P(),
        P(),
        P("seq", None, "tp", None),
        P("seq", None, "tp"),
    )
    out_specs = (
        P("seq", None, "tp", None),
        P("seq", None, "tp"),
        P("seq", None, None, None),
        P("seq", "tp"),
        P("seq", "tp"),
        P("seq", "tp"),
        P("tp", "seq"),
        P("seq", "tp"),
        P("seq", "tp"),
        P("seq", "tp"),
        P("tp", "seq"),
        P("seq", "tp"),
        P("tp", "seq"),
        P(),
        P(),
        P(),
    )
    return jax.shard_map(body, mesh=mesh, in_specs=in_specs, out_specs=out_specs, check_vma=False)
```

```python
import jax
import jax.numpy as jnp
from jax import lax
from jax.experimental import pallas as pl
from jax.experimental.pallas import tpu as pltpu
from jax.sharding import PartitionSpec as P

HEAD = 64
COUT = 80
PLANE = 32
IMG = 4096
LOG2E = 1.4426950408889634
bf16 = jnp.bfloat16
f32 = jnp.float32
GROUPS = 16


highest = lax.Precision.HIGHEST
epsilon = 1e-06


def with_halo(x, sides, width):
    for axis, dim in sides:
        peers, length = (lax.axis_size(axis), x.shape[dim])
        up = [(i, (i + 1) % peers) for i in range(peers - 1)]
        down = [(j, i) for i, j in up]
        last = lax.slice_in_dim(x, length - width, length, axis=dim)
        initial = lax.slice_in_dim(x, 0, width, axis=dim)
        before = lax.ppermute(last, axis, up)
        after = lax.ppermute(initial, axis, down)
        x = jnp.concatenate([before, x, after], axis=dim)
    return x


def spread_taps(padded, upper, lower):
    even_rows = padded[1:-1, :, :, 1] + upper * padded[:-2, :, :, 3]
    odd_rows = lower * padded[2:, :, :, 0] + padded[1:-1, :, :, 2]
    rows_both = jnp.stack([even_rows, odd_rows], axis=1)
    even_cols = rows_both[:, :, :, 1:-1, 1] + rows_both[:, :, :, :-2, 3]
    odd_cols = rows_both[:, :, :, 2:, 0] + rows_both[:, :, :, 1:-1, 2]
    joined = jnp.stack([even_cols, odd_cols], axis=4)
    shape = joined.shape
    return joined.reshape(shape[0] * 2, shape[2], shape[3] * 2 * shape[5])


def norm_parts(value):
    centred = value - jnp.mean(value, axis=-1, keepdims=True)
    inverse = lax.rsqrt(jnp.mean(centred * centred, axis=-1, keepdims=True) + epsilon)
    return (centred * inverse, inverse)


def norm_back(normed, inverse, incoming):
    return inverse * (
        incoming
        - jnp.mean(incoming, axis=-1, keepdims=True)
        - normed * jnp.mean(incoming * normed, axis=-1, keepdims=True)
    )


NT = (((1,), (1,)), ((), ()))
BLOCKS = 4
KV_ROWS, Q_ROWS, SO_ROWS, OUT_ROWS, QUERY_ROWS = 0, 256, 384, 512, 640


def dot_nt(a, b):
    return lax.dot_general(a, b, NT, preferred_element_type=f32)


def dot_nn(a, b):
    return jnp.dot(a, b, preferred_element_type=f32)


def flip(x):
    return x.astype(f32).T.astype(bf16)


def chunk_of(keys):
    return 512 if keys % 512 == 0 else keys


def softmax_sweep(scores, values, chunks, columns):
    top = jnp.full((1, columns), -1e30, f32)
    total = jnp.zeros((1, columns), f32)
    mixed = None
    ahead = scores(0)
    for c in range(chunks):
        now = ahead
        ahead = scores(c + 1) if c + 1 < chunks else None
        new_top = jnp.maximum(top, jnp.max(now, axis=0, keepdims=True))
        fade = jnp.exp2((top - new_top) * LOG2E)
        expon = jnp.exp2(now * LOG2E - new_top * LOG2E)
        total = total * fade + jnp.sum(expon, axis=0, keepdims=True)
        parts = values(c, expon.astype(bf16))
        width = columns // len(parts)
        if mixed is None:
            mixed = parts
        else:
            mixed = [
                m * fade[:, j * width : (j + 1) * width] + part
                for j, (m, part) in enumerate(zip(mixed, parts))
            ]
        top = new_top
    width = columns // len(mixed)
    inverse = 1.0 / total
    mixed = [m * inverse[:, j * width : (j + 1) * width] for j, m in enumerate(mixed)]
    return mixed, top + jnp.log(total)


def cross_forward(q, k, vt, tp):
    items, queries, width = q.shape
    tile = queries // tp
    keys = k.shape[1]
    heads = width // HEAD
    step = chunk_of(keys)

    def kernel(q_ref, k_ref, vt_ref, o_ref, wide_ref, log_ref):
        pair = pl.program_id(1)
        owner = lax.broadcasted_iota(jnp.int32, (queries, width), 1) // HEAD
        both = jnp.concatenate(
            [jnp.where(owner == pair * 2 + j, q_ref[0], 0.0).astype(bf16) for j in range(2)], axis=0
        )

        def scores(c):
            return dot_nt(k_ref[0, pl.ds(c * step, step), :], both)

        def values(c, p):
            out = []
            for j in range(2):
                rows = pl.ds(pl.multiple_of((pair * 2 + j) * HEAD, HEAD), HEAD)
                v = vt_ref[0, rows, pl.ds(c * step, step)]
                out.append(dot_nn(v, p[:, j * queries : (j + 1) * queries]))
            return out

        mixed, log_total = softmax_sweep(scores, values, keys // step, 2 * queries)
        rows = jnp.concatenate(mixed, axis=0).T.reshape(tp, 1, tile, 2 * HEAD)
        o_ref[...] = rows.astype(bf16)
        wide_ref[...] = rows
        for j in range(2):
            log_ref[0, j] = jnp.broadcast_to(
                log_total[:, j * queries : (j + 1) * queries], (8, queries)
            )

    return pl.pallas_call(
        kernel,
        grid=(items, heads // 2),
        in_specs=[
            pl.BlockSpec((1, queries, width), lambda i, h: (i, 0, 0)),
            pl.BlockSpec((1, keys, width), lambda i, h: (i, 0, 0)),
            pl.BlockSpec((1, width, keys), lambda i, h: (i, 0, 0)),
        ],
        out_specs=[
            pl.BlockSpec((tp, 1, tile, 2 * HEAD), lambda i, h: (0, i, 0, h)),
            pl.BlockSpec((tp, 1, tile, 2 * HEAD), lambda i, h: (0, i, 0, h)),
            pl.BlockSpec((1, 2, 8, queries), lambda i, h: (i, h, 0, 0)),
        ],
        out_shape=[
            jax.ShapeDtypeStruct((tp, items, tile, width), bf16),
            jax.ShapeDtypeStruct((tp, items, tile, width), f32),
            jax.ShapeDtypeStruct((items, heads, 8, queries), f32),
        ],
        compiler_params=pltpu.CompilerParams(vmem_limit_bytes=48 << 20),
        cost_estimate=pl.CostEstimate(
            flops=16 * items * queries * keys * width,
            bytes_accessed=4 * items * (queries + keys) * width,
            transcendentals=items * queries * keys * heads,
        ),
        name="cross_forward",
    )(q, k, vt)


def cross_backward(q, do, o, logs, k, vt, start, items):
    _, queries, width = q.shape
    tp, _, tile, _ = do.shape
    keys = k.shape[1]
    heads = width // HEAD
    step = chunk_of(keys)

    def kernel(q_ref, do_ref, o_ref, log_ref, k_ref, vt_ref, dq_ref, dk_ref, dv_ref, qt, dot):
        head = pl.program_id(1)

        @pl.when(head == 0)
        def _():
            qt[...] = flip(q_ref[0])
            dot[...] = do_ref[...].astype(f32).reshape(queries, width).T.astype(bf16)

        mine = lax.broadcasted_iota(jnp.int32, (queries, width), 1) // HEAD == head
        q_mine = jnp.where(mine, q_ref[0], 0.0).astype(bf16)
        do_wide = jnp.where(mine, do_ref[...].astype(f32).reshape(queries, width), 0.0)
        do_mine = do_wide.astype(bf16)
        o_wide = o_ref[...].reshape(queries, width)
        delta = jnp.sum(do_wide * o_wide, axis=1, keepdims=True)
        log_total = log_ref[0, 0].T[:, :1] * LOG2E
        rows = pl.ds(pl.multiple_of(head * HEAD, HEAD), HEAD)
        qt_mine = qt[rows, :]
        dot_mine = dot[rows, :]

        def scores(c):
            s = dot_nt(q_mine, k_ref[0, pl.ds(c * step, step), :])
            return s, dot_nn(do_mine, vt_ref[0, :, pl.ds(c * step, step)])

        dq = jnp.zeros((queries, width), f32)
        ahead = scores(0)
        for c in range(keys // step):
            s, dp = ahead
            ahead = scores(c + 1) if c + 1 < keys // step else None
            p = jnp.exp2(s * LOG2E - log_total)
            ds = (p * (dp - delta)).astype(bf16)
            cols = pl.ds(c * step, step)
            dv_ref[0, :, cols] = dot_nn(dot_mine, p.astype(bf16)).astype(bf16)
            dk_ref[0, :, cols] = dot_nn(qt_mine, ds).astype(bf16)
            dq = dq + dot_nn(ds, k_ref[0, cols, :])
        dq = (dq * 0.125).astype(bf16)
        rest = jnp.where(head == 0, jnp.zeros_like(dq), dq_ref[0])
        dq_ref[0] = jnp.where(mine, dq, rest)

    rows_spec = pl.BlockSpec((1, queries, width), lambda i, h: (i + start, 0, 0))
    tiles_spec = pl.BlockSpec((tp, 1, tile, width), lambda i, h: (0, i + start, 0, 0))
    grads_spec = pl.BlockSpec((1, HEAD, keys), lambda i, h: (i, h, 0))
    return pl.pallas_call(
        kernel,
        grid=(items, heads),
        in_specs=[
            rows_spec,
            tiles_spec,
            tiles_spec,
            pl.BlockSpec((1, 1, 8, queries), lambda i, h: (i + start, h, 0, 0)),
            pl.BlockSpec((1, keys, width), lambda i, h: (i + start, 0, 0)),
            pl.BlockSpec((1, width, keys), lambda i, h: (i + start, 0, 0)),
        ],
        out_specs=[
            pl.BlockSpec((1, queries, width), lambda i, h: (i, 0, 0)),
            grads_spec,
            grads_spec,
        ],
        out_shape=[
            jax.ShapeDtypeStruct((items, queries, width), bf16),
            jax.ShapeDtypeStruct((items, width, keys), bf16),
            jax.ShapeDtypeStruct((items, width, keys), bf16),
        ],
        scratch_shapes=[pltpu.VMEM((width, queries), bf16), pltpu.VMEM((width, queries), bf16)],
        compiler_params=pltpu.CompilerParams(vmem_limit_bytes=48 << 20),
        cost_estimate=pl.CostEstimate(
            flops=40 * items * queries * keys * width,
            bytes_accessed=8 * items * (queries + keys) * width,
            transcendentals=items * queries * keys * heads,
        ),
        name="cross_backward",
    )(q, do, o, logs, k, vt)


def split_wide(x):
    low = lax.broadcasted_iota(jnp.int32, x.shape, 1) < HEAD
    wide = x.astype(f32)
    first = jnp.where(low, wide, 0.0)
    second = jnp.where(low, pltpu.roll(wide, HEAD, 1), 0.0)
    return jnp.concatenate([first, second], axis=0)


def split_pair(x):
    return split_wide(x).astype(bf16)


def part_specs(parts, half):
    if len(parts) == 1:
        return [pl.BlockSpec(parts[0].shape, lambda i: (0, 0, 0))]
    rows = parts[1].shape[0] // BLOCKS
    return [
        pl.BlockSpec(parts[0].shape, lambda i: (0, 0)),
        pl.BlockSpec((rows, 2 * HEAD), lambda i: (i, 0)),
    ]


def read_keys(refs, half):
    if len(refs) == 2:
        return refs[0][...]
    devices = refs[0].shape[0]
    return refs[0][:, : 2 * half, :].reshape(devices * 2 * half, 2 * HEAD)


def read_queries(refs, half, i, share):
    if len(refs) == 2:
        return refs[1][...]
    return refs[0][pl.ds(i * share, share), 2 * half :, :].reshape(share * half, 2 * HEAD)


def self_forward(parts, devices, half):
    tile = 2 * half
    keys = devices * tile
    blocks = BLOCKS
    share = devices // blocks
    block = share * half
    step = chunk_of(keys)

    def kernel(*refs):
        ins, (o_ref, wide_ref, log_ref, kv, vt) = refs[: len(parts)], refs[len(parts) :]
        i = pl.program_id(0)

        @pl.when(i == 0)
        def _():
            kv[...] = read_keys(ins, half)
            vt[...] = flip(kv[...])

        both = split_pair(read_queries(ins, half, i, share))

        def scores(c):
            return dot_nt(kv[pl.ds(c * step, step), :], both)

        def values(c, p):
            return [dot_nn(vt[HEAD:, pl.ds(c * step, step)], p)]

        mixed, log_total = softmax_sweep(scores, values, keys // step, 2 * block)
        mixed = mixed[0]
        rows = jnp.concatenate([mixed[:, :block], mixed[:, block:]], axis=0).T
        o_ref[...] = rows.astype(bf16)
        wide_ref[...] = rows
        log_ref[0] = jnp.broadcast_to(log_total, (8, 2 * block))

    return pl.pallas_call(
        kernel,
        grid=(blocks,),
        in_specs=part_specs(parts, half),
        out_specs=[
            pl.BlockSpec((block, 2 * HEAD), lambda i: (i, 0)),
            pl.BlockSpec((block, 2 * HEAD), lambda i: (i, 0)),
            pl.BlockSpec((1, 8, 2 * block), lambda i: (i, 0, 0)),
        ],
        out_shape=[
            jax.ShapeDtypeStruct((devices * half, 2 * HEAD), bf16),
            jax.ShapeDtypeStruct((devices * half, 2 * HEAD), f32),
            jax.ShapeDtypeStruct((blocks, 8, 2 * block), f32),
        ],
        scratch_shapes=[pltpu.VMEM((keys, 2 * HEAD), bf16), pltpu.VMEM((2 * HEAD, keys), bf16)],
        compiler_params=pltpu.CompilerParams(vmem_limit_bytes=48 << 20),
        cost_estimate=pl.CostEstimate(
            flops=16 * keys * keys * HEAD,
            bytes_accessed=8 * keys * 2 * HEAD,
            transcendentals=keys * keys,
        ),
        name="self_forward",
    )(*parts)


def self_backward(parts, do, o, logs, devices, half):
    tile = 2 * half
    keys = devices * tile
    blocks = logs.shape[0]
    share = devices // blocks
    block = share * half
    step = chunk_of(keys)

    def kernel(*refs):
        n = len(parts)
        ins, (do_ref, o_ref, log_ref), outs = refs[:n], refs[n : n + 3], refs[n + 3 : 2 * n + 3]
        kv, vt, grads = refs[2 * n + 3 :]
        i = pl.program_id(0)
        mine = pl.ds(i * share, share)

        @pl.when(i == 0)
        def _():
            kv[...] = read_keys(ins, half)
            vt[...] = flip(kv[...])
            grads[...] = jnp.zeros_like(grads)

        q_both = split_pair(read_queries(ins, half, i, share))
        do_both = split_pair(do_ref[...])
        delta = jnp.sum(do_both.astype(f32) * split_wide(o_ref[...]), axis=1, keepdims=True)
        log_total = log_ref[0].T[:, :1] * LOG2E
        qt = flip(q_both)[:HEAD]
        dot = flip(do_both)[:HEAD]
        do_low = do_both[:, :HEAD]

        def scores(c):
            s = dot_nt(q_both, kv[pl.ds(c * step, step), :])
            return s, dot_nn(do_low, vt[HEAD:, pl.ds(c * step, step)])

        dq = jnp.zeros((2 * block, 2 * HEAD), f32)
        ahead = scores(0)
        for c in range(keys // step):
            s, dp = ahead
            ahead = scores(c + 1) if c + 1 < keys // step else None
            p = jnp.exp2(s * LOG2E - log_total)
            ds = (p * (dp - delta)).astype(bf16)
            cols = pl.ds(c * step, step)
            grads[:HEAD, cols] += dot_nn(qt, ds)
            grads[HEAD:, cols] += dot_nn(dot, p.astype(bf16))
            dq = dq + dot_nn(ds, kv[cols, :])
        dq = dq * 0.125
        low = lax.broadcasted_iota(jnp.int32, (block, 2 * HEAD), 1) < HEAD
        packed = jnp.where(low, dq[:block], pltpu.roll(dq[block:], HEAD, 1)).astype(bf16)
        if n == 1:
            outs[0][mine, tile:, :] = packed.reshape(share, half, 2 * HEAD)
        else:
            outs[1][...] = packed

        @pl.when(i == blocks - 1)
        def _():
            dkv = grads[...].T.astype(bf16)
            if n == 1:
                outs[0][:, :tile, :] = dkv.reshape(devices, tile, 2 * HEAD)
            else:
                outs[0][...] = dkv

    rows_spec = pl.BlockSpec((block, 2 * HEAD), lambda i: (i, 0))
    return pl.pallas_call(
        kernel,
        grid=(blocks,),
        in_specs=part_specs(parts, half)
        + [rows_spec, rows_spec, pl.BlockSpec((1, 8, 2 * block), lambda i: (i, 0, 0))],
        out_specs=part_specs(parts, half),
        out_shape=[jax.ShapeDtypeStruct(p.shape, bf16) for p in parts],
        scratch_shapes=[
            pltpu.VMEM((keys, 2 * HEAD), bf16),
            pltpu.VMEM((2 * HEAD, keys), bf16),
            pltpu.VMEM((2 * HEAD, keys), f32),
        ],
        compiler_params=pltpu.CompilerParams(vmem_limit_bytes=48 << 20),
        cost_estimate=pl.CostEstimate(
            flops=40 * keys * keys * HEAD,
            bytes_accessed=16 * keys * 2 * HEAD,
            transcendentals=keys * keys,
        ),
        name="self_backward",
    )(*parts, do, o, logs)


def swap_pairs(first, second):
    low = lax.broadcasted_iota(jnp.int32, first.shape, 1) < HEAD
    return (
        jnp.where(low, first, pltpu.roll(second, HEAD, 1)),
        jnp.where(low, pltpu.roll(first, HEAD, 1), second),
    )


def tile_places(items, turns, groups, tile):
    return [(i * tile, i % turns, i // turns) for i in range(items)]


def slot_rows(weights, first, size):
    return pl.BlockSpec((1, size, weights.shape[2]), lambda i: (i, first // size, 0))


def project_pack(x, weights, items, turns, groups):
    rows, width = x.shape
    slots = weights.shape[0]
    tile = rows // items
    half = tile // 2

    def kernel(x_ref, kv_ref, q_ref, out_ref):
        kv = dot_nt(x_ref[...], kv_ref[0]).astype(bf16)
        q = dot_nt(x_ref[...], q_ref[0]).astype(bf16).astype(f32) * 0.125
        for start, turn, group in tile_places(items, turns, groups, tile):
            upper, lower = swap_pairs(q[start : start + half], q[start + half : start + tile])
            for h, part in enumerate((upper, lower)):
                out_ref[turn, group, 0, h, :tile, :] = kv[
                    start : start + tile, h * 2 * HEAD : (h + 1) * 2 * HEAD
                ]
                out_ref[turn, group, 0, h, tile:, :] = part.astype(bf16)

    shape = (turns, groups, slots, 2, 3 * half, 2 * HEAD)
    return pl.pallas_call(
        kernel,
        grid=(slots,),
        in_specs=[
            pl.BlockSpec((rows, width), lambda i: (0, 0)),
            slot_rows(weights, KV_ROWS, 4 * HEAD),
            slot_rows(weights, Q_ROWS, 2 * HEAD),
        ],
        out_specs=pl.BlockSpec(
            (turns, groups, 1, 2, 3 * half, 2 * HEAD), lambda i: (0, 0, i, 0, 0, 0)
        ),
        out_shape=jax.ShapeDtypeStruct(shape, bf16),
        compiler_params=pltpu.CompilerParams(vmem_limit_bytes=40 << 20),
        cost_estimate=pl.CostEstimate(
            flops=2 * rows * width * slots * 6 * HEAD,
            bytes_accessed=2 * (rows + slots * 6 * HEAD) * width,
            transcendentals=0,
        ),
        name="project_pack",
    )(x, weights, weights)


def unpack_project(blocks, weights, items, groups):
    turns = len(blocks)
    slots = weights.shape[0]
    half = blocks[0].shape[3]
    tile = 2 * half
    width = weights.shape[2]

    def kernel(*refs):
        ins, w_ref, flat_ref, out_ref = refs[:turns], refs[turns], refs[turns + 1], refs[turns + 2]
        slot = pl.program_id(0)
        for start, turn, group in tile_places(items, turns, groups, tile):
            pair = [ins[turn][group, 0, h].astype(f32) for h in range(2)]
            upper, lower = swap_pairs(*pair)
            flat_ref[start : start + half, :] = upper.astype(bf16)
            flat_ref[start + half : start + tile, :] = lower.astype(bf16)
        part = dot_nn(flat_ref[...], w_ref[0])

        @pl.when(slot == 0)
        def _():
            out_ref[...] = part

        @pl.when(slot > 0)
        def _():
            out_ref[...] += part

    return pl.pallas_call(
        kernel,
        grid=(slots,),
        in_specs=[
            pl.BlockSpec((groups, 1, 2, half, 2 * HEAD), lambda i: (0, i, 0, 0, 0))
            for _ in range(turns)
        ]
        + [slot_rows(weights, SO_ROWS, 2 * HEAD)],
        out_specs=[
            pl.BlockSpec((items * tile, 2 * HEAD), lambda i: (0, i)),
            pl.BlockSpec((items * tile, width), lambda i: (0, 0)),
        ],
        out_shape=[
            jax.ShapeDtypeStruct((items * tile, slots * 2 * HEAD), bf16),
            jax.ShapeDtypeStruct((items * tile, width), f32),
        ],
        compiler_params=pltpu.CompilerParams(vmem_limit_bytes=40 << 20),
        cost_estimate=pl.CostEstimate(
            flops=2 * items * tile * width * slots * 2 * HEAD,
            bytes_accessed=4 * items * tile * width,
            transcendentals=0,
        ),
        name="unpack_project",
    )(*blocks, weights)


def back_pack(x, weights, items, turns, groups):
    rows, width = x.shape
    slots = weights.shape[0]
    tile = rows // items
    half = tile // 2

    def kernel(x_ref, w_ref, out_ref):
        grads = dot_nt(x_ref[...], w_ref[0])
        for start, turn, group in tile_places(items, turns, groups, tile):
            pair = swap_pairs(grads[start : start + half], grads[start + half : start + tile])
            for h, part in enumerate(pair):
                out_ref[turn, group, 0, h] = part.astype(bf16)

    return pl.pallas_call(
        kernel,
        grid=(slots,),
        in_specs=[
            pl.BlockSpec((rows, width), lambda i: (0, 0)),
            slot_rows(weights, SO_ROWS, 2 * HEAD),
        ],
        out_specs=pl.BlockSpec(
            (turns, groups, 1, 2, half, 2 * HEAD), lambda i: (0, 0, i, 0, 0, 0)
        ),
        out_shape=jax.ShapeDtypeStruct((turns, groups, slots, 2, half, 2 * HEAD), bf16),
        compiler_params=pltpu.CompilerParams(vmem_limit_bytes=40 << 20),
        cost_estimate=pl.CostEstimate(
            flops=2 * rows * width * slots * 2 * HEAD,
            bytes_accessed=2 * (rows + slots * 2 * HEAD) * width,
            transcendentals=0,
        ),
        name="back_pack",
    )(x, weights)


def unpack_back(blocks, weights, items, groups):
    turns = len(blocks)
    slots, _, width = weights.shape
    half = blocks[0].shape[3] // 3
    tile = 2 * half
    rows = items * tile

    def kernel(*refs):
        ins = refs[:turns]
        kv_ref, q_ref, flat_ref, out_ref = refs[turns:]
        slot = pl.program_id(0)
        for start, turn, group in tile_places(items, turns, groups, tile):
            pair = []
            for h in range(2):
                flat_ref[0, start : start + tile, h * 2 * HEAD : (h + 1) * 2 * HEAD] = ins[turn][
                    group, 0, h, :tile, :
                ]
                pair.append(ins[turn][group, 0, h, tile:, :].astype(f32))
            upper, lower = swap_pairs(*pair)
            flat_ref[0, start : start + half, 4 * HEAD :] = upper.astype(bf16)
            flat_ref[0, start + half : start + tile, 4 * HEAD :] = lower.astype(bf16)
        part = dot_nn(flat_ref[0, :, : 4 * HEAD], kv_ref[0])
        part = part + dot_nn(flat_ref[0, :, 4 * HEAD :], q_ref[0])

        @pl.when(slot == 0)
        def _():
            out_ref[...] = part

        @pl.when(slot > 0)
        def _():
            out_ref[...] += part

    return pl.pallas_call(
        kernel,
        grid=(slots,),
        in_specs=[
            pl.BlockSpec((groups, 1, 2, 3 * half, 2 * HEAD), lambda i: (0, i, 0, 0, 0))
            for _ in range(turns)
        ]
        + [slot_rows(weights, KV_ROWS, 4 * HEAD), slot_rows(weights, Q_ROWS, 2 * HEAD)],
        out_specs=[
            pl.BlockSpec((1, rows, 6 * HEAD), lambda i: (i, 0, 0)),
            pl.BlockSpec((rows, width), lambda i: (0, 0)),
        ],
        out_shape=[
            jax.ShapeDtypeStruct((slots, rows, 6 * HEAD), bf16),
            jax.ShapeDtypeStruct((rows, width), f32),
        ],
        compiler_params=pltpu.CompilerParams(vmem_limit_bytes=40 << 20),
        cost_estimate=pl.CostEstimate(
            flops=2 * rows * width * slots * 6 * HEAD,
            bytes_accessed=4 * rows * width,
            transcendentals=0,
        ),
        name="unpack_back",
    )(*blocks, weights, weights)


def out_project(mixed, weights):
    tp, items, tile, local = mixed.shape
    slots, _, width = weights.shape
    rows = items * tile

    def kernel(x_ref, w_ref, out_ref):
        slot = pl.program_id(0)
        part = dot_nn(x_ref[0].reshape(rows, local // 2), w_ref[0])

        @pl.when(slot == 0)
        def _():
            out_ref[...] = part

        @pl.when(slot > 0)
        def _():
            out_ref[...] += part

    return pl.pallas_call(
        kernel,
        grid=(slots,),
        in_specs=[
            pl.BlockSpec((1, items, tile, local // 2), lambda i: (i % tp, 0, 0, i // tp)),
            slot_rows(weights, OUT_ROWS, 2 * HEAD),
        ],
        out_specs=pl.BlockSpec((rows, width), lambda i: (0, 0)),
        out_shape=jax.ShapeDtypeStruct((rows, width), f32),
        compiler_params=pltpu.CompilerParams(vmem_limit_bytes=40 << 20),
        cost_estimate=pl.CostEstimate(
            flops=2 * rows * width * tp * local,
            bytes_accessed=4 * rows * width,
            transcendentals=0,
        ),
        name="out_project",
    )(mixed, weights)


def out_back(x, weights, shape):
    tp, items, tile, local = shape
    rows, width = x.shape

    def kernel(x_ref, w_ref, out_ref):
        part = dot_nt(x_ref[...], w_ref[0])
        out_ref[0] = part.astype(bf16).reshape(items, tile, local // 2)

    return pl.pallas_call(
        kernel,
        grid=(2 * tp,),
        in_specs=[
            pl.BlockSpec((rows, width), lambda i: (0, 0)),
            slot_rows(weights, OUT_ROWS, 2 * HEAD),
        ],
        out_specs=pl.BlockSpec((1, items, tile, local // 2), lambda i: (i % tp, 0, 0, i // tp)),
        out_shape=jax.ShapeDtypeStruct(shape, bf16),
        compiler_params=pltpu.CompilerParams(vmem_limit_bytes=40 << 20),
        cost_estimate=pl.CostEstimate(
            flops=2 * rows * width * tp * local,
            bytes_accessed=4 * rows * width,
            transcendentals=0,
        ),
        name="out_back",
    )(x, weights)


def first_kernel(tokens, shift, scale, w, tp):
    rows, items, cols, width = tokens.shape
    cols_here = cols // tp
    tile = rows * cols_here
    local = w.shape[1]

    def kernel(x_ref, shift_ref, scale_ref, w_ref, in_ref, q_ref):
        hat, _ = norm_parts(x_ref[...].astype(f32).reshape(rows, cols, width))
        value = hat * (1.0 + scale_ref[0]) + shift_ref[0]
        for t in range(tp):
            part = value[:, t * cols_here : (t + 1) * cols_here, :].reshape(tile, width)
            in_ref[0, t * tile : (t + 1) * tile, :] = part.astype(bf16)
        q = dot_nn(in_ref[0], w_ref[...]).astype(bf16).astype(f32) * 0.125
        q_ref[0] = q.astype(bf16)

    piece_spec = pl.BlockSpec((1, 1, width), lambda i: (i, 0, 0))
    return pl.pallas_call(
        kernel,
        grid=(items,),
        in_specs=[
            pl.BlockSpec((rows, 1, cols, width), lambda i: (0, i, 0, 0)),
            piece_spec,
            piece_spec,
            pl.BlockSpec(w.shape, lambda i: (0, 0)),
        ],
        out_specs=[
            pl.BlockSpec((1, tp * tile, width), lambda i: (i, 0, 0)),
            pl.BlockSpec((1, tp * tile, local), lambda i: (i, 0, 0)),
        ],
        out_shape=[
            jax.ShapeDtypeStruct((items, tp * tile, width), bf16),
            jax.ShapeDtypeStruct((items, tp * tile, local), bf16),
        ],
        compiler_params=pltpu.CompilerParams(vmem_limit_bytes=48 << 20),
        cost_estimate=pl.CostEstimate(
            flops=2 * items * tp * tile * width * local,
            bytes_accessed=4 * items * tp * tile * width,
            transcendentals=0,
        ),
        name="first_kernel",
    )(tokens, shift, scale, w)


def key_value_kernel(context, w_key, w_value_t):
    items, keys, depth = context.shape
    local = w_key.shape[1]
    step = 1024 if keys % 1024 == 0 else keys

    def kernel(x_ref, wk_ref, wv_ref, k_ref, vt_ref):
        k_ref[0] = dot_nn(x_ref[0], wk_ref[...]).astype(bf16)
        vt_ref[0] = dot_nt(wv_ref[...], x_ref[0]).astype(bf16)

    return pl.pallas_call(
        kernel,
        grid=(items, keys // step),
        in_specs=[
            pl.BlockSpec((1, step, depth), lambda i, j: (i, j, 0)),
            pl.BlockSpec(w_key.shape, lambda i, j: (0, 0)),
            pl.BlockSpec(w_value_t.shape, lambda i, j: (0, 0)),
        ],
        out_specs=[
            pl.BlockSpec((1, step, local), lambda i, j: (i, j, 0)),
            pl.BlockSpec((1, local, step), lambda i, j: (i, 0, j)),
        ],
        out_shape=[
            jax.ShapeDtypeStruct((items, keys, local), bf16),
            jax.ShapeDtypeStruct((items, local, keys), bf16),
        ],
        compiler_params=pltpu.CompilerParams(vmem_limit_bytes=40 << 20),
        cost_estimate=pl.CostEstimate(
            flops=4 * items * keys * depth * local,
            bytes_accessed=2 * items * keys * (depth + 2 * local),
            transcendentals=0,
        ),
        name="key_value_kernel",
    )(context, w_key, w_value_t)


def key_value_grads(dk_t, dv_t, context, start):
    items, local, keys = dk_t.shape
    depth = context.shape[2]
    step = 1024 if keys % 1024 == 0 else keys

    def kernel(dk_ref, dv_ref, x_ref, out_ref):
        first = (pl.program_id(0) == 0) & (pl.program_id(1) == 0)
        both = jnp.concatenate([dk_ref[0], dv_ref[0]], axis=0)
        part = dot_nn(both, x_ref[0])

        @pl.when(first)
        def _():
            out_ref[...] = part

        @pl.when(jnp.logical_not(first))
        def _():
            out_ref[...] += part

    grads_spec = pl.BlockSpec((1, local, step), lambda i, j: (i, 0, j))
    return pl.pallas_call(
        kernel,
        grid=(items, keys // step),
        in_specs=[
            grads_spec,
            grads_spec,
            pl.BlockSpec((1, step, depth), lambda i, j: (i + start, j, 0)),
        ],
        out_specs=pl.BlockSpec((2 * local, depth), lambda i, j: (0, 0)),
        out_shape=jax.ShapeDtypeStruct((2 * local, depth), f32),
        compiler_params=pltpu.CompilerParams(vmem_limit_bytes=40 << 20),
        cost_estimate=pl.CostEstimate(
            flops=4 * items * keys * depth * local,
            bytes_accessed=2 * items * keys * (depth + 2 * local),
            transcendentals=0,
        ),
        name="key_value_grads",
    )(dk_t, dv_t, context)


def feed_forward(x, g, up, down):
    rows, width = x.shape
    slots, _, hidden = up.shape
    parts = 4 if rows % 64 == 0 else 1
    size = rows // parts

    def kernel(x_ref, g_ref, up_ref, down_ref, active_ref, dh_ref, branch_ref, back_ref):
        slot = pl.program_id(0)

        @pl.when(slot == 0)
        def _():
            branch_ref[...] = jnp.zeros_like(branch_ref)
            back_ref[...] = jnp.zeros_like(back_ref)

        def products(r):
            mine = pl.ds(r * size, size)
            return dot_nn(x_ref[mine, :], up_ref[0]), dot_nt(g_ref[mine, :], down_ref[0])

        ahead = products(0)
        for r in range(parts):
            h, da = ahead
            ahead = products(r + 1) if r + 1 < parts else None
            mine = pl.ds(r * size, size)
            below = 0.5 * (1.0 + lax.erf(h * 0.7071067811865476))
            slope = below + h * (jnp.exp(h * h * -0.5) * 0.3989422804014327)
            active = (h * below).astype(bf16)
            dh = (da * slope).astype(bf16)
            active_ref[0, mine, :] = active
            dh_ref[0, mine, :] = dh
            branch_ref[mine, :] += dot_nn(active, down_ref[0])
            back_ref[mine, :] += dot_nt(dh, up_ref[0])

    rows_spec = pl.BlockSpec((rows, width), lambda i: (0, 0))
    hidden_spec = pl.BlockSpec((1, rows, hidden), lambda i: (i, 0, 0))
    return pl.pallas_call(
        kernel,
        grid=(slots,),
        in_specs=[
            rows_spec,
            rows_spec,
            pl.BlockSpec((1, width, hidden), lambda i: (i, 0, 0)),
            pl.BlockSpec((1, hidden, width), lambda i: (i, 0, 0)),
        ],
        out_specs=[hidden_spec, hidden_spec, rows_spec, rows_spec],
        out_shape=[
            jax.ShapeDtypeStruct((slots, rows, hidden), bf16),
            jax.ShapeDtypeStruct((slots, rows, hidden), bf16),
            jax.ShapeDtypeStruct((rows, width), f32),
            jax.ShapeDtypeStruct((rows, width), f32),
        ],
        compiler_params=pltpu.CompilerParams(vmem_limit_bytes=52 << 20),
        cost_estimate=pl.CostEstimate(
            flops=8 * slots * rows * width * hidden,
            bytes_accessed=4 * slots * width * hidden,
            transcendentals=2 * slots * rows * hidden,
        ),
        name="feed_forward",
    )(x, g, up, down)


def weight_terms(buffer, shape, lhs, lhs_block, lhs_place, rhs, tp, size, first):
    count, width = rhs.shape
    devices, _, share = shape
    seq = devices // tp
    depth = lhs_block[-1]

    def kernel(*refs):
        a_ref, b_ref, out_ref = refs[0], refs[1], refs[-1]
        a = a_ref[...]
        if len(lhs_block) > 3:
            a = a.astype(f32)
        a = a.reshape(count, depth).astype(bf16)
        terms = lax.dot_general(a, b_ref[...], (((0,), (0,)), ((), ())), preferred_element_type=f32)
        for s in range(seq):
            out_ref[s] = terms[:, s * share : (s + 1) * share].astype(bf16)

    return pl.pallas_call(
        kernel,
        grid=(tp, 2),
        in_specs=[
            pl.BlockSpec(lhs_block, lhs_place),
            pl.BlockSpec(rhs.shape, lambda t, c: (0, 0)),
        ]
        + ([] if buffer is None else [pl.BlockSpec(memory_space=pl.ANY)]),
        out_specs=pl.BlockSpec((seq, size, share), lambda t, c: (t, first // size + c, 0)),
        out_shape=jax.ShapeDtypeStruct(shape, bf16),
        input_output_aliases={} if buffer is None else {2: 0},
        compiler_params=pltpu.CompilerParams(vmem_limit_bytes=40 << 20),
        cost_estimate=pl.CostEstimate(
            flops=4 * tp * count * depth * width,
            bytes_accessed=4 * tp * (count + width) * depth,
            transcendentals=0,
        ),
        name="weight_terms",
    )(lhs, rhs, *([] if buffer is None else [buffer]))


def last_kernel(buffer, tokens, scale, middle, dq, small, start):
    rows, _, cols, width = tokens.shape
    tp, items, queries, local = dq.shape
    slots = small.shape[0]
    cols_here = cols // tp
    tile = rows * cols_here
    slot_width = local // 2

    def kernel(x_ref, scale_ref, middle_ref, dq_ref, w_ref, *refs):
        out_ref, sums_ref = refs[-2:]
        hat, inverse = norm_parts(x_ref[...].astype(f32).reshape(rows, cols, width))
        weights = w_ref[...].reshape(tp * local, width)
        shift_sum = jnp.zeros((1, width), f32)
        scale_sum = jnp.zeros((1, width), f32)
        for t in range(tp):
            pieces = [
                dq_ref[u, 0, t * tile : (t + 1) * tile, c * slot_width : (c + 1) * slot_width]
                for c in range(2)
                for u in range(tp)
            ]
            g = dot_nn(jnp.concatenate(pieces, axis=1), weights)
            mine = slice(t * cols_here, (t + 1) * cols_here)
            hat_t = hat[:, mine, :].reshape(tile, width)
            inverse_t = inverse[:, mine, :].reshape(tile, 1)
            shift_sum = shift_sum + jnp.sum(g, axis=0, keepdims=True)
            scale_sum = scale_sum + jnp.sum(g * hat_t, axis=0, keepdims=True)
            value = middle_ref[t, 0].astype(f32) + norm_back(
                hat_t, inverse_t, g * (1.0 + scale_ref[0])
            )
            out_ref[:, 0, mine, :] = value.reshape(rows, cols_here, width)
        sums_ref[0, 0:1, :] = shift_sum
        sums_ref[0, 1:2, :] = scale_sum

    return pl.pallas_call(
        kernel,
        grid=(items,),
        in_specs=[
            pl.BlockSpec((rows, 1, cols, width), lambda i: (0, i + start, 0, 0)),
            pl.BlockSpec((1, 1, width), lambda i: (i + start, 0, 0)),
            pl.BlockSpec((tp, 1, tile, width), lambda i: (0, i + start, 0, 0)),
            pl.BlockSpec((tp, 1, queries, local), lambda i: (0, i, 0, 0)),
            pl.BlockSpec((slots, slot_width, width), lambda i: (0, QUERY_ROWS // slot_width, 0)),
        ]
        + ([] if buffer is None else [pl.BlockSpec(memory_space=pl.ANY)]),
        out_specs=[
            pl.BlockSpec((rows, 1, cols, width), lambda i: (0, i + start, 0, 0)),
            pl.BlockSpec((1, 2, width), lambda i: (i, 0, 0)),
        ],
        out_shape=[
            jax.ShapeDtypeStruct(tokens.shape, f32),
            jax.ShapeDtypeStruct((items, 2, width), f32),
        ],
        input_output_aliases={} if buffer is None else {5: 0},
        compiler_params=pltpu.CompilerParams(vmem_limit_bytes=52 << 20),
        cost_estimate=pl.CostEstimate(
            flops=2 * items * queries * width * tp * local,
            bytes_accessed=10 * items * queries * width,
            transcendentals=0,
        ),
        name="last_kernel",
    )(tokens, scale, middle, dq, small, *([] if buffer is None else [buffer]))


def exchange(x, axis):
    return lax.all_to_all(x, axis, 0, 0, tiled=True)


def gather(x, axis):
    names = axis if isinstance(axis, tuple) else (axis,)
    count = 1
    for name in names:
        count *= lax.axis_size(name)
    return exchange(jnp.broadcast_to(x[None], (count,) + x.shape), axis)


def reduce_blocks(x, axis):
    return jnp.sum(exchange(x.astype(bf16), axis).astype(f32), axis=0)


def body(
    tokens,
    context,
    group_ids,
    source_table,
    w_query,
    w_key,
    w_value,
    w_out,
    w_self_query,
    w_self_key,
    w_self_value,
    w_self_out,
    w_up,
    w_down,
    w_deconv,
    deconv_bias,
    out_cotangent,
    plane_cotangent,
):
    rows_here, items, plane_cols, width = tokens.shape
    cols_here = out_cotangent.shape[2]
    tp = lax.axis_size("tp")
    seq = lax.axis_size("seq")
    both_axes = ("seq", "tp")
    devices = tp * seq
    local = w_query.shape[1]
    hidden_here = w_up.shape[1]
    slots = 2 * tp
    slot_heads = local // HEAD // 2
    slot_width = local // 2
    heads = slots * slot_heads
    tile = rows_here * cols_here
    half = tile // 2
    groups = devices // heads
    turns = -(-items // groups)
    share = width // seq
    fast = slot_heads == 2 and half % 16 == 0 and items == groups * turns and share % 128 == 0
    me_tp = lax.axis_index("tp")
    core = lax.axis_index("seq") % 2

    picker = (group_ids[:, None] == jnp.arange(GROUPS, dtype=jnp.int32)[None, :]).astype(f32)
    mods = jnp.dot(picker, source_table, precision=highest).reshape(items, 9, 1, width)

    def piece(index):
        return mods[:, index]

    def dot(spec, a, b):
        return jnp.einsum(spec, a, b, preferred_element_type=f32)

    def to_tile(x):
        return x.transpose(1, 0, 2, 3).reshape(items, tile, width)

    def from_tile(x):
        return x.reshape(items, rows_here, cols_here, width).transpose(1, 0, 2, 3)

    teams = [
        [(2 * pair + c) * tp + t for c in range(2) for t in range(tp)] for pair in range(seq // 2)
    ]

    def whole(x):
        return lax.all_gather(x, both_axes, axis=0, tiled=False, axis_index_groups=teams)

    def my_rows(x):
        return lax.dynamic_slice_in_dim(x, core * slot_width, slot_width, 0)

    def my_columns(x):
        size = x.shape[1] // 2
        return lax.dynamic_slice_in_dim(x, core * size, size, 1)

    key_value = jnp.stack(
        [
            my_columns(w_self_key).T.reshape(slot_heads, HEAD, width),
            my_columns(w_self_value).T.reshape(slot_heads, HEAD, width),
        ],
        axis=1,
    ).reshape(2 * slot_width, width)
    small = whole(
        jnp.concatenate(
            [
                key_value,
                my_columns(w_self_query).T,
                my_rows(w_self_out),
                my_rows(w_out),
                my_columns(w_query).T,
            ],
            axis=0,
        )
    )
    cuts = [slot_width * k for k in (0, 2, 3, 4, 5, 6)]
    kv_slots, q_slots, so_slots, out_slots, query_slots = [
        small[:, a:b] for a, b in zip(cuts[:-1], cuts[1:])
    ]
    up_slots = whole(my_columns(w_up))
    down_slots = whole(
        lax.dynamic_slice_in_dim(w_down, core * (hidden_here // 2), hidden_here // 2, 0)
    )

    def by_tp(x):
        return x.reshape(2, tp, slot_width, width).transpose(1, 0, 2, 3).reshape(tp, local, width)

    incoming = plane_cotangent.reshape(2 * rows_here, items, 2 * cols_here, COUT)
    plane_row = (lax.axis_index("seq") * rows_here + jnp.arange(rows_here, dtype=jnp.int32)) % PLANE
    upper_keep = (plane_row != 0).astype(f32)
    lower_keep = (plane_row != PLANE - 1).astype(f32)
    grad_edges = with_halo(incoming, (("seq", 0), ("tp", 2)), 1)
    upper_mask = upper_keep.astype(bf16)[:, None, None, None]
    lower_mask = lower_keep.astype(bf16)[:, None, None, None]
    first_pair = grad_edges[:-2].reshape(rows_here, 2, items, 2 * cols_here + 2, COUT)
    last_pair = grad_edges[2:].reshape(rows_here, 2, items, 2 * cols_here + 2, COUT)
    row_taps = jnp.stack(
        [
            first_pair[:, 0] * upper_mask,
            first_pair[:, 1],
            last_pair[:, 0],
            last_pair[:, 1] * lower_mask,
        ],
        axis=3,
    )
    left_pair = row_taps[:, :, :-2].reshape(rows_here, items, cols_here, 2, 4, COUT)
    right_pair = row_taps[:, :, 2:].reshape(rows_here, items, cols_here, 2, 4, COUT)
    tap_grads = jnp.stack(
        [
            left_pair[:, :, :, 0],
            left_pair[:, :, :, 1],
            right_pair[:, :, :, 0],
            right_pair[:, :, :, 1],
        ],
        axis=4,
    )
    tap_grads = tap_grads.reshape(rows_here, items, cols_here, 16 * COUT)
    grad_result = to_tile(out_cotangent.astype(f32) + dot("rict,dt->ricd", tap_grads, w_deconv))
    grad_bias = jnp.sum(incoming.astype(f32), axis=(0, 1, 2))
    grad_mlp = (piece(8) * grad_result).astype(bf16)

    if fast:
        first_in, queries = first_kernel(tokens, piece(0), piece(1), w_query, tp)
    else:
        ordered = (
            tokens.reshape(rows_here, items, tp, cols_here, width)
            .transpose(1, 2, 0, 3, 4)
            .reshape(items, tp * tile, width)
        )
        first_hat, first_inv = norm_parts(ordered.astype(f32))
        first_in = (first_hat * (1.0 + piece(1)) + piece(0)).astype(bf16)
        queries = dot("iqd,de->iqe", first_in, w_query).astype(bf16) * bf16(0.125)
    image = context.transpose(1, 0, 2)
    keys, values_t = key_value_kernel(image, w_key, w_value.T)
    mixed, mixed_wide, cross_logs = cross_forward(queries, keys, values_t, tp)
    mixed_tile = exchange(mixed, "tp")
    if fast:
        branch_a = out_project(mixed_tile, small).reshape(items, tile, width)
    else:
        branch_a = dot("time,tef->imf", mixed_tile, by_tp(out_slots))
    residual = to_tile(lax.dynamic_slice_in_dim(tokens, me_tp * cols_here, cols_here, 2)).astype(f32)
    middle = residual + piece(2) * branch_a

    self_hat, self_inv = norm_parts(middle)
    self_in = (self_hat * (1.0 + piece(4)) + piece(3)).astype(bf16)
    flat = (items * tile, width)
    spare = groups * turns - items

    def spread_items(x):
        if spare:
            x = jnp.pad(x, ((0, 0), (0, spare)) + ((0, 0),) * (x.ndim - 2))
        return x.reshape((slots, groups, turns) + x.shape[2:])

    def pack_keys(x):
        x = spread_items(x.reshape(slots, items, tile, slot_heads, 2 * HEAD))
        return x.transpose(2, 1, 0, 4, 3, 5).reshape(turns, devices, tile, 2 * HEAD)

    def unpack_keys(x):
        x = x.reshape(turns, groups, slots, slot_heads, tile, 2 * HEAD).transpose(2, 1, 0, 4, 3, 5)
        x = x.reshape(slots, groups * turns, tile, 2 * slot_width)[:, :items]
        return x.reshape(slots, items * tile, 2 * slot_width)

    def pack_rows(x):
        x = spread_items(x.reshape(slots, items, 2, half, slot_heads, HEAD))
        return x.transpose(2, 1, 0, 5, 4, 3, 6).reshape(turns, devices, half, 2 * HEAD)

    def unpack_rows(x):
        x = x.reshape(turns, groups, slots, slot_heads, half, 2, HEAD).transpose(2, 1, 0, 5, 4, 3, 6)
        x = x.reshape(slots, groups * turns, tile, slot_width)[:, :items]
        return x.reshape(slots, items * tile, slot_width)

    if fast:
        sends = project_pack(self_in.reshape(flat), small, items, turns, groups)
        sends = sends.reshape(turns, devices, 3 * half, 2 * HEAD)
        sends = [sends[turn] for turn in range(turns)]
    else:
        kv_sends = pack_keys(dot("nd,xed->xne", self_in.reshape(flat), kv_slots).astype(bf16))
        q_sends = dot("nd,xed->xne", self_in.reshape(flat), q_slots).astype(bf16)
        q_sends = pack_rows(q_sends * bf16(0.125))
        parts = [
            [
                exchange(kv_sends[turn], both_axes).reshape(devices * tile, 2 * HEAD),
                exchange(q_sends[turn], both_axes).reshape(devices * half, 2 * HEAD),
            ]
            for turn in range(turns)
        ]
    if fast:
        parts, forward = [], []
        for turn in range(turns):
            if turn >= 2:
                sends[turn], forward[turn - 2] = lax.optimization_barrier(
                    (sends[turn], forward[turn - 2])
                )
            arrived = exchange(sends[turn], both_axes)
            if turn == 0:
                arrived, grad_result, grad_mlp = lax.optimization_barrier(
                    (arrived, grad_result, grad_mlp)
                )
            parts.append([arrived])
            forward.append(self_forward(parts[turn], devices, half))
    else:
        forward = [self_forward(parts[turn], devices, half) for turn in range(turns)]
    so_back = [exchange(so.reshape(devices, half, 2 * HEAD), both_axes) for so, _, _ in forward]
    if fast:
        blocks = [x.reshape(groups, slots, 2, half, 2 * HEAD) for x in so_back]
        so_tile, branch_s = unpack_project(blocks, small, items, groups)
    else:
        so_tile = unpack_rows(jnp.stack(so_back)).transpose(1, 0, 2)
        branch_s = dot("nxe,xed->nd", so_tile, so_slots)
        so_tile = so_tile.reshape(items * tile, heads * HEAD)
    branch_s = branch_s.reshape(items, tile, width)
    middle_two = middle + piece(5) * branch_s

    second_hat, second_inv = norm_parts(middle_two)
    second_in = (second_hat * (1.0 + piece(7)) + piece(6)).astype(bf16)
    active, grad_hidden, branch_b, grad_second = feed_forward(
        second_in.reshape(flat), grad_mlp.reshape(flat), up_slots, down_slots
    )
    branch_b = branch_b.reshape(items, tile, width)
    grad_second = grad_second.reshape(items, tile, width)
    result = middle_two + piece(8) * branch_b
    out_tile = from_tile(result.astype(bf16))

    grad_gate_b = jnp.sum(grad_result * branch_b, axis=1)
    grad_shift_b = jnp.sum(grad_second, axis=1)
    grad_scale_b = jnp.sum(grad_second * second_hat, axis=1)
    grad_mid_two = grad_result + norm_back(second_hat, second_inv, grad_second * (1.0 + piece(7)))

    widened = with_halo(out_tile, (("seq", 0), ("tp", 2)), 1)
    taps = dot("ricd,dt->rict", widened, w_deconv)
    taps = taps.reshape(rows_here + 2, items, cols_here + 2, 4, 4, COUT)
    planes = spread_taps(
        taps, upper_keep[:, None, None, None, None], lower_keep[:, None, None, None, None]
    )
    planes = planes + jnp.tile(deconv_bias, 2 * cols_here)

    def by_device(x):
        lead = x.shape[0] // tp
        x = x.reshape(lead, tp, x.shape[1], seq, share).transpose(1, 3, 0, 2, 4)
        return x.reshape(devices, -1, share).astype(bf16)

    def total(terms, *cuts):
        summed = lax.psum_scatter(terms, ("tp", "seq"), scatter_dimension=0, tiled=True)[0]
        return jnp.split(summed.astype(f32), cuts, axis=0)

    terms_deconv = dot("ricd,rict->dt", out_tile, tap_grads).astype(bf16)
    piece_rows = width // devices
    terms_deconv = (
        terms_deconv.reshape(devices, piece_rows, -1, share)
        .transpose(0, 2, 1, 3)
        .reshape(devices, -1, share)
    )
    size_b = (hidden_here // 2, hidden_here, 2 * hidden_here)
    if fast:
        shape = (devices, size_b[2] + terms_deconv.shape[1], share)
        hidden_block = (1, items * tile, size_b[0])

        def slot_place(t, c):
            return (c * tp + t, 0, 0)

        terms_b = None
        for lhs, rhs, first in (
            (grad_hidden, second_in, 0),
            (active, grad_mlp, size_b[1]),
        ):
            terms_b = weight_terms(
                terms_b, shape, lhs, hidden_block, slot_place, rhs.reshape(flat), tp, size_b[0], first
            )
        terms_b = lax.dynamic_update_slice_in_dim(terms_b, terms_deconv, size_b[2], 1)
    else:
        terms_b = jnp.concatenate(
            [
                by_device(dot("xnf,nd->xfd", grad_hidden, second_in.reshape(flat))),
                by_device(dot("xnf,nd->xfd", active, grad_mlp.reshape(flat))),
                terms_deconv,
            ],
            axis=1,
        )

    grad_self = (piece(5) * grad_mid_two).astype(bf16)
    grad_gate_s = jnp.sum(grad_mid_two * branch_s, axis=1)
    if fast:
        dso_send = back_pack(grad_self.reshape(flat), small, items, turns, groups)
        dso_send = dso_send.reshape(turns, devices, half, 2 * HEAD)
    else:
        dso_send = pack_rows(dot("nd,xed->xne", grad_self.reshape(flat), so_slots).astype(bf16))
    dso_send = [dso_send[turn] for turn in range(turns)]
    dso_mine, backward = [], []
    for turn in range(turns):
        if turn >= 2:
            dso_send[turn], backward[turn - 2] = lax.optimization_barrier(
                (dso_send[turn], backward[turn - 2])
            )
        arrived = exchange(dso_send[turn], both_axes).reshape(devices * half, 2 * HEAD)
        if turn == 0:
            arrived, terms_b = lax.optimization_barrier((arrived, terms_b))
        dso_mine.append(arrived)
        backward.append(
            self_backward(parts[turn], dso_mine[turn], *forward[turn][1:], devices, half)
        )
    grad_up, grad_down, grad_deconv = total(terms_b, *size_b[1:])
    if fast:
        blocks = [
            exchange(x[0], both_axes).reshape(groups, slots, 2, 3 * half, 2 * HEAD)
            for x in backward
        ]
        blocks[-1], planes = lax.optimization_barrier((blocks[-1], planes))
        grad_projected, grad_third = unpack_back(blocks, small, items, groups)
    else:
        dkv = [exchange(x[0].reshape(devices, tile, 2 * HEAD), both_axes) for x in backward]
        dq = [exchange(x[1].reshape(devices, half, 2 * HEAD), both_axes) for x in backward]
        grad_projected = jnp.concatenate(
            [unpack_keys(jnp.stack(dkv)), unpack_rows(jnp.stack(dq))], axis=2
        )
        grad_third = dot(
            "xne,xed->nd", grad_projected, jnp.concatenate([kv_slots, q_slots], axis=1)
        )
    grad_third = grad_third.reshape(items, tile, width)
    grad_shift_s = jnp.sum(grad_third, axis=1)
    grad_scale_s = jnp.sum(grad_third * self_hat, axis=1)
    grad_middle = grad_mid_two + norm_back(self_hat, self_inv, grad_third * (1.0 + piece(4)))

    grad_attn = (piece(2) * grad_middle).astype(bf16)
    grad_gate_a = jnp.sum(grad_middle * branch_a, axis=1)
    if fast:
        do_send = out_back(grad_attn.reshape(flat), small, mixed.shape)
    else:
        do_send = dot("imf,tef->time", grad_attn, by_tp(out_slots)).astype(bf16)
    do_mine = exchange(do_send, "tp")
    middle_all = gather(grad_middle.astype(bf16), "tp")
    early = jnp.stack(
        [
            grad_gate_a,
            grad_shift_s,
            grad_scale_s,
            grad_gate_s,
            grad_shift_b,
            grad_scale_b,
            grad_gate_b,
        ],
        axis=0,
    ).reshape(7 * items, width)
    early = jnp.concatenate(
        [early, jnp.pad(grad_bias, (0, width - COUT))[None]], axis=0
    )
    spots = -(-early.shape[0] // (16 * tp)) * 16
    early = jnp.pad(early, ((0, spots * tp - early.shape[0]), (0, 0))).reshape(tp, spots, width)
    early = by_device(early)
    size_a = [slot_width * k for k in (6, 8, 10)]
    if fast:
        shape = (devices, size_a[2] + early.shape[1], share)
        terms_a = weight_terms(
            None,
            shape,
            grad_projected,
            (1, items * tile, 3 * slot_width),
            lambda t, c: (c * tp + t, 0, 0),
            self_in.reshape(flat),
            tp,
            3 * slot_width,
            0,
        )
        terms_a = weight_terms(
            terms_a,
            shape,
            so_tile,
            (items * tile, slot_width),
            lambda t, c: (0, c * tp + t),
            grad_self.reshape(flat),
            tp,
            slot_width,
            size_a[0],
        )
        terms_a = weight_terms(
            terms_a,
            shape,
            mixed_tile,
            (1, items, tile, slot_width),
            lambda t, c: (t, 0, 0, c),
            grad_attn.reshape(flat),
            tp,
            slot_width,
            size_a[1],
        )
        terms_a = lax.dynamic_update_slice_in_dim(terms_a, early, size_a[2], 1)
    else:
        so_terms = dot("ne,nd->ed", so_tile, grad_self.reshape(flat))
        terms_a = jnp.concatenate(
            [
                by_device(dot("xne,nd->xed", grad_projected, self_in.reshape(flat))),
                by_device(so_terms.reshape(slots, slot_width, width)),
                by_device(dot("time,imf->tef", mixed_tile, grad_attn)),
                early,
            ],
            axis=1,
        )
    do_mine, terms_a = lax.optimization_barrier((do_mine, terms_a))
    terms_a, grad_up = lax.optimization_barrier((terms_a, grad_up))
    grad_three, grad_self_out, grad_out, grad_early = total(terms_a, *size_a)
    first_part = items // 2
    cross = (queries, do_mine, mixed_wide, cross_logs, keys, values_t)
    one = cross_backward(*cross, 0, first_part)
    one, middle_all = lax.optimization_barrier((one, middle_all))
    dq_one = gather(one[0], "tp")
    do_late, _ = lax.optimization_barrier((do_mine, one[0]))
    two = cross_backward(queries, do_late, *cross[2:], first_part, items - first_part)
    one, two, dq_one = lax.optimization_barrier((one, two, dq_one))
    dq_two = gather(two[0], "tp")
    two, dq_two = lax.optimization_barrier((two, dq_two))
    dq_cross = jnp.concatenate([one[0], two[0]], axis=0)
    grad_three = grad_three.reshape(2, 3 * slot_width, share)
    grad_pair = grad_three[:, : 2 * slot_width].reshape(2, slot_heads, 2, HEAD, share)
    grad_self_key = grad_pair[:, :, 0].reshape(local, share).T
    grad_self_value = grad_pair[:, :, 1].reshape(local, share).T
    grad_self_query = grad_three[:, 2 * slot_width :].reshape(local, share).T

    def by_seq(x):
        return x.reshape((seq, x.shape[0] // seq) + x.shape[1:]).astype(bf16)

    grad_image = (
        key_value_grads(one[1], one[2], image, 0) + key_value_grads(two[1], two[2], image, first_part)
    ).T
    last = jnp.concatenate(
        [
            by_seq(dot("iqd,iqe->de", first_in, dq_cross)),
            by_seq(grad_image[:, :local]),
            by_seq(grad_image[:, local:]),
        ],
        axis=1,
    )
    grad_deconv, grad_image = lax.optimization_barrier((grad_deconv, grad_image))
    grad_deconv = grad_deconv.reshape(-1, piece_rows, share).transpose(1, 0, 2)
    grad_deconv = lax.all_gather(
        grad_deconv.reshape(piece_rows, 16 * COUT), ("tp", "seq"), axis=0, tiled=True
    )
    last, dq_one, dq_two = lax.optimization_barrier((last, dq_one, dq_two))
    last = jnp.sum(exchange(last, "seq").astype(f32), axis=0)
    if fast:
        grad_tokens, late_one = last_kernel(None, tokens, piece(1), middle_all, dq_one, small, 0)
        grad_tokens, late_two = last_kernel(
            grad_tokens, tokens, piece(1), middle_all, dq_two, small, first_part
        )
        late = jnp.concatenate([late_one, late_two], axis=0).transpose(1, 0, 2)
    else:
        dq_all = jnp.concatenate([dq_one, dq_two], axis=1)
        grad_first = dot("tiqe,ted->iqd", dq_all, by_tp(query_slots))
        grad_shift_a = jnp.sum(grad_first, axis=1)
        grad_scale_a = jnp.sum(grad_first * first_hat, axis=1)
        grad_tokens = middle_all.astype(f32).transpose(1, 0, 2, 3).reshape(
            items, tp * tile, width
        ) + norm_back(first_hat, first_inv, grad_first * (1.0 + piece(1)))
        grad_tokens = (
            grad_tokens.reshape(items, tp, rows_here, cols_here, width)
            .transpose(2, 0, 1, 3, 4)
            .reshape(rows_here, items, plane_cols, width)
        )
        late = jnp.stack([grad_shift_a, grad_scale_a], axis=0)

    late, last = lax.optimization_barrier((late, last))
    late = jnp.sum(gather(late, "seq"), axis=0)
    early = gather(grad_early, ("tp", "seq")).reshape(tp, seq, spots, share)
    early = early.transpose(0, 2, 1, 3).reshape(tp * spots, width)
    grad_bias = early[7 * items, :COUT]
    early = early[: 7 * items].reshape(7, items, width)
    depth = (last.shape[0] - share) // 2
    grad_query, grad_key, grad_value = (
        last[:share],
        last[share : share + depth],
        last[share + depth :],
    )
    grad_mods = jnp.concatenate([late, early], axis=0).transpose(1, 0, 2)
    grad_table = jnp.dot(picker.T, grad_mods.reshape(items, 9 * width), precision=highest)
    return (
        out_tile,
        planes,
        grad_tokens,
        grad_query,
        grad_key,
        grad_value,
        grad_out,
        grad_self_query,
        grad_self_key,
        grad_self_value,
        grad_self_out.reshape(local, share),
        grad_up.T,
        grad_down,
        grad_deconv,
        grad_bias,
        grad_table,
    )


def solution(mesh):
    in_specs = (
        P("seq", None, None, None),
        P(),
        P(),
        P(),
        P(None, "tp"),
        P(None, "tp"),
        P(None, "tp"),
        P("tp", None),
        P(None, "tp"),
        P(None, "tp"),
        P(None, "tp"),
        P("tp", None),
        P(None, "tp"),
        P("tp", None),
        P(),
        P(),
        P("seq", None, "tp", None),
        P("seq", None, "tp"),
    )
    out_specs = (
        P("seq", None, "tp", None),
        P("seq", None, "tp"),
        P("seq", None, None, None),
        P("seq", "tp"),
        P("seq", "tp"),
        P("seq", "tp"),
        P("tp", "seq"),
        P("seq", "tp"),
        P("seq", "tp"),
        P("seq", "tp"),
        P("tp", "seq"),
        P("seq", "tp"),
        P("tp", "seq"),
        P(),
        P(),
        P(),
    )
    return jax.shard_map(body, mesh=mesh, in_specs=in_specs, out_specs=out_specs, check_vma=False)
```

```python
import jax
import jax.numpy as jnp
from jax import lax
from jax.experimental import pallas as pl
from jax.experimental.pallas import tpu as pltpu
from jax.sharding import PartitionSpec as P

HEAD = 64
COUT = 80
PLANE = 32
IMG = 4096
LOG2E = 1.4426950408889634
bf16 = jnp.bfloat16
f32 = jnp.float32
GROUPS = 16


highest = lax.Precision.HIGHEST
epsilon = 1e-06


def with_halo(x, sides, width):
    for axis, dim in sides:
        peers, length = (lax.axis_size(axis), x.shape[dim])
        up = [(i, (i + 1) % peers) for i in range(peers - 1)]
        down = [(j, i) for i, j in up]
        last = lax.slice_in_dim(x, length - width, length, axis=dim)
        initial = lax.slice_in_dim(x, 0, width, axis=dim)
        before = lax.ppermute(last, axis, up)
        after = lax.ppermute(initial, axis, down)
        x = jnp.concatenate([before, x, after], axis=dim)
    return x


def spread_taps(padded, upper, lower):
    even_rows = padded[1:-1, :, :, 1] + upper * padded[:-2, :, :, 3]
    odd_rows = lower * padded[2:, :, :, 0] + padded[1:-1, :, :, 2]
    rows_both = jnp.stack([even_rows, odd_rows], axis=1)
    even_cols = rows_both[:, :, :, 1:-1, 1] + rows_both[:, :, :, :-2, 3]
    odd_cols = rows_both[:, :, :, 2:, 0] + rows_both[:, :, :, 1:-1, 2]
    joined = jnp.stack([even_cols, odd_cols], axis=4)
    shape = joined.shape
    return joined.reshape(shape[0] * 2, shape[2], shape[3] * 2 * shape[5])


def norm_parts(value):
    centred = value - jnp.mean(value, axis=-1, keepdims=True)
    inverse = lax.rsqrt(jnp.mean(centred * centred, axis=-1, keepdims=True) + epsilon)
    return (centred * inverse, inverse)


def norm_back(normed, inverse, incoming):
    return inverse * (
        incoming
        - jnp.mean(incoming, axis=-1, keepdims=True)
        - normed * jnp.mean(incoming * normed, axis=-1, keepdims=True)
    )


NT = (((1,), (1,)), ((), ()))
BLOCKS = 4
KV_ROWS, Q_ROWS, SO_ROWS, OUT_ROWS, QUERY_ROWS = 0, 256, 384, 512, 640


def dot_nt(a, b):
    return lax.dot_general(a, b, NT, preferred_element_type=f32)


def dot_nn(a, b):
    return jnp.dot(a, b, preferred_element_type=f32)


def flip(x):
    return x.astype(f32).T.astype(bf16)


def chunk_of(keys):
    return 512 if keys % 512 == 0 else keys


def softmax_sweep(scores, values, chunks, columns):
    top = jnp.full((1, columns), -1e30, f32)
    total = jnp.zeros((1, columns), f32)
    mixed = None
    ahead = scores(0)
    for c in range(chunks):
        now = ahead
        ahead = scores(c + 1) if c + 1 < chunks else None
        new_top = jnp.maximum(top, jnp.max(now, axis=0, keepdims=True))
        fade = jnp.exp2((top - new_top) * LOG2E)
        expon = jnp.exp2(now * LOG2E - new_top * LOG2E)
        total = total * fade + jnp.sum(expon, axis=0, keepdims=True)
        parts = values(c, expon.astype(bf16))
        width = columns // len(parts)
        if mixed is None:
            mixed = parts
        else:
            mixed = [
                m * fade[:, j * width : (j + 1) * width] + part
                for j, (m, part) in enumerate(zip(mixed, parts))
            ]
        top = new_top
    width = columns // len(mixed)
    inverse = 1.0 / total
    mixed = [m * inverse[:, j * width : (j + 1) * width] for j, m in enumerate(mixed)]
    return mixed, top + jnp.log(total)


def cross_forward(q, k, vt, tp):
    items, queries, width = q.shape
    tile = queries // tp
    keys = k.shape[1]
    heads = width // HEAD
    step = chunk_of(keys)

    def kernel(q_ref, k_ref, vt_ref, o_ref, wide_ref, log_ref):
        pair = pl.program_id(1)
        owner = lax.broadcasted_iota(jnp.int32, (queries, width), 1) // HEAD
        both = jnp.concatenate(
            [jnp.where(owner == pair * 2 + j, q_ref[0], 0.0).astype(bf16) for j in range(2)], axis=0
        )

        def scores(c):
            return dot_nt(k_ref[0, pl.ds(c * step, step), :], both)

        def values(c, p):
            out = []
            for j in range(2):
                rows = pl.ds(pl.multiple_of((pair * 2 + j) * HEAD, HEAD), HEAD)
                v = vt_ref[0, rows, pl.ds(c * step, step)]
                out.append(dot_nn(v, p[:, j * queries : (j + 1) * queries]))
            return out

        mixed, log_total = softmax_sweep(scores, values, keys // step, 2 * queries)
        rows = jnp.concatenate(mixed, axis=0).T.reshape(tp, 1, tile, 2 * HEAD)
        o_ref[...] = rows.astype(bf16)
        wide_ref[...] = rows
        for j in range(2):
            log_ref[0, j] = jnp.broadcast_to(
                log_total[:, j * queries : (j + 1) * queries], (8, queries)
            )

    return pl.pallas_call(
        kernel,
        grid=(items, heads // 2),
        in_specs=[
            pl.BlockSpec((1, queries, width), lambda i, h: (i, 0, 0)),
            pl.BlockSpec((1, keys, width), lambda i, h: (i, 0, 0)),
            pl.BlockSpec((1, width, keys), lambda i, h: (i, 0, 0)),
        ],
        out_specs=[
            pl.BlockSpec((tp, 1, tile, 2 * HEAD), lambda i, h: (0, i, 0, h)),
            pl.BlockSpec((tp, 1, tile, 2 * HEAD), lambda i, h: (0, i, 0, h)),
            pl.BlockSpec((1, 2, 8, queries), lambda i, h: (i, h, 0, 0)),
        ],
        out_shape=[
            jax.ShapeDtypeStruct((tp, items, tile, width), bf16),
            jax.ShapeDtypeStruct((tp, items, tile, width), f32),
            jax.ShapeDtypeStruct((items, heads, 8, queries), f32),
        ],
        compiler_params=pltpu.CompilerParams(vmem_limit_bytes=48 << 20),
        cost_estimate=pl.CostEstimate(
            flops=16 * items * queries * keys * width,
            bytes_accessed=4 * items * (queries + keys) * width,
            transcendentals=items * queries * keys * heads,
        ),
        name="cross_forward",
    )(q, k, vt)


def cross_backward(q, do, o, logs, k, vt, start, items):
    _, queries, width = q.shape
    tp, _, tile, _ = do.shape
    keys = k.shape[1]
    heads = width // HEAD
    step = chunk_of(keys)

    def kernel(q_ref, do_ref, o_ref, log_ref, k_ref, vt_ref, dq_ref, dk_ref, dv_ref, qt, dot):
        head = pl.program_id(1)

        @pl.when(head == 0)
        def _():
            qt[...] = flip(q_ref[0])
            dot[...] = do_ref[...].astype(f32).reshape(queries, width).T.astype(bf16)

        mine = lax.broadcasted_iota(jnp.int32, (queries, width), 1) // HEAD == head
        q_mine = jnp.where(mine, q_ref[0], 0.0).astype(bf16)
        do_wide = jnp.where(mine, do_ref[...].astype(f32).reshape(queries, width), 0.0)
        do_mine = do_wide.astype(bf16)
        o_wide = o_ref[...].reshape(queries, width)
        delta = jnp.sum(do_wide * o_wide, axis=1, keepdims=True)
        log_total = log_ref[0, 0].T[:, :1] * LOG2E
        rows = pl.ds(pl.multiple_of(head * HEAD, HEAD), HEAD)
        qt_mine = qt[rows, :]
        dot_mine = dot[rows, :]

        def scores(c):
            s = dot_nt(q_mine, k_ref[0, pl.ds(c * step, step), :])
            return s, dot_nn(do_mine, vt_ref[0, :, pl.ds(c * step, step)])

        dq = jnp.zeros((queries, width), f32)
        ahead = scores(0)
        for c in range(keys // step):
            s, dp = ahead
            ahead = scores(c + 1) if c + 1 < keys // step else None
            p = jnp.exp2(s * LOG2E - log_total)
            ds = (p * (dp - delta)).astype(bf16)
            cols = pl.ds(c * step, step)
            dv_ref[0, :, cols] = dot_nn(dot_mine, p.astype(bf16)).astype(bf16)
            dk_ref[0, :, cols] = dot_nn(qt_mine, ds).astype(bf16)
            dq = dq + dot_nn(ds, k_ref[0, cols, :])
        dq = (dq * 0.125).astype(bf16)
        rest = jnp.where(head == 0, jnp.zeros_like(dq), dq_ref[0])
        dq_ref[0] = jnp.where(mine, dq, rest)

    rows_spec = pl.BlockSpec((1, queries, width), lambda i, h: (i + start, 0, 0))
    tiles_spec = pl.BlockSpec((tp, 1, tile, width), lambda i, h: (0, i + start, 0, 0))
    grads_spec = pl.BlockSpec((1, HEAD, keys), lambda i, h: (i, h, 0))
    return pl.pallas_call(
        kernel,
        grid=(items, heads),
        in_specs=[
            rows_spec,
            tiles_spec,
            tiles_spec,
            pl.BlockSpec((1, 1, 8, queries), lambda i, h: (i + start, h, 0, 0)),
            pl.BlockSpec((1, keys, width), lambda i, h: (i + start, 0, 0)),
            pl.BlockSpec((1, width, keys), lambda i, h: (i + start, 0, 0)),
        ],
        out_specs=[
            pl.BlockSpec((1, queries, width), lambda i, h: (i, 0, 0)),
            grads_spec,
            grads_spec,
        ],
        out_shape=[
            jax.ShapeDtypeStruct((items, queries, width), bf16),
            jax.ShapeDtypeStruct((items, width, keys), bf16),
            jax.ShapeDtypeStruct((items, width, keys), bf16),
        ],
        scratch_shapes=[pltpu.VMEM((width, queries), bf16), pltpu.VMEM((width, queries), bf16)],
        compiler_params=pltpu.CompilerParams(vmem_limit_bytes=48 << 20),
        cost_estimate=pl.CostEstimate(
            flops=40 * items * queries * keys * width,
            bytes_accessed=8 * items * (queries + keys) * width,
            transcendentals=items * queries * keys * heads,
        ),
        name="cross_backward",
    )(q, do, o, logs, k, vt)


def split_wide(x):
    low = lax.broadcasted_iota(jnp.int32, x.shape, 1) < HEAD
    wide = x.astype(f32)
    first = jnp.where(low, wide, 0.0)
    second = jnp.where(low, pltpu.roll(wide, HEAD, 1), 0.0)
    return jnp.concatenate([first, second], axis=0)


def split_pair(x):
    return split_wide(x).astype(bf16)


def part_specs(parts, half):
    if len(parts) == 1:
        return [pl.BlockSpec(parts[0].shape, lambda i: (0, 0, 0))]
    rows = parts[1].shape[0] // BLOCKS
    return [
        pl.BlockSpec(parts[0].shape, lambda i: (0, 0)),
        pl.BlockSpec((rows, 2 * HEAD), lambda i: (i, 0)),
    ]


def read_keys(refs, half):
    if len(refs) == 2:
        return refs[0][...]
    devices = refs[0].shape[0]
    return refs[0][:, : 2 * half, :].reshape(devices * 2 * half, 2 * HEAD)


def read_queries(refs, half, i, share):
    if len(refs) == 2:
        return refs[1][...]
    return refs[0][pl.ds(i * share, share), 2 * half :, :].reshape(share * half, 2 * HEAD)


def self_forward(parts, devices, half):
    tile = 2 * half
    keys = devices * tile
    blocks = BLOCKS
    share = devices // blocks
    block = share * half
    step = chunk_of(keys)

    def kernel(*refs):
        ins, (o_ref, wide_ref, log_ref, kv, vt) = refs[: len(parts)], refs[len(parts) :]
        i = pl.program_id(0)

        @pl.when(i == 0)
        def _():
            kv[...] = read_keys(ins, half)
            vt[...] = flip(kv[...])

        both = split_pair(read_queries(ins, half, i, share))

        def scores(c):
            return dot_nt(kv[pl.ds(c * step, step), :], both)

        def values(c, p):
            return [dot_nn(vt[HEAD:, pl.ds(c * step, step)], p)]

        mixed, log_total = softmax_sweep(scores, values, keys // step, 2 * block)
        mixed = mixed[0]
        rows = jnp.concatenate([mixed[:, :block], mixed[:, block:]], axis=0).T
        o_ref[...] = rows.astype(bf16)
        wide_ref[...] = rows
        log_ref[0] = jnp.broadcast_to(log_total, (8, 2 * block))

    return pl.pallas_call(
        kernel,
        grid=(blocks,),
        in_specs=part_specs(parts, half),
        out_specs=[
            pl.BlockSpec((block, 2 * HEAD), lambda i: (i, 0)),
            pl.BlockSpec((block, 2 * HEAD), lambda i: (i, 0)),
            pl.BlockSpec((1, 8, 2 * block), lambda i: (i, 0, 0)),
        ],
        out_shape=[
            jax.ShapeDtypeStruct((devices * half, 2 * HEAD), bf16),
            jax.ShapeDtypeStruct((devices * half, 2 * HEAD), f32),
            jax.ShapeDtypeStruct((blocks, 8, 2 * block), f32),
        ],
        scratch_shapes=[pltpu.VMEM((keys, 2 * HEAD), bf16), pltpu.VMEM((2 * HEAD, keys), bf16)],
        compiler_params=pltpu.CompilerParams(vmem_limit_bytes=48 << 20),
        cost_estimate=pl.CostEstimate(
            flops=16 * keys * keys * HEAD,
            bytes_accessed=8 * keys * 2 * HEAD,
            transcendentals=keys * keys,
        ),
        name="self_forward",
    )(*parts)


def self_backward(parts, do, o, logs, devices, half):
    tile = 2 * half
    keys = devices * tile
    blocks = logs.shape[0]
    share = devices // blocks
    block = share * half
    step = chunk_of(keys)

    def kernel(*refs):
        n = len(parts)
        ins, (do_ref, o_ref, log_ref), outs = refs[:n], refs[n : n + 3], refs[n + 3 : 2 * n + 3]
        kv, vt, grads = refs[2 * n + 3 :]
        i = pl.program_id(0)
        mine = pl.ds(i * share, share)

        @pl.when(i == 0)
        def _():
            kv[...] = read_keys(ins, half)
            vt[...] = flip(kv[...])
            grads[...] = jnp.zeros_like(grads)

        q_both = split_pair(read_queries(ins, half, i, share))
        do_both = split_pair(do_ref[...])
        delta = jnp.sum(do_both.astype(f32) * split_wide(o_ref[...]), axis=1, keepdims=True)
        log_total = log_ref[0].T[:, :1] * LOG2E
        qt = flip(q_both)[:HEAD]
        dot = flip(do_both)[:HEAD]
        do_low = do_both[:, :HEAD]

        def scores(c):
            s = dot_nt(q_both, kv[pl.ds(c * step, step), :])
            return s, dot_nn(do_low, vt[HEAD:, pl.ds(c * step, step)])

        dq = jnp.zeros((2 * block, 2 * HEAD), f32)
        ahead = scores(0)
        for c in range(keys // step):
            s, dp = ahead
            ahead = scores(c + 1) if c + 1 < keys // step else None
            p = jnp.exp2(s * LOG2E - log_total)
            ds = (p * (dp - delta)).astype(bf16)
            cols = pl.ds(c * step, step)
            grads[:HEAD, cols] += dot_nn(qt, ds)
            grads[HEAD:, cols] += dot_nn(dot, p.astype(bf16))
            dq = dq + dot_nn(ds, kv[cols, :])
        dq = dq * 0.125
        low = lax.broadcasted_iota(jnp.int32, (block, 2 * HEAD), 1) < HEAD
        packed = jnp.where(low, dq[:block], pltpu.roll(dq[block:], HEAD, 1)).astype(bf16)
        if n == 1:
            outs[0][mine, tile:, :] = packed.reshape(share, half, 2 * HEAD)
        else:
            outs[1][...] = packed

        @pl.when(i == blocks - 1)
        def _():
            dkv = grads[...].T.astype(bf16)
            if n == 1:
                outs[0][:, :tile, :] = dkv.reshape(devices, tile, 2 * HEAD)
            else:
                outs[0][...] = dkv

    rows_spec = pl.BlockSpec((block, 2 * HEAD), lambda i: (i, 0))
    return pl.pallas_call(
        kernel,
        grid=(blocks,),
        in_specs=part_specs(parts, half)
        + [rows_spec, rows_spec, pl.BlockSpec((1, 8, 2 * block), lambda i: (i, 0, 0))],
        out_specs=part_specs(parts, half),
        out_shape=[jax.ShapeDtypeStruct(p.shape, bf16) for p in parts],
        scratch_shapes=[
            pltpu.VMEM((keys, 2 * HEAD), bf16),
            pltpu.VMEM((2 * HEAD, keys), bf16),
            pltpu.VMEM((2 * HEAD, keys), f32),
        ],
        compiler_params=pltpu.CompilerParams(vmem_limit_bytes=48 << 20),
        cost_estimate=pl.CostEstimate(
            flops=40 * keys * keys * HEAD,
            bytes_accessed=16 * keys * 2 * HEAD,
            transcendentals=keys * keys,
        ),
        name="self_backward",
    )(*parts, do, o, logs)


def swap_pairs(first, second):
    low = lax.broadcasted_iota(jnp.int32, first.shape, 1) < HEAD
    return (
        jnp.where(low, first, pltpu.roll(second, HEAD, 1)),
        jnp.where(low, pltpu.roll(first, HEAD, 1), second),
    )


def tile_places(items, turns, groups, tile):
    return [(i * tile, i % turns, i // turns) for i in range(items)]


def slot_rows(weights, first, size):
    return pl.BlockSpec((1, size, weights.shape[2]), lambda i: (i, first // size, 0))


def project_pack(x, weights, items, turns, groups):
    rows, width = x.shape
    slots = weights.shape[0]
    tile = rows // items
    half = tile // 2

    def kernel(x_ref, kv_ref, q_ref, out_ref):
        kv = dot_nt(x_ref[...], kv_ref[0]).astype(bf16)
        q = dot_nt(x_ref[...], q_ref[0]).astype(bf16).astype(f32) * 0.125
        for start, turn, group in tile_places(items, turns, groups, tile):
            upper, lower = swap_pairs(q[start : start + half], q[start + half : start + tile])
            for h, part in enumerate((upper, lower)):
                out_ref[turn, group, 0, h, :tile, :] = kv[
                    start : start + tile, h * 2 * HEAD : (h + 1) * 2 * HEAD
                ]
                out_ref[turn, group, 0, h, tile:, :] = part.astype(bf16)

    shape = (turns, groups, slots, 2, 3 * half, 2 * HEAD)
    return pl.pallas_call(
        kernel,
        grid=(slots,),
        in_specs=[
            pl.BlockSpec((rows, width), lambda i: (0, 0)),
            slot_rows(weights, KV_ROWS, 4 * HEAD),
            slot_rows(weights, Q_ROWS, 2 * HEAD),
        ],
        out_specs=pl.BlockSpec(
            (turns, groups, 1, 2, 3 * half, 2 * HEAD), lambda i: (0, 0, i, 0, 0, 0)
        ),
        out_shape=jax.ShapeDtypeStruct(shape, bf16),
        compiler_params=pltpu.CompilerParams(vmem_limit_bytes=40 << 20),
        cost_estimate=pl.CostEstimate(
            flops=2 * rows * width * slots * 6 * HEAD,
            bytes_accessed=2 * (rows + slots * 6 * HEAD) * width,
            transcendentals=0,
        ),
        name="project_pack",
    )(x, weights, weights)


def unpack_project(blocks, weights, items, groups):
    turns = len(blocks)
    slots = weights.shape[0]
    half = blocks[0].shape[3]
    tile = 2 * half
    width = weights.shape[2]

    def kernel(*refs):
        ins, w_ref, flat_ref, out_ref = refs[:turns], refs[turns], refs[turns + 1], refs[turns + 2]
        slot = pl.program_id(0)
        for start, turn, group in tile_places(items, turns, groups, tile):
            pair = [ins[turn][group, 0, h].astype(f32) for h in range(2)]
            upper, lower = swap_pairs(*pair)
            flat_ref[start : start + half, :] = upper.astype(bf16)
            flat_ref[start + half : start + tile, :] = lower.astype(bf16)
        part = dot_nn(flat_ref[...], w_ref[0])

        @pl.when(slot == 0)
        def _():
            out_ref[...] = part

        @pl.when(slot > 0)
        def _():
            out_ref[...] += part

    return pl.pallas_call(
        kernel,
        grid=(slots,),
        in_specs=[
            pl.BlockSpec((groups, 1, 2, half, 2 * HEAD), lambda i: (0, i, 0, 0, 0))
            for _ in range(turns)
        ]
        + [slot_rows(weights, SO_ROWS, 2 * HEAD)],
        out_specs=[
            pl.BlockSpec((items * tile, 2 * HEAD), lambda i: (0, i)),
            pl.BlockSpec((items * tile, width), lambda i: (0, 0)),
        ],
        out_shape=[
            jax.ShapeDtypeStruct((items * tile, slots * 2 * HEAD), bf16),
            jax.ShapeDtypeStruct((items * tile, width), f32),
        ],
        compiler_params=pltpu.CompilerParams(vmem_limit_bytes=40 << 20),
        cost_estimate=pl.CostEstimate(
            flops=2 * items * tile * width * slots * 2 * HEAD,
            bytes_accessed=4 * items * tile * width,
            transcendentals=0,
        ),
        name="unpack_project",
    )(*blocks, weights)


def back_pack(x, weights, items, turns, groups):
    rows, width = x.shape
    slots = weights.shape[0]
    tile = rows // items
    half = tile // 2

    def kernel(x_ref, w_ref, out_ref):
        grads = dot_nt(x_ref[...], w_ref[0])
        for start, turn, group in tile_places(items, turns, groups, tile):
            pair = swap_pairs(grads[start : start + half], grads[start + half : start + tile])
            for h, part in enumerate(pair):
                out_ref[turn, group, 0, h] = part.astype(bf16)

    return pl.pallas_call(
        kernel,
        grid=(slots,),
        in_specs=[
            pl.BlockSpec((rows, width), lambda i: (0, 0)),
            slot_rows(weights, SO_ROWS, 2 * HEAD),
        ],
        out_specs=pl.BlockSpec(
            (turns, groups, 1, 2, half, 2 * HEAD), lambda i: (0, 0, i, 0, 0, 0)
        ),
        out_shape=jax.ShapeDtypeStruct((turns, groups, slots, 2, half, 2 * HEAD), bf16),
        compiler_params=pltpu.CompilerParams(vmem_limit_bytes=40 << 20),
        cost_estimate=pl.CostEstimate(
            flops=2 * rows * width * slots * 2 * HEAD,
            bytes_accessed=2 * (rows + slots * 2 * HEAD) * width,
            transcendentals=0,
        ),
        name="back_pack",
    )(x, weights)


def unpack_back(blocks, weights, items, groups):
    turns = len(blocks)
    slots, _, width = weights.shape
    half = blocks[0].shape[3] // 3
    tile = 2 * half
    rows = items * tile

    def kernel(*refs):
        ins = refs[:turns]
        kv_ref, q_ref, flat_ref, out_ref = refs[turns:]
        slot = pl.program_id(0)
        for start, turn, group in tile_places(items, turns, groups, tile):
            pair = []
            for h in range(2):
                flat_ref[0, start : start + tile, h * 2 * HEAD : (h + 1) * 2 * HEAD] = ins[turn][
                    group, 0, h, :tile, :
                ]
                pair.append(ins[turn][group, 0, h, tile:, :].astype(f32))
            upper, lower = swap_pairs(*pair)
            flat_ref[0, start : start + half, 4 * HEAD :] = upper.astype(bf16)
            flat_ref[0, start + half : start + tile, 4 * HEAD :] = lower.astype(bf16)
        part = dot_nn(flat_ref[0, :, : 4 * HEAD], kv_ref[0])
        part = part + dot_nn(flat_ref[0, :, 4 * HEAD :], q_ref[0])

        @pl.when(slot == 0)
        def _():
            out_ref[...] = part

        @pl.when(slot > 0)
        def _():
            out_ref[...] += part

    return pl.pallas_call(
        kernel,
        grid=(slots,),
        in_specs=[
            pl.BlockSpec((groups, 1, 2, 3 * half, 2 * HEAD), lambda i: (0, i, 0, 0, 0))
            for _ in range(turns)
        ]
        + [slot_rows(weights, KV_ROWS, 4 * HEAD), slot_rows(weights, Q_ROWS, 2 * HEAD)],
        out_specs=[
            pl.BlockSpec((1, rows, 6 * HEAD), lambda i: (i, 0, 0)),
            pl.BlockSpec((rows, width), lambda i: (0, 0)),
        ],
        out_shape=[
            jax.ShapeDtypeStruct((slots, rows, 6 * HEAD), bf16),
            jax.ShapeDtypeStruct((rows, width), f32),
        ],
        compiler_params=pltpu.CompilerParams(vmem_limit_bytes=40 << 20),
        cost_estimate=pl.CostEstimate(
            flops=2 * rows * width * slots * 6 * HEAD,
            bytes_accessed=4 * rows * width,
            transcendentals=0,
        ),
        name="unpack_back",
    )(*blocks, weights, weights)


def out_project(mixed, weights):
    tp, items, tile, local = mixed.shape
    slots, _, width = weights.shape
    rows = items * tile

    def kernel(x_ref, w_ref, out_ref):
        slot = pl.program_id(0)
        part = dot_nn(x_ref[0].reshape(rows, local // 2), w_ref[0])

        @pl.when(slot == 0)
        def _():
            out_ref[...] = part

        @pl.when(slot > 0)
        def _():
            out_ref[...] += part

    return pl.pallas_call(
        kernel,
        grid=(slots,),
        in_specs=[
            pl.BlockSpec((1, items, tile, local // 2), lambda i: (i % tp, 0, 0, i // tp)),
            slot_rows(weights, OUT_ROWS, 2 * HEAD),
        ],
        out_specs=pl.BlockSpec((rows, width), lambda i: (0, 0)),
        out_shape=jax.ShapeDtypeStruct((rows, width), f32),
        compiler_params=pltpu.CompilerParams(vmem_limit_bytes=40 << 20),
        cost_estimate=pl.CostEstimate(
            flops=2 * rows * width * tp * local,
            bytes_accessed=4 * rows * width,
            transcendentals=0,
        ),
        name="out_project",
    )(mixed, weights)


def out_back(x, weights, shape):
    tp, items, tile, local = shape
    rows, width = x.shape

    def kernel(x_ref, w_ref, out_ref):
        part = dot_nt(x_ref[...], w_ref[0])
        out_ref[0] = part.astype(bf16).reshape(items, tile, local // 2)

    return pl.pallas_call(
        kernel,
        grid=(2 * tp,),
        in_specs=[
            pl.BlockSpec((rows, width), lambda i: (0, 0)),
            slot_rows(weights, OUT_ROWS, 2 * HEAD),
        ],
        out_specs=pl.BlockSpec((1, items, tile, local // 2), lambda i: (i % tp, 0, 0, i // tp)),
        out_shape=jax.ShapeDtypeStruct(shape, bf16),
        compiler_params=pltpu.CompilerParams(vmem_limit_bytes=40 << 20),
        cost_estimate=pl.CostEstimate(
            flops=2 * rows * width * tp * local,
            bytes_accessed=4 * rows * width,
            transcendentals=0,
        ),
        name="out_back",
    )(x, weights)


def first_kernel(tokens, shift, scale, w, tp):
    rows, items, cols, width = tokens.shape
    cols_here = cols // tp
    tile = rows * cols_here
    local = w.shape[1]

    def kernel(x_ref, shift_ref, scale_ref, w_ref, in_ref, q_ref):
        hat, _ = norm_parts(x_ref[...].astype(f32).reshape(rows, cols, width))
        value = hat * (1.0 + scale_ref[0]) + shift_ref[0]
        for t in range(tp):
            part = value[:, t * cols_here : (t + 1) * cols_here, :].reshape(tile, width)
            in_ref[0, t * tile : (t + 1) * tile, :] = part.astype(bf16)
        q = dot_nn(in_ref[0], w_ref[...]).astype(bf16).astype(f32) * 0.125
        q_ref[0] = q.astype(bf16)

    piece_spec = pl.BlockSpec((1, 1, width), lambda i: (i, 0, 0))
    return pl.pallas_call(
        kernel,
        grid=(items,),
        in_specs=[
            pl.BlockSpec((rows, 1, cols, width), lambda i: (0, i, 0, 0)),
            piece_spec,
            piece_spec,
            pl.BlockSpec(w.shape, lambda i: (0, 0)),
        ],
        out_specs=[
            pl.BlockSpec((1, tp * tile, width), lambda i: (i, 0, 0)),
            pl.BlockSpec((1, tp * tile, local), lambda i: (i, 0, 0)),
        ],
        out_shape=[
            jax.ShapeDtypeStruct((items, tp * tile, width), bf16),
            jax.ShapeDtypeStruct((items, tp * tile, local), bf16),
        ],
        compiler_params=pltpu.CompilerParams(vmem_limit_bytes=48 << 20),
        cost_estimate=pl.CostEstimate(
            flops=2 * items * tp * tile * width * local,
            bytes_accessed=4 * items * tp * tile * width,
            transcendentals=0,
        ),
        name="first_kernel",
    )(tokens, shift, scale, w)


def key_value_kernel(context, w_key, w_value_t):
    items, keys, depth = context.shape
    local = w_key.shape[1]
    step = 1024 if keys % 1024 == 0 else keys

    def kernel(x_ref, wk_ref, wv_ref, k_ref, vt_ref):
        k_ref[0] = dot_nn(x_ref[0], wk_ref[...]).astype(bf16)
        vt_ref[0] = dot_nt(wv_ref[...], x_ref[0]).astype(bf16)

    return pl.pallas_call(
        kernel,
        grid=(items, keys // step),
        in_specs=[
            pl.BlockSpec((1, step, depth), lambda i, j: (i, j, 0)),
            pl.BlockSpec(w_key.shape, lambda i, j: (0, 0)),
            pl.BlockSpec(w_value_t.shape, lambda i, j: (0, 0)),
        ],
        out_specs=[
            pl.BlockSpec((1, step, local), lambda i, j: (i, j, 0)),
            pl.BlockSpec((1, local, step), lambda i, j: (i, 0, j)),
        ],
        out_shape=[
            jax.ShapeDtypeStruct((items, keys, local), bf16),
            jax.ShapeDtypeStruct((items, local, keys), bf16),
        ],
        compiler_params=pltpu.CompilerParams(vmem_limit_bytes=40 << 20),
        cost_estimate=pl.CostEstimate(
            flops=4 * items * keys * depth * local,
            bytes_accessed=2 * items * keys * (depth + 2 * local),
            transcendentals=0,
        ),
        name="key_value_kernel",
    )(context, w_key, w_value_t)


def key_value_grads(dk_t, dv_t, context, start):
    items, local, keys = dk_t.shape
    depth = context.shape[2]
    step = 1024 if keys % 1024 == 0 else keys

    def kernel(dk_ref, dv_ref, x_ref, out_ref):
        first = (pl.program_id(0) == 0) & (pl.program_id(1) == 0)
        both = jnp.concatenate([dk_ref[0], dv_ref[0]], axis=0)
        part = dot_nn(both, x_ref[0])

        @pl.when(first)
        def _():
            out_ref[...] = part

        @pl.when(jnp.logical_not(first))
        def _():
            out_ref[...] += part

    grads_spec = pl.BlockSpec((1, local, step), lambda i, j: (i, 0, j))
    return pl.pallas_call(
        kernel,
        grid=(items, keys // step),
        in_specs=[
            grads_spec,
            grads_spec,
            pl.BlockSpec((1, step, depth), lambda i, j: (i + start, j, 0)),
        ],
        out_specs=pl.BlockSpec((2 * local, depth), lambda i, j: (0, 0)),
        out_shape=jax.ShapeDtypeStruct((2 * local, depth), f32),
        compiler_params=pltpu.CompilerParams(vmem_limit_bytes=40 << 20),
        cost_estimate=pl.CostEstimate(
            flops=4 * items * keys * depth * local,
            bytes_accessed=2 * items * keys * (depth + 2 * local),
            transcendentals=0,
        ),
        name="key_value_grads",
    )(dk_t, dv_t, context)


def feed_forward(x, g, up, down):
    rows, width = x.shape
    slots, _, hidden = up.shape
    parts = 4 if rows % 64 == 0 else 1
    size = rows // parts

    def kernel(x_ref, g_ref, up_ref, down_ref, active_ref, dh_ref, branch_ref, back_ref):
        slot = pl.program_id(0)

        @pl.when(slot == 0)
        def _():
            branch_ref[...] = jnp.zeros_like(branch_ref)
            back_ref[...] = jnp.zeros_like(back_ref)

        def products(r):
            mine = pl.ds(r * size, size)
            return dot_nn(x_ref[mine, :], up_ref[0]), dot_nt(g_ref[mine, :], down_ref[0])

        ahead = products(0)
        for r in range(parts):
            h, da = ahead
            ahead = products(r + 1) if r + 1 < parts else None
            mine = pl.ds(r * size, size)
            below = 0.5 * (1.0 + lax.erf(h * 0.7071067811865476))
            slope = below + h * (jnp.exp(h * h * -0.5) * 0.3989422804014327)
            active = (h * below).astype(bf16)
            dh = (da * slope).astype(bf16)
            active_ref[0, mine, :] = active
            dh_ref[0, mine, :] = dh
            branch_ref[mine, :] += dot_nn(active, down_ref[0])
            back_ref[mine, :] += dot_nt(dh, up_ref[0])

    rows_spec = pl.BlockSpec((rows, width), lambda i: (0, 0))
    hidden_spec = pl.BlockSpec((1, rows, hidden), lambda i: (i, 0, 0))
    return pl.pallas_call(
        kernel,
        grid=(slots,),
        in_specs=[
            rows_spec,
            rows_spec,
            pl.BlockSpec((1, width, hidden), lambda i: (i, 0, 0)),
            pl.BlockSpec((1, hidden, width), lambda i: (i, 0, 0)),
        ],
        out_specs=[hidden_spec, hidden_spec, rows_spec, rows_spec],
        out_shape=[
            jax.ShapeDtypeStruct((slots, rows, hidden), bf16),
            jax.ShapeDtypeStruct((slots, rows, hidden), bf16),
            jax.ShapeDtypeStruct((rows, width), f32),
            jax.ShapeDtypeStruct((rows, width), f32),
        ],
        compiler_params=pltpu.CompilerParams(vmem_limit_bytes=52 << 20),
        cost_estimate=pl.CostEstimate(
            flops=8 * slots * rows * width * hidden,
            bytes_accessed=4 * slots * width * hidden,
            transcendentals=2 * slots * rows * hidden,
        ),
        name="feed_forward",
    )(x, g, up, down)


def weight_terms(buffer, shape, lhs, lhs_block, lhs_place, rhs, tp, size, first):
    count, width = rhs.shape
    share = shape[-1]
    seq = width // share
    depth = lhs_block[-1]
    by_core = len(shape) == 5

    def kernel(*refs):
        a_ref, b_ref, out_ref = refs[0], refs[1], refs[-1]
        a = a_ref[...]
        if len(lhs_block) > 3:
            a = a.astype(f32)
        a = a.reshape(count, depth).astype(bf16)
        terms = lax.dot_general(a, b_ref[...], (((0,), (0,)), ((), ())), preferred_element_type=f32)
        for s in range(seq):
            block = terms[:, s * share : (s + 1) * share].astype(bf16)
            if by_core:
                out_ref[s % 2, 0, s // 2] = block
            else:
                out_ref[s] = block

    return pl.pallas_call(
        kernel,
        grid=(tp, 2),
        in_specs=[
            pl.BlockSpec(lhs_block, lhs_place),
            pl.BlockSpec(rhs.shape, lambda t, c: (0, 0)),
        ]
        + ([] if buffer is None else [pl.BlockSpec(memory_space=pl.ANY)]),
        out_specs=pl.BlockSpec((2, 1, seq // 2, size, share), lambda t, c: (0, t, 0, first // size + c, 0))
        if by_core
        else pl.BlockSpec((seq, size, share), lambda t, c: (t, first // size + c, 0)),
        out_shape=jax.ShapeDtypeStruct(shape, bf16),
        input_output_aliases={} if buffer is None else {2: 0},
        compiler_params=pltpu.CompilerParams(vmem_limit_bytes=40 << 20),
        cost_estimate=pl.CostEstimate(
            flops=4 * tp * count * depth * width,
            bytes_accessed=4 * tp * (count + width) * depth,
            transcendentals=0,
        ),
        name="weight_terms",
    )(lhs, rhs, *([] if buffer is None else [buffer]))


def last_kernel(buffer, tokens, scale, middle, dq, small, start):
    rows, _, cols, width = tokens.shape
    tp, items, queries, local = dq.shape
    slots = small.shape[0]
    cols_here = cols // tp
    tile = rows * cols_here
    slot_width = local // 2

    def kernel(x_ref, scale_ref, middle_ref, dq_ref, w_ref, *refs):
        out_ref, sums_ref = refs[-2:]
        hat, inverse = norm_parts(x_ref[...].astype(f32).reshape(rows, cols, width))
        weights = w_ref[...].reshape(tp * local, width)
        shift_sum = jnp.zeros((1, width), f32)
        scale_sum = jnp.zeros((1, width), f32)
        for t in range(tp):
            pieces = [
                dq_ref[u, 0, t * tile : (t + 1) * tile, c * slot_width : (c + 1) * slot_width]
                for c in range(2)
                for u in range(tp)
            ]
            g = dot_nn(jnp.concatenate(pieces, axis=1), weights)
            mine = slice(t * cols_here, (t + 1) * cols_here)
            hat_t = hat[:, mine, :].reshape(tile, width)
            inverse_t = inverse[:, mine, :].reshape(tile, 1)
            shift_sum = shift_sum + jnp.sum(g, axis=0, keepdims=True)
            scale_sum = scale_sum + jnp.sum(g * hat_t, axis=0, keepdims=True)
            value = middle_ref[t, 0].astype(f32) + norm_back(
                hat_t, inverse_t, g * (1.0 + scale_ref[0])
            )
            out_ref[:, 0, mine, :] = value.reshape(rows, cols_here, width)
        sums_ref[0, 0:1, :] = shift_sum
        sums_ref[0, 1:2, :] = scale_sum

    return pl.pallas_call(
        kernel,
        grid=(items,),
        in_specs=[
            pl.BlockSpec((rows, 1, cols, width), lambda i: (0, i + start, 0, 0)),
            pl.BlockSpec((1, 1, width), lambda i: (i + start, 0, 0)),
            pl.BlockSpec((tp, 1, tile, width), lambda i: (0, i + start, 0, 0)),
            pl.BlockSpec((tp, 1, queries, local), lambda i: (0, i, 0, 0)),
            pl.BlockSpec((slots, slot_width, width), lambda i: (0, QUERY_ROWS // slot_width, 0)),
        ]
        + ([] if buffer is None else [pl.BlockSpec(memory_space=pl.ANY)]),
        out_specs=[
            pl.BlockSpec((rows, 1, cols, width), lambda i: (0, i + start, 0, 0)),
            pl.BlockSpec((1, 2, width), lambda i: (i, 0, 0)),
        ],
        out_shape=[
            jax.ShapeDtypeStruct(tokens.shape, f32),
            jax.ShapeDtypeStruct((items, 2, width), f32),
        ],
        input_output_aliases={} if buffer is None else {5: 0},
        compiler_params=pltpu.CompilerParams(vmem_limit_bytes=52 << 20),
        cost_estimate=pl.CostEstimate(
            flops=2 * items * queries * width * tp * local,
            bytes_accessed=10 * items * queries * width,
            transcendentals=0,
        ),
        name="last_kernel",
    )(tokens, scale, middle, dq, small, *([] if buffer is None else [buffer]))


def exchange(x, axis):
    return lax.all_to_all(x, axis, 0, 0, tiled=True)


def gather(x, axis):
    names = axis if isinstance(axis, tuple) else (axis,)
    count = 1
    for name in names:
        count *= lax.axis_size(name)
    return exchange(jnp.broadcast_to(x[None], (count,) + x.shape), axis)


def reduce_blocks(x, axis):
    return jnp.sum(exchange(x.astype(bf16), axis).astype(f32), axis=0)


def body(
    tokens,
    context,
    group_ids,
    source_table,
    w_query,
    w_key,
    w_value,
    w_out,
    w_self_query,
    w_self_key,
    w_self_value,
    w_self_out,
    w_up,
    w_down,
    w_deconv,
    deconv_bias,
    out_cotangent,
    plane_cotangent,
):
    rows_here, items, plane_cols, width = tokens.shape
    cols_here = out_cotangent.shape[2]
    tp = lax.axis_size("tp")
    seq = lax.axis_size("seq")
    both_axes = ("seq", "tp")
    devices = tp * seq
    local = w_query.shape[1]
    hidden_here = w_up.shape[1]
    slots = 2 * tp
    slot_heads = local // HEAD // 2
    slot_width = local // 2
    heads = slots * slot_heads
    tile = rows_here * cols_here
    half = tile // 2
    groups = devices // heads
    turns = -(-items // groups)
    share = width // seq
    fast = slot_heads == 2 and half % 16 == 0 and items == groups * turns and share % 128 == 0
    me_tp = lax.axis_index("tp")
    core = lax.axis_index("seq") % 2

    picker = (group_ids[:, None] == jnp.arange(GROUPS, dtype=jnp.int32)[None, :]).astype(f32)
    mods = jnp.dot(picker, source_table, precision=highest).reshape(items, 9, 1, width)

    def piece(index):
        return mods[:, index]

    def dot(spec, a, b):
        return jnp.einsum(spec, a, b, preferred_element_type=f32)

    def to_tile(x):
        return x.transpose(1, 0, 2, 3).reshape(items, tile, width)

    def from_tile(x):
        return x.reshape(items, rows_here, cols_here, width).transpose(1, 0, 2, 3)

    teams = [
        [(2 * pair + c) * tp + t for c in range(2) for t in range(tp)] for pair in range(seq // 2)
    ]

    def whole(x):
        return lax.all_gather(x, both_axes, axis=0, tiled=False, axis_index_groups=teams)

    def my_rows(x):
        return lax.dynamic_slice_in_dim(x, core * slot_width, slot_width, 0)

    def my_columns(x):
        size = x.shape[1] // 2
        return lax.dynamic_slice_in_dim(x, core * size, size, 1)

    key_value = jnp.stack(
        [
            my_columns(w_self_key).T.reshape(slot_heads, HEAD, width),
            my_columns(w_self_value).T.reshape(slot_heads, HEAD, width),
        ],
        axis=1,
    ).reshape(2 * slot_width, width)
    small = whole(
        jnp.concatenate(
            [
                key_value,
                my_columns(w_self_query).T,
                my_rows(w_self_out),
                my_rows(w_out),
                my_columns(w_query).T,
            ],
            axis=0,
        )
    )
    cuts = [slot_width * k for k in (0, 2, 3, 4, 5, 6)]
    kv_slots, q_slots, so_slots, out_slots, query_slots = [
        small[:, a:b] for a, b in zip(cuts[:-1], cuts[1:])
    ]
    up_slots = whole(my_columns(w_up))
    down_slots = whole(
        lax.dynamic_slice_in_dim(w_down, core * (hidden_here // 2), hidden_here // 2, 0)
    )

    def by_tp(x):
        return x.reshape(2, tp, slot_width, width).transpose(1, 0, 2, 3).reshape(tp, local, width)

    incoming = plane_cotangent.reshape(2 * rows_here, items, 2 * cols_here, COUT)
    plane_row = (lax.axis_index("seq") * rows_here + jnp.arange(rows_here, dtype=jnp.int32)) % PLANE
    upper_keep = (plane_row != 0).astype(f32)
    lower_keep = (plane_row != PLANE - 1).astype(f32)
    grad_edges = with_halo(incoming, (("seq", 0), ("tp", 2)), 1)
    upper_mask = upper_keep.astype(bf16)[:, None, None, None]
    lower_mask = lower_keep.astype(bf16)[:, None, None, None]
    first_pair = grad_edges[:-2].reshape(rows_here, 2, items, 2 * cols_here + 2, COUT)
    last_pair = grad_edges[2:].reshape(rows_here, 2, items, 2 * cols_here + 2, COUT)
    row_taps = jnp.stack(
        [
            first_pair[:, 0] * upper_mask,
            first_pair[:, 1],
            last_pair[:, 0],
            last_pair[:, 1] * lower_mask,
        ],
        axis=3,
    )
    left_pair = row_taps[:, :, :-2].reshape(rows_here, items, cols_here, 2, 4, COUT)
    right_pair = row_taps[:, :, 2:].reshape(rows_here, items, cols_here, 2, 4, COUT)
    tap_grads = jnp.stack(
        [
            left_pair[:, :, :, 0],
            left_pair[:, :, :, 1],
            right_pair[:, :, :, 0],
            right_pair[:, :, :, 1],
        ],
        axis=4,
    )
    tap_grads = tap_grads.reshape(rows_here, items, cols_here, 16 * COUT)
    grad_result = to_tile(out_cotangent.astype(f32) + dot("rict,dt->ricd", tap_grads, w_deconv))
    grad_bias = jnp.sum(incoming.astype(f32), axis=(0, 1, 2))
    grad_mlp = (piece(8) * grad_result).astype(bf16)

    if fast:
        first_in, queries = first_kernel(tokens, piece(0), piece(1), w_query, tp)
    else:
        ordered = (
            tokens.reshape(rows_here, items, tp, cols_here, width)
            .transpose(1, 2, 0, 3, 4)
            .reshape(items, tp * tile, width)
        )
        first_hat, first_inv = norm_parts(ordered.astype(f32))
        first_in = (first_hat * (1.0 + piece(1)) + piece(0)).astype(bf16)
        queries = dot("iqd,de->iqe", first_in, w_query).astype(bf16) * bf16(0.125)
    image = context.transpose(1, 0, 2)
    keys, values_t = key_value_kernel(image, w_key, w_value.T)
    mixed, mixed_wide, cross_logs = cross_forward(queries, keys, values_t, tp)
    mixed_tile = exchange(mixed, "tp")
    if fast:
        branch_a = out_project(mixed_tile, small).reshape(items, tile, width)
    else:
        branch_a = dot("time,tef->imf", mixed_tile, by_tp(out_slots))
    residual = to_tile(lax.dynamic_slice_in_dim(tokens, me_tp * cols_here, cols_here, 2)).astype(f32)
    middle = residual + piece(2) * branch_a

    self_hat, self_inv = norm_parts(middle)
    self_in = (self_hat * (1.0 + piece(4)) + piece(3)).astype(bf16)
    flat = (items * tile, width)
    spare = groups * turns - items

    def spread_items(x):
        if spare:
            x = jnp.pad(x, ((0, 0), (0, spare)) + ((0, 0),) * (x.ndim - 2))
        return x.reshape((slots, groups, turns) + x.shape[2:])

    def pack_keys(x):
        x = spread_items(x.reshape(slots, items, tile, slot_heads, 2 * HEAD))
        return x.transpose(2, 1, 0, 4, 3, 5).reshape(turns, devices, tile, 2 * HEAD)

    def unpack_keys(x):
        x = x.reshape(turns, groups, slots, slot_heads, tile, 2 * HEAD).transpose(2, 1, 0, 4, 3, 5)
        x = x.reshape(slots, groups * turns, tile, 2 * slot_width)[:, :items]
        return x.reshape(slots, items * tile, 2 * slot_width)

    def pack_rows(x):
        x = spread_items(x.reshape(slots, items, 2, half, slot_heads, HEAD))
        return x.transpose(2, 1, 0, 5, 4, 3, 6).reshape(turns, devices, half, 2 * HEAD)

    def unpack_rows(x):
        x = x.reshape(turns, groups, slots, slot_heads, half, 2, HEAD).transpose(2, 1, 0, 5, 4, 3, 6)
        x = x.reshape(slots, groups * turns, tile, slot_width)[:, :items]
        return x.reshape(slots, items * tile, slot_width)

    if fast:
        sends = project_pack(self_in.reshape(flat), small, items, turns, groups)
        sends = sends.reshape(turns, devices, 3 * half, 2 * HEAD)
        sends = [sends[turn] for turn in range(turns)]
    else:
        kv_sends = pack_keys(dot("nd,xed->xne", self_in.reshape(flat), kv_slots).astype(bf16))
        q_sends = dot("nd,xed->xne", self_in.reshape(flat), q_slots).astype(bf16)
        q_sends = pack_rows(q_sends * bf16(0.125))
        parts = [
            [
                exchange(kv_sends[turn], both_axes).reshape(devices * tile, 2 * HEAD),
                exchange(q_sends[turn], both_axes).reshape(devices * half, 2 * HEAD),
            ]
            for turn in range(turns)
        ]
    if fast:
        parts, forward = [], []
        for turn in range(turns):
            if turn >= 2:
                sends[turn], forward[turn - 2] = lax.optimization_barrier(
                    (sends[turn], forward[turn - 2])
                )
            arrived = exchange(sends[turn], both_axes)
            if turn == 0:
                arrived, grad_result, grad_mlp = lax.optimization_barrier(
                    (arrived, grad_result, grad_mlp)
                )
            parts.append([arrived])
            forward.append(self_forward(parts[turn], devices, half))
    else:
        forward = [self_forward(parts[turn], devices, half) for turn in range(turns)]
    outs = [x[0] for x in forward]
    if fast:
        outs[0], parts[-1][0] = lax.optimization_barrier((outs[0], parts[-1][0]))
    so_back = [exchange(so.reshape(devices, half, 2 * HEAD), both_axes) for so in outs]
    if fast:
        blocks = [x.reshape(groups, slots, 2, half, 2 * HEAD) for x in so_back]
        so_tile, branch_s = unpack_project(blocks, small, items, groups)
    else:
        so_tile = unpack_rows(jnp.stack(so_back)).transpose(1, 0, 2)
        branch_s = dot("nxe,xed->nd", so_tile, so_slots)
        so_tile = so_tile.reshape(items * tile, heads * HEAD)
    branch_s = branch_s.reshape(items, tile, width)
    middle_two = middle + piece(5) * branch_s

    second_hat, second_inv = norm_parts(middle_two)
    second_in = (second_hat * (1.0 + piece(7)) + piece(6)).astype(bf16)
    active, grad_hidden, branch_b, grad_second = feed_forward(
        second_in.reshape(flat), grad_mlp.reshape(flat), up_slots, down_slots
    )
    branch_b = branch_b.reshape(items, tile, width)
    grad_second = grad_second.reshape(items, tile, width)
    result = middle_two + piece(8) * branch_b
    out_tile = from_tile(result.astype(bf16))

    grad_gate_b = jnp.sum(grad_result * branch_b, axis=1)
    grad_shift_b = jnp.sum(grad_second, axis=1)
    grad_scale_b = jnp.sum(grad_second * second_hat, axis=1)
    grad_mid_two = grad_result + norm_back(second_hat, second_inv, grad_second * (1.0 + piece(7)))

    widened = with_halo(out_tile, (("seq", 0), ("tp", 2)), 1)
    taps = dot("ricd,dt->rict", widened, w_deconv)
    taps = taps.reshape(rows_here + 2, items, cols_here + 2, 4, 4, COUT)
    planes = spread_taps(
        taps, upper_keep[:, None, None, None, None], lower_keep[:, None, None, None, None]
    )
    planes = planes + jnp.tile(deconv_bias, 2 * cols_here)

    def by_device(x):
        lead = x.shape[0] // tp
        x = x.reshape(lead, tp, x.shape[1], seq, share).transpose(1, 3, 0, 2, 4)
        return x.reshape(devices, -1, share).astype(bf16)

    def of_cores(x):
        return x.reshape((tp, seq // 2, 2) + x.shape[1:]).transpose(2, 0, 1, 3, 4)

    def total_near(terms, after, *cuts):
        keep = lax.dynamic_index_in_dim(terms, core, 0, False)
        give = lax.dynamic_index_in_dim(terms, 1 - core, 0, False)
        got = lax.ppermute(give, "seq", [(i, i ^ 1) for i in range(seq)])
        got, _ = lax.optimization_barrier((got, after))
        x = (keep.astype(f32) + got.astype(f32)).astype(bf16)
        x = lax.psum_scatter(x, "tp", scatter_dimension=0, tiled=True)[0]
        lines = [list(range(c, seq, 2)) for c in range(2)]
        x = lax.psum_scatter(x, "seq", scatter_dimension=0, axis_index_groups=lines, tiled=True)[0]
        return jnp.split(x.astype(f32), cuts, axis=0)

    def total(terms, *cuts):
        summed = lax.psum_scatter(terms, ("tp", "seq"), scatter_dimension=0, tiled=True)[0]
        return jnp.split(summed.astype(f32), cuts, axis=0)

    terms_deconv = dot("ricd,rict->dt", out_tile, tap_grads).astype(bf16)
    piece_rows = width // devices
    terms_deconv = (
        terms_deconv.reshape(devices, piece_rows, -1, share)
        .transpose(0, 2, 1, 3)
        .reshape(devices, -1, share)
    )
    size_b = (hidden_here // 2, hidden_here, 2 * hidden_here)
    if fast:
        shape = (2, tp, seq // 2, size_b[2] + terms_deconv.shape[1], share)
        hidden_block = (1, items * tile, size_b[0])

        def slot_place(t, c):
            return (c * tp + t, 0, 0)

        terms_b = None
        for lhs, rhs, first in (
            (grad_hidden, second_in, 0),
            (active, grad_mlp, size_b[1]),
        ):
            terms_b = weight_terms(
                terms_b, shape, lhs, hidden_block, slot_place, rhs.reshape(flat), tp, size_b[0], first
            )
        terms_b = lax.dynamic_update_slice_in_dim(terms_b, of_cores(terms_deconv), size_b[2], 3)
    else:
        terms_b = jnp.concatenate(
            [
                by_device(dot("xnf,nd->xfd", grad_hidden, second_in.reshape(flat))),
                by_device(dot("xnf,nd->xfd", active, grad_mlp.reshape(flat))),
                terms_deconv,
            ],
            axis=1,
        )
        terms_b = of_cores(terms_b)

    grad_self = (piece(5) * grad_mid_two).astype(bf16)
    grad_gate_s = jnp.sum(grad_mid_two * branch_s, axis=1)
    if fast:
        dso_send = back_pack(grad_self.reshape(flat), small, items, turns, groups)
        dso_send = dso_send.reshape(turns, devices, half, 2 * HEAD)
    else:
        dso_send = pack_rows(dot("nd,xed->xne", grad_self.reshape(flat), so_slots).astype(bf16))
    dso_send = [dso_send[turn] for turn in range(turns)]
    dso_mine, backward = [], []
    for turn in range(turns):
        if turn >= 2:
            dso_send[turn], backward[turn - 2] = lax.optimization_barrier(
                (dso_send[turn], backward[turn - 2])
            )
        arrived = exchange(dso_send[turn], both_axes).reshape(devices * half, 2 * HEAD)
        if turn == 0:
            arrived, terms_b = lax.optimization_barrier((arrived, terms_b))
        dso_mine.append(arrived)
        backward.append(
            self_backward(parts[turn], dso_mine[turn], *forward[turn][1:], devices, half)
        )
    grad_up, grad_down, grad_deconv = total_near(
        terms_b, (backward[0][0], dso_mine[min(1, turns - 1)]), *size_b[1:]
    )
    if fast:
        blocks = [
            exchange(x[0], both_axes).reshape(groups, slots, 2, 3 * half, 2 * HEAD)
            for x in backward
        ]
        blocks[-1], planes = lax.optimization_barrier((blocks[-1], planes))
        grad_projected, grad_third = unpack_back(blocks, small, items, groups)
    else:
        dkv = [exchange(x[0].reshape(devices, tile, 2 * HEAD), both_axes) for x in backward]
        dq = [exchange(x[1].reshape(devices, half, 2 * HEAD), both_axes) for x in backward]
        grad_projected = jnp.concatenate(
            [unpack_keys(jnp.stack(dkv)), unpack_rows(jnp.stack(dq))], axis=2
        )
        grad_third = dot(
            "xne,xed->nd", grad_projected, jnp.concatenate([kv_slots, q_slots], axis=1)
        )
    grad_third = grad_third.reshape(items, tile, width)
    grad_shift_s = jnp.sum(grad_third, axis=1)
    grad_scale_s = jnp.sum(grad_third * self_hat, axis=1)
    grad_middle = grad_mid_two + norm_back(self_hat, self_inv, grad_third * (1.0 + piece(4)))

    grad_attn = (piece(2) * grad_middle).astype(bf16)
    grad_gate_a = jnp.sum(grad_middle * branch_a, axis=1)
    if fast:
        do_send = out_back(grad_attn.reshape(flat), small, mixed.shape)
    else:
        do_send = dot("imf,tef->time", grad_attn, by_tp(out_slots)).astype(bf16)
    do_mine = exchange(do_send, "tp")
    middle_all = gather(grad_middle.astype(bf16), "tp")
    early = jnp.stack(
        [
            grad_gate_a,
            grad_shift_s,
            grad_scale_s,
            grad_gate_s,
            grad_shift_b,
            grad_scale_b,
            grad_gate_b,
        ],
        axis=0,
    ).reshape(7 * items, width)
    early = jnp.concatenate(
        [early, jnp.pad(grad_bias, (0, width - COUT))[None]], axis=0
    )
    spots = -(-early.shape[0] // (16 * tp)) * 16
    early = jnp.pad(early, ((0, spots * tp - early.shape[0]), (0, 0))).reshape(tp, spots, width)
    early = by_device(early)
    size_a = [slot_width * k for k in (6, 8, 10)]
    if fast:
        shape = (devices, size_a[2] + early.shape[1], share)
        terms_a = weight_terms(
            None,
            shape,
            grad_projected,
            (1, items * tile, 3 * slot_width),
            lambda t, c: (c * tp + t, 0, 0),
            self_in.reshape(flat),
            tp,
            3 * slot_width,
            0,
        )
        terms_a = weight_terms(
            terms_a,
            shape,
            so_tile,
            (items * tile, slot_width),
            lambda t, c: (0, c * tp + t),
            grad_self.reshape(flat),
            tp,
            slot_width,
            size_a[0],
        )
        terms_a = weight_terms(
            terms_a,
            shape,
            mixed_tile,
            (1, items, tile, slot_width),
            lambda t, c: (t, 0, 0, c),
            grad_attn.reshape(flat),
            tp,
            slot_width,
            size_a[1],
        )
        terms_a = lax.dynamic_update_slice_in_dim(terms_a, early, size_a[2], 1)
    else:
        so_terms = dot("ne,nd->ed", so_tile, grad_self.reshape(flat))
        terms_a = jnp.concatenate(
            [
                by_device(dot("xne,nd->xed", grad_projected, self_in.reshape(flat))),
                by_device(so_terms.reshape(slots, slot_width, width)),
                by_device(dot("time,imf->tef", mixed_tile, grad_attn)),
                early,
            ],
            axis=1,
        )
    do_mine, terms_a = lax.optimization_barrier((do_mine, terms_a))
    terms_a, grad_up = lax.optimization_barrier((terms_a, grad_up))
    grad_three, grad_self_out, grad_out, grad_early = total(terms_a, *size_a)
    first_part = items // 2
    cross = (queries, do_mine, mixed_wide, cross_logs, keys, values_t)
    one = cross_backward(*cross, 0, first_part)
    one, middle_all = lax.optimization_barrier((one, middle_all))
    dq_one = gather(one[0], "tp")
    do_late, _ = lax.optimization_barrier((do_mine, one[0]))
    two = cross_backward(queries, do_late, *cross[2:], first_part, items - first_part)
    one, two, dq_one = lax.optimization_barrier((one, two, dq_one))
    dq_two = gather(two[0], "tp")
    two, dq_two = lax.optimization_barrier((two, dq_two))
    dq_cross = jnp.concatenate([one[0], two[0]], axis=0)
    grad_three = grad_three.reshape(2, 3 * slot_width, share)
    grad_pair = grad_three[:, : 2 * slot_width].reshape(2, slot_heads, 2, HEAD, share)
    grad_self_key = grad_pair[:, :, 0].reshape(local, share).T
    grad_self_value = grad_pair[:, :, 1].reshape(local, share).T
    grad_self_query = grad_three[:, 2 * slot_width :].reshape(local, share).T

    def by_seq(x):
        return x.reshape((seq, x.shape[0] // seq) + x.shape[1:]).astype(bf16)

    grad_image = (
        key_value_grads(one[1], one[2], image, 0) + key_value_grads(two[1], two[2], image, first_part)
    ).T
    last = jnp.concatenate(
        [
            by_seq(dot("iqd,iqe->de", first_in, dq_cross)),
            by_seq(grad_image[:, :local]),
            by_seq(grad_image[:, local:]),
        ],
        axis=1,
    )
    grad_deconv, grad_image = lax.optimization_barrier((grad_deconv, grad_image))
    grad_deconv = grad_deconv.reshape(-1, piece_rows, share).transpose(1, 0, 2)
    grad_deconv = lax.all_gather(
        grad_deconv.reshape(piece_rows, 16 * COUT), ("tp", "seq"), axis=0, tiled=True
    )
    early = gather(grad_early, ("tp", "seq")).reshape(tp, seq, spots, share)
    early = early.transpose(0, 2, 1, 3).reshape(tp * spots, width)
    last, dq_one, dq_two, early = lax.optimization_barrier((last, dq_one, dq_two, early))
    last = jnp.sum(exchange(last, "seq").astype(f32), axis=0)
    if fast:
        grad_tokens, late_one = last_kernel(None, tokens, piece(1), middle_all, dq_one, small, 0)
        grad_tokens, late_two = last_kernel(
            grad_tokens, tokens, piece(1), middle_all, dq_two, small, first_part
        )
        late = jnp.concatenate([late_one, late_two], axis=0).transpose(1, 0, 2)
    else:
        dq_all = jnp.concatenate([dq_one, dq_two], axis=1)
        grad_first = dot("tiqe,ted->iqd", dq_all, by_tp(query_slots))
        grad_shift_a = jnp.sum(grad_first, axis=1)
        grad_scale_a = jnp.sum(grad_first * first_hat, axis=1)
        grad_tokens = middle_all.astype(f32).transpose(1, 0, 2, 3).reshape(
            items, tp * tile, width
        ) + norm_back(first_hat, first_inv, grad_first * (1.0 + piece(1)))
        grad_tokens = (
            grad_tokens.reshape(items, tp, rows_here, cols_here, width)
            .transpose(2, 0, 1, 3, 4)
            .reshape(rows_here, items, plane_cols, width)
        )
        late = jnp.stack([grad_shift_a, grad_scale_a], axis=0)

    late, last = lax.optimization_barrier((late, last))
    late = jnp.sum(gather(late, "seq"), axis=0)
    grad_bias = early[7 * items, :COUT]
    early = early[: 7 * items].reshape(7, items, width)
    depth = (last.shape[0] - share) // 2
    grad_query, grad_key, grad_value = (
        last[:share],
        last[share : share + depth],
        last[share + depth :],
    )
    late, grad_deconv = lax.optimization_barrier((late, grad_deconv))
    grad_mods = jnp.concatenate([late, early], axis=0).transpose(1, 0, 2)
    grad_table = jnp.dot(picker.T, grad_mods.reshape(items, 9 * width), precision=highest)
    return (
        out_tile,
        planes,
        grad_tokens,
        grad_query,
        grad_key,
        grad_value,
        grad_out,
        grad_self_query,
        grad_self_key,
        grad_self_value,
        grad_self_out.reshape(local, share),
        grad_up.T,
        grad_down,
        grad_deconv,
        grad_bias,
        grad_table,
    )


def solution(mesh):
    in_specs = (
        P("seq", None, None, None),
        P(),
        P(),
        P(),
        P(None, "tp"),
        P(None, "tp"),
        P(None, "tp"),
        P("tp", None),
        P(None, "tp"),
        P(None, "tp"),
        P(None, "tp"),
        P("tp", None),
        P(None, "tp"),
        P("tp", None),
        P(),
        P(),
        P("seq", None, "tp", None),
        P("seq", None, "tp"),
    )
    out_specs = (
        P("seq", None, "tp", None),
        P("seq", None, "tp"),
        P("seq", None, None, None),
        P("seq", "tp"),
        P("seq", "tp"),
        P("seq", "tp"),
        P("tp", "seq"),
        P("seq", "tp"),
        P("seq", "tp"),
        P("seq", "tp"),
        P("tp", "seq"),
        P("seq", "tp"),
        P("tp", "seq"),
        P(),
        P(),
        P(),
    )
    return jax.shard_map(body, mesh=mesh, in_specs=in_specs, out_specs=out_specs, check_vma=False)
```

```python
import jax
import jax.numpy as jnp
from jax import lax
from jax.experimental import pallas as pl
from jax.experimental.pallas import tpu as pltpu
from jax.sharding import PartitionSpec as P

HEAD = 64
COUT = 80
PLANE = 32
IMG = 4096
LOG2E = 1.4426950408889634
bf16 = jnp.bfloat16
f32 = jnp.float32
GROUPS = 16


highest = lax.Precision.HIGHEST
epsilon = 1e-06


def with_halo(x, sides, width):
    for axis, dim in sides:
        peers, length = (lax.axis_size(axis), x.shape[dim])
        up = [(i, (i + 1) % peers) for i in range(peers - 1)]
        down = [(j, i) for i, j in up]
        last = lax.slice_in_dim(x, length - width, length, axis=dim)
        initial = lax.slice_in_dim(x, 0, width, axis=dim)
        before = lax.ppermute(last, axis, up)
        after = lax.ppermute(initial, axis, down)
        x = jnp.concatenate([before, x, after], axis=dim)
    return x


def spread_taps(padded, upper, lower):
    even_rows = padded[1:-1, :, :, 1] + upper * padded[:-2, :, :, 3]
    odd_rows = lower * padded[2:, :, :, 0] + padded[1:-1, :, :, 2]
    rows_both = jnp.stack([even_rows, odd_rows], axis=1)
    even_cols = rows_both[:, :, :, 1:-1, 1] + rows_both[:, :, :, :-2, 3]
    odd_cols = rows_both[:, :, :, 2:, 0] + rows_both[:, :, :, 1:-1, 2]
    joined = jnp.stack([even_cols, odd_cols], axis=4)
    shape = joined.shape
    return joined.reshape(shape[0] * 2, shape[2], shape[3] * 2 * shape[5])


def norm_parts(value):
    centred = value - jnp.mean(value, axis=-1, keepdims=True)
    inverse = lax.rsqrt(jnp.mean(centred * centred, axis=-1, keepdims=True) + epsilon)
    return (centred * inverse, inverse)


def norm_back(normed, inverse, incoming):
    return inverse * (
        incoming
        - jnp.mean(incoming, axis=-1, keepdims=True)
        - normed * jnp.mean(incoming * normed, axis=-1, keepdims=True)
    )


NT = (((1,), (1,)), ((), ()))
BLOCKS = 4
KV_ROWS, Q_ROWS, SO_ROWS, OUT_ROWS, QUERY_ROWS = 0, 256, 384, 512, 640


def dot_nt(a, b):
    return lax.dot_general(a, b, NT, preferred_element_type=f32)


def dot_nn(a, b):
    return jnp.dot(a, b, preferred_element_type=f32)


def flip(x):
    return x.astype(f32).T.astype(bf16)


def chunk_of(keys):
    return 512 if keys % 512 == 0 else keys


SAFE = 40.0


def softmax_sweep(scores, values, chunks, columns, write):
    def spread(mixed, total, top):
        width = columns // len(mixed)
        inverse = 1.0 / total
        mixed = [m * inverse[:, j * width : (j + 1) * width] for j, m in enumerate(mixed)]
        write(mixed, top + jnp.log(total))

    ahead = scores(0)
    top = jnp.max(ahead, axis=0, keepdims=True)
    base = top * LOG2E
    peak = top
    total = jnp.zeros((1, columns), f32)
    mixed = None
    for c in range(chunks):
        now = ahead
        ahead = scores(c + 1) if c + 1 < chunks else None
        expon = jnp.exp2(now * LOG2E - base)
        if c > 0:
            peak = jnp.maximum(peak, jnp.max(now, axis=0, keepdims=True))
        total = total + jnp.sum(expon, axis=0, keepdims=True)
        parts = values(c, expon.astype(bf16))
        mixed = parts if mixed is None else [m + part for m, part in zip(mixed, parts)]
    spread(mixed, total, top)

    @pl.when(jnp.max(peak - top) > SAFE)
    def _():
        def body(c, carry):
            top, total, mixed = carry
            now = scores(c)
            new_top = jnp.maximum(top, jnp.max(now, axis=0, keepdims=True))
            fade = jnp.exp2((top - new_top) * LOG2E)
            expon = jnp.exp2((now - new_top) * LOG2E)
            total = total * fade + jnp.sum(expon, axis=0, keepdims=True)
            parts = values(c, expon.astype(bf16))
            width = columns // len(parts)
            mixed = [
                m * fade[:, j * width : (j + 1) * width] + part
                for j, (m, part) in enumerate(zip(mixed, parts))
            ]
            return new_top, total, mixed

        start = (
            jnp.full((1, columns), -3e38, f32),
            jnp.zeros((1, columns), f32),
            [jnp.zeros(m.shape, f32) for m in mixed],
        )
        top, total, again = lax.fori_loop(0, chunks, body, start)
        spread(again, total, top)


def at_chunk(c, step):
    return pl.ds(c * step if isinstance(c, int) else pl.multiple_of(c * step, step), step)


def cross_forward(q, k, vt, tp):
    items, queries, width = q.shape
    tile = queries // tp
    keys = k.shape[1]
    heads = width // HEAD
    step = chunk_of(keys)

    def kernel(q_ref, k_ref, vt_ref, o_ref, wide_ref, log_ref):
        pair = pl.program_id(1)
        owner = lax.broadcasted_iota(jnp.int32, (queries, width), 1) // HEAD
        both = jnp.concatenate(
            [jnp.where(owner == pair * 2 + j, q_ref[0], 0.0).astype(bf16) for j in range(2)], axis=0
        )

        def scores(c):
            return dot_nt(k_ref[0, at_chunk(c, step), :], both)

        def values(c, p):
            out = []
            for j in range(2):
                rows = pl.ds(pl.multiple_of((pair * 2 + j) * HEAD, HEAD), HEAD)
                v = vt_ref[0, rows, at_chunk(c, step)]
                out.append(dot_nn(v, p[:, j * queries : (j + 1) * queries]))
            return out

        def write(mixed, log_total):
            rows = jnp.concatenate(mixed, axis=0).T.reshape(tp, 1, tile, 2 * HEAD)
            o_ref[...] = rows.astype(bf16)
            wide_ref[...] = rows
            for j in range(2):
                log_ref[0, j] = jnp.broadcast_to(
                    log_total[:, j * queries : (j + 1) * queries], (8, queries)
                )

        softmax_sweep(scores, values, keys // step, 2 * queries, write)

    return pl.pallas_call(
        kernel,
        grid=(items, heads // 2),
        in_specs=[
            pl.BlockSpec((1, queries, width), lambda i, h: (i, 0, 0)),
            pl.BlockSpec((1, keys, width), lambda i, h: (i, 0, 0)),
            pl.BlockSpec((1, width, keys), lambda i, h: (i, 0, 0)),
        ],
        out_specs=[
            pl.BlockSpec((tp, 1, tile, 2 * HEAD), lambda i, h: (0, i, 0, h)),
            pl.BlockSpec((tp, 1, tile, 2 * HEAD), lambda i, h: (0, i, 0, h)),
            pl.BlockSpec((1, 2, 8, queries), lambda i, h: (i, h, 0, 0)),
        ],
        out_shape=[
            jax.ShapeDtypeStruct((tp, items, tile, width), bf16),
            jax.ShapeDtypeStruct((tp, items, tile, width), f32),
            jax.ShapeDtypeStruct((items, heads, 8, queries), f32),
        ],
        compiler_params=pltpu.CompilerParams(vmem_limit_bytes=48 << 20),
        cost_estimate=pl.CostEstimate(
            flops=16 * items * queries * keys * width,
            bytes_accessed=4 * items * (queries + keys) * width,
            transcendentals=items * queries * keys * heads,
        ),
        name="cross_forward",
    )(q, k, vt)


def cross_backward(q, do, o, logs, k, vt, start, items):
    _, queries, width = q.shape
    tp, _, tile, _ = do.shape
    keys = k.shape[1]
    heads = width // HEAD
    step = chunk_of(keys)

    def kernel(q_ref, do_ref, o_ref, log_ref, k_ref, vt_ref, dq_ref, dk_ref, dv_ref, qt, dot):
        head = pl.program_id(1)

        @pl.when(head == 0)
        def _():
            qt[...] = flip(q_ref[0])
            dot[...] = do_ref[...].astype(f32).reshape(queries, width).T.astype(bf16)

        mine = lax.broadcasted_iota(jnp.int32, (queries, width), 1) // HEAD == head
        q_mine = jnp.where(mine, q_ref[0], 0.0).astype(bf16)
        do_wide = jnp.where(mine, do_ref[...].astype(f32).reshape(queries, width), 0.0)
        do_mine = do_wide.astype(bf16)
        o_wide = o_ref[...].reshape(queries, width)
        delta = jnp.sum(do_wide * o_wide, axis=1, keepdims=True)
        log_total = log_ref[0, 0].T[:, :1] * LOG2E
        rows = pl.ds(pl.multiple_of(head * HEAD, HEAD), HEAD)
        qt_mine = qt[rows, :]
        dot_mine = dot[rows, :]

        def scores(c):
            s = dot_nt(q_mine, k_ref[0, pl.ds(c * step, step), :])
            return s, dot_nn(do_mine, vt_ref[0, :, pl.ds(c * step, step)])

        dq = jnp.zeros((queries, width), f32)
        ahead = scores(0)
        for c in range(keys // step):
            s, dp = ahead
            ahead = scores(c + 1) if c + 1 < keys // step else None
            p = jnp.exp2(s * LOG2E - log_total)
            ds = (p * (dp - delta)).astype(bf16)
            cols = pl.ds(c * step, step)
            dv_ref[0, :, cols] = dot_nn(dot_mine, p.astype(bf16)).astype(bf16)
            dk_ref[0, :, cols] = dot_nn(qt_mine, ds).astype(bf16)
            dq = dq + dot_nn(ds, k_ref[0, cols, :])
        dq = (dq * 0.125).astype(bf16)
        rest = jnp.where(head == 0, jnp.zeros_like(dq), dq_ref[0])
        dq_ref[0] = jnp.where(mine, dq, rest)

    rows_spec = pl.BlockSpec((1, queries, width), lambda i, h: (i + start, 0, 0))
    tiles_spec = pl.BlockSpec((tp, 1, tile, width), lambda i, h: (0, i + start, 0, 0))
    grads_spec = pl.BlockSpec((1, HEAD, keys), lambda i, h: (i, h, 0))
    return pl.pallas_call(
        kernel,
        grid=(items, heads),
        in_specs=[
            rows_spec,
            tiles_spec,
            tiles_spec,
            pl.BlockSpec((1, 1, 8, queries), lambda i, h: (i + start, h, 0, 0)),
            pl.BlockSpec((1, keys, width), lambda i, h: (i + start, 0, 0)),
            pl.BlockSpec((1, width, keys), lambda i, h: (i + start, 0, 0)),
        ],
        out_specs=[
            pl.BlockSpec((1, queries, width), lambda i, h: (i, 0, 0)),
            grads_spec,
            grads_spec,
        ],
        out_shape=[
            jax.ShapeDtypeStruct((items, queries, width), bf16),
            jax.ShapeDtypeStruct((items, width, keys), bf16),
            jax.ShapeDtypeStruct((items, width, keys), bf16),
        ],
        scratch_shapes=[pltpu.VMEM((width, queries), bf16), pltpu.VMEM((width, queries), bf16)],
        compiler_params=pltpu.CompilerParams(vmem_limit_bytes=48 << 20),
        cost_estimate=pl.CostEstimate(
            flops=40 * items * queries * keys * width,
            bytes_accessed=8 * items * (queries + keys) * width,
            transcendentals=items * queries * keys * heads,
        ),
        name="cross_backward",
    )(q, do, o, logs, k, vt)


def split_wide(x):
    low = lax.broadcasted_iota(jnp.int32, x.shape, 1) < HEAD
    wide = x.astype(f32)
    first = jnp.where(low, wide, 0.0)
    second = jnp.where(low, pltpu.roll(wide, HEAD, 1), 0.0)
    return jnp.concatenate([first, second], axis=0)


def split_pair(x):
    return split_wide(x).astype(bf16)


def part_specs(parts, half):
    if len(parts) == 1:
        return [pl.BlockSpec(parts[0].shape, lambda i: (0, 0, 0))]
    rows = parts[1].shape[0] // BLOCKS
    return [
        pl.BlockSpec(parts[0].shape, lambda i: (0, 0)),
        pl.BlockSpec((rows, 2 * HEAD), lambda i: (i, 0)),
    ]


def read_keys(refs, half):
    if len(refs) == 2:
        return refs[0][...]
    devices = refs[0].shape[0]
    return refs[0][:, : 2 * half, :].reshape(devices * 2 * half, 2 * HEAD)


def read_queries(refs, half, i, share):
    if len(refs) == 2:
        return refs[1][...]
    return refs[0][pl.ds(i * share, share), 2 * half :, :].reshape(share * half, 2 * HEAD)


def self_forward(parts, devices, half):
    tile = 2 * half
    keys = devices * tile
    blocks = BLOCKS
    share = devices // blocks
    block = share * half
    step = chunk_of(keys)

    def kernel(*refs):
        ins, (o_ref, wide_ref, log_ref, kv, vt) = refs[: len(parts)], refs[len(parts) :]
        i = pl.program_id(0)

        @pl.when(i == 0)
        def _():
            kv[...] = read_keys(ins, half)
            vt[...] = flip(kv[...])

        both = split_pair(read_queries(ins, half, i, share))

        def scores(c):
            return dot_nt(kv[at_chunk(c, step), :], both)

        def values(c, p):
            return [dot_nn(vt[HEAD:, at_chunk(c, step)], p)]

        def write(mixed, log_total):
            mixed = mixed[0]
            rows = jnp.concatenate([mixed[:, :block], mixed[:, block:]], axis=0).T
            o_ref[...] = rows.astype(bf16)
            wide_ref[...] = rows
            log_ref[0] = jnp.broadcast_to(log_total, (8, 2 * block))

        softmax_sweep(scores, values, keys // step, 2 * block, write)

    return pl.pallas_call(
        kernel,
        grid=(blocks,),
        in_specs=part_specs(parts, half),
        out_specs=[
            pl.BlockSpec((block, 2 * HEAD), lambda i: (i, 0)),
            pl.BlockSpec((block, 2 * HEAD), lambda i: (i, 0)),
            pl.BlockSpec((1, 8, 2 * block), lambda i: (i, 0, 0)),
        ],
        out_shape=[
            jax.ShapeDtypeStruct((devices * half, 2 * HEAD), bf16),
            jax.ShapeDtypeStruct((devices * half, 2 * HEAD), f32),
            jax.ShapeDtypeStruct((blocks, 8, 2 * block), f32),
        ],
        scratch_shapes=[pltpu.VMEM((keys, 2 * HEAD), bf16), pltpu.VMEM((2 * HEAD, keys), bf16)],
        compiler_params=pltpu.CompilerParams(vmem_limit_bytes=48 << 20),
        cost_estimate=pl.CostEstimate(
            flops=16 * keys * keys * HEAD,
            bytes_accessed=8 * keys * 2 * HEAD,
            transcendentals=keys * keys,
        ),
        name="self_forward",
    )(*parts)


def self_backward(parts, do, o, logs, devices, half):
    tile = 2 * half
    keys = devices * tile
    blocks = logs.shape[0]
    share = devices // blocks
    block = share * half
    step = chunk_of(keys)

    def kernel(*refs):
        n = len(parts)
        ins, (do_ref, o_ref, log_ref), outs = refs[:n], refs[n : n + 3], refs[n + 3 : 2 * n + 3]
        kv, vt, grads = refs[2 * n + 3 :]
        i = pl.program_id(0)
        mine = pl.ds(i * share, share)

        @pl.when(i == 0)
        def _():
            kv[...] = read_keys(ins, half)
            vt[...] = flip(kv[...])
            grads[...] = jnp.zeros_like(grads)

        q_both = split_pair(read_queries(ins, half, i, share))
        do_both = split_pair(do_ref[...])
        delta = jnp.sum(do_both.astype(f32) * split_wide(o_ref[...]), axis=1, keepdims=True)
        log_total = log_ref[0].T[:, :1] * LOG2E
        qt = flip(q_both)[:HEAD]
        dot = flip(do_both)[:HEAD]
        do_low = do_both[:, :HEAD]

        def scores(c):
            s = dot_nt(q_both, kv[pl.ds(c * step, step), :])
            return s, dot_nn(do_low, vt[HEAD:, pl.ds(c * step, step)])

        dq = jnp.zeros((2 * block, 2 * HEAD), f32)
        ahead = scores(0)
        for c in range(keys // step):
            s, dp = ahead
            ahead = scores(c + 1) if c + 1 < keys // step else None
            p = jnp.exp2(s * LOG2E - log_total)
            ds = (p * (dp - delta)).astype(bf16)
            cols = pl.ds(c * step, step)
            grads[:HEAD, cols] += dot_nn(qt, ds)
            grads[HEAD:, cols] += dot_nn(dot, p.astype(bf16))
            dq = dq + dot_nn(ds, kv[cols, :])
        dq = dq * 0.125
        low = lax.broadcasted_iota(jnp.int32, (block, 2 * HEAD), 1) < HEAD
        packed = jnp.where(low, dq[:block], pltpu.roll(dq[block:], HEAD, 1)).astype(bf16)
        if n == 1:
            outs[0][mine, tile:, :] = packed.reshape(share, half, 2 * HEAD)
        else:
            outs[1][...] = packed

        @pl.when(i == blocks - 1)
        def _():
            dkv = grads[...].T.astype(bf16)
            if n == 1:
                outs[0][:, :tile, :] = dkv.reshape(devices, tile, 2 * HEAD)
            else:
                outs[0][...] = dkv

    rows_spec = pl.BlockSpec((block, 2 * HEAD), lambda i: (i, 0))
    return pl.pallas_call(
        kernel,
        grid=(blocks,),
        in_specs=part_specs(parts, half)
        + [rows_spec, rows_spec, pl.BlockSpec((1, 8, 2 * block), lambda i: (i, 0, 0))],
        out_specs=part_specs(parts, half),
        out_shape=[jax.ShapeDtypeStruct(p.shape, bf16) for p in parts],
        scratch_shapes=[
            pltpu.VMEM((keys, 2 * HEAD), bf16),
            pltpu.VMEM((2 * HEAD, keys), bf16),
            pltpu.VMEM((2 * HEAD, keys), f32),
        ],
        compiler_params=pltpu.CompilerParams(vmem_limit_bytes=48 << 20),
        cost_estimate=pl.CostEstimate(
            flops=40 * keys * keys * HEAD,
            bytes_accessed=16 * keys * 2 * HEAD,
            transcendentals=keys * keys,
        ),
        name="self_backward",
    )(*parts, do, o, logs)


def swap_pairs(first, second):
    low = lax.broadcasted_iota(jnp.int32, first.shape, 1) < HEAD
    return (
        jnp.where(low, first, pltpu.roll(second, HEAD, 1)),
        jnp.where(low, pltpu.roll(first, HEAD, 1), second),
    )


def tile_places(items, turns, groups, tile):
    return [(i * tile, i % turns, i // turns) for i in range(items)]


def slot_rows(weights, first, size):
    return pl.BlockSpec((1, size, weights.shape[2]), lambda i: (i, first // size, 0))


def project_pack(x, weights, items, turns, groups):
    rows, width = x.shape
    slots = weights.shape[0]
    tile = rows // items
    half = tile // 2

    def kernel(x_ref, kv_ref, q_ref, out_ref):
        kv = dot_nt(x_ref[...], kv_ref[0]).astype(bf16)
        q = dot_nt(x_ref[...], q_ref[0]).astype(bf16).astype(f32) * 0.125
        for start, turn, group in tile_places(items, turns, groups, tile):
            upper, lower = swap_pairs(q[start : start + half], q[start + half : start + tile])
            for h, part in enumerate((upper, lower)):
                out_ref[turn, group, 0, h, :tile, :] = kv[
                    start : start + tile, h * 2 * HEAD : (h + 1) * 2 * HEAD
                ]
                out_ref[turn, group, 0, h, tile:, :] = part.astype(bf16)

    shape = (turns, groups, slots, 2, 3 * half, 2 * HEAD)
    return pl.pallas_call(
        kernel,
        grid=(slots,),
        in_specs=[
            pl.BlockSpec((rows, width), lambda i: (0, 0)),
            slot_rows(weights, KV_ROWS, 4 * HEAD),
            slot_rows(weights, Q_ROWS, 2 * HEAD),
        ],
        out_specs=pl.BlockSpec(
            (turns, groups, 1, 2, 3 * half, 2 * HEAD), lambda i: (0, 0, i, 0, 0, 0)
        ),
        out_shape=jax.ShapeDtypeStruct(shape, bf16),
        compiler_params=pltpu.CompilerParams(vmem_limit_bytes=40 << 20),
        cost_estimate=pl.CostEstimate(
            flops=2 * rows * width * slots * 6 * HEAD,
            bytes_accessed=2 * (rows + slots * 6 * HEAD) * width,
            transcendentals=0,
        ),
        name="project_pack",
    )(x, weights, weights)


def unpack_project(blocks, weights, items, groups):
    turns = len(blocks)
    slots = weights.shape[0]
    half = blocks[0].shape[3]
    tile = 2 * half
    width = weights.shape[2]

    def kernel(*refs):
        ins, w_ref, flat_ref, out_ref = refs[:turns], refs[turns], refs[turns + 1], refs[turns + 2]
        slot = pl.program_id(0)
        for start, turn, group in tile_places(items, turns, groups, tile):
            pair = [ins[turn][group, 0, h].astype(f32) for h in range(2)]
            upper, lower = swap_pairs(*pair)
            flat_ref[start : start + half, :] = upper.astype(bf16)
            flat_ref[start + half : start + tile, :] = lower.astype(bf16)
        part = dot_nn(flat_ref[...], w_ref[0])

        @pl.when(slot == 0)
        def _():
            out_ref[...] = part

        @pl.when(slot > 0)
        def _():
            out_ref[...] += part

    return pl.pallas_call(
        kernel,
        grid=(slots,),
        in_specs=[
            pl.BlockSpec((groups, 1, 2, half, 2 * HEAD), lambda i: (0, i, 0, 0, 0))
            for _ in range(turns)
        ]
        + [slot_rows(weights, SO_ROWS, 2 * HEAD)],
        out_specs=[
            pl.BlockSpec((items * tile, 2 * HEAD), lambda i: (0, i)),
            pl.BlockSpec((items * tile, width), lambda i: (0, 0)),
        ],
        out_shape=[
            jax.ShapeDtypeStruct((items * tile, slots * 2 * HEAD), bf16),
            jax.ShapeDtypeStruct((items * tile, width), f32),
        ],
        compiler_params=pltpu.CompilerParams(vmem_limit_bytes=40 << 20),
        cost_estimate=pl.CostEstimate(
            flops=2 * items * tile * width * slots * 2 * HEAD,
            bytes_accessed=4 * items * tile * width,
            transcendentals=0,
        ),
        name="unpack_project",
    )(*blocks, weights)


def back_pack(x, weights, items, turns, groups):
    rows, width = x.shape
    slots = weights.shape[0]
    tile = rows // items
    half = tile // 2

    def kernel(x_ref, w_ref, out_ref):
        grads = dot_nt(x_ref[...], w_ref[0])
        for start, turn, group in tile_places(items, turns, groups, tile):
            pair = swap_pairs(grads[start : start + half], grads[start + half : start + tile])
            for h, part in enumerate(pair):
                out_ref[turn, group, 0, h] = part.astype(bf16)

    return pl.pallas_call(
        kernel,
        grid=(slots,),
        in_specs=[
            pl.BlockSpec((rows, width), lambda i: (0, 0)),
            slot_rows(weights, SO_ROWS, 2 * HEAD),
        ],
        out_specs=pl.BlockSpec(
            (turns, groups, 1, 2, half, 2 * HEAD), lambda i: (0, 0, i, 0, 0, 0)
        ),
        out_shape=jax.ShapeDtypeStruct((turns, groups, slots, 2, half, 2 * HEAD), bf16),
        compiler_params=pltpu.CompilerParams(vmem_limit_bytes=40 << 20),
        cost_estimate=pl.CostEstimate(
            flops=2 * rows * width * slots * 2 * HEAD,
            bytes_accessed=2 * (rows + slots * 2 * HEAD) * width,
            transcendentals=0,
        ),
        name="back_pack",
    )(x, weights)


def unpack_back(blocks, weights, items, groups):
    turns = len(blocks)
    slots, _, width = weights.shape
    half = blocks[0].shape[3] // 3
    tile = 2 * half
    rows = items * tile

    def kernel(*refs):
        ins = refs[:turns]
        kv_ref, q_ref, flat_ref, out_ref = refs[turns:]
        slot = pl.program_id(0)
        for start, turn, group in tile_places(items, turns, groups, tile):
            pair = []
            for h in range(2):
                flat_ref[0, start : start + tile, h * 2 * HEAD : (h + 1) * 2 * HEAD] = ins[turn][
                    group, 0, h, :tile, :
                ]
                pair.append(ins[turn][group, 0, h, tile:, :].astype(f32))
            upper, lower = swap_pairs(*pair)
            flat_ref[0, start : start + half, 4 * HEAD :] = upper.astype(bf16)
            flat_ref[0, start + half : start + tile, 4 * HEAD :] = lower.astype(bf16)
        part = dot_nn(flat_ref[0, :, : 4 * HEAD], kv_ref[0])
        part = part + dot_nn(flat_ref[0, :, 4 * HEAD :], q_ref[0])

        @pl.when(slot == 0)
        def _():
            out_ref[...] = part

        @pl.when(slot > 0)
        def _():
            out_ref[...] += part

    return pl.pallas_call(
        kernel,
        grid=(slots,),
        in_specs=[
            pl.BlockSpec((groups, 1, 2, 3 * half, 2 * HEAD), lambda i: (0, i, 0, 0, 0))
            for _ in range(turns)
        ]
        + [slot_rows(weights, KV_ROWS, 4 * HEAD), slot_rows(weights, Q_ROWS, 2 * HEAD)],
        out_specs=[
            pl.BlockSpec((1, rows, 6 * HEAD), lambda i: (i, 0, 0)),
            pl.BlockSpec((rows, width), lambda i: (0, 0)),
        ],
        out_shape=[
            jax.ShapeDtypeStruct((slots, rows, 6 * HEAD), bf16),
            jax.ShapeDtypeStruct((rows, width), f32),
        ],
        compiler_params=pltpu.CompilerParams(vmem_limit_bytes=40 << 20),
        cost_estimate=pl.CostEstimate(
            flops=2 * rows * width * slots * 6 * HEAD,
            bytes_accessed=4 * rows * width,
            transcendentals=0,
        ),
        name="unpack_back",
    )(*blocks, weights, weights)


def norm_forward(base, branch, gate, shift, scale):
    items, tile, width = base.shape

    def kernel(base_ref, branch_ref, gate_ref, shift_ref, scale_ref, sum_ref, out_ref):
        value = base_ref[0] + gate_ref[0] * branch_ref[0]
        hat, _ = norm_parts(value)
        sum_ref[0] = value
        out_ref[0] = (hat * (1.0 + scale_ref[0]) + shift_ref[0]).astype(bf16)

    tile_spec = pl.BlockSpec((1, tile, width), lambda i: (i, 0, 0))
    piece_spec = pl.BlockSpec((1, 1, width), lambda i: (i, 0, 0))
    return pl.pallas_call(
        kernel,
        grid=(items,),
        in_specs=[tile_spec, tile_spec, piece_spec, piece_spec, piece_spec],
        out_specs=[tile_spec, tile_spec],
        out_shape=[
            jax.ShapeDtypeStruct(base.shape, f32),
            jax.ShapeDtypeStruct(base.shape, bf16),
        ],
        cost_estimate=pl.CostEstimate(
            flops=16 * items * tile * width,
            bytes_accessed=14 * items * tile * width,
            transcendentals=0,
        ),
        name="norm_forward",
    )(base, branch, gate, shift, scale)


def norm_backward(g, value, incoming, branch, scale, gate):
    items, tile, width = g.shape

    def kernel(g_ref, value_ref, in_ref, branch_ref, scale_ref, gate_ref, *outs):
        out_ref, gated_ref, low_ref, sums_ref = outs
        hat, inverse = norm_parts(value_ref[0])
        incoming = in_ref[0]
        sums_ref[0, 0:1] = jnp.sum(incoming, axis=0, keepdims=True)
        sums_ref[0, 1:2] = jnp.sum(incoming * hat, axis=0, keepdims=True)
        sums_ref[0, 2:3] = jnp.sum(g_ref[0] * branch_ref[0], axis=0, keepdims=True)
        out = g_ref[0] + norm_back(hat, inverse, incoming * (1.0 + scale_ref[0]))
        out_ref[0] = out
        gated_ref[0] = (gate_ref[0] * out).astype(bf16)
        low_ref[0] = out.astype(bf16)

    tile_spec = pl.BlockSpec((1, tile, width), lambda i: (i, 0, 0))
    piece_spec = pl.BlockSpec((1, 1, width), lambda i: (i, 0, 0))
    return pl.pallas_call(
        kernel,
        grid=(items,),
        in_specs=[tile_spec] * 4 + [piece_spec, piece_spec],
        out_specs=[
            tile_spec,
            tile_spec,
            tile_spec,
            pl.BlockSpec((1, 3, width), lambda i: (i, 0, 0)),
        ],
        out_shape=[
            jax.ShapeDtypeStruct(g.shape, f32),
            jax.ShapeDtypeStruct(g.shape, bf16),
            jax.ShapeDtypeStruct(g.shape, bf16),
            jax.ShapeDtypeStruct((items, 3, width), f32),
        ],
        cost_estimate=pl.CostEstimate(
            flops=30 * items * tile * width,
            bytes_accessed=24 * items * tile * width,
            transcendentals=0,
        ),
        name="norm_backward",
    )(g, value, incoming, branch, scale, gate)


def out_project(mixed, weights):
    tp, items, tile, local = mixed.shape
    slots, _, width = weights.shape
    rows = items * tile

    def kernel(x_ref, w_ref, out_ref):
        slot = pl.program_id(0)
        part = dot_nn(x_ref[0].reshape(rows, local // 2), w_ref[0])

        @pl.when(slot == 0)
        def _():
            out_ref[...] = part

        @pl.when(slot > 0)
        def _():
            out_ref[...] += part

    return pl.pallas_call(
        kernel,
        grid=(slots,),
        in_specs=[
            pl.BlockSpec((1, items, tile, local // 2), lambda i: (i % tp, 0, 0, i // tp)),
            slot_rows(weights, OUT_ROWS, 2 * HEAD),
        ],
        out_specs=pl.BlockSpec((rows, width), lambda i: (0, 0)),
        out_shape=jax.ShapeDtypeStruct((rows, width), f32),
        compiler_params=pltpu.CompilerParams(vmem_limit_bytes=40 << 20),
        cost_estimate=pl.CostEstimate(
            flops=2 * rows * width * tp * local,
            bytes_accessed=4 * rows * width,
            transcendentals=0,
        ),
        name="out_project",
    )(mixed, weights)


def out_back(x, weights, shape):
    tp, items, tile, local = shape
    rows, width = x.shape

    def kernel(x_ref, w_ref, out_ref):
        part = dot_nt(x_ref[...], w_ref[0])
        out_ref[0] = part.astype(bf16).reshape(items, tile, local // 2)

    return pl.pallas_call(
        kernel,
        grid=(2 * tp,),
        in_specs=[
            pl.BlockSpec((rows, width), lambda i: (0, 0)),
            slot_rows(weights, OUT_ROWS, 2 * HEAD),
        ],
        out_specs=pl.BlockSpec((1, items, tile, local // 2), lambda i: (i % tp, 0, 0, i // tp)),
        out_shape=jax.ShapeDtypeStruct(shape, bf16),
        compiler_params=pltpu.CompilerParams(vmem_limit_bytes=40 << 20),
        cost_estimate=pl.CostEstimate(
            flops=2 * rows * width * tp * local,
            bytes_accessed=4 * rows * width,
            transcendentals=0,
        ),
        name="out_back",
    )(x, weights)


def first_kernel(tokens, shift, scale, w, tp):
    rows, items, cols, width = tokens.shape
    cols_here = cols // tp
    tile = rows * cols_here
    local = w.shape[1]

    def kernel(x_ref, shift_ref, scale_ref, w_ref, in_ref, q_ref):
        hat, _ = norm_parts(x_ref[...].astype(f32).reshape(rows, cols, width))
        value = hat * (1.0 + scale_ref[0]) + shift_ref[0]
        for t in range(tp):
            part = value[:, t * cols_here : (t + 1) * cols_here, :].reshape(tile, width)
            in_ref[0, t * tile : (t + 1) * tile, :] = part.astype(bf16)
        q = dot_nn(in_ref[0], w_ref[...]).astype(bf16).astype(f32) * 0.125
        q_ref[0] = q.astype(bf16)

    piece_spec = pl.BlockSpec((1, 1, width), lambda i: (i, 0, 0))
    return pl.pallas_call(
        kernel,
        grid=(items,),
        in_specs=[
            pl.BlockSpec((rows, 1, cols, width), lambda i: (0, i, 0, 0)),
            piece_spec,
            piece_spec,
            pl.BlockSpec(w.shape, lambda i: (0, 0)),
        ],
        out_specs=[
            pl.BlockSpec((1, tp * tile, width), lambda i: (i, 0, 0)),
            pl.BlockSpec((1, tp * tile, local), lambda i: (i, 0, 0)),
        ],
        out_shape=[
            jax.ShapeDtypeStruct((items, tp * tile, width), bf16),
            jax.ShapeDtypeStruct((items, tp * tile, local), bf16),
        ],
        compiler_params=pltpu.CompilerParams(vmem_limit_bytes=48 << 20),
        cost_estimate=pl.CostEstimate(
            flops=2 * items * tp * tile * width * local,
            bytes_accessed=4 * items * tp * tile * width,
            transcendentals=0,
        ),
        name="first_kernel",
    )(tokens, shift, scale, w)


def key_value_kernel(context, w_key, w_value_t):
    items, keys, depth = context.shape
    local = w_key.shape[1]
    step = 1024 if keys % 1024 == 0 else keys

    def kernel(x_ref, wk_ref, wv_ref, k_ref, vt_ref):
        k_ref[0] = dot_nn(x_ref[0], wk_ref[...]).astype(bf16)
        vt_ref[0] = dot_nt(wv_ref[...], x_ref[0]).astype(bf16)

    return pl.pallas_call(
        kernel,
        grid=(items, keys // step),
        in_specs=[
            pl.BlockSpec((1, step, depth), lambda i, j: (i, j, 0)),
            pl.BlockSpec(w_key.shape, lambda i, j: (0, 0)),
            pl.BlockSpec(w_value_t.shape, lambda i, j: (0, 0)),
        ],
        out_specs=[
            pl.BlockSpec((1, step, local), lambda i, j: (i, j, 0)),
            pl.BlockSpec((1, local, step), lambda i, j: (i, 0, j)),
        ],
        out_shape=[
            jax.ShapeDtypeStruct((items, keys, local), bf16),
            jax.ShapeDtypeStruct((items, local, keys), bf16),
        ],
        compiler_params=pltpu.CompilerParams(vmem_limit_bytes=40 << 20),
        cost_estimate=pl.CostEstimate(
            flops=4 * items * keys * depth * local,
            bytes_accessed=2 * items * keys * (depth + 2 * local),
            transcendentals=0,
        ),
        name="key_value_kernel",
    )(context, w_key, w_value_t)


def key_value_grads(dk_t, dv_t, context, start):
    items, local, keys = dk_t.shape
    depth = context.shape[2]
    step = 1024 if keys % 1024 == 0 else keys

    def kernel(dk_ref, dv_ref, x_ref, out_ref):
        first = (pl.program_id(0) == 0) & (pl.program_id(1) == 0)
        both = jnp.concatenate([dk_ref[0], dv_ref[0]], axis=0)
        part = dot_nn(both, x_ref[0])

        @pl.when(first)
        def _():
            out_ref[...] = part

        @pl.when(jnp.logical_not(first))
        def _():
            out_ref[...] += part

    grads_spec = pl.BlockSpec((1, local, step), lambda i, j: (i, 0, j))
    return pl.pallas_call(
        kernel,
        grid=(items, keys // step),
        in_specs=[
            grads_spec,
            grads_spec,
            pl.BlockSpec((1, step, depth), lambda i, j: (i + start, j, 0)),
        ],
        out_specs=pl.BlockSpec((2 * local, depth), lambda i, j: (0, 0)),
        out_shape=jax.ShapeDtypeStruct((2 * local, depth), f32),
        compiler_params=pltpu.CompilerParams(vmem_limit_bytes=40 << 20),
        cost_estimate=pl.CostEstimate(
            flops=4 * items * keys * depth * local,
            bytes_accessed=2 * items * keys * (depth + 2 * local),
            transcendentals=0,
        ),
        name="key_value_grads",
    )(dk_t, dv_t, context)


def feed_forward(x, g, up, down):
    rows, width = x.shape
    slots, _, hidden = up.shape
    parts = 4 if rows % 64 == 0 else 1
    size = rows // parts

    def kernel(x_ref, g_ref, up_ref, down_ref, active_ref, dh_ref, branch_ref, back_ref):
        slot = pl.program_id(0)

        @pl.when(slot == 0)
        def _():
            branch_ref[...] = jnp.zeros_like(branch_ref)
            back_ref[...] = jnp.zeros_like(back_ref)

        def products(r):
            mine = pl.ds(r * size, size)
            return dot_nn(x_ref[mine, :], up_ref[0]), dot_nt(g_ref[mine, :], down_ref[0])

        ahead = products(0)
        for r in range(parts):
            h, da = ahead
            ahead = products(r + 1) if r + 1 < parts else None
            mine = pl.ds(r * size, size)
            below = 0.5 * (1.0 + lax.erf(h * 0.7071067811865476))
            slope = below + h * (jnp.exp(h * h * -0.5) * 0.3989422804014327)
            active = (h * below).astype(bf16)
            dh = (da * slope).astype(bf16)
            active_ref[0, mine, :] = active
            dh_ref[0, mine, :] = dh
            branch_ref[mine, :] += dot_nn(active, down_ref[0])
            back_ref[mine, :] += dot_nt(dh, up_ref[0])

    rows_spec = pl.BlockSpec((rows, width), lambda i: (0, 0))
    hidden_spec = pl.BlockSpec((1, rows, hidden), lambda i: (i, 0, 0))
    return pl.pallas_call(
        kernel,
        grid=(slots,),
        in_specs=[
            rows_spec,
            rows_spec,
            pl.BlockSpec((1, width, hidden), lambda i: (i, 0, 0)),
            pl.BlockSpec((1, hidden, width), lambda i: (i, 0, 0)),
        ],
        out_specs=[hidden_spec, hidden_spec, rows_spec, rows_spec],
        out_shape=[
            jax.ShapeDtypeStruct((slots, rows, hidden), bf16),
            jax.ShapeDtypeStruct((slots, rows, hidden), bf16),
            jax.ShapeDtypeStruct((rows, width), f32),
            jax.ShapeDtypeStruct((rows, width), f32),
        ],
        compiler_params=pltpu.CompilerParams(vmem_limit_bytes=52 << 20),
        cost_estimate=pl.CostEstimate(
            flops=8 * slots * rows * width * hidden,
            bytes_accessed=4 * slots * width * hidden,
            transcendentals=2 * slots * rows * hidden,
        ),
        name="feed_forward",
    )(x, g, up, down)


def weight_terms(buffer, shape, lhs, lhs_block, lhs_place, rhs, tp, size, first):
    count, width = rhs.shape
    share = shape[-1]
    seq = width // share
    depth = lhs_block[-1]
    by_core = len(shape) == 5

    def kernel(*refs):
        a_ref, b_ref, out_ref = refs[0], refs[1], refs[-1]
        a = a_ref[...]
        if len(lhs_block) > 3:
            a = a.astype(f32)
        a = a.reshape(count, depth).astype(bf16)
        terms = lax.dot_general(a, b_ref[...], (((0,), (0,)), ((), ())), preferred_element_type=f32)
        for s in range(seq):
            block = terms[:, s * share : (s + 1) * share].astype(bf16)
            if by_core:
                out_ref[s % 2, 0, s // 2] = block
            else:
                out_ref[s] = block

    return pl.pallas_call(
        kernel,
        grid=(tp, 2),
        in_specs=[
            pl.BlockSpec(lhs_block, lhs_place),
            pl.BlockSpec(rhs.shape, lambda t, c: (0, 0)),
        ]
        + ([] if buffer is None else [pl.BlockSpec(memory_space=pl.ANY)]),
        out_specs=pl.BlockSpec((2, 1, seq // 2, size, share), lambda t, c: (0, t, 0, first // size + c, 0))
        if by_core
        else pl.BlockSpec((seq, size, share), lambda t, c: (t, first // size + c, 0)),
        out_shape=jax.ShapeDtypeStruct(shape, bf16),
        input_output_aliases={} if buffer is None else {2: 0},
        compiler_params=pltpu.CompilerParams(vmem_limit_bytes=40 << 20),
        cost_estimate=pl.CostEstimate(
            flops=4 * tp * count * depth * width,
            bytes_accessed=4 * tp * (count + width) * depth,
            transcendentals=0,
        ),
        name="weight_terms",
    )(lhs, rhs, *([] if buffer is None else [buffer]))


def last_kernel(buffer, tokens, scale, middle, dq, small, start):
    rows, _, cols, width = tokens.shape
    tp, items, queries, local = dq.shape
    slots = small.shape[0]
    cols_here = cols // tp
    tile = rows * cols_here
    slot_width = local // 2

    def kernel(x_ref, scale_ref, middle_ref, dq_ref, w_ref, *refs):
        out_ref, sums_ref = refs[-2:]
        hat, inverse = norm_parts(x_ref[...].astype(f32).reshape(rows, cols, width))
        weights = w_ref[...].reshape(tp * local, width)
        shift_sum = jnp.zeros((1, width), f32)
        scale_sum = jnp.zeros((1, width), f32)
        for t in range(tp):
            pieces = [
                dq_ref[u, 0, t * tile : (t + 1) * tile, c * slot_width : (c + 1) * slot_width]
                for c in range(2)
                for u in range(tp)
            ]
            g = dot_nn(jnp.concatenate(pieces, axis=1), weights)
            mine = slice(t * cols_here, (t + 1) * cols_here)
            hat_t = hat[:, mine, :].reshape(tile, width)
            inverse_t = inverse[:, mine, :].reshape(tile, 1)
            shift_sum = shift_sum + jnp.sum(g, axis=0, keepdims=True)
            scale_sum = scale_sum + jnp.sum(g * hat_t, axis=0, keepdims=True)
            value = middle_ref[t, 0].astype(f32) + norm_back(
                hat_t, inverse_t, g * (1.0 + scale_ref[0])
            )
            out_ref[:, 0, mine, :] = value.reshape(rows, cols_here, width)
        sums_ref[0, 0:1, :] = shift_sum
        sums_ref[0, 1:2, :] = scale_sum

    return pl.pallas_call(
        kernel,
        grid=(items,),
        in_specs=[
            pl.BlockSpec((rows, 1, cols, width), lambda i: (0, i + start, 0, 0)),
            pl.BlockSpec((1, 1, width), lambda i: (i + start, 0, 0)),
            pl.BlockSpec((tp, 1, tile, width), lambda i: (0, i + start, 0, 0)),
            pl.BlockSpec((tp, 1, queries, local), lambda i: (0, i, 0, 0)),
            pl.BlockSpec((slots, slot_width, width), lambda i: (0, QUERY_ROWS // slot_width, 0)),
        ]
        + ([] if buffer is None else [pl.BlockSpec(memory_space=pl.ANY)]),
        out_specs=[
            pl.BlockSpec((rows, 1, cols, width), lambda i: (0, i + start, 0, 0)),
            pl.BlockSpec((1, 2, width), lambda i: (i, 0, 0)),
        ],
        out_shape=[
            jax.ShapeDtypeStruct(tokens.shape, f32),
            jax.ShapeDtypeStruct((items, 2, width), f32),
        ],
        input_output_aliases={} if buffer is None else {5: 0},
        compiler_params=pltpu.CompilerParams(vmem_limit_bytes=52 << 20),
        cost_estimate=pl.CostEstimate(
            flops=2 * items * queries * width * tp * local,
            bytes_accessed=10 * items * queries * width,
            transcendentals=0,
        ),
        name="last_kernel",
    )(tokens, scale, middle, dq, small, *([] if buffer is None else [buffer]))


def exchange(x, axis):
    return lax.all_to_all(x, axis, 0, 0, tiled=True)


def gather(x, axis):
    names = axis if isinstance(axis, tuple) else (axis,)
    count = 1
    for name in names:
        count *= lax.axis_size(name)
    return exchange(jnp.broadcast_to(x[None], (count,) + x.shape), axis)


def reduce_blocks(x, axis):
    return jnp.sum(exchange(x.astype(bf16), axis).astype(f32), axis=0)


def body(
    tokens,
    context,
    group_ids,
    source_table,
    w_query,
    w_key,
    w_value,
    w_out,
    w_self_query,
    w_self_key,
    w_self_value,
    w_self_out,
    w_up,
    w_down,
    w_deconv,
    deconv_bias,
    out_cotangent,
    plane_cotangent,
):
    rows_here, items, plane_cols, width = tokens.shape
    cols_here = out_cotangent.shape[2]
    tp = lax.axis_size("tp")
    seq = lax.axis_size("seq")
    both_axes = ("seq", "tp")
    devices = tp * seq
    local = w_query.shape[1]
    hidden_here = w_up.shape[1]
    slots = 2 * tp
    slot_heads = local // HEAD // 2
    slot_width = local // 2
    heads = slots * slot_heads
    tile = rows_here * cols_here
    half = tile // 2
    groups = devices // heads
    turns = -(-items // groups)
    share = width // seq
    fast = slot_heads == 2 and half % 16 == 0 and items == groups * turns and share % 128 == 0
    me_tp = lax.axis_index("tp")
    core = lax.axis_index("seq") % 2

    picker = (group_ids[:, None] == jnp.arange(GROUPS, dtype=jnp.int32)[None, :]).astype(f32)
    mods = jnp.dot(picker, source_table, precision=highest).reshape(items, 9, 1, width)

    def piece(index):
        return mods[:, index]

    def dot(spec, a, b):
        return jnp.einsum(spec, a, b, preferred_element_type=f32)

    def to_tile(x):
        return x.transpose(1, 0, 2, 3).reshape(items, tile, width)

    def from_tile(x):
        return x.reshape(items, rows_here, cols_here, width).transpose(1, 0, 2, 3)

    teams = [
        [(2 * pair + c) * tp + t for c in range(2) for t in range(tp)] for pair in range(seq // 2)
    ]

    def whole(x):
        return lax.all_gather(x, both_axes, axis=0, tiled=False, axis_index_groups=teams)

    def my_rows(x):
        return lax.dynamic_slice_in_dim(x, core * slot_width, slot_width, 0)

    def my_columns(x):
        size = x.shape[1] // 2
        return lax.dynamic_slice_in_dim(x, core * size, size, 1)

    key_value = jnp.stack(
        [
            my_columns(w_self_key).T.reshape(slot_heads, HEAD, width),
            my_columns(w_self_value).T.reshape(slot_heads, HEAD, width),
        ],
        axis=1,
    ).reshape(2 * slot_width, width)
    small = whole(
        jnp.concatenate(
            [
                key_value,
                my_columns(w_self_query).T,
                my_rows(w_self_out),
                my_rows(w_out),
                my_columns(w_query).T,
            ],
            axis=0,
        )
    )
    cuts = [slot_width * k for k in (0, 2, 3, 4, 5, 6)]
    kv_slots, q_slots, so_slots, out_slots, query_slots = [
        small[:, a:b] for a, b in zip(cuts[:-1], cuts[1:])
    ]
    up_slots = whole(my_columns(w_up))
    down_slots = whole(
        lax.dynamic_slice_in_dim(w_down, core * (hidden_here // 2), hidden_here // 2, 0)
    )

    def by_tp(x):
        return x.reshape(2, tp, slot_width, width).transpose(1, 0, 2, 3).reshape(tp, local, width)

    incoming = plane_cotangent.reshape(2 * rows_here, items, 2 * cols_here, COUT)
    plane_row = (lax.axis_index("seq") * rows_here + jnp.arange(rows_here, dtype=jnp.int32)) % PLANE
    upper_keep = (plane_row != 0).astype(f32)
    lower_keep = (plane_row != PLANE - 1).astype(f32)
    grad_edges = with_halo(incoming, (("seq", 0), ("tp", 2)), 1)
    if fast:
        first_in, queries = first_kernel(tokens, piece(0), piece(1), w_query, tp)
    else:
        ordered = (
            tokens.reshape(rows_here, items, tp, cols_here, width)
            .transpose(1, 2, 0, 3, 4)
            .reshape(items, tp * tile, width)
        )
        first_hat, first_inv = norm_parts(ordered.astype(f32))
        first_in = (first_hat * (1.0 + piece(1)) + piece(0)).astype(bf16)
        queries = dot("iqd,de->iqe", first_in, w_query).astype(bf16) * bf16(0.125)
    image = context.transpose(1, 0, 2)
    queries, grad_edges = lax.optimization_barrier((queries, grad_edges))
    keys, values_t = key_value_kernel(image, w_key, w_value.T)
    upper_mask = upper_keep.astype(bf16)[:, None, None, None]
    lower_mask = lower_keep.astype(bf16)[:, None, None, None]
    first_pair = grad_edges[:-2].reshape(rows_here, 2, items, 2 * cols_here + 2, COUT)
    last_pair = grad_edges[2:].reshape(rows_here, 2, items, 2 * cols_here + 2, COUT)
    row_taps = jnp.stack(
        [
            first_pair[:, 0] * upper_mask,
            first_pair[:, 1],
            last_pair[:, 0],
            last_pair[:, 1] * lower_mask,
        ],
        axis=3,
    )
    left_pair = row_taps[:, :, :-2].reshape(rows_here, items, cols_here, 2, 4, COUT)
    right_pair = row_taps[:, :, 2:].reshape(rows_here, items, cols_here, 2, 4, COUT)
    tap_grads = jnp.stack(
        [
            left_pair[:, :, :, 0],
            left_pair[:, :, :, 1],
            right_pair[:, :, :, 0],
            right_pair[:, :, :, 1],
        ],
        axis=4,
    )
    tap_grads = tap_grads.reshape(rows_here, items, cols_here, 16 * COUT)
    grad_result = to_tile(out_cotangent.astype(f32) + dot("rict,dt->ricd", tap_grads, w_deconv))
    grad_bias = jnp.sum(incoming.astype(f32), axis=(0, 1, 2))
    grad_mlp = (piece(8) * grad_result).astype(bf16)
    mixed, mixed_wide, cross_logs = cross_forward(queries, keys, values_t, tp)
    mixed_tile = exchange(mixed, "tp")
    if fast:
        branch_a = out_project(mixed_tile, small).reshape(items, tile, width)
    else:
        branch_a = dot("time,tef->imf", mixed_tile, by_tp(out_slots))
    residual = to_tile(lax.dynamic_slice_in_dim(tokens, me_tp * cols_here, cols_here, 2)).astype(f32)
    middle, self_in = norm_forward(residual, branch_a, piece(2), piece(3), piece(4))

    flat = (items * tile, width)
    spare = groups * turns - items

    def spread_items(x):
        if spare:
            x = jnp.pad(x, ((0, 0), (0, spare)) + ((0, 0),) * (x.ndim - 2))
        return x.reshape((slots, groups, turns) + x.shape[2:])

    def pack_keys(x):
        x = spread_items(x.reshape(slots, items, tile, slot_heads, 2 * HEAD))
        return x.transpose(2, 1, 0, 4, 3, 5).reshape(turns, devices, tile, 2 * HEAD)

    def unpack_keys(x):
        x = x.reshape(turns, groups, slots, slot_heads, tile, 2 * HEAD).transpose(2, 1, 0, 4, 3, 5)
        x = x.reshape(slots, groups * turns, tile, 2 * slot_width)[:, :items]
        return x.reshape(slots, items * tile, 2 * slot_width)

    def pack_rows(x):
        x = spread_items(x.reshape(slots, items, 2, half, slot_heads, HEAD))
        return x.transpose(2, 1, 0, 5, 4, 3, 6).reshape(turns, devices, half, 2 * HEAD)

    def unpack_rows(x):
        x = x.reshape(turns, groups, slots, slot_heads, half, 2, HEAD).transpose(2, 1, 0, 5, 4, 3, 6)
        x = x.reshape(slots, groups * turns, tile, slot_width)[:, :items]
        return x.reshape(slots, items * tile, slot_width)

    if fast:
        sends = project_pack(self_in.reshape(flat), small, items, turns, groups)
        sends = sends.reshape(turns, devices, 3 * half, 2 * HEAD)
        sends = [sends[turn] for turn in range(turns)]
    else:
        kv_sends = pack_keys(dot("nd,xed->xne", self_in.reshape(flat), kv_slots).astype(bf16))
        q_sends = dot("nd,xed->xne", self_in.reshape(flat), q_slots).astype(bf16)
        q_sends = pack_rows(q_sends * bf16(0.125))
        parts = [
            [
                exchange(kv_sends[turn], both_axes).reshape(devices * tile, 2 * HEAD),
                exchange(q_sends[turn], both_axes).reshape(devices * half, 2 * HEAD),
            ]
            for turn in range(turns)
        ]
    if fast:
        parts, forward = [], []
        for turn in range(turns):
            if turn >= 2:
                sends[turn], forward[turn - 2] = lax.optimization_barrier(
                    (sends[turn], forward[turn - 2])
                )
            arrived = exchange(sends[turn], both_axes)
            if turn == 0:
                arrived, grad_result, grad_mlp = lax.optimization_barrier(
                    (arrived, grad_result, grad_mlp)
                )
            parts.append([arrived])
            forward.append(self_forward(parts[turn], devices, half))
    else:
        forward = [self_forward(parts[turn], devices, half) for turn in range(turns)]
    outs = [x[0] for x in forward]
    if fast:
        outs[0], parts[-1][0] = lax.optimization_barrier((outs[0], parts[-1][0]))
    so_back = [exchange(so.reshape(devices, half, 2 * HEAD), both_axes) for so in outs]
    if fast:
        blocks = [x.reshape(groups, slots, 2, half, 2 * HEAD) for x in so_back]
        so_tile, branch_s = unpack_project(blocks, small, items, groups)
    else:
        so_tile = unpack_rows(jnp.stack(so_back)).transpose(1, 0, 2)
        branch_s = dot("nxe,xed->nd", so_tile, so_slots)
        so_tile = so_tile.reshape(items * tile, heads * HEAD)
    branch_s = branch_s.reshape(items, tile, width)
    middle_two, second_in = norm_forward(middle, branch_s, piece(5), piece(6), piece(7))

    active, grad_hidden, branch_b, grad_second = feed_forward(
        second_in.reshape(flat), grad_mlp.reshape(flat), up_slots, down_slots
    )
    branch_b = branch_b.reshape(items, tile, width)
    grad_second = grad_second.reshape(items, tile, width)
    result = middle_two + piece(8) * branch_b
    out_tile = from_tile(result.astype(bf16))

    grad_mid_two, grad_self, _, sums_b = norm_backward(
        grad_result, middle_two, grad_second, branch_b, piece(7), piece(5)
    )

    widened = with_halo(out_tile, (("seq", 0), ("tp", 2)), 1)
    taps = dot("ricd,dt->rict", widened, w_deconv)
    taps = taps.reshape(rows_here + 2, items, cols_here + 2, 4, 4, COUT)
    planes = spread_taps(
        taps, upper_keep[:, None, None, None, None], lower_keep[:, None, None, None, None]
    )
    planes = planes + jnp.tile(deconv_bias, 2 * cols_here)

    def by_device(x):
        lead = x.shape[0] // tp
        x = x.reshape(lead, tp, x.shape[1], seq, share).transpose(1, 3, 0, 2, 4)
        return x.reshape(devices, -1, share).astype(bf16)

    def of_cores(x):
        return x.reshape((tp, seq // 2, 2) + x.shape[1:]).transpose(2, 0, 1, 3, 4)

    def total_near(terms, after):
        keep = lax.dynamic_index_in_dim(terms, core, 0, False)
        give = lax.dynamic_index_in_dim(terms, 1 - core, 0, False)
        got = lax.ppermute(give, "seq", [(i, i ^ 1) for i in range(seq)])
        got, _ = lax.optimization_barrier((got, after))
        x = (keep.astype(f32) + got.astype(f32)).astype(bf16)
        return lax.psum_scatter(x, "tp", scatter_dimension=0, tiled=True)[0]

    def total_far(x, after, *cuts):
        x, _ = lax.optimization_barrier((x, after))
        lines = [list(range(c, seq, 2)) for c in range(2)]
        x = lax.psum_scatter(x, "seq", scatter_dimension=0, axis_index_groups=lines, tiled=True)[0]
        return jnp.split(x.astype(f32), cuts, axis=0)

    def total(terms, *cuts):
        summed = lax.psum_scatter(terms, ("tp", "seq"), scatter_dimension=0, tiled=True)[0]
        return jnp.split(summed.astype(f32), cuts, axis=0)

    terms_deconv = dot("ricd,rict->dt", out_tile, tap_grads).astype(bf16)
    piece_rows = width // devices
    terms_deconv = (
        terms_deconv.reshape(devices, piece_rows, -1, share)
        .transpose(0, 2, 1, 3)
        .reshape(devices, -1, share)
    )
    size_b = (hidden_here // 2, hidden_here, 2 * hidden_here)
    if fast:
        shape = (2, tp, seq // 2, size_b[2] + terms_deconv.shape[1], share)
        hidden_block = (1, items * tile, size_b[0])

        def slot_place(t, c):
            return (c * tp + t, 0, 0)

        terms_b = None
        for lhs, rhs, first in (
            (grad_hidden, second_in, 0),
            (active, grad_mlp, size_b[1]),
        ):
            terms_b = weight_terms(
                terms_b, shape, lhs, hidden_block, slot_place, rhs.reshape(flat), tp, size_b[0], first
            )
        terms_b = lax.dynamic_update_slice_in_dim(terms_b, of_cores(terms_deconv), size_b[2], 3)
    else:
        terms_b = jnp.concatenate(
            [
                by_device(dot("xnf,nd->xfd", grad_hidden, second_in.reshape(flat))),
                by_device(dot("xnf,nd->xfd", active, grad_mlp.reshape(flat))),
                terms_deconv,
            ],
            axis=1,
        )
        terms_b = of_cores(terms_b)

    if fast:
        dso_send = back_pack(grad_self.reshape(flat), small, items, turns, groups)
        dso_send = dso_send.reshape(turns, devices, half, 2 * HEAD)
    else:
        dso_send = pack_rows(dot("nd,xed->xne", grad_self.reshape(flat), so_slots).astype(bf16))
    dso_send = [dso_send[turn] for turn in range(turns)]
    dso_mine, backward = [], []
    for turn in range(turns):
        if turn >= 2:
            dso_send[turn], backward[turn - 2] = lax.optimization_barrier(
                (dso_send[turn], backward[turn - 2])
            )
        arrived = exchange(dso_send[turn], both_axes).reshape(devices * half, 2 * HEAD)
        if turn == 0:
            arrived, terms_b = lax.optimization_barrier((arrived, terms_b))
        dso_mine.append(arrived)
        backward.append(
            self_backward(parts[turn], dso_mine[turn], *forward[turn][1:], devices, half)
        )
    near_b = total_near(terms_b, (backward[0][0], dso_mine[min(1, turns - 1)]))
    if fast:
        blocks = [
            exchange(x[0], both_axes).reshape(groups, slots, 2, 3 * half, 2 * HEAD)
            for x in backward
        ]
        blocks[-1], planes = lax.optimization_barrier((blocks[-1], planes))
        grad_projected, grad_third = unpack_back(blocks, small, items, groups)
    else:
        dkv = [exchange(x[0].reshape(devices, tile, 2 * HEAD), both_axes) for x in backward]
        dq = [exchange(x[1].reshape(devices, half, 2 * HEAD), both_axes) for x in backward]
        grad_projected = jnp.concatenate(
            [unpack_keys(jnp.stack(dkv)), unpack_rows(jnp.stack(dq))], axis=2
        )
        grad_third = dot(
            "xne,xed->nd", grad_projected, jnp.concatenate([kv_slots, q_slots], axis=1)
        )
    grad_up, grad_down, grad_deconv = total_far(near_b, grad_third, *size_b[1:])
    grad_third = grad_third.reshape(items, tile, width)
    grad_middle, grad_attn, middle_low, sums_s = norm_backward(
        grad_mid_two, middle, grad_third, branch_s, piece(4), piece(2)
    )

    grad_gate_a = jnp.sum(grad_middle * branch_a, axis=1)
    if fast:
        do_send = out_back(grad_attn.reshape(flat), small, mixed.shape)
    else:
        do_send = dot("imf,tef->time", grad_attn, by_tp(out_slots)).astype(bf16)
    do_mine = exchange(do_send, "tp")
    middle_all = gather(middle_low, "tp")
    early = jnp.concatenate([grad_gate_a[:, None], sums_s, sums_b], axis=1)
    early = early.transpose(1, 0, 2).reshape(7 * items, width)
    early = jnp.concatenate(
        [early, jnp.pad(grad_bias, (0, width - COUT))[None]], axis=0
    )
    spots = -(-early.shape[0] // (16 * tp)) * 16
    early = jnp.pad(early, ((0, spots * tp - early.shape[0]), (0, 0))).reshape(tp, spots, width)
    early = by_device(early)
    size_a = [slot_width * k for k in (6, 8, 10)]
    if fast:
        shape = (devices, size_a[2] + early.shape[1], share)
        terms_a = weight_terms(
            None,
            shape,
            grad_projected,
            (1, items * tile, 3 * slot_width),
            lambda t, c: (c * tp + t, 0, 0),
            self_in.reshape(flat),
            tp,
            3 * slot_width,
            0,
        )
        terms_a = weight_terms(
            terms_a,
            shape,
            so_tile,
            (items * tile, slot_width),
            lambda t, c: (0, c * tp + t),
            grad_self.reshape(flat),
            tp,
            slot_width,
            size_a[0],
        )
        terms_a = weight_terms(
            terms_a,
            shape,
            mixed_tile,
            (1, items, tile, slot_width),
            lambda t, c: (t, 0, 0, c),
            grad_attn.reshape(flat),
            tp,
            slot_width,
            size_a[1],
        )
        terms_a = lax.dynamic_update_slice_in_dim(terms_a, early, size_a[2], 1)
    else:
        so_terms = dot("ne,nd->ed", so_tile, grad_self.reshape(flat))
        terms_a = jnp.concatenate(
            [
                by_device(dot("xne,nd->xed", grad_projected, self_in.reshape(flat))),
                by_device(so_terms.reshape(slots, slot_width, width)),
                by_device(dot("time,imf->tef", mixed_tile, grad_attn)),
                early,
            ],
            axis=1,
        )
    do_mine, terms_a = lax.optimization_barrier((do_mine, terms_a))
    terms_a, grad_up = lax.optimization_barrier((terms_a, grad_up))
    grad_three, grad_self_out, grad_out, grad_early = total(terms_a, *size_a)
    first_part = items // 2
    cross = (queries, do_mine, mixed_wide, cross_logs, keys, values_t)
    one = cross_backward(*cross, 0, first_part)
    one, middle_all = lax.optimization_barrier((one, middle_all))
    dq_one = gather(one[0], "tp")
    do_late, _ = lax.optimization_barrier((do_mine, one[0]))
    two = cross_backward(queries, do_late, *cross[2:], first_part, items - first_part)
    one, two, dq_one = lax.optimization_barrier((one, two, dq_one))
    dq_two = gather(two[0], "tp")
    two, dq_two = lax.optimization_barrier((two, dq_two))
    dq_cross = jnp.concatenate([one[0], two[0]], axis=0)
    grad_three = grad_three.reshape(2, 3 * slot_width, share)
    grad_pair = grad_three[:, : 2 * slot_width].reshape(2, slot_heads, 2, HEAD, share)
    grad_self_key = grad_pair[:, :, 0].reshape(local, share).T
    grad_self_value = grad_pair[:, :, 1].reshape(local, share).T
    grad_self_query = grad_three[:, 2 * slot_width :].reshape(local, share).T

    def by_seq(x):
        return x.reshape((seq, x.shape[0] // seq) + x.shape[1:]).astype(bf16)

    grad_image = (
        key_value_grads(one[1], one[2], image, 0) + key_value_grads(two[1], two[2], image, first_part)
    ).T
    last = jnp.concatenate(
        [
            by_seq(dot("iqd,iqe->de", first_in, dq_cross)),
            by_seq(grad_image[:, :local]),
            by_seq(grad_image[:, local:]),
        ],
        axis=1,
    )
    grad_deconv, grad_image = lax.optimization_barrier((grad_deconv, grad_image))
    grad_deconv = grad_deconv.reshape(-1, piece_rows, share).transpose(1, 0, 2)
    grad_deconv = lax.all_gather(
        grad_deconv.reshape(piece_rows, 16 * COUT).astype(bf16), ("tp", "seq"), axis=0, tiled=True
    )
    last, dq_one, dq_two = lax.optimization_barrier((last, dq_one, dq_two))
    last = jnp.sum(exchange(last, "seq").astype(f32), axis=0)
    if fast:
        grad_tokens, late_one = last_kernel(None, tokens, piece(1), middle_all, dq_one, small, 0)
        grad_tokens, late_two = last_kernel(
            grad_tokens, tokens, piece(1), middle_all, dq_two, small, first_part
        )
        late = jnp.concatenate([late_one, late_two], axis=0).transpose(1, 0, 2)
    else:
        dq_all = jnp.concatenate([dq_one, dq_two], axis=1)
        grad_first = dot("tiqe,ted->iqd", dq_all, by_tp(query_slots))
        grad_shift_a = jnp.sum(grad_first, axis=1)
        grad_scale_a = jnp.sum(grad_first * first_hat, axis=1)
        grad_tokens = middle_all.astype(f32).transpose(1, 0, 2, 3).reshape(
            items, tp * tile, width
        ) + norm_back(first_hat, first_inv, grad_first * (1.0 + piece(1)))
        grad_tokens = (
            grad_tokens.reshape(items, tp, rows_here, cols_here, width)
            .transpose(2, 0, 1, 3, 4)
            .reshape(rows_here, items, plane_cols, width)
        )
        late = jnp.stack([grad_shift_a, grad_scale_a], axis=0)

    late, last = lax.optimization_barrier((late, last))
    part = 2 * items * width // tp
    mine = lax.dynamic_slice_in_dim(late.reshape(-1, share), me_tp * (part // share), part // share, 0)
    sums = gather(jnp.concatenate([mine, grad_early], axis=0), ("tp", "seq"))
    sums = sums.reshape(tp, seq, part // share + spots, share)
    late = jnp.sum(sums[:, :, : part // share], axis=1).reshape(2, items, width)
    early = sums[:, :, part // share :].transpose(0, 2, 1, 3).reshape(tp * spots, width)
    grad_bias = early[7 * items, :COUT]
    early = early[: 7 * items].reshape(7, items, width)
    depth = (last.shape[0] - share) // 2
    grad_query, grad_key, grad_value = (
        last[:share],
        last[share : share + depth],
        last[share + depth :],
    )
    late, grad_deconv = lax.optimization_barrier((late, grad_deconv))
    grad_mods = jnp.concatenate([late, early], axis=0).transpose(1, 0, 2)
    grad_table = jnp.dot(picker.T, grad_mods.reshape(items, 9 * width), precision=highest)
    return (
        out_tile,
        planes,
        grad_tokens,
        grad_query,
        grad_key,
        grad_value,
        grad_out,
        grad_self_query,
        grad_self_key,
        grad_self_value,
        grad_self_out.reshape(local, share),
        grad_up.T,
        grad_down,
        grad_deconv.astype(f32),
        grad_bias,
        grad_table,
    )


def solution(mesh):
    in_specs = (
        P("seq", None, None, None),
        P(),
        P(),
        P(),
        P(None, "tp"),
        P(None, "tp"),
        P(None, "tp"),
        P("tp", None),
        P(None, "tp"),
        P(None, "tp"),
        P(None, "tp"),
        P("tp", None),
        P(None, "tp"),
        P("tp", None),
        P(),
        P(),
        P("seq", None, "tp", None),
        P("seq", None, "tp"),
    )
    out_specs = (
        P("seq", None, "tp", None),
        P("seq", None, "tp"),
        P("seq", None, None, None),
        P("seq", "tp"),
        P("seq", "tp"),
        P("seq", "tp"),
        P("tp", "seq"),
        P("seq", "tp"),
        P("seq", "tp"),
        P("seq", "tp"),
        P("tp", "seq"),
        P("seq", "tp"),
        P("tp", "seq"),
        P(),
        P(),
        P(),
    )
    return jax.shard_map(body, mesh=mesh, in_specs=in_specs, out_specs=out_specs, check_vma=False)
```

```python
import jax
import jax.numpy as jnp
from jax import lax
from jax.experimental import pallas as pl
from jax.experimental.pallas import tpu as pltpu
from jax.sharding import PartitionSpec as P

HEAD = 64
COUT = 80
PLANE = 32
IMG = 4096
LOG2E = 1.4426950408889634
bf16 = jnp.bfloat16
f32 = jnp.float32
GROUPS = 16


highest = lax.Precision.HIGHEST
epsilon = 1e-06


def with_halo(x, sides, width):
    for axis, dim in sides:
        peers, length = (lax.axis_size(axis), x.shape[dim])
        up = [(i, (i + 1) % peers) for i in range(peers - 1)]
        down = [(j, i) for i, j in up]
        last = lax.slice_in_dim(x, length - width, length, axis=dim)
        initial = lax.slice_in_dim(x, 0, width, axis=dim)
        before = lax.ppermute(last, axis, up)
        after = lax.ppermute(initial, axis, down)
        x = jnp.concatenate([before, x, after], axis=dim)
    return x


def spread_taps(padded, upper, lower):
    even_rows = padded[1:-1, :, :, 1] + upper * padded[:-2, :, :, 3]
    odd_rows = lower * padded[2:, :, :, 0] + padded[1:-1, :, :, 2]
    rows_both = jnp.stack([even_rows, odd_rows], axis=1)
    even_cols = rows_both[:, :, :, 1:-1, 1] + rows_both[:, :, :, :-2, 3]
    odd_cols = rows_both[:, :, :, 2:, 0] + rows_both[:, :, :, 1:-1, 2]
    joined = jnp.stack([even_cols, odd_cols], axis=4)
    shape = joined.shape
    return joined.reshape(shape[0] * 2, shape[2], shape[3] * 2 * shape[5])


def norm_parts(value):
    centred = value - jnp.mean(value, axis=-1, keepdims=True)
    inverse = lax.rsqrt(jnp.mean(centred * centred, axis=-1, keepdims=True) + epsilon)
    return (centred * inverse, inverse)


def norm_back(normed, inverse, incoming):
    return inverse * (
        incoming
        - jnp.mean(incoming, axis=-1, keepdims=True)
        - normed * jnp.mean(incoming * normed, axis=-1, keepdims=True)
    )


NT = (((1,), (1,)), ((), ()))
BLOCKS = 4
KV_ROWS, Q_ROWS, SO_ROWS, OUT_ROWS, QUERY_ROWS = 0, 256, 384, 512, 640


def dot_nt(a, b):
    return lax.dot_general(a, b, NT, preferred_element_type=f32)


def dot_nn(a, b):
    return jnp.dot(a, b, preferred_element_type=f32)


def flip(x):
    return x.astype(f32).T.astype(bf16)


def chunk_of(keys):
    return 512 if keys % 512 == 0 else keys


SAFE = 40.0


def softmax_sweep(scores, values, chunks, columns, write):
    def spread(mixed, total, top):
        width = columns // len(mixed)
        inverse = 1.0 / total
        mixed = [m * inverse[:, j * width : (j + 1) * width] for j, m in enumerate(mixed)]
        write(mixed, top + jnp.log(total))

    ahead = scores(0)
    top = jnp.max(ahead, axis=0, keepdims=True)
    base = top * LOG2E
    peak = top
    total = jnp.zeros((1, columns), f32)
    mixed = None
    for c in range(chunks):
        now = ahead
        ahead = scores(c + 1) if c + 1 < chunks else None
        expon = jnp.exp2(now * LOG2E - base)
        if c > 0:
            peak = jnp.maximum(peak, jnp.max(now, axis=0, keepdims=True))
        total = total + jnp.sum(expon, axis=0, keepdims=True)
        parts = values(c, expon.astype(bf16))
        mixed = parts if mixed is None else [m + part for m, part in zip(mixed, parts)]
    spread(mixed, total, top)

    @pl.when(jnp.max(peak - top) > SAFE)
    def _():
        def body(c, carry):
            top, total, mixed = carry
            now = scores(c)
            new_top = jnp.maximum(top, jnp.max(now, axis=0, keepdims=True))
            fade = jnp.exp2((top - new_top) * LOG2E)
            expon = jnp.exp2((now - new_top) * LOG2E)
            total = total * fade + jnp.sum(expon, axis=0, keepdims=True)
            parts = values(c, expon.astype(bf16))
            width = columns // len(parts)
            mixed = [
                m * fade[:, j * width : (j + 1) * width] + part
                for j, (m, part) in enumerate(zip(mixed, parts))
            ]
            return new_top, total, mixed

        start = (
            jnp.full((1, columns), -3e38, f32),
            jnp.zeros((1, columns), f32),
            [jnp.zeros(m.shape, f32) for m in mixed],
        )
        top, total, again = lax.fori_loop(0, chunks, body, start)
        spread(again, total, top)


def at_chunk(c, step):
    return pl.ds(c * step if isinstance(c, int) else pl.multiple_of(c * step, step), step)


def cross_forward(q, k, vt, tp):
    items, queries, width = q.shape
    tile = queries // tp
    keys = k.shape[1]
    heads = width // HEAD
    step = chunk_of(keys)

    def kernel(q_ref, k_ref, vt_ref, o_ref, wide_ref, log_ref):
        pair = pl.program_id(1)
        owner = lax.broadcasted_iota(jnp.int32, (queries, width), 1) // HEAD
        both = jnp.concatenate(
            [jnp.where(owner == pair * 2 + j, q_ref[0], 0.0).astype(bf16) for j in range(2)], axis=0
        )

        def scores(c):
            return dot_nt(k_ref[0, at_chunk(c, step), :], both)

        def values(c, p):
            out = []
            for j in range(2):
                rows = pl.ds(pl.multiple_of((pair * 2 + j) * HEAD, HEAD), HEAD)
                v = vt_ref[0, rows, at_chunk(c, step)]
                out.append(dot_nn(v, p[:, j * queries : (j + 1) * queries]))
            return out

        def write(mixed, log_total):
            rows = jnp.concatenate(mixed, axis=0).T.reshape(tp, 1, tile, 2 * HEAD)
            o_ref[...] = rows.astype(bf16)
            wide_ref[...] = rows
            for j in range(2):
                log_ref[0, j] = jnp.broadcast_to(
                    log_total[:, j * queries : (j + 1) * queries], (8, queries)
                )

        softmax_sweep(scores, values, keys // step, 2 * queries, write)

    return pl.pallas_call(
        kernel,
        grid=(items, heads // 2),
        in_specs=[
            pl.BlockSpec((1, queries, width), lambda i, h: (i, 0, 0)),
            pl.BlockSpec((1, keys, width), lambda i, h: (i, 0, 0)),
            pl.BlockSpec((1, width, keys), lambda i, h: (i, 0, 0)),
        ],
        out_specs=[
            pl.BlockSpec((tp, 1, tile, 2 * HEAD), lambda i, h: (0, i, 0, h)),
            pl.BlockSpec((tp, 1, tile, 2 * HEAD), lambda i, h: (0, i, 0, h)),
            pl.BlockSpec((1, 2, 8, queries), lambda i, h: (i, h, 0, 0)),
        ],
        out_shape=[
            jax.ShapeDtypeStruct((tp, items, tile, width), bf16),
            jax.ShapeDtypeStruct((tp, items, tile, width), f32),
            jax.ShapeDtypeStruct((items, heads, 8, queries), f32),
        ],
        compiler_params=pltpu.CompilerParams(vmem_limit_bytes=60 << 20),
        cost_estimate=pl.CostEstimate(
            flops=16 * items * queries * keys * width,
            bytes_accessed=4 * items * (queries + keys) * width,
            transcendentals=items * queries * keys * heads,
        ),
        name="cross_forward",
    )(q, k, vt)


def cross_backward(q, do, o, logs, k, vt, start, items):
    _, queries, width = q.shape
    tp, _, tile, _ = do.shape
    keys = k.shape[1]
    heads = width // HEAD
    step = chunk_of(keys)

    def kernel(q_ref, do_ref, o_ref, log_ref, k_ref, vt_ref, dq_ref, dk_ref, dv_ref, qt, dot):
        head = pl.program_id(1)

        @pl.when(head == 0)
        def _():
            qt[...] = flip(q_ref[0])
            dot[...] = do_ref[...].astype(f32).reshape(queries, width).T.astype(bf16)

        mine = lax.broadcasted_iota(jnp.int32, (queries, width), 1) // HEAD == head
        q_mine = jnp.where(mine, q_ref[0], 0.0).astype(bf16)
        do_wide = jnp.where(mine, do_ref[...].astype(f32).reshape(queries, width), 0.0)
        do_mine = do_wide.astype(bf16)
        o_wide = o_ref[...].reshape(queries, width)
        delta = jnp.sum(do_wide * o_wide, axis=1, keepdims=True)
        log_total = log_ref[0, 0].T[:, :1] * LOG2E
        rows = pl.ds(pl.multiple_of(head * HEAD, HEAD), HEAD)
        qt_mine = qt[rows, :]
        dot_mine = dot[rows, :]

        def scores(c):
            s = dot_nt(q_mine, k_ref[0, pl.ds(c * step, step), :])
            return s, dot_nn(do_mine, vt_ref[0, :, pl.ds(c * step, step)])

        dq = jnp.zeros((queries, width), f32)
        ahead = scores(0)
        for c in range(keys // step):
            s, dp = ahead
            ahead = scores(c + 1) if c + 1 < keys // step else None
            p = jnp.exp2(s * LOG2E - log_total)
            ds = (p * (dp - delta)).astype(bf16)
            cols = pl.ds(c * step, step)
            dv_ref[0, :, cols] = dot_nn(dot_mine, p.astype(bf16)).astype(bf16)
            dk_ref[0, :, cols] = dot_nn(qt_mine, ds).astype(bf16)
            dq = dq + dot_nn(ds, k_ref[0, cols, :])
        dq = (dq * 0.125).astype(bf16)
        rest = jnp.where(head == 0, jnp.zeros_like(dq), dq_ref[0])
        dq_ref[0] = jnp.where(mine, dq, rest)

    rows_spec = pl.BlockSpec((1, queries, width), lambda i, h: (i + start, 0, 0))
    tiles_spec = pl.BlockSpec((tp, 1, tile, width), lambda i, h: (0, i + start, 0, 0))
    grads_spec = pl.BlockSpec((1, HEAD, keys), lambda i, h: (i, h, 0))
    return pl.pallas_call(
        kernel,
        grid=(items, heads),
        in_specs=[
            rows_spec,
            tiles_spec,
            tiles_spec,
            pl.BlockSpec((1, 1, 8, queries), lambda i, h: (i + start, h, 0, 0)),
            pl.BlockSpec((1, keys, width), lambda i, h: (i + start, 0, 0)),
            pl.BlockSpec((1, width, keys), lambda i, h: (i + start, 0, 0)),
        ],
        out_specs=[
            pl.BlockSpec((1, queries, width), lambda i, h: (i, 0, 0)),
            grads_spec,
            grads_spec,
        ],
        out_shape=[
            jax.ShapeDtypeStruct((items, queries, width), bf16),
            jax.ShapeDtypeStruct((items, width, keys), bf16),
            jax.ShapeDtypeStruct((items, width, keys), bf16),
        ],
        scratch_shapes=[pltpu.VMEM((width, queries), bf16), pltpu.VMEM((width, queries), bf16)],
        compiler_params=pltpu.CompilerParams(vmem_limit_bytes=60 << 20),
        cost_estimate=pl.CostEstimate(
            flops=40 * items * queries * keys * width,
            bytes_accessed=8 * items * (queries + keys) * width,
            transcendentals=items * queries * keys * heads,
        ),
        name="cross_backward",
    )(q, do, o, logs, k, vt)


def split_wide(x):
    low = lax.broadcasted_iota(jnp.int32, x.shape, 1) < HEAD
    wide = x.astype(f32)
    first = jnp.where(low, wide, 0.0)
    second = jnp.where(low, pltpu.roll(wide, HEAD, 1), 0.0)
    return jnp.concatenate([first, second], axis=0)


def split_pair(x):
    return split_wide(x).astype(bf16)


def part_specs(parts, half):
    if len(parts) == 1:
        return [pl.BlockSpec(parts[0].shape, lambda i: (0, 0, 0))]
    rows = parts[1].shape[0] // BLOCKS
    return [
        pl.BlockSpec(parts[0].shape, lambda i: (0, 0)),
        pl.BlockSpec((rows, 2 * HEAD), lambda i: (i, 0)),
    ]


def read_keys(refs, half):
    if len(refs) == 2:
        return refs[0][...]
    devices = refs[0].shape[0]
    return refs[0][:, : 2 * half, :].reshape(devices * 2 * half, 2 * HEAD)


def read_queries(refs, half, i, share):
    if len(refs) == 2:
        return refs[1][...]
    return refs[0][pl.ds(i * share, share), 2 * half :, :].reshape(share * half, 2 * HEAD)


def self_forward(parts, devices, half):
    tile = 2 * half
    keys = devices * tile
    blocks = BLOCKS
    share = devices // blocks
    block = share * half
    step = chunk_of(keys)

    def kernel(*refs):
        ins, (o_ref, wide_ref, log_ref, kv, vt) = refs[: len(parts)], refs[len(parts) :]
        i = pl.program_id(0)

        @pl.when(i == 0)
        def _():
            kv[...] = read_keys(ins, half)
            vt[...] = flip(kv[...])

        both = split_pair(read_queries(ins, half, i, share))

        def scores(c):
            return dot_nt(kv[at_chunk(c, step), :], both)

        def values(c, p):
            return [dot_nn(vt[HEAD:, at_chunk(c, step)], p)]

        def write(mixed, log_total):
            mixed = mixed[0]
            rows = jnp.concatenate([mixed[:, :block], mixed[:, block:]], axis=0).T
            o_ref[...] = rows.astype(bf16)
            wide_ref[...] = rows
            log_ref[0] = jnp.broadcast_to(log_total, (8, 2 * block))

        softmax_sweep(scores, values, keys // step, 2 * block, write)

    return pl.pallas_call(
        kernel,
        grid=(blocks,),
        in_specs=part_specs(parts, half),
        out_specs=[
            pl.BlockSpec((block, 2 * HEAD), lambda i: (i, 0)),
            pl.BlockSpec((block, 2 * HEAD), lambda i: (i, 0)),
            pl.BlockSpec((1, 8, 2 * block), lambda i: (i, 0, 0)),
        ],
        out_shape=[
            jax.ShapeDtypeStruct((devices * half, 2 * HEAD), bf16),
            jax.ShapeDtypeStruct((devices * half, 2 * HEAD), f32),
            jax.ShapeDtypeStruct((blocks, 8, 2 * block), f32),
        ],
        scratch_shapes=[pltpu.VMEM((keys, 2 * HEAD), bf16), pltpu.VMEM((2 * HEAD, keys), bf16)],
        compiler_params=pltpu.CompilerParams(vmem_limit_bytes=60 << 20),
        cost_estimate=pl.CostEstimate(
            flops=16 * keys * keys * HEAD,
            bytes_accessed=8 * keys * 2 * HEAD,
            transcendentals=keys * keys,
        ),
        name="self_forward",
    )(*parts)


def self_backward(parts, do, o, logs, devices, half):
    tile = 2 * half
    keys = devices * tile
    blocks = logs.shape[0]
    share = devices // blocks
    block = share * half
    step = chunk_of(keys)

    def kernel(*refs):
        n = len(parts)
        ins, (do_ref, o_ref, log_ref), outs = refs[:n], refs[n : n + 3], refs[n + 3 : 2 * n + 3]
        kv, vt, grads = refs[2 * n + 3 :]
        i = pl.program_id(0)
        mine = pl.ds(i * share, share)

        @pl.when(i == 0)
        def _():
            kv[...] = read_keys(ins, half)
            vt[...] = flip(kv[...])
            grads[...] = jnp.zeros_like(grads)

        q_both = split_pair(read_queries(ins, half, i, share))
        do_both = split_pair(do_ref[...])
        delta = jnp.sum(do_both.astype(f32) * split_wide(o_ref[...]), axis=1, keepdims=True)
        log_total = log_ref[0].T[:, :1] * LOG2E
        qt = flip(q_both)[:HEAD]
        dot = flip(do_both)[:HEAD]
        do_low = do_both[:, :HEAD]

        def scores(c):
            s = dot_nt(q_both, kv[pl.ds(c * step, step), :])
            return s, dot_nn(do_low, vt[HEAD:, pl.ds(c * step, step)])

        dq = jnp.zeros((2 * block, 2 * HEAD), f32)
        ahead = scores(0)
        for c in range(keys // step):
            s, dp = ahead
            ahead = scores(c + 1) if c + 1 < keys // step else None
            p = jnp.exp2(s * LOG2E - log_total)
            ds = (p * (dp - delta)).astype(bf16)
            cols = pl.ds(c * step, step)
            grads[:HEAD, cols] += dot_nn(qt, ds)
            grads[HEAD:, cols] += dot_nn(dot, p.astype(bf16))
            dq = dq + dot_nn(ds, kv[cols, :])
        dq = dq * 0.125
        low = lax.broadcasted_iota(jnp.int32, (block, 2 * HEAD), 1) < HEAD
        packed = jnp.where(low, dq[:block], pltpu.roll(dq[block:], HEAD, 1)).astype(bf16)
        if n == 1:
            outs[0][mine, tile:, :] = packed.reshape(share, half, 2 * HEAD)
        else:
            outs[1][...] = packed

        @pl.when(i == blocks - 1)
        def _():
            dkv = grads[...].T.astype(bf16)
            if n == 1:
                outs[0][:, :tile, :] = dkv.reshape(devices, tile, 2 * HEAD)
            else:
                outs[0][...] = dkv

    rows_spec = pl.BlockSpec((block, 2 * HEAD), lambda i: (i, 0))
    return pl.pallas_call(
        kernel,
        grid=(blocks,),
        in_specs=part_specs(parts, half)
        + [rows_spec, rows_spec, pl.BlockSpec((1, 8, 2 * block), lambda i: (i, 0, 0))],
        out_specs=part_specs(parts, half),
        out_shape=[jax.ShapeDtypeStruct(p.shape, bf16) for p in parts],
        scratch_shapes=[
            pltpu.VMEM((keys, 2 * HEAD), bf16),
            pltpu.VMEM((2 * HEAD, keys), bf16),
            pltpu.VMEM((2 * HEAD, keys), f32),
        ],
        compiler_params=pltpu.CompilerParams(vmem_limit_bytes=60 << 20),
        cost_estimate=pl.CostEstimate(
            flops=40 * keys * keys * HEAD,
            bytes_accessed=16 * keys * 2 * HEAD,
            transcendentals=keys * keys,
        ),
        name="self_backward",
    )(*parts, do, o, logs)


def swap_pairs(first, second):
    low = lax.broadcasted_iota(jnp.int32, first.shape, 1) < HEAD
    return (
        jnp.where(low, first, pltpu.roll(second, HEAD, 1)),
        jnp.where(low, pltpu.roll(first, HEAD, 1), second),
    )


def tile_places(items, turns, groups, tile):
    return [(i * tile, i % turns, i // turns) for i in range(items)]


def slot_rows(weights, first, size):
    return pl.BlockSpec((1, size, weights.shape[2]), lambda i: (i, first // size, 0))


def project_pack(x, weights, items, turns, groups):
    rows, width = x.shape
    slots = weights.shape[0]
    tile = rows // items
    half = tile // 2

    def kernel(x_ref, kv_ref, q_ref, out_ref):
        kv = dot_nt(x_ref[...], kv_ref[0]).astype(bf16)
        q = dot_nt(x_ref[...], q_ref[0]).astype(bf16).astype(f32) * 0.125
        for start, turn, group in tile_places(items, turns, groups, tile):
            upper, lower = swap_pairs(q[start : start + half], q[start + half : start + tile])
            for h, part in enumerate((upper, lower)):
                out_ref[turn, group, 0, h, :tile, :] = kv[
                    start : start + tile, h * 2 * HEAD : (h + 1) * 2 * HEAD
                ]
                out_ref[turn, group, 0, h, tile:, :] = part.astype(bf16)

    shape = (turns, groups, slots, 2, 3 * half, 2 * HEAD)
    return pl.pallas_call(
        kernel,
        grid=(slots,),
        in_specs=[
            pl.BlockSpec((rows, width), lambda i: (0, 0)),
            slot_rows(weights, KV_ROWS, 4 * HEAD),
            slot_rows(weights, Q_ROWS, 2 * HEAD),
        ],
        out_specs=pl.BlockSpec(
            (turns, groups, 1, 2, 3 * half, 2 * HEAD), lambda i: (0, 0, i, 0, 0, 0)
        ),
        out_shape=jax.ShapeDtypeStruct(shape, bf16),
        compiler_params=pltpu.CompilerParams(vmem_limit_bytes=60 << 20),
        cost_estimate=pl.CostEstimate(
            flops=2 * rows * width * slots * 6 * HEAD,
            bytes_accessed=2 * (rows + slots * 6 * HEAD) * width,
            transcendentals=0,
        ),
        name="project_pack",
    )(x, weights, weights)


def unpack_project(blocks, weights, items, groups):
    turns = len(blocks)
    slots = weights.shape[0]
    half = blocks[0].shape[3]
    tile = 2 * half
    width = weights.shape[2]

    def kernel(*refs):
        ins, w_ref, flat_ref, out_ref = refs[:turns], refs[turns], refs[turns + 1], refs[turns + 2]
        slot = pl.program_id(0)
        for start, turn, group in tile_places(items, turns, groups, tile):
            pair = [ins[turn][group, 0, h].astype(f32) for h in range(2)]
            upper, lower = swap_pairs(*pair)
            flat_ref[start : start + half, :] = upper.astype(bf16)
            flat_ref[start + half : start + tile, :] = lower.astype(bf16)
        part = dot_nn(flat_ref[...], w_ref[0])

        @pl.when(slot == 0)
        def _():
            out_ref[...] = part

        @pl.when(slot > 0)
        def _():
            out_ref[...] += part

    return pl.pallas_call(
        kernel,
        grid=(slots,),
        in_specs=[
            pl.BlockSpec((groups, 1, 2, half, 2 * HEAD), lambda i: (0, i, 0, 0, 0))
            for _ in range(turns)
        ]
        + [slot_rows(weights, SO_ROWS, 2 * HEAD)],
        out_specs=[
            pl.BlockSpec((items * tile, 2 * HEAD), lambda i: (0, i)),
            pl.BlockSpec((items * tile, width), lambda i: (0, 0)),
        ],
        out_shape=[
            jax.ShapeDtypeStruct((items * tile, slots * 2 * HEAD), bf16),
            jax.ShapeDtypeStruct((items * tile, width), f32),
        ],
        compiler_params=pltpu.CompilerParams(vmem_limit_bytes=60 << 20),
        cost_estimate=pl.CostEstimate(
            flops=2 * items * tile * width * slots * 2 * HEAD,
            bytes_accessed=4 * items * tile * width,
            transcendentals=0,
        ),
        name="unpack_project",
    )(*blocks, weights)


def back_pack(x, weights, items, turns, groups):
    rows, width = x.shape
    slots = weights.shape[0]
    tile = rows // items
    half = tile // 2

    def kernel(x_ref, w_ref, out_ref):
        grads = dot_nt(x_ref[...], w_ref[0])
        for start, turn, group in tile_places(items, turns, groups, tile):
            pair = swap_pairs(grads[start : start + half], grads[start + half : start + tile])
            for h, part in enumerate(pair):
                out_ref[turn, group, 0, h] = part.astype(bf16)

    return pl.pallas_call(
        kernel,
        grid=(slots,),
        in_specs=[
            pl.BlockSpec((rows, width), lambda i: (0, 0)),
            slot_rows(weights, SO_ROWS, 2 * HEAD),
        ],
        out_specs=pl.BlockSpec(
            (turns, groups, 1, 2, half, 2 * HEAD), lambda i: (0, 0, i, 0, 0, 0)
        ),
        out_shape=jax.ShapeDtypeStruct((turns, groups, slots, 2, half, 2 * HEAD), bf16),
        compiler_params=pltpu.CompilerParams(vmem_limit_bytes=60 << 20),
        cost_estimate=pl.CostEstimate(
            flops=2 * rows * width * slots * 2 * HEAD,
            bytes_accessed=2 * (rows + slots * 2 * HEAD) * width,
            transcendentals=0,
        ),
        name="back_pack",
    )(x, weights)


def unpack_back(blocks, weights, items, groups):
    turns = len(blocks)
    slots, _, width = weights.shape
    half = blocks[0].shape[3] // 3
    tile = 2 * half
    rows = items * tile

    def kernel(*refs):
        ins = refs[:turns]
        kv_ref, q_ref, flat_ref, out_ref = refs[turns:]
        slot = pl.program_id(0)
        for start, turn, group in tile_places(items, turns, groups, tile):
            pair = []
            for h in range(2):
                flat_ref[0, start : start + tile, h * 2 * HEAD : (h + 1) * 2 * HEAD] = ins[turn][
                    group, 0, h, :tile, :
                ]
                pair.append(ins[turn][group, 0, h, tile:, :].astype(f32))
            upper, lower = swap_pairs(*pair)
            flat_ref[0, start : start + half, 4 * HEAD :] = upper.astype(bf16)
            flat_ref[0, start + half : start + tile, 4 * HEAD :] = lower.astype(bf16)
        part = dot_nn(flat_ref[0, :, : 4 * HEAD], kv_ref[0])
        part = part + dot_nn(flat_ref[0, :, 4 * HEAD :], q_ref[0])

        @pl.when(slot == 0)
        def _():
            out_ref[...] = part

        @pl.when(slot > 0)
        def _():
            out_ref[...] += part

    return pl.pallas_call(
        kernel,
        grid=(slots,),
        in_specs=[
            pl.BlockSpec((groups, 1, 2, 3 * half, 2 * HEAD), lambda i: (0, i, 0, 0, 0))
            for _ in range(turns)
        ]
        + [slot_rows(weights, KV_ROWS, 4 * HEAD), slot_rows(weights, Q_ROWS, 2 * HEAD)],
        out_specs=[
            pl.BlockSpec((1, rows, 6 * HEAD), lambda i: (i, 0, 0)),
            pl.BlockSpec((rows, width), lambda i: (0, 0)),
        ],
        out_shape=[
            jax.ShapeDtypeStruct((slots, rows, 6 * HEAD), bf16),
            jax.ShapeDtypeStruct((rows, width), f32),
        ],
        compiler_params=pltpu.CompilerParams(vmem_limit_bytes=60 << 20),
        cost_estimate=pl.CostEstimate(
            flops=2 * rows * width * slots * 6 * HEAD,
            bytes_accessed=4 * rows * width,
            transcendentals=0,
        ),
        name="unpack_back",
    )(*blocks, weights, weights)


def norm_forward(base, branch, gate, shift, scale):
    items, tile, width = base.shape

    def kernel(base_ref, branch_ref, gate_ref, shift_ref, scale_ref, sum_ref, out_ref):
        value = base_ref[0] + gate_ref[0] * branch_ref[0]
        hat, _ = norm_parts(value)
        sum_ref[0] = value
        out_ref[0] = (hat * (1.0 + scale_ref[0]) + shift_ref[0]).astype(bf16)

    tile_spec = pl.BlockSpec((1, tile, width), lambda i: (i, 0, 0))
    piece_spec = pl.BlockSpec((1, 1, width), lambda i: (i, 0, 0))
    return pl.pallas_call(
        kernel,
        grid=(items,),
        in_specs=[tile_spec, tile_spec, piece_spec, piece_spec, piece_spec],
        out_specs=[tile_spec, tile_spec],
        out_shape=[
            jax.ShapeDtypeStruct(base.shape, f32),
            jax.ShapeDtypeStruct(base.shape, bf16),
        ],
        compiler_params=pltpu.CompilerParams(vmem_limit_bytes=60 << 20),
        cost_estimate=pl.CostEstimate(
            flops=16 * items * tile * width,
            bytes_accessed=14 * items * tile * width,
            transcendentals=0,
        ),
        name="norm_forward",
    )(base, branch, gate, shift, scale)


def norm_backward(g, value, incoming, branch, scale, gate):
    items, tile, width = g.shape

    def kernel(g_ref, value_ref, in_ref, branch_ref, scale_ref, gate_ref, *outs):
        out_ref, gated_ref, low_ref, sums_ref = outs
        hat, inverse = norm_parts(value_ref[0])
        incoming = in_ref[0]
        sums_ref[0, 0:1] = jnp.sum(incoming, axis=0, keepdims=True)
        sums_ref[0, 1:2] = jnp.sum(incoming * hat, axis=0, keepdims=True)
        sums_ref[0, 2:3] = jnp.sum(g_ref[0] * branch_ref[0], axis=0, keepdims=True)
        out = g_ref[0] + norm_back(hat, inverse, incoming * (1.0 + scale_ref[0]))
        out_ref[0] = out
        gated_ref[0] = (gate_ref[0] * out).astype(bf16)
        low_ref[0] = out.astype(bf16)

    tile_spec = pl.BlockSpec((1, tile, width), lambda i: (i, 0, 0))
    piece_spec = pl.BlockSpec((1, 1, width), lambda i: (i, 0, 0))
    return pl.pallas_call(
        kernel,
        grid=(items,),
        in_specs=[tile_spec] * 4 + [piece_spec, piece_spec],
        out_specs=[
            tile_spec,
            tile_spec,
            tile_spec,
            pl.BlockSpec((1, 3, width), lambda i: (i, 0, 0)),
        ],
        out_shape=[
            jax.ShapeDtypeStruct(g.shape, f32),
            jax.ShapeDtypeStruct(g.shape, bf16),
            jax.ShapeDtypeStruct(g.shape, bf16),
            jax.ShapeDtypeStruct((items, 3, width), f32),
        ],
        compiler_params=pltpu.CompilerParams(vmem_limit_bytes=60 << 20),
        cost_estimate=pl.CostEstimate(
            flops=30 * items * tile * width,
            bytes_accessed=24 * items * tile * width,
            transcendentals=0,
        ),
        name="norm_backward",
    )(g, value, incoming, branch, scale, gate)


def out_project(mixed, weights):
    tp, items, tile, local = mixed.shape
    slots, _, width = weights.shape
    rows = items * tile

    def kernel(x_ref, w_ref, out_ref):
        slot = pl.program_id(0)
        part = dot_nn(x_ref[0].reshape(rows, local // 2), w_ref[0])

        @pl.when(slot == 0)
        def _():
            out_ref[...] = part

        @pl.when(slot > 0)
        def _():
            out_ref[...] += part

    return pl.pallas_call(
        kernel,
        grid=(slots,),
        in_specs=[
            pl.BlockSpec((1, items, tile, local // 2), lambda i: (i % tp, 0, 0, i // tp)),
            slot_rows(weights, OUT_ROWS, 2 * HEAD),
        ],
        out_specs=pl.BlockSpec((rows, width), lambda i: (0, 0)),
        out_shape=jax.ShapeDtypeStruct((rows, width), f32),
        compiler_params=pltpu.CompilerParams(vmem_limit_bytes=60 << 20),
        cost_estimate=pl.CostEstimate(
            flops=2 * rows * width * tp * local,
            bytes_accessed=4 * rows * width,
            transcendentals=0,
        ),
        name="out_project",
    )(mixed, weights)


def out_back(x, weights, shape):
    tp, items, tile, local = shape
    rows, width = x.shape

    def kernel(x_ref, w_ref, out_ref):
        part = dot_nt(x_ref[...], w_ref[0])
        out_ref[0] = part.astype(bf16).reshape(items, tile, local // 2)

    return pl.pallas_call(
        kernel,
        grid=(2 * tp,),
        in_specs=[
            pl.BlockSpec((rows, width), lambda i: (0, 0)),
            slot_rows(weights, OUT_ROWS, 2 * HEAD),
        ],
        out_specs=pl.BlockSpec((1, items, tile, local // 2), lambda i: (i % tp, 0, 0, i // tp)),
        out_shape=jax.ShapeDtypeStruct(shape, bf16),
        compiler_params=pltpu.CompilerParams(vmem_limit_bytes=60 << 20),
        cost_estimate=pl.CostEstimate(
            flops=2 * rows * width * tp * local,
            bytes_accessed=4 * rows * width,
            transcendentals=0,
        ),
        name="out_back",
    )(x, weights)


def first_kernel(tokens, shift, scale, w, tp):
    rows, items, cols, width = tokens.shape
    cols_here = cols // tp
    tile = rows * cols_here
    local = w.shape[1]

    def kernel(x_ref, shift_ref, scale_ref, w_ref, in_ref, q_ref):
        hat, _ = norm_parts(x_ref[...].astype(f32).reshape(rows, cols, width))
        value = hat * (1.0 + scale_ref[0]) + shift_ref[0]
        for t in range(tp):
            part = value[:, t * cols_here : (t + 1) * cols_here, :].reshape(tile, width)
            in_ref[0, t * tile : (t + 1) * tile, :] = part.astype(bf16)
        q = dot_nn(in_ref[0], w_ref[...]).astype(bf16).astype(f32) * 0.125
        q_ref[0] = q.astype(bf16)

    piece_spec = pl.BlockSpec((1, 1, width), lambda i: (i, 0, 0))
    return pl.pallas_call(
        kernel,
        grid=(items,),
        in_specs=[
            pl.BlockSpec((rows, 1, cols, width), lambda i: (0, i, 0, 0)),
            piece_spec,
            piece_spec,
            pl.BlockSpec(w.shape, lambda i: (0, 0)),
        ],
        out_specs=[
            pl.BlockSpec((1, tp * tile, width), lambda i: (i, 0, 0)),
            pl.BlockSpec((1, tp * tile, local), lambda i: (i, 0, 0)),
        ],
        out_shape=[
            jax.ShapeDtypeStruct((items, tp * tile, width), bf16),
            jax.ShapeDtypeStruct((items, tp * tile, local), bf16),
        ],
        compiler_params=pltpu.CompilerParams(vmem_limit_bytes=60 << 20),
        cost_estimate=pl.CostEstimate(
            flops=2 * items * tp * tile * width * local,
            bytes_accessed=4 * items * tp * tile * width,
            transcendentals=0,
        ),
        name="first_kernel",
    )(tokens, shift, scale, w)


def key_value_kernel(context, w_key, w_value_t):
    items, keys, depth = context.shape
    local = w_key.shape[1]
    step = 4096 if keys % 4096 == 0 else keys

    def kernel(x_ref, wk_ref, wv_ref, k_ref, vt_ref):
        k_ref[0] = dot_nn(x_ref[0], wk_ref[...]).astype(bf16)
        vt_ref[0] = dot_nt(wv_ref[...], x_ref[0]).astype(bf16)

    return pl.pallas_call(
        kernel,
        grid=(items, keys // step),
        in_specs=[
            pl.BlockSpec((1, step, depth), lambda i, j: (i, j, 0)),
            pl.BlockSpec(w_key.shape, lambda i, j: (0, 0)),
            pl.BlockSpec(w_value_t.shape, lambda i, j: (0, 0)),
        ],
        out_specs=[
            pl.BlockSpec((1, step, local), lambda i, j: (i, j, 0)),
            pl.BlockSpec((1, local, step), lambda i, j: (i, 0, j)),
        ],
        out_shape=[
            jax.ShapeDtypeStruct((items, keys, local), bf16),
            jax.ShapeDtypeStruct((items, local, keys), bf16),
        ],
        compiler_params=pltpu.CompilerParams(vmem_limit_bytes=60 << 20),
        cost_estimate=pl.CostEstimate(
            flops=4 * items * keys * depth * local,
            bytes_accessed=2 * items * keys * (depth + 2 * local),
            transcendentals=0,
        ),
        name="key_value_kernel",
    )(context, w_key, w_value_t)


def key_value_grads(dk_t, dv_t, context, start):
    items, local, keys = dk_t.shape
    depth = context.shape[2]
    step = 4096 if keys % 4096 == 0 else keys

    def kernel(dk_ref, dv_ref, x_ref, out_ref):
        first = (pl.program_id(0) == 0) & (pl.program_id(1) == 0)
        both = jnp.concatenate([dk_ref[0], dv_ref[0]], axis=0)
        part = dot_nn(both, x_ref[0])

        @pl.when(first)
        def _():
            out_ref[...] = part

        @pl.when(jnp.logical_not(first))
        def _():
            out_ref[...] += part

    grads_spec = pl.BlockSpec((1, local, step), lambda i, j: (i, 0, j))
    return pl.pallas_call(
        kernel,
        grid=(items, keys // step),
        in_specs=[
            grads_spec,
            grads_spec,
            pl.BlockSpec((1, step, depth), lambda i, j: (i + start, j, 0)),
        ],
        out_specs=pl.BlockSpec((2 * local, depth), lambda i, j: (0, 0)),
        out_shape=jax.ShapeDtypeStruct((2 * local, depth), f32),
        compiler_params=pltpu.CompilerParams(vmem_limit_bytes=60 << 20),
        cost_estimate=pl.CostEstimate(
            flops=4 * items * keys * depth * local,
            bytes_accessed=2 * items * keys * (depth + 2 * local),
            transcendentals=0,
        ),
        name="key_value_grads",
    )(dk_t, dv_t, context)


def feed_forward(x, g, up, down):
    rows, width = x.shape
    slots, _, hidden = up.shape
    parts = 4 if rows % 64 == 0 else 1
    size = rows // parts

    def kernel(x_ref, g_ref, up_ref, down_ref, active_ref, dh_ref, branch_ref, back_ref):
        slot = pl.program_id(0)

        @pl.when(slot == 0)
        def _():
            branch_ref[...] = jnp.zeros_like(branch_ref)
            back_ref[...] = jnp.zeros_like(back_ref)

        def products(r):
            mine = pl.ds(r * size, size)
            return dot_nn(x_ref[mine, :], up_ref[0]), dot_nt(g_ref[mine, :], down_ref[0])

        ahead = products(0)
        for r in range(parts):
            h, da = ahead
            ahead = products(r + 1) if r + 1 < parts else None
            mine = pl.ds(r * size, size)
            below = 0.5 * (1.0 + lax.erf(h * 0.7071067811865476))
            slope = below + h * (jnp.exp(h * h * -0.5) * 0.3989422804014327)
            active = (h * below).astype(bf16)
            dh = (da * slope).astype(bf16)
            active_ref[0, mine, :] = active
            dh_ref[0, mine, :] = dh
            branch_ref[mine, :] += dot_nn(active, down_ref[0])
            back_ref[mine, :] += dot_nt(dh, up_ref[0])

    rows_spec = pl.BlockSpec((rows, width), lambda i: (0, 0))
    hidden_spec = pl.BlockSpec((1, rows, hidden), lambda i: (i, 0, 0))
    return pl.pallas_call(
        kernel,
        grid=(slots,),
        in_specs=[
            rows_spec,
            rows_spec,
            pl.BlockSpec((1, width, hidden), lambda i: (i, 0, 0)),
            pl.BlockSpec((1, hidden, width), lambda i: (i, 0, 0)),
        ],
        out_specs=[hidden_spec, hidden_spec, rows_spec, rows_spec],
        out_shape=[
            jax.ShapeDtypeStruct((slots, rows, hidden), bf16),
            jax.ShapeDtypeStruct((slots, rows, hidden), bf16),
            jax.ShapeDtypeStruct((rows, width), f32),
            jax.ShapeDtypeStruct((rows, width), f32),
        ],
        compiler_params=pltpu.CompilerParams(vmem_limit_bytes=60 << 20),
        cost_estimate=pl.CostEstimate(
            flops=8 * slots * rows * width * hidden,
            bytes_accessed=4 * slots * width * hidden,
            transcendentals=2 * slots * rows * hidden,
        ),
        name="feed_forward",
    )(x, g, up, down)


def weight_terms(buffer, shape, lhs, lhs_block, lhs_place, rhs, tp, size, first):
    count, width = rhs.shape
    share = shape[-1]
    seq = width // share
    depth = lhs_block[-1]
    by_core = len(shape) == 5

    def kernel(*refs):
        a_ref, b_ref, out_ref = refs[0], refs[1], refs[-1]
        a = a_ref[...]
        if len(lhs_block) > 3:
            a = a.astype(f32)
        a = a.reshape(count, depth).astype(bf16)
        terms = lax.dot_general(a, b_ref[...], (((0,), (0,)), ((), ())), preferred_element_type=f32)
        for s in range(seq):
            block = terms[:, s * share : (s + 1) * share].astype(bf16)
            if by_core:
                out_ref[s % 2, 0, s // 2] = block
            else:
                out_ref[s] = block

    return pl.pallas_call(
        kernel,
        grid=(tp, 2),
        in_specs=[
            pl.BlockSpec(lhs_block, lhs_place),
            pl.BlockSpec(rhs.shape, lambda t, c: (0, 0)),
        ]
        + ([] if buffer is None else [pl.BlockSpec(memory_space=pl.ANY)]),
        out_specs=pl.BlockSpec((2, 1, seq // 2, size, share), lambda t, c: (0, t, 0, first // size + c, 0))
        if by_core
        else pl.BlockSpec((seq, size, share), lambda t, c: (t, first // size + c, 0)),
        out_shape=jax.ShapeDtypeStruct(shape, bf16),
        input_output_aliases={} if buffer is None else {2: 0},
        compiler_params=pltpu.CompilerParams(vmem_limit_bytes=60 << 20),
        cost_estimate=pl.CostEstimate(
            flops=4 * tp * count * depth * width,
            bytes_accessed=4 * tp * (count + width) * depth,
            transcendentals=0,
        ),
        name="weight_terms",
    )(lhs, rhs, *([] if buffer is None else [buffer]))


def last_kernel(buffer, tokens, scale, middle, dq, small, start):
    rows, _, cols, width = tokens.shape
    tp, items, queries, local = dq.shape
    slots = small.shape[0]
    cols_here = cols // tp
    tile = rows * cols_here
    slot_width = local // 2

    def kernel(x_ref, scale_ref, middle_ref, dq_ref, w_ref, *refs):
        out_ref, sums_ref = refs[-2:]
        hat, inverse = norm_parts(x_ref[...].astype(f32).reshape(rows, cols, width))
        weights = w_ref[...].reshape(tp * local, width)
        shift_sum = jnp.zeros((1, width), f32)
        scale_sum = jnp.zeros((1, width), f32)
        for t in range(tp):
            pieces = [
                dq_ref[u, 0, t * tile : (t + 1) * tile, c * slot_width : (c + 1) * slot_width]
                for c in range(2)
                for u in range(tp)
            ]
            g = dot_nn(jnp.concatenate(pieces, axis=1), weights)
            mine = slice(t * cols_here, (t + 1) * cols_here)
            hat_t = hat[:, mine, :].reshape(tile, width)
            inverse_t = inverse[:, mine, :].reshape(tile, 1)
            shift_sum = shift_sum + jnp.sum(g, axis=0, keepdims=True)
            scale_sum = scale_sum + jnp.sum(g * hat_t, axis=0, keepdims=True)
            value = middle_ref[t, 0].astype(f32) + norm_back(
                hat_t, inverse_t, g * (1.0 + scale_ref[0])
            )
            out_ref[:, 0, mine, :] = value.reshape(rows, cols_here, width)
        sums_ref[0, 0:1, :] = shift_sum
        sums_ref[0, 1:2, :] = scale_sum

    return pl.pallas_call(
        kernel,
        grid=(items,),
        in_specs=[
            pl.BlockSpec((rows, 1, cols, width), lambda i: (0, i + start, 0, 0)),
            pl.BlockSpec((1, 1, width), lambda i: (i + start, 0, 0)),
            pl.BlockSpec((tp, 1, tile, width), lambda i: (0, i + start, 0, 0)),
            pl.BlockSpec((tp, 1, queries, local), lambda i: (0, i, 0, 0)),
            pl.BlockSpec((slots, slot_width, width), lambda i: (0, QUERY_ROWS // slot_width, 0)),
        ]
        + ([] if buffer is None else [pl.BlockSpec(memory_space=pl.ANY)]),
        out_specs=[
            pl.BlockSpec((rows, 1, cols, width), lambda i: (0, i + start, 0, 0)),
            pl.BlockSpec((1, 2, width), lambda i: (i, 0, 0)),
        ],
        out_shape=[
            jax.ShapeDtypeStruct(tokens.shape, f32),
            jax.ShapeDtypeStruct((items, 2, width), f32),
        ],
        input_output_aliases={} if buffer is None else {5: 0},
        compiler_params=pltpu.CompilerParams(vmem_limit_bytes=60 << 20),
        cost_estimate=pl.CostEstimate(
            flops=2 * items * queries * width * tp * local,
            bytes_accessed=10 * items * queries * width,
            transcendentals=0,
        ),
        name="last_kernel",
    )(tokens, scale, middle, dq, small, *([] if buffer is None else [buffer]))


def exchange(x, axis):
    return lax.all_to_all(x, axis, 0, 0, tiled=True)


def gather(x, axis):
    names = axis if isinstance(axis, tuple) else (axis,)
    count = 1
    for name in names:
        count *= lax.axis_size(name)
    return exchange(jnp.broadcast_to(x[None], (count,) + x.shape), axis)


def reduce_blocks(x, axis):
    return jnp.sum(exchange(x.astype(bf16), axis).astype(f32), axis=0)


def body(
    tokens,
    context,
    group_ids,
    source_table,
    w_query,
    w_key,
    w_value,
    w_out,
    w_self_query,
    w_self_key,
    w_self_value,
    w_self_out,
    w_up,
    w_down,
    w_deconv,
    deconv_bias,
    out_cotangent,
    plane_cotangent,
):
    rows_here, items, plane_cols, width = tokens.shape
    cols_here = out_cotangent.shape[2]
    tp = lax.axis_size("tp")
    seq = lax.axis_size("seq")
    both_axes = ("seq", "tp")
    devices = tp * seq
    local = w_query.shape[1]
    hidden_here = w_up.shape[1]
    slots = 2 * tp
    slot_heads = local // HEAD // 2
    slot_width = local // 2
    heads = slots * slot_heads
    tile = rows_here * cols_here
    half = tile // 2
    groups = devices // heads
    turns = -(-items // groups)
    share = width // seq
    fast = slot_heads == 2 and half % 16 == 0 and items == groups * turns and share % 128 == 0
    me_tp = lax.axis_index("tp")
    core = lax.axis_index("seq") % 2

    picker = (group_ids[:, None] == jnp.arange(GROUPS, dtype=jnp.int32)[None, :]).astype(f32)
    mods = jnp.dot(picker, source_table, precision=highest).reshape(items, 9, 1, width)

    def piece(index):
        return mods[:, index]

    def dot(spec, a, b):
        return jnp.einsum(spec, a, b, preferred_element_type=f32)

    def to_tile(x):
        return x.transpose(1, 0, 2, 3).reshape(items, tile, width)

    def from_tile(x):
        return x.reshape(items, rows_here, cols_here, width).transpose(1, 0, 2, 3)

    teams = [
        [(2 * pair + c) * tp + t for c in range(2) for t in range(tp)] for pair in range(seq // 2)
    ]

    def whole(x):
        return lax.all_gather(x, both_axes, axis=0, tiled=False, axis_index_groups=teams)

    def my_rows(x):
        return lax.dynamic_slice_in_dim(x, core * slot_width, slot_width, 0)

    def my_columns(x):
        size = x.shape[1] // 2
        return lax.dynamic_slice_in_dim(x, core * size, size, 1)

    key_value = jnp.stack(
        [
            my_columns(w_self_key).T.reshape(slot_heads, HEAD, width),
            my_columns(w_self_value).T.reshape(slot_heads, HEAD, width),
        ],
        axis=1,
    ).reshape(2 * slot_width, width)
    small = whole(
        jnp.concatenate(
            [
                key_value,
                my_columns(w_self_query).T,
                my_rows(w_self_out),
                my_rows(w_out),
                my_columns(w_query).T,
            ],
            axis=0,
        )
    )
    cuts = [slot_width * k for k in (0, 2, 3, 4, 5, 6)]
    kv_slots, q_slots, so_slots, out_slots, query_slots = [
        small[:, a:b] for a, b in zip(cuts[:-1], cuts[1:])
    ]
    up_slots = whole(my_columns(w_up))
    down_slots = whole(
        lax.dynamic_slice_in_dim(w_down, core * (hidden_here // 2), hidden_here // 2, 0)
    )

    def by_tp(x):
        return x.reshape(2, tp, slot_width, width).transpose(1, 0, 2, 3).reshape(tp, local, width)

    incoming = plane_cotangent.reshape(2 * rows_here, items, 2 * cols_here, COUT)
    plane_row = (lax.axis_index("seq") * rows_here + jnp.arange(rows_here, dtype=jnp.int32)) % PLANE
    upper_keep = (plane_row != 0).astype(f32)
    lower_keep = (plane_row != PLANE - 1).astype(f32)
    grad_edges = with_halo(incoming, (("seq", 0), ("tp", 2)), 1)
    if fast:
        first_in, queries = first_kernel(tokens, piece(0), piece(1), w_query, tp)
    else:
        ordered = (
            tokens.reshape(rows_here, items, tp, cols_here, width)
            .transpose(1, 2, 0, 3, 4)
            .reshape(items, tp * tile, width)
        )
        first_hat, first_inv = norm_parts(ordered.astype(f32))
        first_in = (first_hat * (1.0 + piece(1)) + piece(0)).astype(bf16)
        queries = dot("iqd,de->iqe", first_in, w_query).astype(bf16) * bf16(0.125)
    image = context.transpose(1, 0, 2)
    queries, grad_edges = lax.optimization_barrier((queries, grad_edges))
    keys, values_t = key_value_kernel(image, w_key, w_value.T)
    upper_mask = upper_keep.astype(bf16)[:, None, None, None]
    lower_mask = lower_keep.astype(bf16)[:, None, None, None]
    first_pair = grad_edges[:-2].reshape(rows_here, 2, items, 2 * cols_here + 2, COUT)
    last_pair = grad_edges[2:].reshape(rows_here, 2, items, 2 * cols_here + 2, COUT)
    row_taps = jnp.stack(
        [
            first_pair[:, 0] * upper_mask,
            first_pair[:, 1],
            last_pair[:, 0],
            last_pair[:, 1] * lower_mask,
        ],
        axis=3,
    )
    left_pair = row_taps[:, :, :-2].reshape(rows_here, items, cols_here, 2, 4, COUT)
    right_pair = row_taps[:, :, 2:].reshape(rows_here, items, cols_here, 2, 4, COUT)
    tap_grads = jnp.stack(
        [
            left_pair[:, :, :, 0],
            left_pair[:, :, :, 1],
            right_pair[:, :, :, 0],
            right_pair[:, :, :, 1],
        ],
        axis=4,
    )
    tap_grads = tap_grads.reshape(rows_here, items, cols_here, 16 * COUT)
    grad_result = to_tile(out_cotangent.astype(f32) + dot("rict,dt->ricd", tap_grads, w_deconv))
    grad_bias = jnp.sum(incoming.astype(f32), axis=(0, 1, 2))
    grad_mlp = (piece(8) * grad_result).astype(bf16)
    mixed, mixed_wide, cross_logs = cross_forward(queries, keys, values_t, tp)
    mixed_tile = exchange(mixed, "tp")
    if fast:
        branch_a = out_project(mixed_tile, small).reshape(items, tile, width)
    else:
        branch_a = dot("time,tef->imf", mixed_tile, by_tp(out_slots))
    residual = to_tile(lax.dynamic_slice_in_dim(tokens, me_tp * cols_here, cols_here, 2)).astype(f32)
    middle, self_in = norm_forward(residual, branch_a, piece(2), piece(3), piece(4))

    flat = (items * tile, width)
    spare = groups * turns - items

    def spread_items(x):
        if spare:
            x = jnp.pad(x, ((0, 0), (0, spare)) + ((0, 0),) * (x.ndim - 2))
        return x.reshape((slots, groups, turns) + x.shape[2:])

    def pack_keys(x):
        x = spread_items(x.reshape(slots, items, tile, slot_heads, 2 * HEAD))
        return x.transpose(2, 1, 0, 4, 3, 5).reshape(turns, devices, tile, 2 * HEAD)

    def unpack_keys(x):
        x = x.reshape(turns, groups, slots, slot_heads, tile, 2 * HEAD).transpose(2, 1, 0, 4, 3, 5)
        x = x.reshape(slots, groups * turns, tile, 2 * slot_width)[:, :items]
        return x.reshape(slots, items * tile, 2 * slot_width)

    def pack_rows(x):
        x = spread_items(x.reshape(slots, items, 2, half, slot_heads, HEAD))
        return x.transpose(2, 1, 0, 5, 4, 3, 6).reshape(turns, devices, half, 2 * HEAD)

    def unpack_rows(x):
        x = x.reshape(turns, groups, slots, slot_heads, half, 2, HEAD).transpose(2, 1, 0, 5, 4, 3, 6)
        x = x.reshape(slots, groups * turns, tile, slot_width)[:, :items]
        return x.reshape(slots, items * tile, slot_width)

    if fast:
        sends = project_pack(self_in.reshape(flat), small, items, turns, groups)
        sends = sends.reshape(turns, devices, 3 * half, 2 * HEAD)
        sends = [sends[turn] for turn in range(turns)]
    else:
        kv_sends = pack_keys(dot("nd,xed->xne", self_in.reshape(flat), kv_slots).astype(bf16))
        q_sends = dot("nd,xed->xne", self_in.reshape(flat), q_slots).astype(bf16)
        q_sends = pack_rows(q_sends * bf16(0.125))
        parts = [
            [
                exchange(kv_sends[turn], both_axes).reshape(devices * tile, 2 * HEAD),
                exchange(q_sends[turn], both_axes).reshape(devices * half, 2 * HEAD),
            ]
            for turn in range(turns)
        ]
    if fast:
        parts, forward = [], []
        for turn in range(turns):
            if turn >= 2:
                sends[turn], forward[turn - 2] = lax.optimization_barrier(
                    (sends[turn], forward[turn - 2])
                )
            arrived = exchange(sends[turn], both_axes)
            if turn == 0:
                arrived, grad_result, grad_mlp = lax.optimization_barrier(
                    (arrived, grad_result, grad_mlp)
                )
            parts.append([arrived])
            forward.append(self_forward(parts[turn], devices, half))
    else:
        forward = [self_forward(parts[turn], devices, half) for turn in range(turns)]
    outs = [x[0] for x in forward]
    if fast:
        outs[0], parts[-1][0] = lax.optimization_barrier((outs[0], parts[-1][0]))
    so_back = [exchange(so.reshape(devices, half, 2 * HEAD), both_axes) for so in outs]
    if fast:
        blocks = [x.reshape(groups, slots, 2, half, 2 * HEAD) for x in so_back]
        so_tile, branch_s = unpack_project(blocks, small, items, groups)
    else:
        so_tile = unpack_rows(jnp.stack(so_back)).transpose(1, 0, 2)
        branch_s = dot("nxe,xed->nd", so_tile, so_slots)
        so_tile = so_tile.reshape(items * tile, heads * HEAD)
    branch_s = branch_s.reshape(items, tile, width)
    middle_two, second_in = norm_forward(middle, branch_s, piece(5), piece(6), piece(7))

    active, grad_hidden, branch_b, grad_second = feed_forward(
        second_in.reshape(flat), grad_mlp.reshape(flat), up_slots, down_slots
    )
    branch_b = branch_b.reshape(items, tile, width)
    grad_second = grad_second.reshape(items, tile, width)
    result = middle_two + piece(8) * branch_b
    out_tile = from_tile(result.astype(bf16))

    grad_mid_two, grad_self, _, sums_b = norm_backward(
        grad_result, middle_two, grad_second, branch_b, piece(7), piece(5)
    )

    widened = with_halo(out_tile, (("seq", 0), ("tp", 2)), 1)
    taps = dot("ricd,dt->rict", widened, w_deconv)
    taps = taps.reshape(rows_here + 2, items, cols_here + 2, 4, 4, COUT)
    planes = spread_taps(
        taps, upper_keep[:, None, None, None, None], lower_keep[:, None, None, None, None]
    )
    planes = planes + jnp.tile(deconv_bias, 2 * cols_here)

    def by_device(x):
        lead = x.shape[0] // tp
        x = x.reshape(lead, tp, x.shape[1], seq, share).transpose(1, 3, 0, 2, 4)
        return x.reshape(devices, -1, share).astype(bf16)

    def of_cores(x):
        return x.reshape((tp, seq // 2, 2) + x.shape[1:]).transpose(2, 0, 1, 3, 4)

    def total_near(terms, after):
        keep = lax.dynamic_index_in_dim(terms, core, 0, False)
        give = lax.dynamic_index_in_dim(terms, 1 - core, 0, False)
        got = lax.ppermute(give, "seq", [(i, i ^ 1) for i in range(seq)])
        got, _ = lax.optimization_barrier((got, after))
        x = (keep.astype(f32) + got.astype(f32)).astype(bf16)
        return lax.psum_scatter(x, "tp", scatter_dimension=0, tiled=True)[0]

    def total_far(x, after, *cuts):
        x, _ = lax.optimization_barrier((x, after))
        lines = [list(range(c, seq, 2)) for c in range(2)]
        x = lax.psum_scatter(x, "seq", scatter_dimension=0, axis_index_groups=lines, tiled=True)[0]
        return jnp.split(x.astype(f32), cuts, axis=0)

    def total(terms, *cuts):
        summed = lax.psum_scatter(terms, ("tp", "seq"), scatter_dimension=0, tiled=True)[0]
        return jnp.split(summed.astype(f32), cuts, axis=0)

    terms_deconv = dot("ricd,rict->dt", out_tile, tap_grads).astype(bf16)
    piece_rows = width // devices
    terms_deconv = (
        terms_deconv.reshape(devices, piece_rows, -1, share)
        .transpose(0, 2, 1, 3)
        .reshape(devices, -1, share)
    )
    size_b = (hidden_here // 2, hidden_here, 2 * hidden_here)
    if fast:
        shape = (2, tp, seq // 2, size_b[2] + terms_deconv.shape[1], share)
        hidden_block = (1, items * tile, size_b[0])

        def slot_place(t, c):
            return (c * tp + t, 0, 0)

        terms_b = None
        for lhs, rhs, first in (
            (grad_hidden, second_in, 0),
            (active, grad_mlp, size_b[1]),
        ):
            terms_b = weight_terms(
                terms_b, shape, lhs, hidden_block, slot_place, rhs.reshape(flat), tp, size_b[0], first
            )
        terms_b = lax.dynamic_update_slice_in_dim(terms_b, of_cores(terms_deconv), size_b[2], 3)
    else:
        terms_b = jnp.concatenate(
            [
                by_device(dot("xnf,nd->xfd", grad_hidden, second_in.reshape(flat))),
                by_device(dot("xnf,nd->xfd", active, grad_mlp.reshape(flat))),
                terms_deconv,
            ],
            axis=1,
        )
        terms_b = of_cores(terms_b)

    if fast:
        dso_send = back_pack(grad_self.reshape(flat), small, items, turns, groups)
        dso_send = dso_send.reshape(turns, devices, half, 2 * HEAD)
    else:
        dso_send = pack_rows(dot("nd,xed->xne", grad_self.reshape(flat), so_slots).astype(bf16))
    dso_send = [dso_send[turn] for turn in range(turns)]
    dso_mine, backward = [], []
    for turn in range(turns):
        if turn >= 2:
            dso_send[turn], backward[turn - 2] = lax.optimization_barrier(
                (dso_send[turn], backward[turn - 2])
            )
        arrived = exchange(dso_send[turn], both_axes).reshape(devices * half, 2 * HEAD)
        if turn == 0:
            arrived, terms_b = lax.optimization_barrier((arrived, terms_b))
        dso_mine.append(arrived)
        backward.append(
            self_backward(parts[turn], dso_mine[turn], *forward[turn][1:], devices, half)
        )
    near_b = total_near(terms_b, (backward[0][0], dso_mine[min(1, turns - 1)]))
    if fast:
        blocks = [
            exchange(x[0], both_axes).reshape(groups, slots, 2, 3 * half, 2 * HEAD)
            for x in backward
        ]
        blocks[-1], planes = lax.optimization_barrier((blocks[-1], planes))
        grad_projected, grad_third = unpack_back(blocks, small, items, groups)
    else:
        dkv = [exchange(x[0].reshape(devices, tile, 2 * HEAD), both_axes) for x in backward]
        dq = [exchange(x[1].reshape(devices, half, 2 * HEAD), both_axes) for x in backward]
        grad_projected = jnp.concatenate(
            [unpack_keys(jnp.stack(dkv)), unpack_rows(jnp.stack(dq))], axis=2
        )
        grad_third = dot(
            "xne,xed->nd", grad_projected, jnp.concatenate([kv_slots, q_slots], axis=1)
        )
    grad_up, grad_down, grad_deconv = total_far(near_b, grad_third, *size_b[1:])
    grad_third = grad_third.reshape(items, tile, width)
    grad_middle, grad_attn, middle_low, sums_s = norm_backward(
        grad_mid_two, middle, grad_third, branch_s, piece(4), piece(2)
    )

    grad_gate_a = jnp.sum(grad_middle * branch_a, axis=1)
    if fast:
        do_send = out_back(grad_attn.reshape(flat), small, mixed.shape)
    else:
        do_send = dot("imf,tef->time", grad_attn, by_tp(out_slots)).astype(bf16)
    do_mine = exchange(do_send, "tp")
    middle_all = gather(middle_low, "tp")
    early = jnp.concatenate([grad_gate_a[:, None], sums_s, sums_b], axis=1)
    early = early.transpose(1, 0, 2).reshape(7 * items, width)
    early = jnp.concatenate(
        [early, jnp.pad(grad_bias, (0, width - COUT))[None]], axis=0
    )
    spots = -(-early.shape[0] // (16 * tp)) * 16
    early = jnp.pad(early, ((0, spots * tp - early.shape[0]), (0, 0))).reshape(tp, spots, width)
    early = by_device(early)
    size_a = [slot_width * k for k in (6, 8, 10)]
    if fast:
        shape = (devices, size_a[2] + early.shape[1], share)
        terms_a = weight_terms(
            None,
            shape,
            grad_projected,
            (1, items * tile, 3 * slot_width),
            lambda t, c: (c * tp + t, 0, 0),
            self_in.reshape(flat),
            tp,
            3 * slot_width,
            0,
        )
        terms_a = weight_terms(
            terms_a,
            shape,
            so_tile,
            (items * tile, slot_width),
            lambda t, c: (0, c * tp + t),
            grad_self.reshape(flat),
            tp,
            slot_width,
            size_a[0],
        )
        terms_a = weight_terms(
            terms_a,
            shape,
            mixed_tile,
            (1, items, tile, slot_width),
            lambda t, c: (t, 0, 0, c),
            grad_attn.reshape(flat),
            tp,
            slot_width,
            size_a[1],
        )
        terms_a = lax.dynamic_update_slice_in_dim(terms_a, early, size_a[2], 1)
    else:
        so_terms = dot("ne,nd->ed", so_tile, grad_self.reshape(flat))
        terms_a = jnp.concatenate(
            [
                by_device(dot("xne,nd->xed", grad_projected, self_in.reshape(flat))),
                by_device(so_terms.reshape(slots, slot_width, width)),
                by_device(dot("time,imf->tef", mixed_tile, grad_attn)),
                early,
            ],
            axis=1,
        )
    do_mine, terms_a = lax.optimization_barrier((do_mine, terms_a))
    terms_a, grad_up = lax.optimization_barrier((terms_a, grad_up))
    grad_three, grad_self_out, grad_out, grad_early = total(terms_a, *size_a)
    first_part = items // 2
    cross = (queries, do_mine, mixed_wide, cross_logs, keys, values_t)
    one = cross_backward(*cross, 0, first_part)
    one, middle_all = lax.optimization_barrier((one, middle_all))
    dq_one = gather(one[0], "tp")
    do_late, _ = lax.optimization_barrier((do_mine, one[0]))
    two = cross_backward(queries, do_late, *cross[2:], first_part, items - first_part)
    one, two, dq_one = lax.optimization_barrier((one, two, dq_one))
    dq_two = gather(two[0], "tp")
    two, dq_two = lax.optimization_barrier((two, dq_two))
    dq_cross = jnp.concatenate([one[0], two[0]], axis=0)
    grad_three = grad_three.reshape(2, 3 * slot_width, share)
    grad_pair = grad_three[:, : 2 * slot_width].reshape(2, slot_heads, 2, HEAD, share)
    grad_self_key = grad_pair[:, :, 0].reshape(local, share).T
    grad_self_value = grad_pair[:, :, 1].reshape(local, share).T
    grad_self_query = grad_three[:, 2 * slot_width :].reshape(local, share).T

    def by_seq(x):
        return x.reshape((seq, x.shape[0] // seq) + x.shape[1:]).astype(bf16)

    grad_image = (
        key_value_grads(one[1], one[2], image, 0) + key_value_grads(two[1], two[2], image, first_part)
    ).T
    last = jnp.concatenate(
        [
            by_seq(dot("iqd,iqe->de", first_in, dq_cross)),
            by_seq(grad_image[:, :local]),
            by_seq(grad_image[:, local:]),
        ],
        axis=1,
    )
    grad_deconv, grad_image = lax.optimization_barrier((grad_deconv, grad_image))
    grad_deconv = grad_deconv.reshape(-1, piece_rows, share).transpose(1, 0, 2)
    grad_deconv = lax.all_gather(
        grad_deconv.reshape(piece_rows, 16 * COUT).astype(bf16), ("tp", "seq"), axis=0, tiled=True
    )
    last, dq_one, dq_two = lax.optimization_barrier((last, dq_one, dq_two))
    last = jnp.sum(exchange(last, "seq").astype(f32), axis=0)
    if fast:
        grad_tokens, late_one = last_kernel(None, tokens, piece(1), middle_all, dq_one, small, 0)
        grad_tokens, late_two = last_kernel(
            grad_tokens, tokens, piece(1), middle_all, dq_two, small, first_part
        )
        late = jnp.concatenate([late_one, late_two], axis=0).transpose(1, 0, 2)
    else:
        dq_all = jnp.concatenate([dq_one, dq_two], axis=1)
        grad_first = dot("tiqe,ted->iqd", dq_all, by_tp(query_slots))
        grad_shift_a = jnp.sum(grad_first, axis=1)
        grad_scale_a = jnp.sum(grad_first * first_hat, axis=1)
        grad_tokens = middle_all.astype(f32).transpose(1, 0, 2, 3).reshape(
            items, tp * tile, width
        ) + norm_back(first_hat, first_inv, grad_first * (1.0 + piece(1)))
        grad_tokens = (
            grad_tokens.reshape(items, tp, rows_here, cols_here, width)
            .transpose(2, 0, 1, 3, 4)
            .reshape(rows_here, items, plane_cols, width)
        )
        late = jnp.stack([grad_shift_a, grad_scale_a], axis=0)

    late, last = lax.optimization_barrier((late, last))
    part = 2 * items * width // tp
    mine = lax.dynamic_slice_in_dim(late.reshape(-1, share), me_tp * (part // share), part // share, 0)
    sums = gather(jnp.concatenate([mine, grad_early], axis=0), ("tp", "seq"))
    sums = sums.reshape(tp, seq, part // share + spots, share)
    late = jnp.sum(sums[:, :, : part // share], axis=1).reshape(2, items, width)
    early = sums[:, :, part // share :].transpose(0, 2, 1, 3).reshape(tp * spots, width)
    grad_bias = early[7 * items, :COUT]
    early = early[: 7 * items].reshape(7, items, width)
    depth = (last.shape[0] - share) // 2
    grad_query, grad_key, grad_value = (
        last[:share],
        last[share : share + depth],
        last[share + depth :],
    )
    late, grad_deconv = lax.optimization_barrier((late, grad_deconv))
    grad_mods = jnp.concatenate([late, early], axis=0).transpose(1, 0, 2)
    grad_table = jnp.dot(picker.T, grad_mods.reshape(items, 9 * width), precision=highest)
    return (
        out_tile,
        planes,
        grad_tokens,
        grad_query,
        grad_key,
        grad_value,
        grad_out,
        grad_self_query,
        grad_self_key,
        grad_self_value,
        grad_self_out.reshape(local, share),
        grad_up.T,
        grad_down,
        grad_deconv.astype(f32),
        grad_bias,
        grad_table,
    )


def solution(mesh):
    in_specs = (
        P("seq", None, None, None),
        P(),
        P(),
        P(),
        P(None, "tp"),
        P(None, "tp"),
        P(None, "tp"),
        P("tp", None),
        P(None, "tp"),
        P(None, "tp"),
        P(None, "tp"),
        P("tp", None),
        P(None, "tp"),
        P("tp", None),
        P(),
        P(),
        P("seq", None, "tp", None),
        P("seq", None, "tp"),
    )
    out_specs = (
        P("seq", None, "tp", None),
        P("seq", None, "tp"),
        P("seq", None, None, None),
        P("seq", "tp"),
        P("seq", "tp"),
        P("seq", "tp"),
        P("tp", "seq"),
        P("seq", "tp"),
        P("seq", "tp"),
        P("seq", "tp"),
        P("tp", "seq"),
        P("seq", "tp"),
        P("tp", "seq"),
        P(),
        P(),
        P(),
    )
    return jax.shard_map(body, mesh=mesh, in_specs=in_specs, out_specs=out_specs, check_vma=False)
```

```python
import jax
import jax.numpy as jnp
from jax import lax
from jax.experimental import pallas as pl
from jax.experimental.pallas import tpu as pltpu
from jax.sharding import PartitionSpec as P

HEAD = 64
COUT = 80
PLANE = 32
IMG = 4096
LOG2E = 1.4426950408889634
bf16 = jnp.bfloat16
f32 = jnp.float32
GROUPS = 16


highest = lax.Precision.HIGHEST
epsilon = 1e-06


def with_halo(x, sides, width):
    for axis, dim in sides:
        peers, length = (lax.axis_size(axis), x.shape[dim])
        up = [(i, (i + 1) % peers) for i in range(peers - 1)]
        down = [(j, i) for i, j in up]
        last = lax.slice_in_dim(x, length - width, length, axis=dim)
        initial = lax.slice_in_dim(x, 0, width, axis=dim)
        before = lax.ppermute(last, axis, up)
        after = lax.ppermute(initial, axis, down)
        x = jnp.concatenate([before, x, after], axis=dim)
    return x


def spread_taps(padded, upper, lower):
    even_rows = padded[1:-1, :, :, 1] + upper * padded[:-2, :, :, 3]
    odd_rows = lower * padded[2:, :, :, 0] + padded[1:-1, :, :, 2]
    rows_both = jnp.stack([even_rows, odd_rows], axis=1)
    even_cols = rows_both[:, :, :, 1:-1, 1] + rows_both[:, :, :, :-2, 3]
    odd_cols = rows_both[:, :, :, 2:, 0] + rows_both[:, :, :, 1:-1, 2]
    joined = jnp.stack([even_cols, odd_cols], axis=4)
    shape = joined.shape
    return joined.reshape(shape[0] * 2, shape[2], shape[3] * 2 * shape[5])


def norm_parts(value):
    centred = value - jnp.mean(value, axis=-1, keepdims=True)
    inverse = lax.rsqrt(jnp.mean(centred * centred, axis=-1, keepdims=True) + epsilon)
    return (centred * inverse, inverse)


def norm_back(normed, inverse, incoming):
    return inverse * (
        incoming
        - jnp.mean(incoming, axis=-1, keepdims=True)
        - normed * jnp.mean(incoming * normed, axis=-1, keepdims=True)
    )


NT = (((1,), (1,)), ((), ()))
BLOCKS = 4
KV_ROWS, Q_ROWS, SO_ROWS, OUT_ROWS, QUERY_ROWS = 0, 256, 384, 512, 640


def dot_nt(a, b):
    return lax.dot_general(a, b, NT, preferred_element_type=f32)


def dot_nn(a, b):
    return jnp.dot(a, b, preferred_element_type=f32)


def flip(x):
    return x.astype(f32).T.astype(bf16)


def chunk_of(keys):
    return 512 if keys % 512 == 0 else keys


SAFE = 40.0


def softmax_sweep(scores, values, chunks, columns, write):
    def spread(mixed, total, top):
        width = columns // len(mixed)
        inverse = 1.0 / total
        mixed = [m * inverse[:, j * width : (j + 1) * width] for j, m in enumerate(mixed)]
        write(mixed, top + jnp.log(total))

    ahead = scores(0)
    top = jnp.max(ahead, axis=0, keepdims=True)
    base = top * LOG2E
    peak = top
    total = jnp.zeros((1, columns), f32)
    mixed = None
    for c in range(chunks):
        now = ahead
        ahead = scores(c + 1) if c + 1 < chunks else None
        expon = jnp.exp2(now * LOG2E - base)
        if c > 0:
            peak = jnp.maximum(peak, jnp.max(now, axis=0, keepdims=True))
        total = total + jnp.sum(expon, axis=0, keepdims=True)
        parts = values(c, expon.astype(bf16))
        mixed = parts if mixed is None else [m + part for m, part in zip(mixed, parts)]
    spread(mixed, total, top)

    @pl.when(jnp.max(peak - top) > SAFE)
    def _():
        def body(c, carry):
            top, total, mixed = carry
            now = scores(c)
            new_top = jnp.maximum(top, jnp.max(now, axis=0, keepdims=True))
            fade = jnp.exp2((top - new_top) * LOG2E)
            expon = jnp.exp2((now - new_top) * LOG2E)
            total = total * fade + jnp.sum(expon, axis=0, keepdims=True)
            parts = values(c, expon.astype(bf16))
            width = columns // len(parts)
            mixed = [
                m * fade[:, j * width : (j + 1) * width] + part
                for j, (m, part) in enumerate(zip(mixed, parts))
            ]
            return new_top, total, mixed

        start = (
            jnp.full((1, columns), -3e38, f32),
            jnp.zeros((1, columns), f32),
            [jnp.zeros(m.shape, f32) for m in mixed],
        )
        top, total, again = lax.fori_loop(0, chunks, body, start)
        spread(again, total, top)


def at_chunk(c, step):
    return pl.ds(c * step if isinstance(c, int) else pl.multiple_of(c * step, step), step)


def cross_forward(q, k, vt, tp):
    items, queries, width = q.shape
    tile = queries // tp
    keys = k.shape[1]
    heads = width // HEAD
    step = chunk_of(keys)

    def kernel(q_ref, k_ref, vt_ref, o_ref, wide_ref, log_ref):
        pair = pl.program_id(1)
        owner = lax.broadcasted_iota(jnp.int32, (queries, width), 1) // HEAD
        both = jnp.concatenate(
            [jnp.where(owner == pair * 2 + j, q_ref[0], 0.0).astype(bf16) for j in range(2)], axis=0
        )

        def scores(c):
            return dot_nt(k_ref[0, at_chunk(c, step), :], both)

        def values(c, p):
            out = []
            for j in range(2):
                rows = pl.ds(pl.multiple_of((pair * 2 + j) * HEAD, HEAD), HEAD)
                v = vt_ref[0, rows, at_chunk(c, step)]
                out.append(dot_nn(v, p[:, j * queries : (j + 1) * queries]))
            return out

        def write(mixed, log_total):
            rows = jnp.concatenate(mixed, axis=0).T.reshape(tp, 1, tile, 2 * HEAD)
            o_ref[...] = rows.astype(bf16)
            wide_ref[...] = rows
            for j in range(2):
                log_ref[0, j] = jnp.broadcast_to(
                    log_total[:, j * queries : (j + 1) * queries], (8, queries)
                )

        softmax_sweep(scores, values, keys // step, 2 * queries, write)

    return pl.pallas_call(
        kernel,
        grid=(items, heads // 2),
        in_specs=[
            pl.BlockSpec((1, queries, width), lambda i, h: (i, 0, 0)),
            pl.BlockSpec((1, keys, width), lambda i, h: (i, 0, 0)),
            pl.BlockSpec((1, width, keys), lambda i, h: (i, 0, 0)),
        ],
        out_specs=[
            pl.BlockSpec((tp, 1, tile, 2 * HEAD), lambda i, h: (0, i, 0, h)),
            pl.BlockSpec((tp, 1, tile, 2 * HEAD), lambda i, h: (0, i, 0, h)),
            pl.BlockSpec((1, 2, 8, queries), lambda i, h: (i, h, 0, 0)),
        ],
        out_shape=[
            jax.ShapeDtypeStruct((tp, items, tile, width), bf16),
            jax.ShapeDtypeStruct((tp, items, tile, width), f32),
            jax.ShapeDtypeStruct((items, heads, 8, queries), f32),
        ],
        compiler_params=pltpu.CompilerParams(vmem_limit_bytes=60 << 20),
        cost_estimate=pl.CostEstimate(
            flops=16 * items * queries * keys * width,
            bytes_accessed=4 * items * (queries + keys) * width,
            transcendentals=items * queries * keys * heads,
        ),
        name="cross_forward",
    )(q, k, vt)


def cross_backward(q, do, o, logs, k, vt, start, items):
    _, queries, width = q.shape
    tp, _, tile, _ = do.shape
    keys = k.shape[1]
    heads = width // HEAD
    step = chunk_of(keys)

    def kernel(q_ref, do_ref, o_ref, log_ref, k_ref, vt_ref, dq_ref, dk_ref, dv_ref, qt, dot):
        head = pl.program_id(1)

        @pl.when(head == 0)
        def _():
            qt[...] = flip(q_ref[0])
            dot[...] = do_ref[...].astype(f32).reshape(queries, width).T.astype(bf16)

        mine = lax.broadcasted_iota(jnp.int32, (queries, width), 1) // HEAD == head
        q_mine = jnp.where(mine, q_ref[0], 0.0).astype(bf16)
        do_wide = jnp.where(mine, do_ref[...].astype(f32).reshape(queries, width), 0.0)
        do_mine = do_wide.astype(bf16)
        o_wide = o_ref[...].reshape(queries, width)
        delta = jnp.sum(do_wide * o_wide, axis=1, keepdims=True)
        log_total = log_ref[0, 0].T[:, :1] * LOG2E
        rows = pl.ds(pl.multiple_of(head * HEAD, HEAD), HEAD)
        qt_mine = qt[rows, :]
        dot_mine = dot[rows, :]

        def scores(c):
            s = dot_nt(q_mine, k_ref[0, pl.ds(c * step, step), :])
            return s, dot_nn(do_mine, vt_ref[0, :, pl.ds(c * step, step)])

        dq = jnp.zeros((queries, width), f32)
        ahead = scores(0)
        for c in range(keys // step):
            s, dp = ahead
            ahead = scores(c + 1) if c + 1 < keys // step else None
            p = jnp.exp2(s * LOG2E - log_total)
            ds = (p * (dp - delta)).astype(bf16)
            cols = pl.ds(c * step, step)
            dv_ref[0, :, cols] = dot_nn(dot_mine, p.astype(bf16)).astype(bf16)
            dk_ref[0, :, cols] = dot_nn(qt_mine, ds).astype(bf16)
            dq = dq + dot_nn(ds, k_ref[0, cols, :])
        dq = (dq * 0.125).astype(bf16)
        rest = jnp.where(head == 0, jnp.zeros_like(dq), dq_ref[0])
        dq_ref[0] = jnp.where(mine, dq, rest)

    rows_spec = pl.BlockSpec((1, queries, width), lambda i, h: (i + start, 0, 0))
    tiles_spec = pl.BlockSpec((tp, 1, tile, width), lambda i, h: (0, i + start, 0, 0))
    grads_spec = pl.BlockSpec((1, HEAD, keys), lambda i, h: (i, h, 0))
    return pl.pallas_call(
        kernel,
        grid=(items, heads),
        in_specs=[
            rows_spec,
            tiles_spec,
            tiles_spec,
            pl.BlockSpec((1, 1, 8, queries), lambda i, h: (i + start, h, 0, 0)),
            pl.BlockSpec((1, keys, width), lambda i, h: (i + start, 0, 0)),
            pl.BlockSpec((1, width, keys), lambda i, h: (i + start, 0, 0)),
        ],
        out_specs=[
            pl.BlockSpec((1, queries, width), lambda i, h: (i, 0, 0)),
            grads_spec,
            grads_spec,
        ],
        out_shape=[
            jax.ShapeDtypeStruct((items, queries, width), bf16),
            jax.ShapeDtypeStruct((items, width, keys), bf16),
            jax.ShapeDtypeStruct((items, width, keys), bf16),
        ],
        scratch_shapes=[pltpu.VMEM((width, queries), bf16), pltpu.VMEM((width, queries), bf16)],
        compiler_params=pltpu.CompilerParams(vmem_limit_bytes=60 << 20),
        cost_estimate=pl.CostEstimate(
            flops=40 * items * queries * keys * width,
            bytes_accessed=8 * items * (queries + keys) * width,
            transcendentals=items * queries * keys * heads,
        ),
        name="cross_backward",
    )(q, do, o, logs, k, vt)


def split_wide(x):
    low = lax.broadcasted_iota(jnp.int32, x.shape, 1) < HEAD
    wide = x.astype(f32)
    first = jnp.where(low, wide, 0.0)
    second = jnp.where(low, pltpu.roll(wide, HEAD, 1), 0.0)
    return jnp.concatenate([first, second], axis=0)


def split_pair(x):
    return split_wide(x).astype(bf16)


def part_specs(parts, half):
    if len(parts) == 1:
        return [pl.BlockSpec(parts[0].shape, lambda i: (0, 0, 0))]
    rows = parts[1].shape[0] // BLOCKS
    return [
        pl.BlockSpec(parts[0].shape, lambda i: (0, 0)),
        pl.BlockSpec((rows, 2 * HEAD), lambda i: (i, 0)),
    ]


def read_keys(refs, half):
    if len(refs) == 2:
        return refs[0][...]
    devices = refs[0].shape[0]
    return refs[0][:, : 2 * half, :].reshape(devices * 2 * half, 2 * HEAD)


def read_queries(refs, half, i, share):
    if len(refs) == 2:
        return refs[1][...]
    return refs[0][pl.ds(i * share, share), 2 * half :, :].reshape(share * half, 2 * HEAD)


def self_forward(parts, devices, half):
    tile = 2 * half
    keys = devices * tile
    blocks = BLOCKS
    share = devices // blocks
    block = share * half
    step = chunk_of(keys)

    def kernel(*refs):
        ins, (o_ref, wide_ref, log_ref, kv, vt) = refs[: len(parts)], refs[len(parts) :]
        i = pl.program_id(0)

        @pl.when(i == 0)
        def _():
            kv[...] = read_keys(ins, half)
            vt[...] = flip(kv[...])

        both = split_pair(read_queries(ins, half, i, share))

        def scores(c):
            return dot_nt(kv[at_chunk(c, step), :], both)

        def values(c, p):
            return [dot_nn(vt[HEAD:, at_chunk(c, step)], p)]

        def write(mixed, log_total):
            mixed = mixed[0]
            rows = jnp.concatenate([mixed[:, :block], mixed[:, block:]], axis=0).T
            o_ref[...] = rows.astype(bf16)
            wide_ref[...] = rows
            log_ref[0] = jnp.broadcast_to(log_total, (8, 2 * block))

        softmax_sweep(scores, values, keys // step, 2 * block, write)

    return pl.pallas_call(
        kernel,
        grid=(blocks,),
        in_specs=part_specs(parts, half),
        out_specs=[
            pl.BlockSpec((block, 2 * HEAD), lambda i: (i, 0)),
            pl.BlockSpec((block, 2 * HEAD), lambda i: (i, 0)),
            pl.BlockSpec((1, 8, 2 * block), lambda i: (i, 0, 0)),
        ],
        out_shape=[
            jax.ShapeDtypeStruct((devices * half, 2 * HEAD), bf16),
            jax.ShapeDtypeStruct((devices * half, 2 * HEAD), f32),
            jax.ShapeDtypeStruct((blocks, 8, 2 * block), f32),
        ],
        scratch_shapes=[pltpu.VMEM((keys, 2 * HEAD), bf16), pltpu.VMEM((2 * HEAD, keys), bf16)],
        compiler_params=pltpu.CompilerParams(vmem_limit_bytes=60 << 20),
        cost_estimate=pl.CostEstimate(
            flops=16 * keys * keys * HEAD,
            bytes_accessed=8 * keys * 2 * HEAD,
            transcendentals=keys * keys,
        ),
        name="self_forward",
    )(*parts)


def self_backward(parts, do, o, logs, devices, half):
    tile = 2 * half
    keys = devices * tile
    blocks = logs.shape[0]
    share = devices // blocks
    block = share * half
    step = chunk_of(keys)

    def kernel(*refs):
        n = len(parts)
        ins, (do_ref, o_ref, log_ref), outs = refs[:n], refs[n : n + 3], refs[n + 3 : 2 * n + 3]
        kv, vt, grads = refs[2 * n + 3 :]
        i = pl.program_id(0)
        mine = pl.ds(i * share, share)

        @pl.when(i == 0)
        def _():
            kv[...] = read_keys(ins, half)
            vt[...] = flip(kv[...])
            grads[...] = jnp.zeros_like(grads)

        q_both = split_pair(read_queries(ins, half, i, share))
        do_both = split_pair(do_ref[...])
        delta = jnp.sum(do_both.astype(f32) * split_wide(o_ref[...]), axis=1, keepdims=True)
        log_total = log_ref[0].T[:, :1] * LOG2E
        qt = flip(q_both)[:HEAD]
        dot = flip(do_both)[:HEAD]
        do_low = do_both[:, :HEAD]

        def scores(c):
            s = dot_nt(q_both, kv[pl.ds(c * step, step), :])
            return s, dot_nn(do_low, vt[HEAD:, pl.ds(c * step, step)])

        dq = jnp.zeros((2 * block, 2 * HEAD), f32)
        ahead = scores(0)
        for c in range(keys // step):
            s, dp = ahead
            ahead = scores(c + 1) if c + 1 < keys // step else None
            p = jnp.exp2(s * LOG2E - log_total)
            ds = (p * (dp - delta)).astype(bf16)
            cols = pl.ds(c * step, step)
            grads[:HEAD, cols] += dot_nn(qt, ds)
            grads[HEAD:, cols] += dot_nn(dot, p.astype(bf16))
            dq = dq + dot_nn(ds, kv[cols, :])
        dq = dq * 0.125
        low = lax.broadcasted_iota(jnp.int32, (block, 2 * HEAD), 1) < HEAD
        packed = jnp.where(low, dq[:block], pltpu.roll(dq[block:], HEAD, 1)).astype(bf16)
        if n == 1:
            outs[0][mine, tile:, :] = packed.reshape(share, half, 2 * HEAD)
        else:
            outs[1][...] = packed

        @pl.when(i == blocks - 1)
        def _():
            dkv = grads[...].T.astype(bf16)
            if n == 1:
                outs[0][:, :tile, :] = dkv.reshape(devices, tile, 2 * HEAD)
            else:
                outs[0][...] = dkv

    rows_spec = pl.BlockSpec((block, 2 * HEAD), lambda i: (i, 0))
    return pl.pallas_call(
        kernel,
        grid=(blocks,),
        in_specs=part_specs(parts, half)
        + [rows_spec, rows_spec, pl.BlockSpec((1, 8, 2 * block), lambda i: (i, 0, 0))],
        out_specs=part_specs(parts, half),
        out_shape=[jax.ShapeDtypeStruct(p.shape, bf16) for p in parts],
        scratch_shapes=[
            pltpu.VMEM((keys, 2 * HEAD), bf16),
            pltpu.VMEM((2 * HEAD, keys), bf16),
            pltpu.VMEM((2 * HEAD, keys), f32),
        ],
        compiler_params=pltpu.CompilerParams(vmem_limit_bytes=60 << 20),
        cost_estimate=pl.CostEstimate(
            flops=40 * keys * keys * HEAD,
            bytes_accessed=16 * keys * 2 * HEAD,
            transcendentals=keys * keys,
        ),
        name="self_backward",
    )(*parts, do, o, logs)


def swap_pairs(first, second):
    low = lax.broadcasted_iota(jnp.int32, first.shape, 1) < HEAD
    return (
        jnp.where(low, first, pltpu.roll(second, HEAD, 1)),
        jnp.where(low, pltpu.roll(first, HEAD, 1), second),
    )


def tile_places(items, turns, groups, tile):
    return [(i * tile, i % turns, i // turns) for i in range(items)]


def slot_rows(weights, first, size):
    return pl.BlockSpec((1, size, weights.shape[2]), lambda i: (i, first // size, 0))


def project_pack(x, weights, items, turns, groups):
    rows, width = x.shape
    slots = weights.shape[0]
    tile = rows // items
    half = tile // 2

    def kernel(x_ref, kv_ref, q_ref, out_ref):
        kv = dot_nt(x_ref[...], kv_ref[0]).astype(bf16)
        q = dot_nt(x_ref[...], q_ref[0]).astype(bf16).astype(f32) * 0.125
        for start, turn, group in tile_places(items, turns, groups, tile):
            upper, lower = swap_pairs(q[start : start + half], q[start + half : start + tile])
            for h, part in enumerate((upper, lower)):
                out_ref[turn, group, 0, h, :tile, :] = kv[
                    start : start + tile, h * 2 * HEAD : (h + 1) * 2 * HEAD
                ]
                out_ref[turn, group, 0, h, tile:, :] = part.astype(bf16)

    shape = (turns, groups, slots, 2, 3 * half, 2 * HEAD)
    return pl.pallas_call(
        kernel,
        grid=(slots,),
        in_specs=[
            pl.BlockSpec((rows, width), lambda i: (0, 0)),
            slot_rows(weights, KV_ROWS, 4 * HEAD),
            slot_rows(weights, Q_ROWS, 2 * HEAD),
        ],
        out_specs=pl.BlockSpec(
            (turns, groups, 1, 2, 3 * half, 2 * HEAD), lambda i: (0, 0, i, 0, 0, 0)
        ),
        out_shape=jax.ShapeDtypeStruct(shape, bf16),
        compiler_params=pltpu.CompilerParams(vmem_limit_bytes=60 << 20),
        cost_estimate=pl.CostEstimate(
            flops=2 * rows * width * slots * 6 * HEAD,
            bytes_accessed=2 * (rows + slots * 6 * HEAD) * width,
            transcendentals=0,
        ),
        name="project_pack",
    )(x, weights, weights)


def unpack_project(blocks, weights, items, groups):
    turns = len(blocks)
    slots = weights.shape[0]
    half = blocks[0].shape[3]
    tile = 2 * half
    width = weights.shape[2]

    def kernel(*refs):
        ins, w_ref, flat_ref, out_ref = refs[:turns], refs[turns], refs[turns + 1], refs[turns + 2]
        slot = pl.program_id(0)
        for start, turn, group in tile_places(items, turns, groups, tile):
            pair = [ins[turn][group, 0, h].astype(f32) for h in range(2)]
            upper, lower = swap_pairs(*pair)
            flat_ref[start : start + half, :] = upper.astype(bf16)
            flat_ref[start + half : start + tile, :] = lower.astype(bf16)
        part = dot_nn(flat_ref[...], w_ref[0])

        @pl.when(slot == 0)
        def _():
            out_ref[...] = part

        @pl.when(slot > 0)
        def _():
            out_ref[...] += part

    return pl.pallas_call(
        kernel,
        grid=(slots,),
        in_specs=[
            pl.BlockSpec((groups, 1, 2, half, 2 * HEAD), lambda i: (0, i, 0, 0, 0))
            for _ in range(turns)
        ]
        + [slot_rows(weights, SO_ROWS, 2 * HEAD)],
        out_specs=[
            pl.BlockSpec((items * tile, 2 * HEAD), lambda i: (0, i)),
            pl.BlockSpec((items * tile, width), lambda i: (0, 0)),
        ],
        out_shape=[
            jax.ShapeDtypeStruct((items * tile, slots * 2 * HEAD), bf16),
            jax.ShapeDtypeStruct((items * tile, width), f32),
        ],
        compiler_params=pltpu.CompilerParams(vmem_limit_bytes=60 << 20),
        cost_estimate=pl.CostEstimate(
            flops=2 * items * tile * width * slots * 2 * HEAD,
            bytes_accessed=4 * items * tile * width,
            transcendentals=0,
        ),
        name="unpack_project",
    )(*blocks, weights)


def back_pack(x, weights, items, turns, groups):
    rows, width = x.shape
    slots = weights.shape[0]
    tile = rows // items
    half = tile // 2

    def kernel(x_ref, w_ref, out_ref):
        grads = dot_nt(x_ref[...], w_ref[0])
        for start, turn, group in tile_places(items, turns, groups, tile):
            pair = swap_pairs(grads[start : start + half], grads[start + half : start + tile])
            for h, part in enumerate(pair):
                out_ref[turn, group, 0, h] = part.astype(bf16)

    return pl.pallas_call(
        kernel,
        grid=(slots,),
        in_specs=[
            pl.BlockSpec((rows, width), lambda i: (0, 0)),
            slot_rows(weights, SO_ROWS, 2 * HEAD),
        ],
        out_specs=pl.BlockSpec(
            (turns, groups, 1, 2, half, 2 * HEAD), lambda i: (0, 0, i, 0, 0, 0)
        ),
        out_shape=jax.ShapeDtypeStruct((turns, groups, slots, 2, half, 2 * HEAD), bf16),
        compiler_params=pltpu.CompilerParams(vmem_limit_bytes=60 << 20),
        cost_estimate=pl.CostEstimate(
            flops=2 * rows * width * slots * 2 * HEAD,
            bytes_accessed=2 * (rows + slots * 2 * HEAD) * width,
            transcendentals=0,
        ),
        name="back_pack",
    )(x, weights)


def unpack_back(blocks, weights, items, groups):
    turns = len(blocks)
    slots, _, width = weights.shape
    half = blocks[0].shape[3] // 3
    tile = 2 * half
    rows = items * tile

    def kernel(*refs):
        ins = refs[:turns]
        kv_ref, q_ref, flat_ref, out_ref = refs[turns:]
        slot = pl.program_id(0)
        for start, turn, group in tile_places(items, turns, groups, tile):
            pair = []
            for h in range(2):
                flat_ref[0, start : start + tile, h * 2 * HEAD : (h + 1) * 2 * HEAD] = ins[turn][
                    group, 0, h, :tile, :
                ]
                pair.append(ins[turn][group, 0, h, tile:, :].astype(f32))
            upper, lower = swap_pairs(*pair)
            flat_ref[0, start : start + half, 4 * HEAD :] = upper.astype(bf16)
            flat_ref[0, start + half : start + tile, 4 * HEAD :] = lower.astype(bf16)
        part = dot_nn(flat_ref[0, :, : 4 * HEAD], kv_ref[0])
        part = part + dot_nn(flat_ref[0, :, 4 * HEAD :], q_ref[0])

        @pl.when(slot == 0)
        def _():
            out_ref[...] = part

        @pl.when(slot > 0)
        def _():
            out_ref[...] += part

    return pl.pallas_call(
        kernel,
        grid=(slots,),
        in_specs=[
            pl.BlockSpec((groups, 1, 2, 3 * half, 2 * HEAD), lambda i: (0, i, 0, 0, 0))
            for _ in range(turns)
        ]
        + [slot_rows(weights, KV_ROWS, 4 * HEAD), slot_rows(weights, Q_ROWS, 2 * HEAD)],
        out_specs=[
            pl.BlockSpec((1, rows, 6 * HEAD), lambda i: (i, 0, 0)),
            pl.BlockSpec((rows, width), lambda i: (0, 0)),
        ],
        out_shape=[
            jax.ShapeDtypeStruct((slots, rows, 6 * HEAD), bf16),
            jax.ShapeDtypeStruct((rows, width), f32),
        ],
        compiler_params=pltpu.CompilerParams(vmem_limit_bytes=60 << 20),
        cost_estimate=pl.CostEstimate(
            flops=2 * rows * width * slots * 6 * HEAD,
            bytes_accessed=4 * rows * width,
            transcendentals=0,
        ),
        name="unpack_back",
    )(*blocks, weights, weights)


def norm_forward(base, branch, gate, shift, scale):
    items, tile, width = base.shape

    def kernel(base_ref, branch_ref, gate_ref, shift_ref, scale_ref, sum_ref, out_ref):
        value = base_ref[0] + gate_ref[0] * branch_ref[0]
        hat, _ = norm_parts(value)
        sum_ref[0] = value
        out_ref[0] = (hat * (1.0 + scale_ref[0]) + shift_ref[0]).astype(bf16)

    tile_spec = pl.BlockSpec((1, tile, width), lambda i: (i, 0, 0))
    piece_spec = pl.BlockSpec((1, 1, width), lambda i: (i, 0, 0))
    return pl.pallas_call(
        kernel,
        grid=(items,),
        in_specs=[tile_spec, tile_spec, piece_spec, piece_spec, piece_spec],
        out_specs=[tile_spec, tile_spec],
        out_shape=[
            jax.ShapeDtypeStruct(base.shape, f32),
            jax.ShapeDtypeStruct(base.shape, bf16),
        ],
        compiler_params=pltpu.CompilerParams(vmem_limit_bytes=60 << 20),
        cost_estimate=pl.CostEstimate(
            flops=16 * items * tile * width,
            bytes_accessed=14 * items * tile * width,
            transcendentals=0,
        ),
        name="norm_forward",
    )(base, branch, gate, shift, scale)


def norm_backward(g, value, incoming, branch, scale, gate):
    items, tile, width = g.shape

    def kernel(g_ref, value_ref, in_ref, branch_ref, scale_ref, gate_ref, *outs):
        out_ref, gated_ref, low_ref, sums_ref = outs
        hat, inverse = norm_parts(value_ref[0])
        incoming = in_ref[0]
        sums_ref[0, 0:1] = jnp.sum(incoming, axis=0, keepdims=True)
        sums_ref[0, 1:2] = jnp.sum(incoming * hat, axis=0, keepdims=True)
        sums_ref[0, 2:3] = jnp.sum(g_ref[0] * branch_ref[0], axis=0, keepdims=True)
        out = g_ref[0] + norm_back(hat, inverse, incoming * (1.0 + scale_ref[0]))
        out_ref[0] = out
        gated_ref[0] = (gate_ref[0] * out).astype(bf16)
        low_ref[0] = out.astype(bf16)

    tile_spec = pl.BlockSpec((1, tile, width), lambda i: (i, 0, 0))
    piece_spec = pl.BlockSpec((1, 1, width), lambda i: (i, 0, 0))
    return pl.pallas_call(
        kernel,
        grid=(items,),
        in_specs=[tile_spec] * 4 + [piece_spec, piece_spec],
        out_specs=[
            tile_spec,
            tile_spec,
            tile_spec,
            pl.BlockSpec((1, 3, width), lambda i: (i, 0, 0)),
        ],
        out_shape=[
            jax.ShapeDtypeStruct(g.shape, f32),
            jax.ShapeDtypeStruct(g.shape, bf16),
            jax.ShapeDtypeStruct(g.shape, bf16),
            jax.ShapeDtypeStruct((items, 3, width), f32),
        ],
        compiler_params=pltpu.CompilerParams(vmem_limit_bytes=60 << 20),
        cost_estimate=pl.CostEstimate(
            flops=30 * items * tile * width,
            bytes_accessed=24 * items * tile * width,
            transcendentals=0,
        ),
        name="norm_backward",
    )(g, value, incoming, branch, scale, gate)


def out_project(mixed, weights):
    tp, items, tile, local = mixed.shape
    slots, _, width = weights.shape
    rows = items * tile

    def kernel(x_ref, w_ref, out_ref):
        slot = pl.program_id(0)
        part = dot_nn(x_ref[0].reshape(rows, local // 2), w_ref[0])

        @pl.when(slot == 0)
        def _():
            out_ref[...] = part

        @pl.when(slot > 0)
        def _():
            out_ref[...] += part

    return pl.pallas_call(
        kernel,
        grid=(slots,),
        in_specs=[
            pl.BlockSpec((1, items, tile, local // 2), lambda i: (i % tp, 0, 0, i // tp)),
            slot_rows(weights, OUT_ROWS, 2 * HEAD),
        ],
        out_specs=pl.BlockSpec((rows, width), lambda i: (0, 0)),
        out_shape=jax.ShapeDtypeStruct((rows, width), f32),
        compiler_params=pltpu.CompilerParams(vmem_limit_bytes=60 << 20),
        cost_estimate=pl.CostEstimate(
            flops=2 * rows * width * tp * local,
            bytes_accessed=4 * rows * width,
            transcendentals=0,
        ),
        name="out_project",
    )(mixed, weights)


def out_back(x, weights, shape):
    tp, items, tile, local = shape
    rows, width = x.shape

    def kernel(x_ref, w_ref, out_ref):
        part = dot_nt(x_ref[...], w_ref[0])
        out_ref[0] = part.astype(bf16).reshape(items, tile, local // 2)

    return pl.pallas_call(
        kernel,
        grid=(2 * tp,),
        in_specs=[
            pl.BlockSpec((rows, width), lambda i: (0, 0)),
            slot_rows(weights, OUT_ROWS, 2 * HEAD),
        ],
        out_specs=pl.BlockSpec((1, items, tile, local // 2), lambda i: (i % tp, 0, 0, i // tp)),
        out_shape=jax.ShapeDtypeStruct(shape, bf16),
        compiler_params=pltpu.CompilerParams(vmem_limit_bytes=60 << 20),
        cost_estimate=pl.CostEstimate(
            flops=2 * rows * width * tp * local,
            bytes_accessed=4 * rows * width,
            transcendentals=0,
        ),
        name="out_back",
    )(x, weights)


def first_kernel(tokens, shift, scale, w, tp):
    rows, items, cols, width = tokens.shape
    cols_here = cols // tp
    tile = rows * cols_here
    local = w.shape[1]

    def kernel(x_ref, shift_ref, scale_ref, w_ref, in_ref, q_ref):
        hat, _ = norm_parts(x_ref[...].astype(f32).reshape(rows, cols, width))
        value = hat * (1.0 + scale_ref[0]) + shift_ref[0]
        for t in range(tp):
            part = value[:, t * cols_here : (t + 1) * cols_here, :].reshape(tile, width)
            in_ref[0, t * tile : (t + 1) * tile, :] = part.astype(bf16)
        q = dot_nn(in_ref[0], w_ref[...]).astype(bf16).astype(f32) * 0.125
        q_ref[0] = q.astype(bf16)

    piece_spec = pl.BlockSpec((1, 1, width), lambda i: (i, 0, 0))
    return pl.pallas_call(
        kernel,
        grid=(items,),
        in_specs=[
            pl.BlockSpec((rows, 1, cols, width), lambda i: (0, i, 0, 0)),
            piece_spec,
            piece_spec,
            pl.BlockSpec(w.shape, lambda i: (0, 0)),
        ],
        out_specs=[
            pl.BlockSpec((1, tp * tile, width), lambda i: (i, 0, 0)),
            pl.BlockSpec((1, tp * tile, local), lambda i: (i, 0, 0)),
        ],
        out_shape=[
            jax.ShapeDtypeStruct((items, tp * tile, width), bf16),
            jax.ShapeDtypeStruct((items, tp * tile, local), bf16),
        ],
        compiler_params=pltpu.CompilerParams(vmem_limit_bytes=60 << 20),
        cost_estimate=pl.CostEstimate(
            flops=2 * items * tp * tile * width * local,
            bytes_accessed=4 * items * tp * tile * width,
            transcendentals=0,
        ),
        name="first_kernel",
    )(tokens, shift, scale, w)


def key_value_kernel(context, w_key, w_value_t):
    items, keys, depth = context.shape
    local = w_key.shape[1]
    step = 4096 if keys % 4096 == 0 else keys

    def kernel(x_ref, wk_ref, wv_ref, k_ref, vt_ref):
        k_ref[0] = dot_nn(x_ref[0], wk_ref[...]).astype(bf16)
        vt_ref[0] = dot_nt(wv_ref[...], x_ref[0]).astype(bf16)

    return pl.pallas_call(
        kernel,
        grid=(items, keys // step),
        in_specs=[
            pl.BlockSpec((1, step, depth), lambda i, j: (i, j, 0)),
            pl.BlockSpec(w_key.shape, lambda i, j: (0, 0)),
            pl.BlockSpec(w_value_t.shape, lambda i, j: (0, 0)),
        ],
        out_specs=[
            pl.BlockSpec((1, step, local), lambda i, j: (i, j, 0)),
            pl.BlockSpec((1, local, step), lambda i, j: (i, 0, j)),
        ],
        out_shape=[
            jax.ShapeDtypeStruct((items, keys, local), bf16),
            jax.ShapeDtypeStruct((items, local, keys), bf16),
        ],
        compiler_params=pltpu.CompilerParams(vmem_limit_bytes=60 << 20),
        cost_estimate=pl.CostEstimate(
            flops=4 * items * keys * depth * local,
            bytes_accessed=2 * items * keys * (depth + 2 * local),
            transcendentals=0,
        ),
        name="key_value_kernel",
    )(context, w_key, w_value_t)


def key_value_grads(dk_t, dv_t, context, start):
    items, local, keys = dk_t.shape
    depth = context.shape[2]
    step = 4096 if keys % 4096 == 0 else keys

    def kernel(dk_ref, dv_ref, x_ref, out_ref):
        first = (pl.program_id(0) == 0) & (pl.program_id(1) == 0)
        both = jnp.concatenate([dk_ref[0], dv_ref[0]], axis=0)
        part = dot_nn(both, x_ref[0])

        @pl.when(first)
        def _():
            out_ref[...] = part

        @pl.when(jnp.logical_not(first))
        def _():
            out_ref[...] += part

    grads_spec = pl.BlockSpec((1, local, step), lambda i, j: (i, 0, j))
    return pl.pallas_call(
        kernel,
        grid=(items, keys // step),
        in_specs=[
            grads_spec,
            grads_spec,
            pl.BlockSpec((1, step, depth), lambda i, j: (i + start, j, 0)),
        ],
        out_specs=pl.BlockSpec((2 * local, depth), lambda i, j: (0, 0)),
        out_shape=jax.ShapeDtypeStruct((2 * local, depth), f32),
        compiler_params=pltpu.CompilerParams(vmem_limit_bytes=60 << 20),
        cost_estimate=pl.CostEstimate(
            flops=4 * items * keys * depth * local,
            bytes_accessed=2 * items * keys * (depth + 2 * local),
            transcendentals=0,
        ),
        name="key_value_grads",
    )(dk_t, dv_t, context)


def feed_forward(x, g, up, down):
    rows, width = x.shape
    slots, _, hidden = up.shape
    parts = 4 if rows % 64 == 0 else 1
    size = rows // parts

    def kernel(x_ref, g_ref, up_ref, down_ref, active_ref, dh_ref, branch_ref, back_ref):
        slot = pl.program_id(0)

        @pl.when(slot == 0)
        def _():
            branch_ref[...] = jnp.zeros_like(branch_ref)
            back_ref[...] = jnp.zeros_like(back_ref)

        def products(r):
            mine = pl.ds(r * size, size)
            return dot_nn(x_ref[mine, :], up_ref[0]), dot_nt(g_ref[mine, :], down_ref[0])

        ahead = products(0)
        for r in range(parts):
            h, da = ahead
            ahead = products(r + 1) if r + 1 < parts else None
            mine = pl.ds(r * size, size)
            below = 0.5 * (1.0 + lax.erf(h * 0.7071067811865476))
            slope = below + h * (jnp.exp(h * h * -0.5) * 0.3989422804014327)
            active = (h * below).astype(bf16)
            dh = (da * slope).astype(bf16)
            active_ref[0, mine, :] = active
            dh_ref[0, mine, :] = dh
            branch_ref[mine, :] += dot_nn(active, down_ref[0])
            back_ref[mine, :] += dot_nt(dh, up_ref[0])

    rows_spec = pl.BlockSpec((rows, width), lambda i: (0, 0))
    hidden_spec = pl.BlockSpec((1, rows, hidden), lambda i: (i, 0, 0))
    return pl.pallas_call(
        kernel,
        grid=(slots,),
        in_specs=[
            rows_spec,
            rows_spec,
            pl.BlockSpec((1, width, hidden), lambda i: (i, 0, 0)),
            pl.BlockSpec((1, hidden, width), lambda i: (i, 0, 0)),
        ],
        out_specs=[hidden_spec, hidden_spec, rows_spec, rows_spec],
        out_shape=[
            jax.ShapeDtypeStruct((slots, rows, hidden), bf16),
            jax.ShapeDtypeStruct((slots, rows, hidden), bf16),
            jax.ShapeDtypeStruct((rows, width), f32),
            jax.ShapeDtypeStruct((rows, width), f32),
        ],
        compiler_params=pltpu.CompilerParams(vmem_limit_bytes=60 << 20),
        cost_estimate=pl.CostEstimate(
            flops=8 * slots * rows * width * hidden,
            bytes_accessed=4 * slots * width * hidden,
            transcendentals=2 * slots * rows * hidden,
        ),
        name="feed_forward",
    )(x, g, up, down)


def weight_terms(buffer, shape, lhs, lhs_block, lhs_place, rhs, tp, size, first):
    count, width = rhs.shape
    share = shape[-1]
    seq = width // share
    depth = lhs_block[-1]
    by_core = len(shape) == 5

    def kernel(*refs):
        a_ref, b_ref, out_ref = refs[0], refs[1], refs[-1]
        a = a_ref[...]
        if len(lhs_block) > 3:
            a = a.astype(f32)
        a = a.reshape(count, depth).astype(bf16)
        terms = lax.dot_general(a, b_ref[...], (((0,), (0,)), ((), ())), preferred_element_type=f32)
        for s in range(seq):
            block = terms[:, s * share : (s + 1) * share].astype(bf16)
            if by_core:
                out_ref[s % 2, 0, s // 2] = block
            else:
                out_ref[s] = block

    return pl.pallas_call(
        kernel,
        grid=(tp, 2),
        in_specs=[
            pl.BlockSpec(lhs_block, lhs_place),
            pl.BlockSpec(rhs.shape, lambda t, c: (0, 0)),
        ]
        + ([] if buffer is None else [pl.BlockSpec(memory_space=pl.ANY)]),
        out_specs=pl.BlockSpec((2, 1, seq // 2, size, share), lambda t, c: (0, t, 0, first // size + c, 0))
        if by_core
        else pl.BlockSpec((seq, size, share), lambda t, c: (t, first // size + c, 0)),
        out_shape=jax.ShapeDtypeStruct(shape, bf16),
        input_output_aliases={} if buffer is None else {2: 0},
        compiler_params=pltpu.CompilerParams(vmem_limit_bytes=60 << 20),
        cost_estimate=pl.CostEstimate(
            flops=4 * tp * count * depth * width,
            bytes_accessed=4 * tp * (count + width) * depth,
            transcendentals=0,
        ),
        name="weight_terms",
    )(lhs, rhs, *([] if buffer is None else [buffer]))


def last_kernel(buffer, tokens, scale, middle, dq, small, start):
    rows, _, cols, width = tokens.shape
    tp, items, queries, local = dq.shape
    slots = small.shape[0]
    cols_here = cols // tp
    tile = rows * cols_here
    slot_width = local // 2

    def kernel(x_ref, scale_ref, middle_ref, dq_ref, w_ref, *refs):
        out_ref, sums_ref = refs[-2:]
        hat, inverse = norm_parts(x_ref[...].astype(f32).reshape(rows, cols, width))
        weights = w_ref[...].reshape(tp * local, width)
        shift_sum = jnp.zeros((1, width), f32)
        scale_sum = jnp.zeros((1, width), f32)
        for t in range(tp):
            pieces = [
                dq_ref[u, 0, t * tile : (t + 1) * tile, c * slot_width : (c + 1) * slot_width]
                for c in range(2)
                for u in range(tp)
            ]
            g = dot_nn(jnp.concatenate(pieces, axis=1), weights)
            mine = slice(t * cols_here, (t + 1) * cols_here)
            hat_t = hat[:, mine, :].reshape(tile, width)
            inverse_t = inverse[:, mine, :].reshape(tile, 1)
            shift_sum = shift_sum + jnp.sum(g, axis=0, keepdims=True)
            scale_sum = scale_sum + jnp.sum(g * hat_t, axis=0, keepdims=True)
            value = middle_ref[t, 0].astype(f32) + norm_back(
                hat_t, inverse_t, g * (1.0 + scale_ref[0])
            )
            out_ref[:, 0, mine, :] = value.reshape(rows, cols_here, width)
        sums_ref[0, 0:1, :] = shift_sum
        sums_ref[0, 1:2, :] = scale_sum

    return pl.pallas_call(
        kernel,
        grid=(items,),
        in_specs=[
            pl.BlockSpec((rows, 1, cols, width), lambda i: (0, i + start, 0, 0)),
            pl.BlockSpec((1, 1, width), lambda i: (i + start, 0, 0)),
            pl.BlockSpec((tp, 1, tile, width), lambda i: (0, i + start, 0, 0)),
            pl.BlockSpec((tp, 1, queries, local), lambda i: (0, i, 0, 0)),
            pl.BlockSpec((slots, slot_width, width), lambda i: (0, QUERY_ROWS // slot_width, 0)),
        ]
        + ([] if buffer is None else [pl.BlockSpec(memory_space=pl.ANY)]),
        out_specs=[
            pl.BlockSpec((rows, 1, cols, width), lambda i: (0, i + start, 0, 0)),
            pl.BlockSpec((1, 2, width), lambda i: (i, 0, 0)),
        ],
        out_shape=[
            jax.ShapeDtypeStruct(tokens.shape, f32),
            jax.ShapeDtypeStruct((items, 2, width), f32),
        ],
        input_output_aliases={} if buffer is None else {5: 0},
        compiler_params=pltpu.CompilerParams(vmem_limit_bytes=60 << 20),
        cost_estimate=pl.CostEstimate(
            flops=2 * items * queries * width * tp * local,
            bytes_accessed=10 * items * queries * width,
            transcendentals=0,
        ),
        name="last_kernel",
    )(tokens, scale, middle, dq, small, *([] if buffer is None else [buffer]))


def exchange(x, axis):
    return lax.all_to_all(x, axis, 0, 0, tiled=True)


def gather(x, axis):
    names = axis if isinstance(axis, tuple) else (axis,)
    count = 1
    for name in names:
        count *= lax.axis_size(name)
    return exchange(jnp.broadcast_to(x[None], (count,) + x.shape), axis)


def reduce_blocks(x, axis):
    return jnp.sum(exchange(x.astype(bf16), axis).astype(f32), axis=0)


def body(
    tokens,
    context,
    group_ids,
    source_table,
    w_query,
    w_key,
    w_value,
    w_out,
    w_self_query,
    w_self_key,
    w_self_value,
    w_self_out,
    w_up,
    w_down,
    w_deconv,
    deconv_bias,
    out_cotangent,
    plane_cotangent,
):
    rows_here, items, plane_cols, width = tokens.shape
    cols_here = out_cotangent.shape[2]
    tp = lax.axis_size("tp")
    seq = lax.axis_size("seq")
    both_axes = ("seq", "tp")
    devices = tp * seq
    local = w_query.shape[1]
    hidden_here = w_up.shape[1]
    slots = 2 * tp
    slot_heads = local // HEAD // 2
    slot_width = local // 2
    heads = slots * slot_heads
    tile = rows_here * cols_here
    half = tile // 2
    groups = devices // heads
    turns = -(-items // groups)
    share = width // seq
    fast = slot_heads == 2 and half % 16 == 0 and items == groups * turns and share % 128 == 0
    me_tp = lax.axis_index("tp")
    core = lax.axis_index("seq") % 2

    picker = (group_ids[:, None] == jnp.arange(GROUPS, dtype=jnp.int32)[None, :]).astype(f32)
    mods = jnp.dot(picker, source_table, precision=highest).reshape(items, 9, 1, width)

    def piece(index):
        return mods[:, index]

    def dot(spec, a, b):
        return jnp.einsum(spec, a, b, preferred_element_type=f32)

    def to_tile(x):
        return x.transpose(1, 0, 2, 3).reshape(items, tile, width)

    def from_tile(x):
        return x.reshape(items, rows_here, cols_here, width).transpose(1, 0, 2, 3)

    teams = [
        [(2 * pair + c) * tp + t for c in range(2) for t in range(tp)] for pair in range(seq // 2)
    ]

    def whole(x):
        return lax.all_gather(x, both_axes, axis=0, tiled=False, axis_index_groups=teams)

    def my_rows(x):
        return lax.dynamic_slice_in_dim(x, core * slot_width, slot_width, 0)

    def my_columns(x):
        size = x.shape[1] // 2
        return lax.dynamic_slice_in_dim(x, core * size, size, 1)

    key_value = jnp.stack(
        [
            my_columns(w_self_key).T.reshape(slot_heads, HEAD, width),
            my_columns(w_self_value).T.reshape(slot_heads, HEAD, width),
        ],
        axis=1,
    ).reshape(2 * slot_width, width)
    small = whole(
        jnp.concatenate(
            [
                key_value,
                my_columns(w_self_query).T,
                my_rows(w_self_out),
                my_rows(w_out),
                my_columns(w_query).T,
            ],
            axis=0,
        )
    )
    cuts = [slot_width * k for k in (0, 2, 3, 4, 5, 6)]
    kv_slots, q_slots, so_slots, out_slots, query_slots = [
        small[:, a:b] for a, b in zip(cuts[:-1], cuts[1:])
    ]
    up_slots = whole(my_columns(w_up))
    down_slots = whole(
        lax.dynamic_slice_in_dim(w_down, core * (hidden_here // 2), hidden_here // 2, 0)
    )

    def by_tp(x):
        return x.reshape(2, tp, slot_width, width).transpose(1, 0, 2, 3).reshape(tp, local, width)

    incoming = plane_cotangent.reshape(2 * rows_here, items, 2 * cols_here, COUT)
    plane_row = (lax.axis_index("seq") * rows_here + jnp.arange(rows_here, dtype=jnp.int32)) % PLANE
    upper_keep = (plane_row != 0).astype(f32)
    lower_keep = (plane_row != PLANE - 1).astype(f32)
    grad_edges = with_halo(incoming, (("seq", 0), ("tp", 2)), 1)
    if fast:
        first_in, queries = first_kernel(tokens, piece(0), piece(1), w_query, tp)
    else:
        ordered = (
            tokens.reshape(rows_here, items, tp, cols_here, width)
            .transpose(1, 2, 0, 3, 4)
            .reshape(items, tp * tile, width)
        )
        first_hat, first_inv = norm_parts(ordered.astype(f32))
        first_in = (first_hat * (1.0 + piece(1)) + piece(0)).astype(bf16)
        queries = dot("iqd,de->iqe", first_in, w_query).astype(bf16) * bf16(0.125)
    image = context.transpose(1, 0, 2)
    queries, grad_edges = lax.optimization_barrier((queries, grad_edges))
    keys, values_t = key_value_kernel(image, w_key, w_value.T)
    upper_mask = upper_keep.astype(bf16)[:, None, None, None]
    lower_mask = lower_keep.astype(bf16)[:, None, None, None]
    first_pair = grad_edges[:-2].reshape(rows_here, 2, items, 2 * cols_here + 2, COUT)
    last_pair = grad_edges[2:].reshape(rows_here, 2, items, 2 * cols_here + 2, COUT)
    row_taps = jnp.stack(
        [
            first_pair[:, 0] * upper_mask,
            first_pair[:, 1],
            last_pair[:, 0],
            last_pair[:, 1] * lower_mask,
        ],
        axis=3,
    )
    left_pair = row_taps[:, :, :-2].reshape(rows_here, items, cols_here, 2, 4, COUT)
    right_pair = row_taps[:, :, 2:].reshape(rows_here, items, cols_here, 2, 4, COUT)
    tap_grads = jnp.stack(
        [
            left_pair[:, :, :, 0],
            left_pair[:, :, :, 1],
            right_pair[:, :, :, 0],
            right_pair[:, :, :, 1],
        ],
        axis=4,
    )
    tap_grads = tap_grads.reshape(rows_here, items, cols_here, 16 * COUT)
    grad_result = to_tile(out_cotangent.astype(f32) + dot("rict,dt->ricd", tap_grads, w_deconv))
    grad_bias = jnp.sum(incoming.astype(f32), axis=(0, 1, 2))
    grad_mlp = (piece(8) * grad_result).astype(bf16)
    mixed, mixed_wide, cross_logs = cross_forward(queries, keys, values_t, tp)
    mixed_tile = exchange(mixed, "tp")
    if fast:
        branch_a = out_project(mixed_tile, small).reshape(items, tile, width)
    else:
        branch_a = dot("time,tef->imf", mixed_tile, by_tp(out_slots))
    residual = to_tile(lax.dynamic_slice_in_dim(tokens, me_tp * cols_here, cols_here, 2)).astype(f32)
    middle, self_in = norm_forward(residual, branch_a, piece(2), piece(3), piece(4))

    flat = (items * tile, width)
    spare = groups * turns - items

    def spread_items(x):
        if spare:
            x = jnp.pad(x, ((0, 0), (0, spare)) + ((0, 0),) * (x.ndim - 2))
        return x.reshape((slots, groups, turns) + x.shape[2:])

    def pack_keys(x):
        x = spread_items(x.reshape(slots, items, tile, slot_heads, 2 * HEAD))
        return x.transpose(2, 1, 0, 4, 3, 5).reshape(turns, devices, tile, 2 * HEAD)

    def unpack_keys(x):
        x = x.reshape(turns, groups, slots, slot_heads, tile, 2 * HEAD).transpose(2, 1, 0, 4, 3, 5)
        x = x.reshape(slots, groups * turns, tile, 2 * slot_width)[:, :items]
        return x.reshape(slots, items * tile, 2 * slot_width)

    def pack_rows(x):
        x = spread_items(x.reshape(slots, items, 2, half, slot_heads, HEAD))
        return x.transpose(2, 1, 0, 5, 4, 3, 6).reshape(turns, devices, half, 2 * HEAD)

    def unpack_rows(x):
        x = x.reshape(turns, groups, slots, slot_heads, half, 2, HEAD).transpose(2, 1, 0, 5, 4, 3, 6)
        x = x.reshape(slots, groups * turns, tile, slot_width)[:, :items]
        return x.reshape(slots, items * tile, slot_width)

    if fast:
        sends = project_pack(self_in.reshape(flat), small, items, turns, groups)
        sends = sends.reshape(turns, devices, 3 * half, 2 * HEAD)
        sends = [sends[turn] for turn in range(turns)]
    else:
        kv_sends = pack_keys(dot("nd,xed->xne", self_in.reshape(flat), kv_slots).astype(bf16))
        q_sends = dot("nd,xed->xne", self_in.reshape(flat), q_slots).astype(bf16)
        q_sends = pack_rows(q_sends * bf16(0.125))
        parts = [
            [
                exchange(kv_sends[turn], both_axes).reshape(devices * tile, 2 * HEAD),
                exchange(q_sends[turn], both_axes).reshape(devices * half, 2 * HEAD),
            ]
            for turn in range(turns)
        ]
    if fast:
        parts, forward = [], []
        for turn in range(turns):
            if turn >= 2:
                sends[turn], forward[turn - 2] = lax.optimization_barrier(
                    (sends[turn], forward[turn - 2])
                )
            arrived = exchange(sends[turn], both_axes)
            if turn == 0:
                arrived, grad_result, grad_mlp = lax.optimization_barrier(
                    (arrived, grad_result, grad_mlp)
                )
            parts.append([arrived])
            forward.append(self_forward(parts[turn], devices, half))
    else:
        forward = [self_forward(parts[turn], devices, half) for turn in range(turns)]
    outs = [x[0] for x in forward]
    if fast:
        outs[0], parts[-1][0] = lax.optimization_barrier((outs[0], parts[-1][0]))
    so_back = [exchange(so.reshape(devices, half, 2 * HEAD), both_axes) for so in outs]
    if fast:
        blocks = [x.reshape(groups, slots, 2, half, 2 * HEAD) for x in so_back]
        so_tile, branch_s = unpack_project(blocks, small, items, groups)
    else:
        so_tile = unpack_rows(jnp.stack(so_back)).transpose(1, 0, 2)
        branch_s = dot("nxe,xed->nd", so_tile, so_slots)
        so_tile = so_tile.reshape(items * tile, heads * HEAD)
    branch_s = branch_s.reshape(items, tile, width)
    middle_two, second_in = norm_forward(middle, branch_s, piece(5), piece(6), piece(7))

    active, grad_hidden, branch_b, grad_second = feed_forward(
        second_in.reshape(flat), grad_mlp.reshape(flat), up_slots, down_slots
    )
    branch_b = branch_b.reshape(items, tile, width)
    grad_second = grad_second.reshape(items, tile, width)
    result = middle_two + piece(8) * branch_b
    out_tile = from_tile(result.astype(bf16))

    grad_mid_two, grad_self, _, sums_b = norm_backward(
        grad_result, middle_two, grad_second, branch_b, piece(7), piece(5)
    )

    widened = with_halo(out_tile, (("seq", 0), ("tp", 2)), 1)

    def by_device(x):
        lead = x.shape[0] // tp
        x = x.reshape(lead, tp, x.shape[1], seq, share).transpose(1, 3, 0, 2, 4)
        return x.reshape(devices, -1, share).astype(bf16)

    def of_cores(x):
        return x.reshape((tp, seq // 2, 2) + x.shape[1:]).transpose(2, 0, 1, 3, 4)

    def total_near(terms, after):
        keep = lax.dynamic_index_in_dim(terms, core, 0, False)
        give = lax.dynamic_index_in_dim(terms, 1 - core, 0, False)
        got = lax.ppermute(give, "seq", [(i, i ^ 1) for i in range(seq)])
        got, _ = lax.optimization_barrier((got, after))
        x = (keep.astype(f32) + got.astype(f32)).astype(bf16)
        return lax.psum_scatter(x, "tp", scatter_dimension=0, tiled=True)[0]

    def total_far(x, after, *cuts):
        x, _ = lax.optimization_barrier((x, after))
        lines = [list(range(c, seq, 2)) for c in range(2)]
        x = lax.psum_scatter(x, "seq", scatter_dimension=0, axis_index_groups=lines, tiled=True)[0]
        return jnp.split(x.astype(f32), cuts, axis=0)

    def total(terms, *cuts):
        summed = lax.psum_scatter(terms, ("tp", "seq"), scatter_dimension=0, tiled=True)[0]
        return jnp.split(summed.astype(f32), cuts, axis=0)

    terms_deconv = dot("ricd,rict->dt", out_tile, tap_grads).astype(bf16)
    piece_rows = width // devices
    terms_deconv = (
        terms_deconv.reshape(devices, piece_rows, -1, share)
        .transpose(0, 2, 1, 3)
        .reshape(devices, -1, share)
    )
    size_b = (hidden_here // 2, hidden_here, 2 * hidden_here)
    if fast:
        shape = (2, tp, seq // 2, size_b[2] + terms_deconv.shape[1], share)
        hidden_block = (1, items * tile, size_b[0])

        def slot_place(t, c):
            return (c * tp + t, 0, 0)

        terms_b = None
        for lhs, rhs, first in (
            (grad_hidden, second_in, 0),
            (active, grad_mlp, size_b[1]),
        ):
            terms_b = weight_terms(
                terms_b, shape, lhs, hidden_block, slot_place, rhs.reshape(flat), tp, size_b[0], first
            )
        terms_b = lax.dynamic_update_slice_in_dim(terms_b, of_cores(terms_deconv), size_b[2], 3)
    else:
        terms_b = jnp.concatenate(
            [
                by_device(dot("xnf,nd->xfd", grad_hidden, second_in.reshape(flat))),
                by_device(dot("xnf,nd->xfd", active, grad_mlp.reshape(flat))),
                terms_deconv,
            ],
            axis=1,
        )
        terms_b = of_cores(terms_b)

    if fast:
        dso_send = back_pack(grad_self.reshape(flat), small, items, turns, groups)
        dso_send = dso_send.reshape(turns, devices, half, 2 * HEAD)
    else:
        dso_send = pack_rows(dot("nd,xed->xne", grad_self.reshape(flat), so_slots).astype(bf16))
    dso_send = [dso_send[turn] for turn in range(turns)]
    dso_mine, backward = [], []
    for turn in range(turns):
        if turn >= 2:
            dso_send[turn], backward[turn - 2] = lax.optimization_barrier(
                (dso_send[turn], backward[turn - 2])
            )
        arrived = exchange(dso_send[turn], both_axes).reshape(devices * half, 2 * HEAD)
        if turn == 0:
            arrived, terms_b, widened = lax.optimization_barrier((arrived, terms_b, widened))
        dso_mine.append(arrived)
        backward.append(
            self_backward(parts[turn], dso_mine[turn], *forward[turn][1:], devices, half)
        )
    taps = dot("ricd,dt->rict", widened, w_deconv)
    taps = taps.reshape(rows_here + 2, items, cols_here + 2, 4, 4, COUT)
    planes = spread_taps(
        taps, upper_keep[:, None, None, None, None], lower_keep[:, None, None, None, None]
    )
    planes = planes + jnp.tile(deconv_bias, 2 * cols_here)

    near_b = total_near(terms_b, (backward[0][0], dso_mine[min(1, turns - 1)]))
    if fast:
        blocks = [
            exchange(x[0], both_axes).reshape(groups, slots, 2, 3 * half, 2 * HEAD)
            for x in backward
        ]
        blocks[-1], planes = lax.optimization_barrier((blocks[-1], planes))
        grad_projected, grad_third = unpack_back(blocks, small, items, groups)
    else:
        dkv = [exchange(x[0].reshape(devices, tile, 2 * HEAD), both_axes) for x in backward]
        dq = [exchange(x[1].reshape(devices, half, 2 * HEAD), both_axes) for x in backward]
        grad_projected = jnp.concatenate(
            [unpack_keys(jnp.stack(dkv)), unpack_rows(jnp.stack(dq))], axis=2
        )
        grad_third = dot(
            "xne,xed->nd", grad_projected, jnp.concatenate([kv_slots, q_slots], axis=1)
        )
    grad_up, grad_down, grad_deconv = total_far(near_b, grad_third, *size_b[1:])
    grad_third = grad_third.reshape(items, tile, width)
    grad_middle, grad_attn, middle_low, sums_s = norm_backward(
        grad_mid_two, middle, grad_third, branch_s, piece(4), piece(2)
    )

    grad_gate_a = jnp.sum(grad_middle * branch_a, axis=1)
    if fast:
        do_send = out_back(grad_attn.reshape(flat), small, mixed.shape)
    else:
        do_send = dot("imf,tef->time", grad_attn, by_tp(out_slots)).astype(bf16)
    do_mine = exchange(do_send, "tp")
    middle_all = gather(middle_low, "tp")
    early = jnp.concatenate([grad_gate_a[:, None], sums_s, sums_b], axis=1)
    early = early.transpose(1, 0, 2).reshape(7 * items, width)
    early = jnp.concatenate(
        [early, jnp.pad(grad_bias, (0, width - COUT))[None]], axis=0
    )
    spots = -(-early.shape[0] // (16 * tp)) * 16
    early = jnp.pad(early, ((0, spots * tp - early.shape[0]), (0, 0))).reshape(tp, spots, width)
    early = by_device(early)
    size_a = [slot_width * k for k in (6, 8, 10)]
    if fast:
        shape = (devices, size_a[2] + early.shape[1], share)
        terms_a = weight_terms(
            None,
            shape,
            grad_projected,
            (1, items * tile, 3 * slot_width),
            lambda t, c: (c * tp + t, 0, 0),
            self_in.reshape(flat),
            tp,
            3 * slot_width,
            0,
        )
        terms_a = weight_terms(
            terms_a,
            shape,
            so_tile,
            (items * tile, slot_width),
            lambda t, c: (0, c * tp + t),
            grad_self.reshape(flat),
            tp,
            slot_width,
            size_a[0],
        )
        terms_a = weight_terms(
            terms_a,
            shape,
            mixed_tile,
            (1, items, tile, slot_width),
            lambda t, c: (t, 0, 0, c),
            grad_attn.reshape(flat),
            tp,
            slot_width,
            size_a[1],
        )
        terms_a = lax.dynamic_update_slice_in_dim(terms_a, early, size_a[2], 1)
    else:
        so_terms = dot("ne,nd->ed", so_tile, grad_self.reshape(flat))
        terms_a = jnp.concatenate(
            [
                by_device(dot("xne,nd->xed", grad_projected, self_in.reshape(flat))),
                by_device(so_terms.reshape(slots, slot_width, width)),
                by_device(dot("time,imf->tef", mixed_tile, grad_attn)),
                early,
            ],
            axis=1,
        )
    do_mine, terms_a = lax.optimization_barrier((do_mine, terms_a))
    terms_a, grad_up = lax.optimization_barrier((terms_a, grad_up))
    grad_three, grad_self_out, grad_out, grad_early = total(terms_a, *size_a)
    first_part = items - items // 3
    cross = (queries, do_mine, mixed_wide, cross_logs, keys, values_t)
    one = cross_backward(*cross, 0, first_part)
    one, middle_all = lax.optimization_barrier((one, middle_all))
    dq_one = gather(one[0], "tp")
    do_late, _ = lax.optimization_barrier((do_mine, one[0]))
    two = cross_backward(queries, do_late, *cross[2:], first_part, items - first_part)
    one, two, dq_one = lax.optimization_barrier((one, two, dq_one))
    dq_two = gather(two[0], "tp")
    grad_query = dot("iqd,iqe->de", first_in, jnp.concatenate([one[0], two[0]], axis=0))
    two, dq_two, grad_query = lax.optimization_barrier((two, dq_two, grad_query))
    grad_three = grad_three.reshape(2, 3 * slot_width, share)
    grad_pair = grad_three[:, : 2 * slot_width].reshape(2, slot_heads, 2, HEAD, share)
    grad_self_key = grad_pair[:, :, 0].reshape(local, share).T
    grad_self_value = grad_pair[:, :, 1].reshape(local, share).T
    grad_self_query = grad_three[:, 2 * slot_width :].reshape(local, share).T

    def by_seq(x):
        return x.reshape((seq, x.shape[0] // seq) + x.shape[1:]).astype(bf16)

    grad_image = (
        key_value_grads(one[1], one[2], image, 0) + key_value_grads(two[1], two[2], image, first_part)
    ).T
    last = jnp.concatenate(
        [
            by_seq(grad_query),
            by_seq(grad_image[:, :local]),
            by_seq(grad_image[:, local:]),
        ],
        axis=1,
    )
    grad_deconv, grad_image = lax.optimization_barrier((grad_deconv, grad_image))
    grad_deconv = grad_deconv.reshape(-1, piece_rows, share).transpose(1, 0, 2)
    grad_deconv = lax.all_gather(
        grad_deconv.reshape(piece_rows, 16 * COUT).astype(bf16), ("tp", "seq"), axis=0, tiled=True
    )
    last, dq_one, dq_two = lax.optimization_barrier((last, dq_one, dq_two))
    last = jnp.sum(exchange(last, "seq").astype(f32), axis=0)
    if fast:
        grad_tokens, late_one = last_kernel(None, tokens, piece(1), middle_all, dq_one, small, 0)
        grad_tokens, late_two = last_kernel(
            grad_tokens, tokens, piece(1), middle_all, dq_two, small, first_part
        )
        late = jnp.concatenate([late_one, late_two], axis=0).transpose(1, 0, 2)
    else:
        dq_all = jnp.concatenate([dq_one, dq_two], axis=1)
        grad_first = dot("tiqe,ted->iqd", dq_all, by_tp(query_slots))
        grad_shift_a = jnp.sum(grad_first, axis=1)
        grad_scale_a = jnp.sum(grad_first * first_hat, axis=1)
        grad_tokens = middle_all.astype(f32).transpose(1, 0, 2, 3).reshape(
            items, tp * tile, width
        ) + norm_back(first_hat, first_inv, grad_first * (1.0 + piece(1)))
        grad_tokens = (
            grad_tokens.reshape(items, tp, rows_here, cols_here, width)
            .transpose(2, 0, 1, 3, 4)
            .reshape(rows_here, items, plane_cols, width)
        )
        late = jnp.stack([grad_shift_a, grad_scale_a], axis=0)

    late, last = lax.optimization_barrier((late, last))
    part = 2 * items * width // tp
    mine = lax.dynamic_slice_in_dim(late.reshape(-1, share), me_tp * (part // share), part // share, 0)
    sums = gather(jnp.concatenate([mine, grad_early], axis=0), ("tp", "seq"))
    sums = sums.reshape(tp, seq, part // share + spots, share)
    late = jnp.sum(sums[:, :, : part // share], axis=1).reshape(2, items, width)
    early = sums[:, :, part // share :].transpose(0, 2, 1, 3).reshape(tp * spots, width)
    grad_bias = early[7 * items, :COUT]
    early = early[: 7 * items].reshape(7, items, width)
    depth = (last.shape[0] - share) // 2
    grad_query, grad_key, grad_value = (
        last[:share],
        last[share : share + depth],
        last[share + depth :],
    )
    late, grad_deconv = lax.optimization_barrier((late, grad_deconv))
    grad_mods = jnp.concatenate([late, early], axis=0).transpose(1, 0, 2)
    grad_table = jnp.dot(picker.T, grad_mods.reshape(items, 9 * width), precision=highest)
    return (
        out_tile,
        planes,
        grad_tokens,
        grad_query,
        grad_key,
        grad_value,
        grad_out,
        grad_self_query,
        grad_self_key,
        grad_self_value,
        grad_self_out.reshape(local, share),
        grad_up.T,
        grad_down,
        grad_deconv.astype(f32),
        grad_bias,
        grad_table,
    )


def solution(mesh):
    in_specs = (
        P("seq", None, None, None),
        P(),
        P(),
        P(),
        P(None, "tp"),
        P(None, "tp"),
        P(None, "tp"),
        P("tp", None),
        P(None, "tp"),
        P(None, "tp"),
        P(None, "tp"),
        P("tp", None),
        P(None, "tp"),
        P("tp", None),
        P(),
        P(),
        P("seq", None, "tp", None),
        P("seq", None, "tp"),
    )
    out_specs = (
        P("seq", None, "tp", None),
        P("seq", None, "tp"),
        P("seq", None, None, None),
        P("seq", "tp"),
        P("seq", "tp"),
        P("seq", "tp"),
        P("tp", "seq"),
        P("seq", "tp"),
        P("seq", "tp"),
        P("seq", "tp"),
        P("tp", "seq"),
        P("seq", "tp"),
        P("tp", "seq"),
        P(),
        P(),
        P(),
    )
    return jax.shard_map(body, mesh=mesh, in_specs=in_specs, out_specs=out_specs, check_vma=False)
```

```python
import jax
import jax.numpy as jnp
from jax import lax
from jax.experimental import pallas as pl
from jax.experimental.pallas import tpu as pltpu
from jax.sharding import PartitionSpec as P

HEAD = 64
COUT = 80
PLANE = 32
IMG = 4096
LOG2E = 1.4426950408889634
bf16 = jnp.bfloat16
f32 = jnp.float32
GROUPS = 16


highest = lax.Precision.HIGHEST
epsilon = 1e-06


def with_halo(x, sides, width):
    for axis, dim in sides:
        peers, length = (lax.axis_size(axis), x.shape[dim])
        up = [(i, (i + 1) % peers) for i in range(peers - 1)]
        down = [(j, i) for i, j in up]
        last = lax.slice_in_dim(x, length - width, length, axis=dim)
        initial = lax.slice_in_dim(x, 0, width, axis=dim)
        before = lax.ppermute(last, axis, up)
        after = lax.ppermute(initial, axis, down)
        x = jnp.concatenate([before, x, after], axis=dim)
    return x


def spread_taps(padded, upper, lower):
    even_rows = padded[1:-1, :, :, 1] + upper * padded[:-2, :, :, 3]
    odd_rows = lower * padded[2:, :, :, 0] + padded[1:-1, :, :, 2]
    rows_both = jnp.stack([even_rows, odd_rows], axis=1)
    even_cols = rows_both[:, :, :, 1:-1, 1] + rows_both[:, :, :, :-2, 3]
    odd_cols = rows_both[:, :, :, 2:, 0] + rows_both[:, :, :, 1:-1, 2]
    joined = jnp.stack([even_cols, odd_cols], axis=4)
    shape = joined.shape
    return joined.reshape(shape[0] * 2, shape[2], shape[3] * 2 * shape[5])


def norm_parts(value):
    centred = value - jnp.mean(value, axis=-1, keepdims=True)
    inverse = lax.rsqrt(jnp.mean(centred * centred, axis=-1, keepdims=True) + epsilon)
    return (centred * inverse, inverse)


def norm_back(normed, inverse, incoming):
    return inverse * (
        incoming
        - jnp.mean(incoming, axis=-1, keepdims=True)
        - normed * jnp.mean(incoming * normed, axis=-1, keepdims=True)
    )


NT = (((1,), (1,)), ((), ()))
BLOCKS = 4
KV_ROWS, Q_ROWS, SO_ROWS, OUT_ROWS, QUERY_ROWS = 0, 256, 384, 512, 640


def dot_nt(a, b):
    return lax.dot_general(a, b, NT, preferred_element_type=f32)


def dot_nn(a, b):
    return jnp.dot(a, b, preferred_element_type=f32)


def flip(x):
    return x.astype(f32).T.astype(bf16)


def chunk_of(keys):
    return 512 if keys % 512 == 0 else keys


SAFE = 40.0


def softmax_sweep(scores, values, chunks, columns, write):
    def spread(mixed, total, top):
        width = columns // len(mixed)
        inverse = 1.0 / total
        mixed = [m * inverse[:, j * width : (j + 1) * width] for j, m in enumerate(mixed)]
        write(mixed, top + jnp.log(total))

    ahead = scores(0)
    top = jnp.max(ahead, axis=0, keepdims=True)
    base = top * LOG2E
    peak = top
    total = jnp.zeros((1, columns), f32)
    mixed = None
    for c in range(chunks):
        now = ahead
        ahead = scores(c + 1) if c + 1 < chunks else None
        expon = jnp.exp2(now * LOG2E - base)
        if c > 0:
            peak = jnp.maximum(peak, jnp.max(now, axis=0, keepdims=True))
        total = total + jnp.sum(expon, axis=0, keepdims=True)
        parts = values(c, expon.astype(bf16))
        mixed = parts if mixed is None else [m + part for m, part in zip(mixed, parts)]
    spread(mixed, total, top)

    @pl.when(jnp.max(peak - top) > SAFE)
    def _():
        def body(c, carry):
            top, total, mixed = carry
            now = scores(c)
            new_top = jnp.maximum(top, jnp.max(now, axis=0, keepdims=True))
            fade = jnp.exp2((top - new_top) * LOG2E)
            expon = jnp.exp2((now - new_top) * LOG2E)
            total = total * fade + jnp.sum(expon, axis=0, keepdims=True)
            parts = values(c, expon.astype(bf16))
            width = columns // len(parts)
            mixed = [
                m * fade[:, j * width : (j + 1) * width] + part
                for j, (m, part) in enumerate(zip(mixed, parts))
            ]
            return new_top, total, mixed

        start = (
            jnp.full((1, columns), -3e38, f32),
            jnp.zeros((1, columns), f32),
            [jnp.zeros(m.shape, f32) for m in mixed],
        )
        top, total, again = lax.fori_loop(0, chunks, body, start)
        spread(again, total, top)


def at_chunk(c, step):
    return pl.ds(c * step if isinstance(c, int) else pl.multiple_of(c * step, step), step)


def cross_forward(q, k, vt, tp):
    items, queries, width = q.shape
    tile = queries // tp
    keys = k.shape[1]
    heads = width // HEAD
    step = chunk_of(keys)

    def kernel(q_ref, k_ref, vt_ref, o_ref, wide_ref, log_ref):
        pair = pl.program_id(1)
        owner = lax.broadcasted_iota(jnp.int32, (queries, width), 1) // HEAD
        both = jnp.concatenate(
            [jnp.where(owner == pair * 2 + j, q_ref[0], 0.0).astype(bf16) for j in range(2)], axis=0
        )

        def scores(c):
            return dot_nt(k_ref[0, at_chunk(c, step), :], both)

        def values(c, p):
            out = []
            for j in range(2):
                rows = pl.ds(pl.multiple_of((pair * 2 + j) * HEAD, HEAD), HEAD)
                v = vt_ref[0, rows, at_chunk(c, step)]
                out.append(dot_nn(v, p[:, j * queries : (j + 1) * queries]))
            return out

        def write(mixed, log_total):
            rows = jnp.concatenate(mixed, axis=0).T.reshape(tp, 1, tile, 2 * HEAD)
            o_ref[...] = rows.astype(bf16)
            wide_ref[...] = rows
            for j in range(2):
                log_ref[0, j] = jnp.broadcast_to(
                    log_total[:, j * queries : (j + 1) * queries], (8, queries)
                )

        softmax_sweep(scores, values, keys // step, 2 * queries, write)

    return pl.pallas_call(
        kernel,
        grid=(items, heads // 2),
        in_specs=[
            pl.BlockSpec((1, queries, width), lambda i, h: (i, 0, 0)),
            pl.BlockSpec((1, keys, width), lambda i, h: (i, 0, 0)),
            pl.BlockSpec((1, width, keys), lambda i, h: (i, 0, 0)),
        ],
        out_specs=[
            pl.BlockSpec((tp, 1, tile, 2 * HEAD), lambda i, h: (0, i, 0, h)),
            pl.BlockSpec((tp, 1, tile, 2 * HEAD), lambda i, h: (0, i, 0, h)),
            pl.BlockSpec((1, 2, 8, queries), lambda i, h: (i, h, 0, 0)),
        ],
        out_shape=[
            jax.ShapeDtypeStruct((tp, items, tile, width), bf16),
            jax.ShapeDtypeStruct((tp, items, tile, width), f32),
            jax.ShapeDtypeStruct((items, heads, 8, queries), f32),
        ],
        compiler_params=pltpu.CompilerParams(vmem_limit_bytes=60 << 20),
        cost_estimate=pl.CostEstimate(
            flops=16 * items * queries * keys * width,
            bytes_accessed=4 * items * (queries + keys) * width,
            transcendentals=items * queries * keys * heads,
        ),
        name="cross_forward",
    )(q, k, vt)


def cross_backward(q, do, o, logs, k, vt, start, items):
    _, queries, width = q.shape
    tp, _, tile, _ = do.shape
    keys = k.shape[1]
    heads = width // HEAD
    step = chunk_of(keys)

    def kernel(q_ref, do_ref, o_ref, log_ref, k_ref, vt_ref, dq_ref, dk_ref, dv_ref, qt, dot):
        head = pl.program_id(1)

        @pl.when(head == 0)
        def _():
            qt[...] = flip(q_ref[0])
            dot[...] = do_ref[...].astype(f32).reshape(queries, width).T.astype(bf16)

        mine = lax.broadcasted_iota(jnp.int32, (queries, width), 1) // HEAD == head
        q_mine = jnp.where(mine, q_ref[0], 0.0).astype(bf16)
        do_wide = jnp.where(mine, do_ref[...].astype(f32).reshape(queries, width), 0.0)
        do_mine = do_wide.astype(bf16)
        o_wide = o_ref[...].reshape(queries, width)
        delta = jnp.sum(do_wide * o_wide, axis=1, keepdims=True)
        log_total = log_ref[0, 0].T[:, :1] * LOG2E
        rows = pl.ds(pl.multiple_of(head * HEAD, HEAD), HEAD)
        qt_mine = qt[rows, :]
        dot_mine = dot[rows, :]

        def scores(c):
            s = dot_nt(q_mine, k_ref[0, pl.ds(c * step, step), :])
            return s, dot_nn(do_mine, vt_ref[0, :, pl.ds(c * step, step)])

        dq = jnp.zeros((queries, width), f32)
        ahead = scores(0)
        for c in range(keys // step):
            s, dp = ahead
            ahead = scores(c + 1) if c + 1 < keys // step else None
            p = jnp.exp2(s * LOG2E - log_total)
            ds = (p * (dp - delta)).astype(bf16)
            cols = pl.ds(c * step, step)
            dv_ref[0, :, cols] = dot_nn(dot_mine, p.astype(bf16)).astype(bf16)
            dk_ref[0, :, cols] = dot_nn(qt_mine, ds).astype(bf16)
            dq = dq + dot_nn(ds, k_ref[0, cols, :])
        dq = (dq * 0.125).astype(bf16)
        rest = jnp.where(head == 0, jnp.zeros_like(dq), dq_ref[0])
        dq_ref[0] = jnp.where(mine, dq, rest)

    rows_spec = pl.BlockSpec((1, queries, width), lambda i, h: (i + start, 0, 0))
    tiles_spec = pl.BlockSpec((tp, 1, tile, width), lambda i, h: (0, i + start, 0, 0))
    grads_spec = pl.BlockSpec((1, HEAD, keys), lambda i, h: (i, h, 0))
    return pl.pallas_call(
        kernel,
        grid=(items, heads),
        in_specs=[
            rows_spec,
            tiles_spec,
            tiles_spec,
            pl.BlockSpec((1, 1, 8, queries), lambda i, h: (i + start, h, 0, 0)),
            pl.BlockSpec((1, keys, width), lambda i, h: (i + start, 0, 0)),
            pl.BlockSpec((1, width, keys), lambda i, h: (i + start, 0, 0)),
        ],
        out_specs=[
            pl.BlockSpec((1, queries, width), lambda i, h: (i, 0, 0)),
            grads_spec,
            grads_spec,
        ],
        out_shape=[
            jax.ShapeDtypeStruct((items, queries, width), bf16),
            jax.ShapeDtypeStruct((items, width, keys), bf16),
            jax.ShapeDtypeStruct((items, width, keys), bf16),
        ],
        scratch_shapes=[pltpu.VMEM((width, queries), bf16), pltpu.VMEM((width, queries), bf16)],
        compiler_params=pltpu.CompilerParams(vmem_limit_bytes=60 << 20),
        cost_estimate=pl.CostEstimate(
            flops=40 * items * queries * keys * width,
            bytes_accessed=8 * items * (queries + keys) * width,
            transcendentals=items * queries * keys * heads,
        ),
        name="cross_backward",
    )(q, do, o, logs, k, vt)


def split_wide(x):
    low = lax.broadcasted_iota(jnp.int32, x.shape, 1) < HEAD
    wide = x.astype(f32)
    first = jnp.where(low, wide, 0.0)
    second = jnp.where(low, pltpu.roll(wide, HEAD, 1), 0.0)
    return jnp.concatenate([first, second], axis=0)


def split_pair(x):
    return split_wide(x).astype(bf16)


def part_specs(parts, half):
    if len(parts) == 1:
        return [pl.BlockSpec(parts[0].shape, lambda i: (0, 0, 0))]
    rows = parts[1].shape[0] // BLOCKS
    return [
        pl.BlockSpec(parts[0].shape, lambda i: (0, 0)),
        pl.BlockSpec((rows, 2 * HEAD), lambda i: (i, 0)),
    ]


def read_keys(refs, half):
    if len(refs) == 2:
        return refs[0][...]
    devices = refs[0].shape[0]
    return refs[0][:, : 2 * half, :].reshape(devices * 2 * half, 2 * HEAD)


def read_queries(refs, half, i, share):
    if len(refs) == 2:
        return refs[1][...]
    return refs[0][pl.ds(i * share, share), 2 * half :, :].reshape(share * half, 2 * HEAD)


def self_forward(parts, devices, half):
    tile = 2 * half
    keys = devices * tile
    blocks = BLOCKS
    share = devices // blocks
    block = share * half
    step = chunk_of(keys)

    def kernel(*refs):
        ins, (o_ref, wide_ref, log_ref, kv, vt) = refs[: len(parts)], refs[len(parts) :]
        i = pl.program_id(0)

        @pl.when(i == 0)
        def _():
            kv[...] = read_keys(ins, half)
            vt[...] = flip(kv[...])

        both = split_pair(read_queries(ins, half, i, share))

        def scores(c):
            return dot_nt(kv[at_chunk(c, step), :], both)

        def values(c, p):
            return [dot_nn(vt[HEAD:, at_chunk(c, step)], p)]

        def write(mixed, log_total):
            mixed = mixed[0]
            rows = jnp.concatenate([mixed[:, :block], mixed[:, block:]], axis=0).T
            o_ref[...] = rows.astype(bf16)
            wide_ref[...] = rows
            log_ref[0] = jnp.broadcast_to(log_total, (8, 2 * block))

        softmax_sweep(scores, values, keys // step, 2 * block, write)

    return pl.pallas_call(
        kernel,
        grid=(blocks,),
        in_specs=part_specs(parts, half),
        out_specs=[
            pl.BlockSpec((block, 2 * HEAD), lambda i: (i, 0)),
            pl.BlockSpec((block, 2 * HEAD), lambda i: (i, 0)),
            pl.BlockSpec((1, 8, 2 * block), lambda i: (i, 0, 0)),
        ],
        out_shape=[
            jax.ShapeDtypeStruct((devices * half, 2 * HEAD), bf16),
            jax.ShapeDtypeStruct((devices * half, 2 * HEAD), f32),
            jax.ShapeDtypeStruct((blocks, 8, 2 * block), f32),
        ],
        scratch_shapes=[pltpu.VMEM((keys, 2 * HEAD), bf16), pltpu.VMEM((2 * HEAD, keys), bf16)],
        compiler_params=pltpu.CompilerParams(vmem_limit_bytes=60 << 20),
        cost_estimate=pl.CostEstimate(
            flops=16 * keys * keys * HEAD,
            bytes_accessed=8 * keys * 2 * HEAD,
            transcendentals=keys * keys,
        ),
        name="self_forward",
    )(*parts)


def self_backward(parts, do, o, logs, devices, half):
    tile = 2 * half
    keys = devices * tile
    blocks = logs.shape[0]
    share = devices // blocks
    block = share * half
    step = chunk_of(keys)

    def kernel(*refs):
        n = len(parts)
        ins, (do_ref, o_ref, log_ref), outs = refs[:n], refs[n : n + 3], refs[n + 3 : 2 * n + 3]
        kv, vt, grads = refs[2 * n + 3 :]
        i = pl.program_id(0)
        mine = pl.ds(i * share, share)

        @pl.when(i == 0)
        def _():
            kv[...] = read_keys(ins, half)
            vt[...] = flip(kv[...])
            grads[...] = jnp.zeros_like(grads)

        q_both = split_pair(read_queries(ins, half, i, share))
        do_both = split_pair(do_ref[...])
        delta = jnp.sum(do_both.astype(f32) * split_wide(o_ref[...]), axis=1, keepdims=True)
        log_total = log_ref[0].T[:, :1] * LOG2E
        qt = flip(q_both)[:HEAD]
        dot = flip(do_both)[:HEAD]
        do_low = do_both[:, :HEAD]

        def scores(c):
            s = dot_nt(q_both, kv[pl.ds(c * step, step), :])
            return s, dot_nn(do_low, vt[HEAD:, pl.ds(c * step, step)])

        dq = jnp.zeros((2 * block, 2 * HEAD), f32)
        ahead = scores(0)
        for c in range(keys // step):
            s, dp = ahead
            ahead = scores(c + 1) if c + 1 < keys // step else None
            p = jnp.exp2(s * LOG2E - log_total)
            ds = (p * (dp - delta)).astype(bf16)
            cols = pl.ds(c * step, step)
            grads[:HEAD, cols] += dot_nn(qt, ds)
            grads[HEAD:, cols] += dot_nn(dot, p.astype(bf16))
            dq = dq + dot_nn(ds, kv[cols, :])
        dq = dq * 0.125
        low = lax.broadcasted_iota(jnp.int32, (block, 2 * HEAD), 1) < HEAD
        packed = jnp.where(low, dq[:block], pltpu.roll(dq[block:], HEAD, 1)).astype(bf16)
        if n == 1:
            outs[0][mine, tile:, :] = packed.reshape(share, half, 2 * HEAD)
        else:
            outs[1][...] = packed

        @pl.when(i == blocks - 1)
        def _():
            dkv = grads[...].T.astype(bf16)
            if n == 1:
                outs[0][:, :tile, :] = dkv.reshape(devices, tile, 2 * HEAD)
            else:
                outs[0][...] = dkv

    rows_spec = pl.BlockSpec((block, 2 * HEAD), lambda i: (i, 0))
    return pl.pallas_call(
        kernel,
        grid=(blocks,),
        in_specs=part_specs(parts, half)
        + [rows_spec, rows_spec, pl.BlockSpec((1, 8, 2 * block), lambda i: (i, 0, 0))],
        out_specs=part_specs(parts, half),
        out_shape=[jax.ShapeDtypeStruct(p.shape, bf16) for p in parts],
        scratch_shapes=[
            pltpu.VMEM((keys, 2 * HEAD), bf16),
            pltpu.VMEM((2 * HEAD, keys), bf16),
            pltpu.VMEM((2 * HEAD, keys), f32),
        ],
        compiler_params=pltpu.CompilerParams(vmem_limit_bytes=60 << 20),
        cost_estimate=pl.CostEstimate(
            flops=40 * keys * keys * HEAD,
            bytes_accessed=16 * keys * 2 * HEAD,
            transcendentals=keys * keys,
        ),
        name="self_backward",
    )(*parts, do, o, logs)


def swap_pairs(first, second):
    low = lax.broadcasted_iota(jnp.int32, first.shape, 1) < HEAD
    return (
        jnp.where(low, first, pltpu.roll(second, HEAD, 1)),
        jnp.where(low, pltpu.roll(first, HEAD, 1), second),
    )


def tile_places(items, turns, groups, tile):
    return [(i * tile, i % turns, i // turns) for i in range(items)]


def slot_rows(weights, first, size):
    return pl.BlockSpec((1, size, weights.shape[2]), lambda i: (i, first // size, 0))


def project_pack(x, weights, items, turns, groups):
    rows, width = x.shape
    slots = weights.shape[0]
    tile = rows // items
    half = tile // 2

    def kernel(x_ref, kv_ref, q_ref, out_ref):
        kv = dot_nt(x_ref[...], kv_ref[0]).astype(bf16)
        q = dot_nt(x_ref[...], q_ref[0]).astype(bf16).astype(f32) * 0.125
        for start, turn, group in tile_places(items, turns, groups, tile):
            upper, lower = swap_pairs(q[start : start + half], q[start + half : start + tile])
            for h, part in enumerate((upper, lower)):
                out_ref[turn, group, 0, h, :tile, :] = kv[
                    start : start + tile, h * 2 * HEAD : (h + 1) * 2 * HEAD
                ]
                out_ref[turn, group, 0, h, tile:, :] = part.astype(bf16)

    shape = (turns, groups, slots, 2, 3 * half, 2 * HEAD)
    return pl.pallas_call(
        kernel,
        grid=(slots,),
        in_specs=[
            pl.BlockSpec((rows, width), lambda i: (0, 0)),
            slot_rows(weights, KV_ROWS, 4 * HEAD),
            slot_rows(weights, Q_ROWS, 2 * HEAD),
        ],
        out_specs=pl.BlockSpec(
            (turns, groups, 1, 2, 3 * half, 2 * HEAD), lambda i: (0, 0, i, 0, 0, 0)
        ),
        out_shape=jax.ShapeDtypeStruct(shape, bf16),
        compiler_params=pltpu.CompilerParams(vmem_limit_bytes=60 << 20),
        cost_estimate=pl.CostEstimate(
            flops=2 * rows * width * slots * 6 * HEAD,
            bytes_accessed=2 * (rows + slots * 6 * HEAD) * width,
            transcendentals=0,
        ),
        name="project_pack",
    )(x, weights, weights)


def unpack_project(blocks, weights, items, groups):
    turns = len(blocks)
    slots = weights.shape[0]
    half = blocks[0].shape[3]
    tile = 2 * half
    width = weights.shape[2]

    def kernel(*refs):
        ins, w_ref, flat_ref, out_ref = refs[:turns], refs[turns], refs[turns + 1], refs[turns + 2]
        slot = pl.program_id(0)
        for start, turn, group in tile_places(items, turns, groups, tile):
            pair = [ins[turn][group, 0, h].astype(f32) for h in range(2)]
            upper, lower = swap_pairs(*pair)
            flat_ref[start : start + half, :] = upper.astype(bf16)
            flat_ref[start + half : start + tile, :] = lower.astype(bf16)
        part = dot_nn(flat_ref[...], w_ref[0])

        @pl.when(slot == 0)
        def _():
            out_ref[...] = part

        @pl.when(slot > 0)
        def _():
            out_ref[...] += part

    return pl.pallas_call(
        kernel,
        grid=(slots,),
        in_specs=[
            pl.BlockSpec((groups, 1, 2, half, 2 * HEAD), lambda i: (0, i, 0, 0, 0))
            for _ in range(turns)
        ]
        + [slot_rows(weights, SO_ROWS, 2 * HEAD)],
        out_specs=[
            pl.BlockSpec((items * tile, 2 * HEAD), lambda i: (0, i)),
            pl.BlockSpec((items * tile, width), lambda i: (0, 0)),
        ],
        out_shape=[
            jax.ShapeDtypeStruct((items * tile, slots * 2 * HEAD), bf16),
            jax.ShapeDtypeStruct((items * tile, width), f32),
        ],
        compiler_params=pltpu.CompilerParams(vmem_limit_bytes=60 << 20),
        cost_estimate=pl.CostEstimate(
            flops=2 * items * tile * width * slots * 2 * HEAD,
            bytes_accessed=4 * items * tile * width,
            transcendentals=0,
        ),
        name="unpack_project",
    )(*blocks, weights)


def back_pack(x, weights, items, turns, groups):
    rows, width = x.shape
    slots = weights.shape[0]
    tile = rows // items
    half = tile // 2

    def kernel(x_ref, w_ref, out_ref):
        grads = dot_nt(x_ref[...], w_ref[0])
        for start, turn, group in tile_places(items, turns, groups, tile):
            pair = swap_pairs(grads[start : start + half], grads[start + half : start + tile])
            for h, part in enumerate(pair):
                out_ref[turn, group, 0, h] = part.astype(bf16)

    return pl.pallas_call(
        kernel,
        grid=(slots,),
        in_specs=[
            pl.BlockSpec((rows, width), lambda i: (0, 0)),
            slot_rows(weights, SO_ROWS, 2 * HEAD),
        ],
        out_specs=pl.BlockSpec(
            (turns, groups, 1, 2, half, 2 * HEAD), lambda i: (0, 0, i, 0, 0, 0)
        ),
        out_shape=jax.ShapeDtypeStruct((turns, groups, slots, 2, half, 2 * HEAD), bf16),
        compiler_params=pltpu.CompilerParams(vmem_limit_bytes=60 << 20),
        cost_estimate=pl.CostEstimate(
            flops=2 * rows * width * slots * 2 * HEAD,
            bytes_accessed=2 * (rows + slots * 2 * HEAD) * width,
            transcendentals=0,
        ),
        name="back_pack",
    )(x, weights)


def unpack_back(blocks, weights, items, groups):
    turns = len(blocks)
    slots, _, width = weights.shape
    half = blocks[0].shape[3] // 3
    tile = 2 * half
    rows = items * tile

    def kernel(*refs):
        ins = refs[:turns]
        kv_ref, q_ref, flat_ref, out_ref = refs[turns:]
        slot = pl.program_id(0)
        for start, turn, group in tile_places(items, turns, groups, tile):
            pair = []
            for h in range(2):
                flat_ref[0, start : start + tile, h * 2 * HEAD : (h + 1) * 2 * HEAD] = ins[turn][
                    group, 0, h, :tile, :
                ]
                pair.append(ins[turn][group, 0, h, tile:, :].astype(f32))
            upper, lower = swap_pairs(*pair)
            flat_ref[0, start : start + half, 4 * HEAD :] = upper.astype(bf16)
            flat_ref[0, start + half : start + tile, 4 * HEAD :] = lower.astype(bf16)
        part = dot_nn(flat_ref[0, :, : 4 * HEAD], kv_ref[0])
        part = part + dot_nn(flat_ref[0, :, 4 * HEAD :], q_ref[0])

        @pl.when(slot == 0)
        def _():
            out_ref[...] = part

        @pl.when(slot > 0)
        def _():
            out_ref[...] += part

    return pl.pallas_call(
        kernel,
        grid=(slots,),
        in_specs=[
            pl.BlockSpec((groups, 1, 2, 3 * half, 2 * HEAD), lambda i: (0, i, 0, 0, 0))
            for _ in range(turns)
        ]
        + [slot_rows(weights, KV_ROWS, 4 * HEAD), slot_rows(weights, Q_ROWS, 2 * HEAD)],
        out_specs=[
            pl.BlockSpec((1, rows, 6 * HEAD), lambda i: (i, 0, 0)),
            pl.BlockSpec((rows, width), lambda i: (0, 0)),
        ],
        out_shape=[
            jax.ShapeDtypeStruct((slots, rows, 6 * HEAD), bf16),
            jax.ShapeDtypeStruct((rows, width), f32),
        ],
        compiler_params=pltpu.CompilerParams(vmem_limit_bytes=60 << 20),
        cost_estimate=pl.CostEstimate(
            flops=2 * rows * width * slots * 6 * HEAD,
            bytes_accessed=4 * rows * width,
            transcendentals=0,
        ),
        name="unpack_back",
    )(*blocks, weights, weights)


def norm_forward(base, branch, gate, shift, scale):
    items, tile, width = base.shape

    def kernel(base_ref, branch_ref, gate_ref, shift_ref, scale_ref, sum_ref, out_ref):
        value = base_ref[0] + gate_ref[0] * branch_ref[0]
        hat, _ = norm_parts(value)
        sum_ref[0] = value
        out_ref[0] = (hat * (1.0 + scale_ref[0]) + shift_ref[0]).astype(bf16)

    tile_spec = pl.BlockSpec((1, tile, width), lambda i: (i, 0, 0))
    piece_spec = pl.BlockSpec((1, 1, width), lambda i: (i, 0, 0))
    return pl.pallas_call(
        kernel,
        grid=(items,),
        in_specs=[tile_spec, tile_spec, piece_spec, piece_spec, piece_spec],
        out_specs=[tile_spec, tile_spec],
        out_shape=[
            jax.ShapeDtypeStruct(base.shape, f32),
            jax.ShapeDtypeStruct(base.shape, bf16),
        ],
        compiler_params=pltpu.CompilerParams(vmem_limit_bytes=60 << 20),
        cost_estimate=pl.CostEstimate(
            flops=16 * items * tile * width,
            bytes_accessed=14 * items * tile * width,
            transcendentals=0,
        ),
        name="norm_forward",
    )(base, branch, gate, shift, scale)


def norm_backward(g, value, incoming, branch, scale, gate):
    items, tile, width = g.shape

    def kernel(g_ref, value_ref, in_ref, branch_ref, scale_ref, gate_ref, *outs):
        out_ref, gated_ref, low_ref, sums_ref = outs
        hat, inverse = norm_parts(value_ref[0])
        incoming = in_ref[0]
        sums_ref[0, 0:1] = jnp.sum(incoming, axis=0, keepdims=True)
        sums_ref[0, 1:2] = jnp.sum(incoming * hat, axis=0, keepdims=True)
        sums_ref[0, 2:3] = jnp.sum(g_ref[0] * branch_ref[0], axis=0, keepdims=True)
        out = g_ref[0] + norm_back(hat, inverse, incoming * (1.0 + scale_ref[0]))
        out_ref[0] = out
        gated_ref[0] = (gate_ref[0] * out).astype(bf16)
        low_ref[0] = out.astype(bf16)

    tile_spec = pl.BlockSpec((1, tile, width), lambda i: (i, 0, 0))
    piece_spec = pl.BlockSpec((1, 1, width), lambda i: (i, 0, 0))
    return pl.pallas_call(
        kernel,
        grid=(items,),
        in_specs=[tile_spec] * 4 + [piece_spec, piece_spec],
        out_specs=[
            tile_spec,
            tile_spec,
            tile_spec,
            pl.BlockSpec((1, 3, width), lambda i: (i, 0, 0)),
        ],
        out_shape=[
            jax.ShapeDtypeStruct(g.shape, f32),
            jax.ShapeDtypeStruct(g.shape, bf16),
            jax.ShapeDtypeStruct(g.shape, bf16),
            jax.ShapeDtypeStruct((items, 3, width), f32),
        ],
        compiler_params=pltpu.CompilerParams(vmem_limit_bytes=60 << 20),
        cost_estimate=pl.CostEstimate(
            flops=30 * items * tile * width,
            bytes_accessed=24 * items * tile * width,
            transcendentals=0,
        ),
        name="norm_backward",
    )(g, value, incoming, branch, scale, gate)


def out_project(mixed, weights):
    tp, items, tile, local = mixed.shape
    slots, _, width = weights.shape
    rows = items * tile

    def kernel(x_ref, w_ref, out_ref):
        slot = pl.program_id(0)
        part = dot_nn(x_ref[0].reshape(rows, local // 2), w_ref[0])

        @pl.when(slot == 0)
        def _():
            out_ref[...] = part

        @pl.when(slot > 0)
        def _():
            out_ref[...] += part

    return pl.pallas_call(
        kernel,
        grid=(slots,),
        in_specs=[
            pl.BlockSpec((1, items, tile, local // 2), lambda i: (i % tp, 0, 0, i // tp)),
            slot_rows(weights, OUT_ROWS, 2 * HEAD),
        ],
        out_specs=pl.BlockSpec((rows, width), lambda i: (0, 0)),
        out_shape=jax.ShapeDtypeStruct((rows, width), f32),
        compiler_params=pltpu.CompilerParams(vmem_limit_bytes=60 << 20),
        cost_estimate=pl.CostEstimate(
            flops=2 * rows * width * tp * local,
            bytes_accessed=4 * rows * width,
            transcendentals=0,
        ),
        name="out_project",
    )(mixed, weights)


def out_back(x, weights, shape):
    tp, items, tile, local = shape
    rows, width = x.shape

    def kernel(x_ref, w_ref, out_ref):
        part = dot_nt(x_ref[...], w_ref[0])
        out_ref[0] = part.astype(bf16).reshape(items, tile, local // 2)

    return pl.pallas_call(
        kernel,
        grid=(2 * tp,),
        in_specs=[
            pl.BlockSpec((rows, width), lambda i: (0, 0)),
            slot_rows(weights, OUT_ROWS, 2 * HEAD),
        ],
        out_specs=pl.BlockSpec((1, items, tile, local // 2), lambda i: (i % tp, 0, 0, i // tp)),
        out_shape=jax.ShapeDtypeStruct(shape, bf16),
        compiler_params=pltpu.CompilerParams(vmem_limit_bytes=60 << 20),
        cost_estimate=pl.CostEstimate(
            flops=2 * rows * width * tp * local,
            bytes_accessed=4 * rows * width,
            transcendentals=0,
        ),
        name="out_back",
    )(x, weights)


def first_kernel(tokens, shift, scale, w, tp):
    rows, items, cols, width = tokens.shape
    cols_here = cols // tp
    tile = rows * cols_here
    local = w.shape[1]

    def kernel(x_ref, shift_ref, scale_ref, w_ref, in_ref, q_ref):
        hat, _ = norm_parts(x_ref[...].astype(f32).reshape(rows, cols, width))
        value = hat * (1.0 + scale_ref[0]) + shift_ref[0]
        for t in range(tp):
            part = value[:, t * cols_here : (t + 1) * cols_here, :].reshape(tile, width)
            in_ref[0, t * tile : (t + 1) * tile, :] = part.astype(bf16)
        q = dot_nn(in_ref[0], w_ref[...]).astype(bf16).astype(f32) * 0.125
        q_ref[0] = q.astype(bf16)

    piece_spec = pl.BlockSpec((1, 1, width), lambda i: (i, 0, 0))
    return pl.pallas_call(
        kernel,
        grid=(items,),
        in_specs=[
            pl.BlockSpec((rows, 1, cols, width), lambda i: (0, i, 0, 0)),
            piece_spec,
            piece_spec,
            pl.BlockSpec(w.shape, lambda i: (0, 0)),
        ],
        out_specs=[
            pl.BlockSpec((1, tp * tile, width), lambda i: (i, 0, 0)),
            pl.BlockSpec((1, tp * tile, local), lambda i: (i, 0, 0)),
        ],
        out_shape=[
            jax.ShapeDtypeStruct((items, tp * tile, width), bf16),
            jax.ShapeDtypeStruct((items, tp * tile, local), bf16),
        ],
        compiler_params=pltpu.CompilerParams(vmem_limit_bytes=60 << 20),
        cost_estimate=pl.CostEstimate(
            flops=2 * items * tp * tile * width * local,
            bytes_accessed=4 * items * tp * tile * width,
            transcendentals=0,
        ),
        name="first_kernel",
    )(tokens, shift, scale, w)


def key_value_kernel(context, w_key, w_value_t):
    items, keys, depth = context.shape
    local = w_key.shape[1]
    step = 4096 if keys % 4096 == 0 else keys

    def kernel(x_ref, wk_ref, wv_ref, k_ref, vt_ref):
        k_ref[0] = dot_nn(x_ref[0], wk_ref[...]).astype(bf16)
        vt_ref[0] = dot_nt(wv_ref[...], x_ref[0]).astype(bf16)

    return pl.pallas_call(
        kernel,
        grid=(items, keys // step),
        in_specs=[
            pl.BlockSpec((1, step, depth), lambda i, j: (i, j, 0)),
            pl.BlockSpec(w_key.shape, lambda i, j: (0, 0)),
            pl.BlockSpec(w_value_t.shape, lambda i, j: (0, 0)),
        ],
        out_specs=[
            pl.BlockSpec((1, step, local), lambda i, j: (i, j, 0)),
            pl.BlockSpec((1, local, step), lambda i, j: (i, 0, j)),
        ],
        out_shape=[
            jax.ShapeDtypeStruct((items, keys, local), bf16),
            jax.ShapeDtypeStruct((items, local, keys), bf16),
        ],
        compiler_params=pltpu.CompilerParams(vmem_limit_bytes=60 << 20),
        cost_estimate=pl.CostEstimate(
            flops=4 * items * keys * depth * local,
            bytes_accessed=2 * items * keys * (depth + 2 * local),
            transcendentals=0,
        ),
        name="key_value_kernel",
    )(context, w_key, w_value_t)


def key_value_grads(dk_t, dv_t, context, start):
    items, local, keys = dk_t.shape
    depth = context.shape[2]
    step = 4096 if keys % 4096 == 0 else keys

    def kernel(dk_ref, dv_ref, x_ref, out_ref):
        first = (pl.program_id(0) == 0) & (pl.program_id(1) == 0)
        both = jnp.concatenate([dk_ref[0], dv_ref[0]], axis=0)
        part = dot_nn(both, x_ref[0])

        @pl.when(first)
        def _():
            out_ref[...] = part

        @pl.when(jnp.logical_not(first))
        def _():
            out_ref[...] += part

    grads_spec = pl.BlockSpec((1, local, step), lambda i, j: (i, 0, j))
    return pl.pallas_call(
        kernel,
        grid=(items, keys // step),
        in_specs=[
            grads_spec,
            grads_spec,
            pl.BlockSpec((1, step, depth), lambda i, j: (i + start, j, 0)),
        ],
        out_specs=pl.BlockSpec((2 * local, depth), lambda i, j: (0, 0)),
        out_shape=jax.ShapeDtypeStruct((2 * local, depth), f32),
        compiler_params=pltpu.CompilerParams(vmem_limit_bytes=60 << 20),
        cost_estimate=pl.CostEstimate(
            flops=4 * items * keys * depth * local,
            bytes_accessed=2 * items * keys * (depth + 2 * local),
            transcendentals=0,
        ),
        name="key_value_grads",
    )(dk_t, dv_t, context)


def feed_forward(x, g, up, down):
    rows, width = x.shape
    slots, _, hidden = up.shape
    parts = 4 if rows % 64 == 0 else 1
    size = rows // parts

    def kernel(x_ref, g_ref, up_ref, down_ref, active_ref, dh_ref, branch_ref, back_ref):
        slot = pl.program_id(0)

        @pl.when(slot == 0)
        def _():
            branch_ref[...] = jnp.zeros_like(branch_ref)
            back_ref[...] = jnp.zeros_like(back_ref)

        def products(r):
            mine = pl.ds(r * size, size)
            return dot_nn(x_ref[mine, :], up_ref[0]), dot_nt(g_ref[mine, :], down_ref[0])

        ahead = products(0)
        for r in range(parts):
            h, da = ahead
            ahead = products(r + 1) if r + 1 < parts else None
            mine = pl.ds(r * size, size)
            below = 0.5 * (1.0 + lax.erf(h * 0.7071067811865476))
            slope = below + h * (jnp.exp(h * h * -0.5) * 0.3989422804014327)
            active = (h * below).astype(bf16)
            dh = (da * slope).astype(bf16)
            active_ref[0, mine, :] = active
            dh_ref[0, mine, :] = dh
            branch_ref[mine, :] += dot_nn(active, down_ref[0])
            back_ref[mine, :] += dot_nt(dh, up_ref[0])

    rows_spec = pl.BlockSpec((rows, width), lambda i: (0, 0))
    hidden_spec = pl.BlockSpec((1, rows, hidden), lambda i: (i, 0, 0))
    return pl.pallas_call(
        kernel,
        grid=(slots,),
        in_specs=[
            rows_spec,
            rows_spec,
            pl.BlockSpec((1, width, hidden), lambda i: (i, 0, 0)),
            pl.BlockSpec((1, hidden, width), lambda i: (i, 0, 0)),
        ],
        out_specs=[hidden_spec, hidden_spec, rows_spec, rows_spec],
        out_shape=[
            jax.ShapeDtypeStruct((slots, rows, hidden), bf16),
            jax.ShapeDtypeStruct((slots, rows, hidden), bf16),
            jax.ShapeDtypeStruct((rows, width), f32),
            jax.ShapeDtypeStruct((rows, width), f32),
        ],
        compiler_params=pltpu.CompilerParams(vmem_limit_bytes=60 << 20),
        cost_estimate=pl.CostEstimate(
            flops=8 * slots * rows * width * hidden,
            bytes_accessed=4 * slots * width * hidden,
            transcendentals=2 * slots * rows * hidden,
        ),
        name="feed_forward",
    )(x, g, up, down)


def weight_terms(buffer, shape, lhs, lhs_block, lhs_place, rhs, tp, size, first):
    count, width = rhs.shape
    share = shape[-1]
    seq = width // share
    depth = lhs_block[-1]
    by_core = len(shape) == 5

    def kernel(*refs):
        a_ref, b_ref, out_ref = refs[0], refs[1], refs[-1]
        a = a_ref[...]
        if len(lhs_block) > 3:
            a = a.astype(f32)
        a = a.reshape(count, depth).astype(bf16)
        terms = lax.dot_general(a, b_ref[...], (((0,), (0,)), ((), ())), preferred_element_type=f32)
        for s in range(seq):
            block = terms[:, s * share : (s + 1) * share].astype(bf16)
            if by_core:
                out_ref[s % 2, 0, s // 2] = block
            else:
                out_ref[s] = block

    return pl.pallas_call(
        kernel,
        grid=(tp, 2),
        in_specs=[
            pl.BlockSpec(lhs_block, lhs_place),
            pl.BlockSpec(rhs.shape, lambda t, c: (0, 0)),
        ]
        + ([] if buffer is None else [pl.BlockSpec(memory_space=pl.ANY)]),
        out_specs=pl.BlockSpec((2, 1, seq // 2, size, share), lambda t, c: (0, t, 0, first // size + c, 0))
        if by_core
        else pl.BlockSpec((seq, size, share), lambda t, c: (t, first // size + c, 0)),
        out_shape=jax.ShapeDtypeStruct(shape, bf16),
        input_output_aliases={} if buffer is None else {2: 0},
        compiler_params=pltpu.CompilerParams(vmem_limit_bytes=60 << 20),
        cost_estimate=pl.CostEstimate(
            flops=4 * tp * count * depth * width,
            bytes_accessed=4 * tp * (count + width) * depth,
            transcendentals=0,
        ),
        name="weight_terms",
    )(lhs, rhs, *([] if buffer is None else [buffer]))


def last_kernel(buffer, tokens, scale, middle, dq, small, start):
    rows, _, cols, width = tokens.shape
    tp, items, queries, local = dq.shape
    slots = small.shape[0]
    cols_here = cols // tp
    tile = rows * cols_here
    slot_width = local // 2

    def kernel(x_ref, scale_ref, middle_ref, dq_ref, w_ref, *refs):
        out_ref, sums_ref = refs[-2:]
        hat, inverse = norm_parts(x_ref[...].astype(f32).reshape(rows, cols, width))
        weights = w_ref[...].reshape(tp * local, width)
        shift_sum = jnp.zeros((1, width), f32)
        scale_sum = jnp.zeros((1, width), f32)
        for t in range(tp):
            pieces = [
                dq_ref[u, 0, t * tile : (t + 1) * tile, c * slot_width : (c + 1) * slot_width]
                for c in range(2)
                for u in range(tp)
            ]
            g = dot_nn(jnp.concatenate(pieces, axis=1), weights)
            mine = slice(t * cols_here, (t + 1) * cols_here)
            hat_t = hat[:, mine, :].reshape(tile, width)
            inverse_t = inverse[:, mine, :].reshape(tile, 1)
            shift_sum = shift_sum + jnp.sum(g, axis=0, keepdims=True)
            scale_sum = scale_sum + jnp.sum(g * hat_t, axis=0, keepdims=True)
            value = middle_ref[t, 0].astype(f32) + norm_back(
                hat_t, inverse_t, g * (1.0 + scale_ref[0])
            )
            out_ref[:, 0, mine, :] = value.reshape(rows, cols_here, width)
        sums_ref[0, 0:1, :] = shift_sum
        sums_ref[0, 1:2, :] = scale_sum

    return pl.pallas_call(
        kernel,
        grid=(items,),
        in_specs=[
            pl.BlockSpec((rows, 1, cols, width), lambda i: (0, i + start, 0, 0)),
            pl.BlockSpec((1, 1, width), lambda i: (i + start, 0, 0)),
            pl.BlockSpec((tp, 1, tile, width), lambda i: (0, i + start, 0, 0)),
            pl.BlockSpec((tp, 1, queries, local), lambda i: (0, i, 0, 0)),
            pl.BlockSpec((slots, slot_width, width), lambda i: (0, QUERY_ROWS // slot_width, 0)),
        ]
        + ([] if buffer is None else [pl.BlockSpec(memory_space=pl.ANY)]),
        out_specs=[
            pl.BlockSpec((rows, 1, cols, width), lambda i: (0, i + start, 0, 0)),
            pl.BlockSpec((1, 2, width), lambda i: (i, 0, 0)),
        ],
        out_shape=[
            jax.ShapeDtypeStruct(tokens.shape, f32),
            jax.ShapeDtypeStruct((items, 2, width), f32),
        ],
        input_output_aliases={} if buffer is None else {5: 0},
        compiler_params=pltpu.CompilerParams(vmem_limit_bytes=60 << 20),
        cost_estimate=pl.CostEstimate(
            flops=2 * items * queries * width * tp * local,
            bytes_accessed=10 * items * queries * width,
            transcendentals=0,
        ),
        name="last_kernel",
    )(tokens, scale, middle, dq, small, *([] if buffer is None else [buffer]))


def exchange(x, axis):
    return lax.all_to_all(x, axis, 0, 0, tiled=True)


def gather(x, axis):
    names = axis if isinstance(axis, tuple) else (axis,)
    count = 1
    for name in names:
        count *= lax.axis_size(name)
    return exchange(jnp.broadcast_to(x[None], (count,) + x.shape), axis)


def reduce_blocks(x, axis):
    return jnp.sum(exchange(x.astype(bf16), axis).astype(f32), axis=0)


def body(
    tokens,
    context,
    group_ids,
    source_table,
    w_query,
    w_key,
    w_value,
    w_out,
    w_self_query,
    w_self_key,
    w_self_value,
    w_self_out,
    w_up,
    w_down,
    w_deconv,
    deconv_bias,
    out_cotangent,
    plane_cotangent,
):
    rows_here, items, plane_cols, width = tokens.shape
    cols_here = out_cotangent.shape[2]
    tp = lax.axis_size("tp")
    seq = lax.axis_size("seq")
    both_axes = ("seq", "tp")
    devices = tp * seq
    local = w_query.shape[1]
    hidden_here = w_up.shape[1]
    slots = 2 * tp
    slot_heads = local // HEAD // 2
    slot_width = local // 2
    heads = slots * slot_heads
    tile = rows_here * cols_here
    half = tile // 2
    groups = devices // heads
    turns = -(-items // groups)
    share = width // seq
    fast = slot_heads == 2 and half % 16 == 0 and items == groups * turns and share % 128 == 0
    me_tp = lax.axis_index("tp")
    core = lax.axis_index("seq") % 2

    picker = (group_ids[:, None] == jnp.arange(GROUPS, dtype=jnp.int32)[None, :]).astype(f32)
    mods = jnp.dot(picker, source_table, precision=highest).reshape(items, 9, 1, width)

    def piece(index):
        return mods[:, index]

    def dot(spec, a, b):
        return jnp.einsum(spec, a, b, preferred_element_type=f32)

    def to_tile(x):
        return x.transpose(1, 0, 2, 3).reshape(items, tile, width)

    def from_tile(x):
        return x.reshape(items, rows_here, cols_here, width).transpose(1, 0, 2, 3)

    teams = [
        [(2 * pair + c) * tp + t for c in range(2) for t in range(tp)] for pair in range(seq // 2)
    ]

    def whole(x):
        return lax.all_gather(x, both_axes, axis=0, tiled=False, axis_index_groups=teams)

    def my_rows(x):
        return lax.dynamic_slice_in_dim(x, core * slot_width, slot_width, 0)

    def my_columns(x):
        size = x.shape[1] // 2
        return lax.dynamic_slice_in_dim(x, core * size, size, 1)

    key_value = jnp.stack(
        [
            my_columns(w_self_key).T.reshape(slot_heads, HEAD, width),
            my_columns(w_self_value).T.reshape(slot_heads, HEAD, width),
        ],
        axis=1,
    ).reshape(2 * slot_width, width)
    small = whole(
        jnp.concatenate(
            [
                key_value,
                my_columns(w_self_query).T,
                my_rows(w_self_out),
                my_rows(w_out),
                my_columns(w_query).T,
            ],
            axis=0,
        )
    )
    cuts = [slot_width * k for k in (0, 2, 3, 4, 5, 6)]
    kv_slots, q_slots, so_slots, out_slots, query_slots = [
        small[:, a:b] for a, b in zip(cuts[:-1], cuts[1:])
    ]
    up_slots = whole(my_columns(w_up))
    down_slots = whole(
        lax.dynamic_slice_in_dim(w_down, core * (hidden_here // 2), hidden_here // 2, 0)
    )

    def by_tp(x):
        return x.reshape(2, tp, slot_width, width).transpose(1, 0, 2, 3).reshape(tp, local, width)

    incoming = plane_cotangent.reshape(2 * rows_here, items, 2 * cols_here, COUT)
    plane_row = (lax.axis_index("seq") * rows_here + jnp.arange(rows_here, dtype=jnp.int32)) % PLANE
    upper_keep = (plane_row != 0).astype(f32)
    lower_keep = (plane_row != PLANE - 1).astype(f32)
    grad_edges = with_halo(incoming, (("seq", 0), ("tp", 2)), 1)
    if fast:
        first_in, queries = first_kernel(tokens, piece(0), piece(1), w_query, tp)
    else:
        ordered = (
            tokens.reshape(rows_here, items, tp, cols_here, width)
            .transpose(1, 2, 0, 3, 4)
            .reshape(items, tp * tile, width)
        )
        first_hat, first_inv = norm_parts(ordered.astype(f32))
        first_in = (first_hat * (1.0 + piece(1)) + piece(0)).astype(bf16)
        queries = dot("iqd,de->iqe", first_in, w_query).astype(bf16) * bf16(0.125)
    image = context.transpose(1, 0, 2)
    queries, grad_edges = lax.optimization_barrier((queries, grad_edges))
    keys, values_t = key_value_kernel(image, w_key, w_value.T)
    upper_mask = upper_keep.astype(bf16)[:, None, None, None]
    lower_mask = lower_keep.astype(bf16)[:, None, None, None]
    first_pair = grad_edges[:-2].reshape(rows_here, 2, items, 2 * cols_here + 2, COUT)
    last_pair = grad_edges[2:].reshape(rows_here, 2, items, 2 * cols_here + 2, COUT)
    row_taps = jnp.stack(
        [
            first_pair[:, 0] * upper_mask,
            first_pair[:, 1],
            last_pair[:, 0],
            last_pair[:, 1] * lower_mask,
        ],
        axis=3,
    )
    left_pair = row_taps[:, :, :-2].reshape(rows_here, items, cols_here, 2, 4, COUT)
    right_pair = row_taps[:, :, 2:].reshape(rows_here, items, cols_here, 2, 4, COUT)
    tap_grads = jnp.stack(
        [
            left_pair[:, :, :, 0],
            left_pair[:, :, :, 1],
            right_pair[:, :, :, 0],
            right_pair[:, :, :, 1],
        ],
        axis=4,
    )
    tap_grads = tap_grads.reshape(rows_here, items, cols_here, 16 * COUT)
    grad_result = to_tile(out_cotangent.astype(f32) + dot("rict,dt->ricd", tap_grads, w_deconv))
    grad_bias = jnp.sum(incoming.astype(f32), axis=(0, 1, 2))
    grad_mlp = (piece(8) * grad_result).astype(bf16)
    mixed, mixed_wide, cross_logs = cross_forward(queries, keys, values_t, tp)
    mixed_tile = exchange(mixed, "tp")
    if fast:
        branch_a = out_project(mixed_tile, small).reshape(items, tile, width)
    else:
        branch_a = dot("time,tef->imf", mixed_tile, by_tp(out_slots))
    residual = to_tile(lax.dynamic_slice_in_dim(tokens, me_tp * cols_here, cols_here, 2)).astype(f32)
    middle, self_in = norm_forward(residual, branch_a, piece(2), piece(3), piece(4))

    flat = (items * tile, width)
    spare = groups * turns - items

    def spread_items(x):
        if spare:
            x = jnp.pad(x, ((0, 0), (0, spare)) + ((0, 0),) * (x.ndim - 2))
        return x.reshape((slots, groups, turns) + x.shape[2:])

    def pack_keys(x):
        x = spread_items(x.reshape(slots, items, tile, slot_heads, 2 * HEAD))
        return x.transpose(2, 1, 0, 4, 3, 5).reshape(turns, devices, tile, 2 * HEAD)

    def unpack_keys(x):
        x = x.reshape(turns, groups, slots, slot_heads, tile, 2 * HEAD).transpose(2, 1, 0, 4, 3, 5)
        x = x.reshape(slots, groups * turns, tile, 2 * slot_width)[:, :items]
        return x.reshape(slots, items * tile, 2 * slot_width)

    def pack_rows(x):
        x = spread_items(x.reshape(slots, items, 2, half, slot_heads, HEAD))
        return x.transpose(2, 1, 0, 5, 4, 3, 6).reshape(turns, devices, half, 2 * HEAD)

    def unpack_rows(x):
        x = x.reshape(turns, groups, slots, slot_heads, half, 2, HEAD).transpose(2, 1, 0, 5, 4, 3, 6)
        x = x.reshape(slots, groups * turns, tile, slot_width)[:, :items]
        return x.reshape(slots, items * tile, slot_width)

    if fast:
        sends = project_pack(self_in.reshape(flat), small, items, turns, groups)
        sends = sends.reshape(turns, devices, 3 * half, 2 * HEAD)
        sends = [sends[turn] for turn in range(turns)]
    else:
        kv_sends = pack_keys(dot("nd,xed->xne", self_in.reshape(flat), kv_slots).astype(bf16))
        q_sends = dot("nd,xed->xne", self_in.reshape(flat), q_slots).astype(bf16)
        q_sends = pack_rows(q_sends * bf16(0.125))
        parts = [
            [
                exchange(kv_sends[turn], both_axes).reshape(devices * tile, 2 * HEAD),
                exchange(q_sends[turn], both_axes).reshape(devices * half, 2 * HEAD),
            ]
            for turn in range(turns)
        ]
    if fast:
        parts, forward = [], []
        for turn in range(turns):
            if turn >= 2:
                sends[turn], forward[turn - 2] = lax.optimization_barrier(
                    (sends[turn], forward[turn - 2])
                )
            arrived = exchange(sends[turn], both_axes)
            if turn == 0:
                arrived, grad_result, grad_mlp = lax.optimization_barrier(
                    (arrived, grad_result, grad_mlp)
                )
            parts.append([arrived])
            forward.append(self_forward(parts[turn], devices, half))
    else:
        forward = [self_forward(parts[turn], devices, half) for turn in range(turns)]
    outs = [x[0].reshape(devices, half, 2 * HEAD) for x in forward]
    if fast and turns > 2:
        joined, _ = lax.optimization_barrier((jnp.stack(outs[:-1], axis=1), parts[-1][0]))
        joined = exchange(joined, both_axes)
        so_back = [joined[:, turn] for turn in range(turns - 1)]
        so_back.append(exchange(outs[-1], both_axes))
    else:
        so_back = [exchange(so, both_axes) for so in outs]
    if fast:
        blocks = [x.reshape(groups, slots, 2, half, 2 * HEAD) for x in so_back]
        so_tile, branch_s = unpack_project(blocks, small, items, groups)
    else:
        so_tile = unpack_rows(jnp.stack(so_back)).transpose(1, 0, 2)
        branch_s = dot("nxe,xed->nd", so_tile, so_slots)
        so_tile = so_tile.reshape(items * tile, heads * HEAD)
    branch_s = branch_s.reshape(items, tile, width)
    middle_two, second_in = norm_forward(middle, branch_s, piece(5), piece(6), piece(7))

    active, grad_hidden, branch_b, grad_second = feed_forward(
        second_in.reshape(flat), grad_mlp.reshape(flat), up_slots, down_slots
    )
    branch_b = branch_b.reshape(items, tile, width)
    grad_second = grad_second.reshape(items, tile, width)
    result = middle_two + piece(8) * branch_b
    out_tile = from_tile(result.astype(bf16))

    grad_mid_two, grad_self, _, sums_b = norm_backward(
        grad_result, middle_two, grad_second, branch_b, piece(7), piece(5)
    )

    widened = with_halo(out_tile, (("seq", 0), ("tp", 2)), 1)

    def by_device(x):
        lead = x.shape[0] // tp
        x = x.reshape(lead, tp, x.shape[1], seq, share).transpose(1, 3, 0, 2, 4)
        return x.reshape(devices, -1, share).astype(bf16)

    def of_cores(x):
        return x.reshape((tp, seq // 2, 2) + x.shape[1:]).transpose(2, 0, 1, 3, 4)

    def total_near(terms, after):
        keep = lax.dynamic_index_in_dim(terms, core, 0, False)
        give = lax.dynamic_index_in_dim(terms, 1 - core, 0, False)
        got = lax.ppermute(give, "seq", [(i, i ^ 1) for i in range(seq)])
        got, _ = lax.optimization_barrier((got, after))
        x = (keep.astype(f32) + got.astype(f32)).astype(bf16)
        return lax.psum_scatter(x, "tp", scatter_dimension=0, tiled=True)[0]

    def total_far(x, after, *cuts):
        x, _ = lax.optimization_barrier((x, after))
        lines = [list(range(c, seq, 2)) for c in range(2)]
        x = lax.psum_scatter(x, "seq", scatter_dimension=0, axis_index_groups=lines, tiled=True)[0]
        return jnp.split(x.astype(f32), cuts, axis=0)

    def total(terms, *cuts):
        summed = lax.psum_scatter(terms, ("tp", "seq"), scatter_dimension=0, tiled=True)[0]
        return jnp.split(summed.astype(f32), cuts, axis=0)

    terms_deconv = dot("ricd,rict->dt", out_tile, tap_grads).astype(bf16)
    piece_rows = width // devices
    terms_deconv = (
        terms_deconv.reshape(devices, piece_rows, -1, share)
        .transpose(0, 2, 1, 3)
        .reshape(devices, -1, share)
    )
    size_b = (hidden_here // 2, hidden_here, 2 * hidden_here)
    if fast:
        shape = (2, tp, seq // 2, size_b[2] + terms_deconv.shape[1], share)
        hidden_block = (1, items * tile, size_b[0])

        def slot_place(t, c):
            return (c * tp + t, 0, 0)

        terms_b = None
        for lhs, rhs, first in (
            (grad_hidden, second_in, 0),
            (active, grad_mlp, size_b[1]),
        ):
            terms_b = weight_terms(
                terms_b, shape, lhs, hidden_block, slot_place, rhs.reshape(flat), tp, size_b[0], first
            )
        terms_b = lax.dynamic_update_slice_in_dim(terms_b, of_cores(terms_deconv), size_b[2], 3)
    else:
        terms_b = jnp.concatenate(
            [
                by_device(dot("xnf,nd->xfd", grad_hidden, second_in.reshape(flat))),
                by_device(dot("xnf,nd->xfd", active, grad_mlp.reshape(flat))),
                terms_deconv,
            ],
            axis=1,
        )
        terms_b = of_cores(terms_b)

    if fast:
        dso_send = back_pack(grad_self.reshape(flat), small, items, turns, groups)
        dso_send = dso_send.reshape(turns, devices, half, 2 * HEAD)
    else:
        dso_send = pack_rows(dot("nd,xed->xne", grad_self.reshape(flat), so_slots).astype(bf16))
    dso_send = [dso_send[turn] for turn in range(turns)]
    dso_mine, backward = [], []
    for turn in range(turns):
        if turn >= 2:
            dso_send[turn], backward[turn - 2] = lax.optimization_barrier(
                (dso_send[turn], backward[turn - 2])
            )
        arrived = exchange(dso_send[turn], both_axes).reshape(devices * half, 2 * HEAD)
        if turn == 0:
            arrived, terms_b, widened = lax.optimization_barrier((arrived, terms_b, widened))
        dso_mine.append(arrived)
        backward.append(
            self_backward(parts[turn], dso_mine[turn], *forward[turn][1:], devices, half)
        )
    taps = dot("ricd,dt->rict", widened, w_deconv)
    taps = taps.reshape(rows_here + 2, items, cols_here + 2, 4, 4, COUT)
    planes = spread_taps(
        taps, upper_keep[:, None, None, None, None], lower_keep[:, None, None, None, None]
    )
    planes = planes + jnp.tile(deconv_bias, 2 * cols_here)

    near_b = total_near(terms_b, (backward[0][0], dso_mine[min(1, turns - 1)]))
    if fast:
        blocks = [
            exchange(x[0], both_axes).reshape(groups, slots, 2, 3 * half, 2 * HEAD)
            for x in backward
        ]
        blocks[-1], planes = lax.optimization_barrier((blocks[-1], planes))
        grad_projected, grad_third = unpack_back(blocks, small, items, groups)
    else:
        dkv = [exchange(x[0].reshape(devices, tile, 2 * HEAD), both_axes) for x in backward]
        dq = [exchange(x[1].reshape(devices, half, 2 * HEAD), both_axes) for x in backward]
        grad_projected = jnp.concatenate(
            [unpack_keys(jnp.stack(dkv)), unpack_rows(jnp.stack(dq))], axis=2
        )
        grad_third = dot(
            "xne,xed->nd", grad_projected, jnp.concatenate([kv_slots, q_slots], axis=1)
        )
    grad_up, grad_down, grad_deconv = total_far(near_b, grad_third, *size_b[1:])
    grad_third = grad_third.reshape(items, tile, width)
    grad_middle, grad_attn, middle_low, sums_s = norm_backward(
        grad_mid_two, middle, grad_third, branch_s, piece(4), piece(2)
    )

    grad_gate_a = jnp.sum(grad_middle * branch_a, axis=1)
    if fast:
        do_send = out_back(grad_attn.reshape(flat), small, mixed.shape)
    else:
        do_send = dot("imf,tef->time", grad_attn, by_tp(out_slots)).astype(bf16)
    do_mine = exchange(do_send, "tp")
    middle_all = gather(middle_low, "tp")
    early = jnp.concatenate([grad_gate_a[:, None], sums_s, sums_b], axis=1)
    early = early.transpose(1, 0, 2).reshape(7 * items, width)
    early = jnp.concatenate(
        [early, jnp.pad(grad_bias, (0, width - COUT))[None]], axis=0
    )
    spots = -(-early.shape[0] // (16 * tp)) * 16
    early = jnp.pad(early, ((0, spots * tp - early.shape[0]), (0, 0))).reshape(tp, spots, width)
    early = by_device(early)
    size_a = [slot_width * k for k in (6, 8, 10)]
    if fast:
        shape = (devices, size_a[2] + early.shape[1], share)
        terms_a = weight_terms(
            None,
            shape,
            grad_projected,
            (1, items * tile, 3 * slot_width),
            lambda t, c: (c * tp + t, 0, 0),
            self_in.reshape(flat),
            tp,
            3 * slot_width,
            0,
        )
        terms_a = weight_terms(
            terms_a,
            shape,
            so_tile,
            (items * tile, slot_width),
            lambda t, c: (0, c * tp + t),
            grad_self.reshape(flat),
            tp,
            slot_width,
            size_a[0],
        )
        terms_a = weight_terms(
            terms_a,
            shape,
            mixed_tile,
            (1, items, tile, slot_width),
            lambda t, c: (t, 0, 0, c),
            grad_attn.reshape(flat),
            tp,
            slot_width,
            size_a[1],
        )
        terms_a = lax.dynamic_update_slice_in_dim(terms_a, early, size_a[2], 1)
    else:
        so_terms = dot("ne,nd->ed", so_tile, grad_self.reshape(flat))
        terms_a = jnp.concatenate(
            [
                by_device(dot("xne,nd->xed", grad_projected, self_in.reshape(flat))),
                by_device(so_terms.reshape(slots, slot_width, width)),
                by_device(dot("time,imf->tef", mixed_tile, grad_attn)),
                early,
            ],
            axis=1,
        )
    do_mine, terms_a = lax.optimization_barrier((do_mine, terms_a))
    terms_a, grad_up = lax.optimization_barrier((terms_a, grad_up))
    grad_three, grad_self_out, grad_out, grad_early = total(terms_a, *size_a)
    first_part = items - items // 3
    cross = (queries, do_mine, mixed_wide, cross_logs, keys, values_t)
    one = cross_backward(*cross, 0, first_part)
    one, middle_all = lax.optimization_barrier((one, middle_all))
    dq_one = gather(one[0], "tp")
    do_late, _ = lax.optimization_barrier((do_mine, one[0]))
    two = cross_backward(queries, do_late, *cross[2:], first_part, items - first_part)
    one, two, dq_one = lax.optimization_barrier((one, two, dq_one))
    dq_two = gather(two[0], "tp")
    grad_query = dot("iqd,iqe->de", first_in, jnp.concatenate([one[0], two[0]], axis=0))
    two, dq_two, grad_query = lax.optimization_barrier((two, dq_two, grad_query))
    grad_three = grad_three.reshape(2, 3 * slot_width, share)
    grad_pair = grad_three[:, : 2 * slot_width].reshape(2, slot_heads, 2, HEAD, share)
    grad_self_key = grad_pair[:, :, 0].reshape(local, share).T
    grad_self_value = grad_pair[:, :, 1].reshape(local, share).T
    grad_self_query = grad_three[:, 2 * slot_width :].reshape(local, share).T

    def by_seq(x):
        return x.reshape((seq, x.shape[0] // seq) + x.shape[1:]).astype(bf16)

    grad_image = (
        key_value_grads(one[1], one[2], image, 0) + key_value_grads(two[1], two[2], image, first_part)
    ).T
    last = jnp.concatenate(
        [
            by_seq(grad_query),
            by_seq(grad_image[:, :local]),
            by_seq(grad_image[:, local:]),
        ],
        axis=1,
    )
    grad_deconv, grad_image = lax.optimization_barrier((grad_deconv, grad_image))
    grad_deconv = grad_deconv.reshape(-1, piece_rows, share).transpose(1, 0, 2)
    grad_deconv = lax.all_gather(
        grad_deconv.reshape(piece_rows, 16 * COUT).astype(bf16), ("tp", "seq"), axis=0, tiled=True
    )
    last, dq_one, dq_two = lax.optimization_barrier((last, dq_one, dq_two))
    last = jnp.sum(exchange(last, "seq").astype(f32), axis=0)
    if fast:
        grad_tokens, late_one = last_kernel(None, tokens, piece(1), middle_all, dq_one, small, 0)
        grad_tokens, late_two = last_kernel(
            grad_tokens, tokens, piece(1), middle_all, dq_two, small, first_part
        )
        late = jnp.concatenate([late_one, late_two], axis=0).transpose(1, 0, 2)
    else:
        dq_all = jnp.concatenate([dq_one, dq_two], axis=1)
        grad_first = dot("tiqe,ted->iqd", dq_all, by_tp(query_slots))
        grad_shift_a = jnp.sum(grad_first, axis=1)
        grad_scale_a = jnp.sum(grad_first * first_hat, axis=1)
        grad_tokens = middle_all.astype(f32).transpose(1, 0, 2, 3).reshape(
            items, tp * tile, width
        ) + norm_back(first_hat, first_inv, grad_first * (1.0 + piece(1)))
        grad_tokens = (
            grad_tokens.reshape(items, tp, rows_here, cols_here, width)
            .transpose(2, 0, 1, 3, 4)
            .reshape(rows_here, items, plane_cols, width)
        )
        late = jnp.stack([grad_shift_a, grad_scale_a], axis=0)

    late, last = lax.optimization_barrier((late, last))
    part = 2 * items * width // tp
    mine = lax.dynamic_slice_in_dim(late.reshape(-1, share), me_tp * (part // share), part // share, 0)
    sums = gather(jnp.concatenate([mine, grad_early], axis=0), ("tp", "seq"))
    sums = sums.reshape(tp, seq, part // share + spots, share)
    late = jnp.sum(sums[:, :, : part // share], axis=1).reshape(2, items, width)
    early = sums[:, :, part // share :].transpose(0, 2, 1, 3).reshape(tp * spots, width)
    grad_bias = early[7 * items, :COUT]
    early = early[: 7 * items].reshape(7, items, width)
    depth = (last.shape[0] - share) // 2
    grad_query, grad_key, grad_value = (
        last[:share],
        last[share : share + depth],
        last[share + depth :],
    )
    late, grad_deconv = lax.optimization_barrier((late, grad_deconv))
    grad_mods = jnp.concatenate([late, early], axis=0).transpose(1, 0, 2)
    grad_table = jnp.dot(picker.T, grad_mods.reshape(items, 9 * width), precision=highest)
    return (
        out_tile,
        planes,
        grad_tokens,
        grad_query,
        grad_key,
        grad_value,
        grad_out,
        grad_self_query,
        grad_self_key,
        grad_self_value,
        grad_self_out.reshape(local, share),
        grad_up.T,
        grad_down,
        grad_deconv.astype(f32),
        grad_bias,
        grad_table,
    )


def solution(mesh):
    in_specs = (
        P("seq", None, None, None),
        P(),
        P(),
        P(),
        P(None, "tp"),
        P(None, "tp"),
        P(None, "tp"),
        P("tp", None),
        P(None, "tp"),
        P(None, "tp"),
        P(None, "tp"),
        P("tp", None),
        P(None, "tp"),
        P("tp", None),
        P(),
        P(),
        P("seq", None, "tp", None),
        P("seq", None, "tp"),
    )
    out_specs = (
        P("seq", None, "tp", None),
        P("seq", None, "tp"),
        P("seq", None, None, None),
        P("seq", "tp"),
        P("seq", "tp"),
        P("seq", "tp"),
        P("tp", "seq"),
        P("seq", "tp"),
        P("seq", "tp"),
        P("seq", "tp"),
        P("tp", "seq"),
        P("seq", "tp"),
        P("tp", "seq"),
        P(),
        P(),
        P(),
    )
    return jax.shard_map(body, mesh=mesh, in_specs=in_specs, out_specs=out_specs, check_vma=False)
```
